32 devices in a mesh: groups: 2 (over y), dp: 4 (over z), tensor: 2 (over x), replica: 2 (over core).
Axes of the slice: x: 2, y: 2, z: 4, core: 2. Of those that a mesh axis runs over, the one named last changes fastest.
Arguments:
- tokens: bfloat16 [2048, 4096], P(('groups', 'dp')), parts along dimension 0, may hold values from -6 to 6
- upstream: bfloat16 [2048, 4096], P(('groups', 'dp'), ('tensor', 'replica')), parts along dimension 0, may hold values from -6 to 6
- blocks: bfloat16 [1024, 128, 128], P(('dp', 'tensor', 'replica')), may hold values from -0.125 to 0.125
- block_ids: int32 [1024], P(('dp', 'tensor', 'replica')), may hold values from 0 to 256, as said below
Outputs:
- projected: bfloat16 [2048, 4096], P(('groups', 'dp'), ('tensor', 'replica')), parts along dimension 0
- token_grad: bfloat16 [2048, 4096], P(('groups', 'dp')), parts along dimension 0
- block_grad: bfloat16 [2048, 128, 128], P(('groups', 'dp', 'tensor', 'replica')), parts along dimension 0
The draws below stay inside these ranges and needn't reach their ends.
There are 2 independent parts, one for each index of `groups`. The reference program is written for one: setup_inputs(seed, part) draws one part's arguments, and reference() takes and returns one part's arrays. A program takes and returns all parts, laid end to end along the dimension named above; an argument that names none is the same for every part. Nothing has to cross between parts.
Inputs may be any that keep to these rules, and one draw needn't show every extreme that they name: `block_ids`: within each slab, every block column holds exactly half of the 32 block rows, each filled block stands in exactly one slot, empty slots carry the id (32) * (4096 // (128 * 2 * 2)), and some device of each slab has all 64 slots filled.
All inputs are finite; a program needn't handle non-finite values.
Results may differ from the reference program's by a relative error of at most 0.012.
Values may be sent and summed in bfloat16 or wider, within the bound.
No kernel may reach another device: no remote copies, remote signals or barrier semaphores. Data moves between devices by JAX's collectives and lax.ppermute only.
A program may use at most 128 MiB of HBM per device.

```python
import jax
import jax.numpy as jnp
from jax import lax

D = 4096
QW = 4096
BLK = 128
TOK = 256
TOKENS = 1024
CAP = 64
SLOTS = 1024
N_DP = 4
N_TENSOR = 2
N_REPLICA = 2


def draw_block_ids(key, part):
    key = jax.random.fold_in(key, 5)
    slabs_u = N_TENSOR * N_REPLICA
    rows_n = D // BLK
    cols_n = QW // (BLK * slabs_u)
    total_b = rows_n * cols_n
    nonzero = total_b // 2
    middle = nonzero // N_DP

    def one_slab(slab_key):
        first, second, third, fourth = jax.random.split(slab_key, 4)
        col_keys = jax.random.split(first, cols_n)
        chosen = jax.vmap(lambda one_key: jax.random.permutation(one_key, rows_n)[:rows_n // 2])(col_keys)
        listed = (chosen * cols_n + jnp.arange(cols_n, dtype=jnp.int32)[:, None]).reshape(-1)
        listed = jax.random.permutation(second, listed)
        deltas = jax.random.randint(third, (N_DP // 2,), 0, middle + 1)
        deltas = deltas.at[0].set(middle)
        paired = jnp.stack([middle + deltas, middle - deltas], 1).reshape(-1)
        counts = jax.random.permutation(fourth, paired)
        offsets = jnp.cumsum(counts) - counts
        place = jnp.arange(2 * middle, dtype=jnp.int32)
        where_at = jnp.clip(offsets[:, None] + place[None, :], 0, nonzero - 1)
        valid = place[None, :] < counts[:, None]
        return jnp.where(valid, listed[where_at], total_b)
    slabs = jax.vmap(one_slab)(jax.random.split(key, slabs_u))
    return slabs.transpose(1, 0, 2).reshape(-1).astype(jnp.int32)


def block_scale(key, dims, cuts, least, high):
    def one(position, shards_of):
        heights = jax.random.uniform(jax.random.fold_in(jax.random.fold_in(key, 6), position), (shards_of,), jnp.float32, least / len(cuts), high / len(cuts))
        return jnp.repeat(jnp.exp(heights), dims[position] // shards_of).reshape((-1,) + (1,) * (len(dims) - position - 1))

    factor_of = one(*cuts[0])
    for cut in cuts[1:]:
        factor_of = factor_of * one(*cut)
    return factor_of


def centred(stream_key, shape, deviation, limit, cuts=(), held_as=jnp.bfloat16):
    result = deviation * jax.random.normal(stream_key, shape, jnp.float32)
    if cuts:
        result = result * block_scale(stream_key, shape, cuts, -0.22, 0.18)
    return jnp.clip(result, -limit, limit).astype(held_as)


def setup_inputs(seed: int = 0, part: int = 0) -> dict:
    splits = jax.random.split(jax.random.key(seed), 5)
    own_keys = jax.random.split(jax.random.fold_in(splits[4], part), 5)
    tokens = centred(own_keys[0], (TOKENS, D), 1.0, 6.0, ((0, 4),))
    upstream = centred(own_keys[1], (TOKENS, QW), 1.0, 6.0, ((0, 4), (1, 4)))
    blocks = centred(splits[2], (SLOTS, BLK, BLK), (D // 2) ** -0.5, 0.125, ((0, 16),))
    block_ids = draw_block_ids(jax.random.fold_in(splits[4], 71), part)
    return {"tokens": tokens, "upstream": upstream, "blocks": blocks, "block_ids": block_ids}


def reference(tokens, upstream, blocks, block_ids):
    slabs_u = N_TENSOR * N_REPLICA
    rows_n = D // BLK
    cols_t = QW // (BLK * slabs_u)
    total_b = rows_n * cols_t
    slot = jnp.arange(block_ids.shape[0], dtype=jnp.int32)
    slab_idx = (slot // CAP) % slabs_u
    filled = block_ids < total_b
    row = jnp.where(filled, block_ids // cols_t, rows_n).astype(jnp.int32)
    col = (slab_idx * cols_t + block_ids % cols_t).astype(jnp.int32)
    grid = jnp.zeros((rows_n, cols_t * slabs_u, BLK, BLK), jnp.float32)
    grid = grid.at[row, col].set(blocks.astype(jnp.float32), mode="drop")
    weight = grid.transpose(0, 2, 1, 3).reshape(D, QW).astype(jnp.bfloat16)
    projected = jnp.dot(tokens, weight, preferred_element_type=jnp.float32).astype(jnp.bfloat16)
    token_grad = jnp.dot(upstream, weight.T, preferred_element_type=jnp.float32).astype(jnp.bfloat16)
    safe_row = jnp.minimum(row, rows_n - 1)
    slabs = TOKENS // TOK
    x_blocks = tokens.reshape(slabs, TOK, rows_n, BLK)
    d_blocks = upstream.reshape(slabs, TOK, cols_t * slabs_u, BLK)
    keep = filled.astype(jnp.float32)[:, None, None]

    def add_slab(total, pair):
        x_slab, d_slab = pair
        x_sel = x_slab[:, safe_row].astype(jnp.float32)
        d_sel = d_slab[:, col].astype(jnp.float32)
        term = jnp.einsum('tsk,tsj->skj', x_sel, d_sel) * keep
        return total + term.astype(jnp.bfloat16).astype(jnp.float32), None

    start = jnp.zeros((block_ids.shape[0], BLK, BLK), jnp.float32)
    total, unused = lax.scan(add_slab, start, (x_blocks, d_blocks))
    return projected, token_grad, total.astype(jnp.bfloat16)
```

```python
import functools

import jax
import jax.numpy as jnp
from jax import lax
from jax.experimental import pallas as pl
from jax.experimental.pallas import tpu as pltpu
from jax.sharding import PartitionSpec as P

VMEM_LIMIT = 60 * 1024 * 1024
INNER = ("tensor", "replica")


def whole(space=pltpu.VMEM):
    return pl.BlockSpec(memory_space=space)


def project_kernel(ids, blocks, tokens, upstream, proj, back, weight):
    slots, size = blocks.shape[0], blocks.shape[1]
    depth, width = weight.shape
    cols_n = width // size
    total = (depth // size) * cols_n
    weight[...] = jnp.zeros_like(weight)

    @pl.loop(0, slots)
    def place(s):
        b = ids[s]

        @pl.when(b < total)
        def put():
            r = pl.multiple_of((b // cols_n) * size, size)
            c = pl.multiple_of((b % cols_n) * size, size)
            weight[pl.ds(r, size), pl.ds(c, size)] = blocks[s]

    step = 256

    @pl.loop(0, width // step)
    def forward(n):
        c = pl.multiple_of(n * step, step)
        proj[:, pl.ds(c, step)] = jnp.dot(
            tokens[...], weight[:, pl.ds(c, step)], preferred_element_type=jnp.float32
        ).astype(proj.dtype)

    @pl.loop(0, depth // step)
    def backward(n):
        r = pl.multiple_of(n * step, step)
        back[:, pl.ds(r, step)] = lax.dot_general(
            upstream[...],
            weight[pl.ds(r, step), :],
            (((1,), (1,)), ((), ())),
            preferred_element_type=jnp.float32,
        ).astype(back.dtype)


def project(ids, blocks, tokens, upstream):
    rows, depth = tokens.shape
    width = upstream.shape[1]
    return pl.pallas_call(
        project_kernel,
        out_shape=(
            jax.ShapeDtypeStruct((rows, width), jnp.bfloat16),
            jax.ShapeDtypeStruct((rows, depth), jnp.bfloat16),
        ),
        in_specs=[whole(pltpu.SMEM), whole(), whole(), whole()],
        out_specs=(whole(), whole()),
        scratch_shapes=[pltpu.VMEM((depth, width), jnp.bfloat16)],
        compiler_params=pltpu.CompilerParams(vmem_limit_bytes=VMEM_LIMIT),
        cost_estimate=pl.CostEstimate(
            flops=4 * rows * depth * width,
            bytes_accessed=blocks.size * 2 + rows * (depth + width) * 4,
            transcendentals=0,
        ),
        name="project",
    )(ids, blocks, tokens, upstream)


def block_grad_kernel(ids, tokens, upstream, grads):
    slots, size = grads.shape[0], grads.shape[1]
    parts, slabs, _, part_width = tokens.shape
    cols_n = upstream.shape[2] // size
    per_part = part_width // size
    total = parts * per_part * cols_n

    @pl.loop(0, slots)
    def one(s):
        b = ids[s]

        @pl.when(b < total)
        def fill():
            row = b // cols_n
            part = row // per_part
            r = pl.multiple_of((row % per_part) * size, size)
            c = pl.multiple_of((b % cols_n) * size, size)
            acc = jnp.zeros((size, size), jnp.float32)
            for k in range(slabs):
                acc += lax.dot_general(
                    tokens[part, k, :, pl.ds(r, size)],
                    upstream[k, :, pl.ds(c, size)],
                    (((0,), (0,)), ((), ())),
                    preferred_element_type=jnp.float32,
                )
            grads[s] = acc.astype(grads.dtype)

        @pl.when(b >= total)
        def clear():
            grads[s] = jnp.zeros((size, size), grads.dtype)


def block_grads(ids, tokens, upstream, size):
    slots = ids.shape[0]
    parts, slabs, rows, part_width = tokens.shape
    return pl.pallas_call(
        block_grad_kernel,
        out_shape=jax.ShapeDtypeStruct((slots, size, size), jnp.bfloat16),
        in_specs=[whole(pltpu.SMEM), whole(), whole()],
        out_specs=whole(),
        compiler_params=pltpu.CompilerParams(vmem_limit_bytes=VMEM_LIMIT),
        cost_estimate=pl.CostEstimate(
            flops=2 * slots * slabs * rows * size * size,
            bytes_accessed=2 * (tokens.size + upstream.size + slots * size * size),
            transcendentals=0,
        ),
        name="block_grads",
    )(ids, tokens, upstream)


def general_body(tokens, upstream, blocks, block_ids):
    size = blocks.shape[1]
    all_blocks = lax.all_gather(blocks, "dp", axis=0, tiled=True)
    all_ids = lax.all_gather(block_ids, "dp", axis=0, tiled=True)
    proj, back = project(all_ids, all_blocks, tokens, upstream)
    terms = block_grads(all_ids, tokens[None, None], upstream[None], size)
    grads = lax.psum_scatter(terms, "dp", scatter_dimension=0, tiled=True)
    return proj, lax.psum(back, INNER), grads


def body(tokens, upstream, blocks, block_ids):
    size = blocks.shape[1]
    inner_n = lax.axis_size("tensor") * lax.axis_size("replica")
    inner = lax.axis_index(INNER)
    quarter_width = tokens.shape[1] // inner_n
    all_blocks = lax.all_gather(blocks, "dp", axis=0, tiled=True)
    all_ids = lax.all_gather(block_ids, "dp", axis=0, tiled=True)
    quarter = lax.dynamic_slice_in_dim(tokens, inner * quarter_width, quarter_width, 1)
    quarters = lax.all_gather(quarter, "dp")
    all_tokens = lax.all_gather(quarters, INNER)
    all_upstream = lax.all_gather(upstream, "dp")
    proj, back = project(all_ids, all_blocks, tokens, upstream)
    token_grad = lax.psum(back, INNER)
    grads = block_grads(block_ids, all_tokens, all_upstream, size)
    return proj, token_grad, grads


def solution(mesh):
    small = mesh.shape["dp"] <= 4
    return jax.shard_map(
        body if small else general_body,
        mesh=mesh,
        in_specs=(
            P(("groups", "dp"), None),
            P(("groups", "dp"), INNER),
            P(("dp",) + INNER, None, None),
            P(("dp",) + INNER),
        ),
        out_specs=(
            P(("groups", "dp"), INNER),
            P(("groups", "dp"), None),
            P(("groups", "dp") + INNER, None, None),
        ),
        check_vma=False,
    )
```

```python
import functools

import jax
import jax.numpy as jnp
from jax import lax
from jax.experimental import pallas as pl
from jax.experimental.pallas import tpu as pltpu
from jax.sharding import PartitionSpec as P

VMEM_LIMIT = 60 * 1024 * 1024
INNER = ("tensor", "replica")


def whole(space=pltpu.VMEM):
    return pl.BlockSpec(memory_space=space)


def project_kernel(ids, blocks, tokens, upstream, proj, back, weight):
    slots, size = blocks.shape[0], blocks.shape[1]
    depth, width = weight.shape
    cols_n = width // size
    total = (depth // size) * cols_n
    weight[...] = jnp.zeros_like(weight)

    @pl.loop(0, slots)
    def place(s):
        b = ids[s]

        @pl.when(b < total)
        def put():
            r = pl.multiple_of((b // cols_n) * size, size)
            c = pl.multiple_of((b % cols_n) * size, size)
            weight[pl.ds(r, size), pl.ds(c, size)] = blocks[s]

    step = 256

    @pl.loop(0, width // step)
    def forward(n):
        c = pl.multiple_of(n * step, step)
        proj[:, pl.ds(c, step)] = jnp.dot(
            tokens[...], weight[:, pl.ds(c, step)], preferred_element_type=jnp.float32
        ).astype(proj.dtype)

    @pl.loop(0, depth // step)
    def backward(n):
        r = pl.multiple_of(n * step, step)
        back[:, pl.ds(r, step)] = lax.dot_general(
            upstream[...],
            weight[pl.ds(r, step), :],
            (((1,), (1,)), ((), ())),
            preferred_element_type=jnp.float32,
        ).astype(back.dtype)


def project(ids, blocks, tokens, upstream):
    rows, depth = tokens.shape
    width = upstream.shape[1]
    return pl.pallas_call(
        project_kernel,
        out_shape=(
            jax.ShapeDtypeStruct((rows, width), jnp.bfloat16),
            jax.ShapeDtypeStruct((rows, depth), jnp.bfloat16),
        ),
        in_specs=[whole(pltpu.SMEM), whole(), whole(), whole()],
        out_specs=(whole(), whole()),
        scratch_shapes=[pltpu.VMEM((depth, width), jnp.bfloat16)],
        compiler_params=pltpu.CompilerParams(vmem_limit_bytes=VMEM_LIMIT),
        cost_estimate=pl.CostEstimate(
            flops=4 * rows * depth * width,
            bytes_accessed=blocks.size * 2 + rows * (depth + width) * 4,
            transcendentals=0,
        ),
        name="project",
    )(ids, blocks, tokens, upstream)


def block_grad_kernel(ids, tokens, upstream, grads):
    slots, size = grads.shape[0], grads.shape[1]
    parts, slabs, _, part_width = tokens.shape
    cols_n = upstream.shape[2] // size
    per_part = part_width // size
    total = parts * per_part * cols_n

    @pl.loop(0, slots)
    def one(s):
        b = ids[s]

        @pl.when(b < total)
        def fill():
            row = b // cols_n
            part = row // per_part
            r = pl.multiple_of((row % per_part) * size, size)
            c = pl.multiple_of((b % cols_n) * size, size)
            acc = jnp.zeros((size, size), jnp.float32)
            for k in range(slabs):
                acc += lax.dot_general(
                    tokens[part, k, :, pl.ds(r, size)],
                    upstream[k, :, pl.ds(c, size)],
                    (((0,), (0,)), ((), ())),
                    preferred_element_type=jnp.float32,
                )
            grads[s] = acc.astype(grads.dtype)

        @pl.when(b >= total)
        def clear():
            grads[s] = jnp.zeros((size, size), grads.dtype)


def block_grads(ids, tokens, upstream, size):
    slots = ids.shape[0]
    parts, slabs, rows, part_width = tokens.shape
    return pl.pallas_call(
        block_grad_kernel,
        out_shape=jax.ShapeDtypeStruct((slots, size, size), jnp.bfloat16),
        in_specs=[whole(pltpu.SMEM), whole(), whole()],
        out_specs=whole(),
        compiler_params=pltpu.CompilerParams(vmem_limit_bytes=VMEM_LIMIT),
        cost_estimate=pl.CostEstimate(
            flops=2 * slots * slabs * rows * size * size,
            bytes_accessed=2 * (tokens.size + upstream.size + slots * size * size),
            transcendentals=0,
        ),
        name="block_grads",
    )(ids, tokens, upstream)


def general_body(tokens, upstream, blocks, block_ids):
    size = blocks.shape[1]
    all_blocks = lax.all_gather(blocks, "dp", axis=0, tiled=True)
    all_ids = lax.all_gather(block_ids, "dp", axis=0, tiled=True)
    proj, back = project(all_ids, all_blocks, tokens, upstream)
    terms = block_grads(all_ids, tokens[None, None], upstream[None], size)
    grads = lax.psum_scatter(terms, "dp", scatter_dimension=0, tiled=True)
    return proj, lax.psum(back, INNER), grads


def place_blocks(ids, first, blocks, weight):
    slots, size = blocks.shape[0], blocks.shape[1]
    depth, width = weight.shape
    cols_n = width // size
    total = (depth // size) * cols_n

    @pl.loop(0, slots)
    def place(s):
        b = ids[first + s]

        @pl.when(b < total)
        def put():
            r = pl.multiple_of((b // cols_n) * size, size)
            c = pl.multiple_of((b % cols_n) * size, size)
            weight[pl.ds(r, size), pl.ds(c, size)] = blocks[s]


def middle_kernel(
    place_of, ids_0, ids_1, ids_2, ids_3, own, near_a, near_b, far_a, far_b, end_a, end_b,
    tokens, end_tokens, upstream, end_upstream,
    proj, end_proj, back, end_back, weight,
):
    is_middle, half = place_of[0], place_of[1]
    half_slots = near_a.shape[0]
    mine, other = half * half_slots, (1 - half) * half_slots
    depth, width = weight.shape
    parts, rows, part_width = end_tokens.shape
    step = 256

    @pl.when(is_middle == 1)
    def work():
        weight[...] = jnp.zeros_like(weight)
        place_blocks(ids_0, 0, own, weight)
        place_blocks(ids_1, mine, near_a, weight)
        place_blocks(ids_1, other, near_b, weight)
        place_blocks(ids_2, mine, far_a, weight)
        place_blocks(ids_2, other, far_b, weight)
        place_blocks(ids_3, mine, end_a, weight)
        place_blocks(ids_3, other, end_b, weight)

        per_part = part_width // step

        @pl.loop(0, depth // step)
        def backward(n):
            r = pl.multiple_of(n * step, step)
            at = pl.multiple_of((n % per_part) * step, step)
            rows_of_w = weight[pl.ds(r, step), :]
            for source, target in ((end_upstream, end_back), (upstream, back)):
                target[n // per_part, :, pl.ds(at, step)] = lax.dot_general(
                    source[...],
                    rows_of_w,
                    (((1,), (1,)), ((), ())),
                    preferred_element_type=jnp.float32,
                ).astype(target.dtype)

        @pl.loop(0, width // step)
        def forward(n):
            c = pl.multiple_of(n * step, step)
            acc = jnp.zeros((rows, step), jnp.float32)
            for q in range(parts):
                acc += jnp.dot(
                    end_tokens[q],
                    weight[q * part_width : (q + 1) * part_width, pl.ds(c, step)],
                    preferred_element_type=jnp.float32,
                )
            end_proj[:, pl.ds(c, step)] = acc.astype(end_proj.dtype)
            proj[:, pl.ds(c, step)] = jnp.dot(
                tokens[...], weight[:, pl.ds(c, step)], preferred_element_type=jnp.float32
            ).astype(proj.dtype)


def middle_project(place_of, ids, pieces, tokens, end_tokens, upstream, end_upstream):
    rows, depth = tokens.shape
    width = upstream.shape[1]
    parts, _, part_width = end_tokens.shape
    out_proj = jax.ShapeDtypeStruct((rows, width), jnp.bfloat16)
    out_back = jax.ShapeDtypeStruct((parts, rows, part_width), jnp.bfloat16)
    return pl.pallas_call(
        middle_kernel,
        out_shape=(out_proj, out_proj, out_back, out_back),
        in_specs=[whole(pltpu.SMEM)] * 5 + [whole()] * 11,
        out_specs=(whole(),) * 4,
        scratch_shapes=[pltpu.VMEM((depth, width), jnp.bfloat16)],
        compiler_params=pltpu.CompilerParams(vmem_limit_bytes=VMEM_LIMIT),
        cost_estimate=pl.CostEstimate(
            flops=8 * rows * depth * width,
            bytes_accessed=depth * width * 2 + rows * (depth + width) * 8,
            transcendentals=0,
        ),
        name="middle_project",
    )(place_of, *ids, *pieces, tokens, end_tokens, upstream, end_upstream)


def line_grads_kernel(
    ids, tokens, tokens_1, tokens_2, tokens_3,
    upstream, upstream_1, upstream_2m, upstream_2o, upstream_3m, upstream_3o,
    grads, sum_2, sum_3,
):
    slots, size = grads.shape[0], grads.shape[1]
    parts, _, part_width = tokens_1.shape
    cols_n = upstream.shape[1] // size
    per_part = part_width // size
    total = parts * per_part * cols_n
    sum_2[...] = upstream_2m[...] + upstream_2o[...]
    sum_3[...] = upstream_3m[...] + upstream_3o[...]

    @pl.loop(0, slots)
    def one(s):
        b = ids[s]

        @pl.when(b < total)
        def fill():
            row = b // cols_n
            part = row // per_part
            r = pl.multiple_of((row % per_part) * size, size)
            c = pl.multiple_of((b % cols_n) * size, size)
            whole_r = pl.multiple_of(row * size, size)
            pairs = (
                (tokens[:, pl.ds(whole_r, size)], upstream),
                (tokens_1[part, :, pl.ds(r, size)], upstream_1),
                (tokens_2[part, :, pl.ds(r, size)], sum_2),
                (tokens_3[part, :, pl.ds(r, size)], sum_3),
            )
            acc = jnp.zeros((size, size), jnp.float32)
            for x, d in pairs:
                acc += lax.dot_general(
                    x,
                    d[:, pl.ds(c, size)],
                    (((0,), (0,)), ((), ())),
                    preferred_element_type=jnp.float32,
                )
            grads[s] = acc.astype(grads.dtype)

        @pl.when(b >= total)
        def clear():
            grads[s] = jnp.zeros((size, size), grads.dtype)


def line_grads(ids, tokens, gathered, upstreams, size):
    slots = ids.shape[0]
    rows, width = upstreams[0].shape
    return pl.pallas_call(
        line_grads_kernel,
        out_shape=jax.ShapeDtypeStruct((slots, size, size), jnp.bfloat16),
        in_specs=[whole(pltpu.SMEM)] + [whole()] * 10,
        out_specs=whole(),
        scratch_shapes=[pltpu.VMEM((rows, width), jnp.bfloat16)] * 2,
        compiler_params=pltpu.CompilerParams(vmem_limit_bytes=VMEM_LIMIT),
        cost_estimate=pl.CostEstimate(
            flops=8 * slots * rows * size * size,
            bytes_accessed=2 * (4 * tokens.size + 6 * rows * width + slots * size * size),
            transcendentals=0,
        ),
        name="line_grads",
    )(ids, tokens, *gathered, *upstreams)


INWARD = ((0, 1), (3, 2))
OUTWARD = ((1, 0), (2, 3))
PAIRS = INWARD + OUTWARD
MIDDLE = ((1, 2), (2, 1))


def after(first, then):
    return lax.optimization_barrier((first, then))[1]


def line_body(tokens, upstream, blocks, block_ids):
    size = blocks.shape[1]
    half_slots = blocks.shape[0] // 2
    inner_n = lax.axis_size("tensor") * lax.axis_size("replica")
    part_width = tokens.shape[1] // inner_n
    at_z, half = lax.axis_index("dp"), lax.axis_index("groups")
    middle = (at_z == 1) | (at_z == 2)
    along = functools.partial(lax.ppermute, axis_name="dp")
    across = functools.partial(lax.ppermute, axis_name="groups", perm=((0, 1), (1, 0)))

    ids_1 = along(block_ids, perm=PAIRS)
    ids_2 = along(block_ids, perm=MIDDLE)
    ids_3 = along(ids_1, perm=MIDDLE)
    mine = lax.dynamic_slice_in_dim(blocks, half * half_slots, half_slots, 0)
    other = lax.dynamic_slice_in_dim(blocks, (1 - half) * half_slots, half_slots, 0)
    part = lax.dynamic_slice_in_dim(
        tokens, lax.axis_index(INNER) * part_width, part_width, 1
    )
    near_a = along(mine, perm=INWARD)
    far_a = along(mine, perm=MIDDLE)
    part_1 = along(after(near_a, part), perm=PAIRS)
    end_a = along(after(far_a, near_a), perm=MIDDLE)
    far_b = across(far_a)
    near_b = along(after(part_1, other), perm=INWARD)
    upstream_1 = along(after(near_b, upstream), perm=PAIRS)
    part_2m = along(after(end_a, part), perm=MIDDLE)
    end_b = across(end_a)
    part_3m = along(after(part_2m, part_1), perm=MIDDLE)
    part_2o = along(part_2m, perm=OUTWARD)
    upstream_2m = along(after(part_3m, upstream), perm=MIDDLE)
    part_3o = along(part_3m, perm=OUTWARD)
    upstream_3m = along(after(upstream_2m, upstream_1), perm=MIDDLE)
    upstream_2o = along(upstream_2m, perm=OUTWARD)
    upstream_3o = along(upstream_3m, perm=OUTWARD)

    tokens_1 = lax.all_gather(part_1, INNER)
    tokens_2 = lax.all_gather(part_2m + part_2o, INNER)
    tokens_3 = lax.all_gather(part_3m + part_3o, INNER)

    place_of = jnp.stack([middle.astype(jnp.int32), half.astype(jnp.int32)])
    proj, end_proj, back, end_back = middle_project(
        place_of,
        (block_ids, ids_1, ids_2, ids_3),
        (blocks, near_a, near_b, far_a, far_b, end_a, end_b),
        tokens,
        tokens_1,
        upstream,
        upstream_1,
    )
    proj_out = along(end_proj, perm=OUTWARD)
    end_sum = lax.psum_scatter(end_back, INNER, scatter_dimension=0)
    own_sum = lax.psum_scatter(back, INNER, scatter_dimension=0)
    sum_out = along(end_sum, perm=OUTWARD)
    projected = jnp.where(middle, proj, proj_out)
    token_grad = lax.all_gather(jnp.where(middle, own_sum, sum_out), INNER, axis=1, tiled=True)
    grads = line_grads(
        block_ids,
        tokens,
        (tokens_1, tokens_2, tokens_3),
        (upstream, upstream_1, upstream_2m, upstream_2o, upstream_3m, upstream_3o),
        size,
    )
    return projected, token_grad, grads


def solution(mesh):
    line = mesh.shape["dp"] == 4 and mesh.shape["groups"] == 2
    return jax.shard_map(
        line_body if line else general_body,
        mesh=mesh,
        in_specs=(
            P(("groups", "dp"), None),
            P(("groups", "dp"), INNER),
            P(("dp",) + INNER, None, None),
            P(("dp",) + INNER),
        ),
        out_specs=(
            P(("groups", "dp"), INNER),
            P(("groups", "dp"), None),
            P(("groups", "dp") + INNER, None, None),
        ),
        check_vma=False,
    )
```

```python
import functools

import jax
import jax.numpy as jnp
from jax import lax
from jax.experimental import pallas as pl
from jax.experimental.pallas import tpu as pltpu
from jax.sharding import PartitionSpec as P

VMEM_LIMIT = 60 * 1024 * 1024
INNER = ("tensor", "replica")


def whole(space=pltpu.VMEM):
    return pl.BlockSpec(memory_space=space)


def project_kernel(ids, blocks, tokens, upstream, proj, back, weight):
    slots, size = blocks.shape[0], blocks.shape[1]
    depth, width = weight.shape
    cols_n = width // size
    total = (depth // size) * cols_n
    weight[...] = jnp.zeros_like(weight)

    @pl.loop(0, slots)
    def place(s):
        b = ids[s]

        @pl.when(b < total)
        def put():
            r = pl.multiple_of((b // cols_n) * size, size)
            c = pl.multiple_of((b % cols_n) * size, size)
            weight[pl.ds(r, size), pl.ds(c, size)] = blocks[s]

    step = 256

    @pl.loop(0, width // step)
    def forward(n):
        c = pl.multiple_of(n * step, step)
        proj[:, pl.ds(c, step)] = jnp.dot(
            tokens[...], weight[:, pl.ds(c, step)], preferred_element_type=jnp.float32
        ).astype(proj.dtype)

    @pl.loop(0, depth // step)
    def backward(n):
        r = pl.multiple_of(n * step, step)
        back[:, pl.ds(r, step)] = lax.dot_general(
            upstream[...],
            weight[pl.ds(r, step), :],
            (((1,), (1,)), ((), ())),
            preferred_element_type=jnp.float32,
        ).astype(back.dtype)


def project(ids, blocks, tokens, upstream):
    rows, depth = tokens.shape
    width = upstream.shape[1]
    return pl.pallas_call(
        project_kernel,
        out_shape=(
            jax.ShapeDtypeStruct((rows, width), jnp.bfloat16),
            jax.ShapeDtypeStruct((rows, depth), jnp.bfloat16),
        ),
        in_specs=[whole(pltpu.SMEM), whole(), whole(), whole()],
        out_specs=(whole(), whole()),
        scratch_shapes=[pltpu.VMEM((depth, width), jnp.bfloat16)],
        compiler_params=pltpu.CompilerParams(vmem_limit_bytes=VMEM_LIMIT),
        cost_estimate=pl.CostEstimate(
            flops=4 * rows * depth * width,
            bytes_accessed=blocks.size * 2 + rows * (depth + width) * 4,
            transcendentals=0,
        ),
        name="project",
    )(ids, blocks, tokens, upstream)


def block_grad_kernel(ids, tokens, upstream, grads):
    slots, size = grads.shape[0], grads.shape[1]
    parts, slabs, _, part_width = tokens.shape
    cols_n = upstream.shape[2] // size
    per_part = part_width // size
    total = parts * per_part * cols_n

    @pl.loop(0, slots)
    def one(s):
        b = ids[s]

        @pl.when(b < total)
        def fill():
            row = b // cols_n
            part = row // per_part
            r = pl.multiple_of((row % per_part) * size, size)
            c = pl.multiple_of((b % cols_n) * size, size)
            acc = jnp.zeros((size, size), jnp.float32)
            for k in range(slabs):
                acc += lax.dot_general(
                    tokens[part, k, :, pl.ds(r, size)],
                    upstream[k, :, pl.ds(c, size)],
                    (((0,), (0,)), ((), ())),
                    preferred_element_type=jnp.float32,
                )
            grads[s] = acc.astype(grads.dtype)

        @pl.when(b >= total)
        def clear():
            grads[s] = jnp.zeros((size, size), grads.dtype)


def block_grads(ids, tokens, upstream, size):
    slots = ids.shape[0]
    parts, slabs, rows, part_width = tokens.shape
    return pl.pallas_call(
        block_grad_kernel,
        out_shape=jax.ShapeDtypeStruct((slots, size, size), jnp.bfloat16),
        in_specs=[whole(pltpu.SMEM), whole(), whole()],
        out_specs=whole(),
        compiler_params=pltpu.CompilerParams(vmem_limit_bytes=VMEM_LIMIT),
        cost_estimate=pl.CostEstimate(
            flops=2 * slots * slabs * rows * size * size,
            bytes_accessed=2 * (tokens.size + upstream.size + slots * size * size),
            transcendentals=0,
        ),
        name="block_grads",
    )(ids, tokens, upstream)


def general_body(tokens, upstream, blocks, block_ids):
    size = blocks.shape[1]
    all_blocks = lax.all_gather(blocks, "dp", axis=0, tiled=True)
    all_ids = lax.all_gather(block_ids, "dp", axis=0, tiled=True)
    proj, back = project(all_ids, all_blocks, tokens, upstream)
    terms = block_grads(all_ids, tokens[None, None], upstream[None], size)
    grads = lax.psum_scatter(terms, "dp", scatter_dimension=0, tiled=True)
    return proj, lax.psum(back, INNER), grads


def place_blocks(ids, first, blocks, weight):
    slots, size = blocks.shape[0], blocks.shape[1]
    depth, width = weight.shape
    cols_n = width // size
    total = (depth // size) * cols_n

    @pl.loop(0, slots)
    def place(s):
        b = ids[first + s]

        @pl.when(b < total)
        def put():
            r = pl.multiple_of((b // cols_n) * size, size)
            c = pl.multiple_of((b % cols_n) * size, size)
            weight[pl.ds(r, size), pl.ds(c, size)] = blocks[s]


def weight_kernel(
    place_of, ids_0, ids_1, ids_2, ids_3, own, near_a, near_b, far_a, far_b, end_a, end_b,
    end_upstream, weight, end_back,
):
    is_middle, half = place_of[0], place_of[1]
    half_slots = near_a.shape[0]
    mine, other = half * half_slots, (1 - half) * half_slots

    @pl.when(is_middle == 1)
    def work():
        weight[...] = jnp.zeros_like(weight)
        place_blocks(ids_0, 0, own, weight)
        place_blocks(ids_1, mine, near_a, weight)
        place_blocks(ids_1, other, near_b, weight)
        place_blocks(ids_2, mine, far_a, weight)
        place_blocks(ids_2, other, far_b, weight)
        place_blocks(ids_3, mine, end_a, weight)
        place_blocks(ids_3, other, end_b, weight)
        backward_rows(end_upstream, weight, end_back)


def backward_rows(upstream, weight, back):
    depth = weight.shape[0]
    step = 256
    per_part = back.shape[2] // step

    @pl.loop(0, depth // step)
    def backward(n):
        r = pl.multiple_of(n * step, step)
        at = pl.multiple_of((n % per_part) * step, step)
        back[n // per_part, :, pl.ds(at, step)] = lax.dot_general(
            upstream[...],
            weight[pl.ds(r, step), :],
            (((1,), (1,)), ((), ())),
            preferred_element_type=jnp.float32,
        ).astype(back.dtype)


def build_weight(place_of, ids, pieces, end_upstream, depth, parts):
    rows, width = end_upstream.shape
    return pl.pallas_call(
        weight_kernel,
        out_shape=(
            jax.ShapeDtypeStruct((depth, width), jnp.bfloat16),
            jax.ShapeDtypeStruct((parts, rows, depth // parts), jnp.bfloat16),
        ),
        in_specs=[whole(pltpu.SMEM)] * 5 + [whole()] * 8,
        out_specs=(whole(),) * 2,
        compiler_params=pltpu.CompilerParams(vmem_limit_bytes=VMEM_LIMIT),
        cost_estimate=pl.CostEstimate(
            flops=2 * rows * depth * width,
            bytes_accessed=depth * width * 4 + rows * (depth + width) * 2,
            transcendentals=0,
        ),
        name="build_weight",
    )(place_of, *ids, *pieces, end_upstream)


def backward_kernel(place_of, weight, upstream, back):
    @pl.when(place_of[0] == 1)
    def work():
        backward_rows(upstream, weight, back)


def project_back(place_of, weight, upstream, parts):
    depth, width = weight.shape
    rows = upstream.shape[0]
    return pl.pallas_call(
        backward_kernel,
        out_shape=jax.ShapeDtypeStruct((parts, rows, depth // parts), jnp.bfloat16),
        in_specs=[whole(pltpu.SMEM)] + [whole()] * 2,
        out_specs=whole(),
        compiler_params=pltpu.CompilerParams(vmem_limit_bytes=VMEM_LIMIT),
        cost_estimate=pl.CostEstimate(
            flops=2 * rows * depth * width,
            bytes_accessed=depth * width * 2 + rows * (depth + width) * 2,
            transcendentals=0,
        ),
        name="project_back",
    )(place_of, weight, upstream)


def forward_kernel(place_of, weight, tokens, end_tokens, proj, end_proj):
    width = weight.shape[1]
    parts, rows, part_width = end_tokens.shape
    step = 256

    @pl.when(place_of[0] == 1)
    def work():
        @pl.loop(0, width // step)
        def forward(n):
            c = pl.multiple_of(n * step, step)
            acc = jnp.zeros((rows, step), jnp.float32)
            for q in range(parts):
                acc += jnp.dot(
                    end_tokens[q],
                    weight[q * part_width : (q + 1) * part_width, pl.ds(c, step)],
                    preferred_element_type=jnp.float32,
                )
            end_proj[:, pl.ds(c, step)] = acc.astype(end_proj.dtype)
            proj[:, pl.ds(c, step)] = jnp.dot(
                tokens[...], weight[:, pl.ds(c, step)], preferred_element_type=jnp.float32
            ).astype(proj.dtype)


def project_forward(place_of, weight, tokens, end_tokens):
    depth, width = weight.shape
    rows = tokens.shape[0]
    out = jax.ShapeDtypeStruct((rows, width), jnp.bfloat16)
    return pl.pallas_call(
        forward_kernel,
        out_shape=(out, out),
        in_specs=[whole(pltpu.SMEM)] + [whole()] * 3,
        out_specs=(whole(),) * 2,
        compiler_params=pltpu.CompilerParams(vmem_limit_bytes=VMEM_LIMIT),
        cost_estimate=pl.CostEstimate(
            flops=4 * rows * depth * width,
            bytes_accessed=depth * width * 2 + rows * (depth + width) * 4,
            transcendentals=0,
        ),
        name="project_forward",
    )(place_of, weight, tokens, end_tokens)


def line_grads_kernel(pairs_n, has_start, parted, ids, *refs):
    refs = list(refs)
    start = refs.pop(0) if has_start else None
    pairs = [(refs[2 * k], refs[2 * k + 1]) for k in range(pairs_n)]
    grads = refs[2 * pairs_n]
    slots, size = grads.shape[0], grads.shape[1]
    parts, _, part_width = pairs[-1][0].shape
    cols_n = pairs[0][1].shape[1] // size
    per_part = part_width // size
    total = parts * per_part * cols_n

    @pl.loop(0, slots)
    def one(s):
        b = ids[s]

        @pl.when(b < total)
        def fill():
            row = b // cols_n
            part = row // per_part
            r = pl.multiple_of((row % per_part) * size, size)
            c = pl.multiple_of((b % cols_n) * size, size)
            whole_r = pl.multiple_of(row * size, size)
            acc = start[s] if has_start else jnp.zeros((size, size), jnp.float32)
            for (x, d), cut in zip(pairs, parted):
                acc += lax.dot_general(
                    x[part, :, pl.ds(r, size)] if cut else x[:, pl.ds(whole_r, size)],
                    d[:, pl.ds(c, size)],
                    (((0,), (0,)), ((), ())),
                    preferred_element_type=jnp.float32,
                )
            grads[s] = acc.astype(grads.dtype)

        @pl.when(b >= total)
        def clear():
            grads[s] = jnp.zeros((size, size), grads.dtype)


def line_grads(ids, start, pairs, size, out_dtype):
    slots = ids.shape[0]
    rows = pairs[0][1].shape[0]
    flat = [a for pair in pairs for a in pair]
    starts = [] if start is None else [start]
    return pl.pallas_call(
        functools.partial(
            line_grads_kernel,
            len(pairs),
            start is not None,
            tuple(x.ndim == 3 for x, _ in pairs),
        ),
        out_shape=jax.ShapeDtypeStruct((slots, size, size), out_dtype),
        in_specs=[whole(pltpu.SMEM)] + [whole()] * (len(starts) + len(flat)),
        out_specs=whole(),
        compiler_params=pltpu.CompilerParams(vmem_limit_bytes=VMEM_LIMIT),
        cost_estimate=pl.CostEstimate(
            flops=4 * len(pairs) * slots * rows * size * size,
            bytes_accessed=sum(2 * a.size for a in flat) + 4 * slots * size * size,
            transcendentals=0,
        ),
        name="line_grads",
    )(ids, *starts, *flat)


INWARD = ((0, 1), (3, 2))
OUTWARD = ((1, 0), (2, 3))
PAIRS = INWARD + OUTWARD
MIDDLE = ((1, 2), (2, 1))
SWAP = ((0, 1), (1, 0))


def plus(a, b):
    return (a.astype(jnp.float32) + b.astype(jnp.float32)).astype(a.dtype)


def scatter_sum(parts, at_tensor, at_replica):
    by_core = parts.reshape((2, 2) + parts.shape[1:])
    keep = lax.dynamic_index_in_dim(by_core, at_replica, 1, keepdims=False)
    give = lax.dynamic_index_in_dim(by_core, 1 - at_replica, 1, keepdims=False)
    chip = plus(keep, lax.ppermute(give, "replica", SWAP))
    keep = lax.dynamic_index_in_dim(chip, at_tensor, 0, keepdims=False)
    give = lax.dynamic_index_in_dim(chip, 1 - at_tensor, 0, keepdims=False)
    return plus(keep, lax.ppermute(give, "tensor", SWAP))


def gather_parts(part, at_tensor, at_replica):
    other = lax.ppermute(part, "tensor", SWAP)
    pair = jnp.where(
        at_tensor == 0, jnp.stack([part, other]), jnp.stack([other, part])
    )
    core = lax.ppermute(pair, "replica", SWAP)
    parts = jnp.where(
        at_replica == 0, jnp.stack([pair, core], 1), jnp.stack([core, pair], 1)
    )
    rows, width = part.shape
    return parts.reshape(4, rows, width).transpose(1, 0, 2).reshape(rows, 4 * width)


def line_body(tokens, upstream, blocks, block_ids):
    size = blocks.shape[1]
    depth = tokens.shape[1]
    half_slots = blocks.shape[0] // 2
    parts = 4
    part_width = depth // parts
    at_z, half = lax.axis_index("dp"), lax.axis_index("groups")
    at_tensor, at_replica = lax.axis_index("tensor"), lax.axis_index("replica")
    middle = (at_z == 1) | (at_z == 2)
    place_of = jnp.stack([middle.astype(jnp.int32), half.astype(jnp.int32)])
    along = functools.partial(lax.ppermute, axis_name="dp")
    across = functools.partial(lax.ppermute, axis_name="groups", perm=SWAP)
    stage = lax.optimization_barrier

    mine = lax.dynamic_slice_in_dim(blocks, half * half_slots, half_slots, 0)
    other = lax.dynamic_slice_in_dim(blocks, (1 - half) * half_slots, half_slots, 0)
    part = lax.dynamic_slice_in_dim(tokens, lax.axis_index(INNER) * part_width, part_width, 1)
    mine, other, part = stage((mine, other, part))

    near_a = along(mine, perm=INWARD)
    far_a = along(mine, perm=MIDDLE)
    part_1o = along(part, perm=OUTWARD)
    upstream_1o = along(upstream, perm=OUTWARD)
    ids_1 = along(block_ids, perm=PAIRS)
    ids_2 = along(block_ids, perm=MIDDLE)
    near_a, far_a, part_1o, upstream_1o, ids_1, ids_2, part, upstream_s, other = stage(
        (near_a, far_a, part_1o, upstream_1o, ids_1, ids_2, part, upstream, other)
    )

    part_1i = along(part, perm=INWARD)
    upstream_1i = along(upstream_s, perm=INWARD)
    end_a = along(near_a, perm=MIDDLE)
    far_b = across(far_a)
    ids_3 = along(ids_1, perm=MIDDLE)
    part_1i, upstream_1i, end_a, far_b, ids_3, part, upstream_s, other = stage(
        (part_1i, upstream_1i, end_a, far_b, ids_3, part, upstream_s, other)
    )
    tokens_1 = lax.all_gather(part_1i + part_1o, INNER)
    upstream_1 = upstream_1i + upstream_1o

    near_b = along(other, perm=INWARD)
    part_2m = along(part, perm=MIDDLE)
    part_3m = along(part_1i, perm=MIDDLE)
    end_b = across(end_a)
    near_b, part_2m, part_3m, end_b, upstream_s, upstream_1i = stage(
        (near_b, part_2m, part_3m, end_b, upstream_s, upstream_1i)
    )

    weight, end_back = build_weight(
        place_of,
        (block_ids, ids_1, ids_2, ids_3),
        (blocks, near_a, near_b, far_a, far_b, end_a, end_b),
        upstream_1i,
        depth,
        parts,
    )
    part_2o = along(part_2m, perm=OUTWARD)
    part_3o = along(part_3m, perm=OUTWARD)
    upstream_2m = along(upstream_s, perm=MIDDLE)
    upstream_3m = along(upstream_1i, perm=MIDDLE)
    part_2o, part_3o, upstream_2m, upstream_3m = stage(
        (part_2o, part_3o, upstream_2m, upstream_3m)
    )
    tokens_2 = lax.all_gather(part_2m + part_2o, INNER)
    tokens_3 = lax.all_gather(part_3m + part_3o, INNER)
    upstream_2o = along(upstream_2m, perm=OUTWARD)
    upstream_3o = along(upstream_3m, perm=OUTWARD)

    end_sum = scatter_sum(end_back, at_tensor, at_replica)
    back = project_back(place_of, weight, upstream, parts)
    own_sum = scatter_sum(back, at_tensor, at_replica)
    proj, end_proj = project_forward(place_of, weight, tokens, tokens_1)
    proj_out = along(end_proj, perm=OUTWARD)
    sum_out = along(end_sum, perm=OUTWARD)
    projected = jnp.where(middle, proj, proj_out)
    token_grad = gather_parts(jnp.where(middle, own_sum, sum_out), at_tensor, at_replica)

    grads = line_grads(
        block_ids, None, ((tokens, upstream), (tokens_1, upstream_1)), size, jnp.float32
    )
    grads = line_grads(
        block_ids, grads, ((tokens_2, upstream_2m + upstream_2o),), size, jnp.float32
    )
    grads = line_grads(
        block_ids, grads, ((tokens_3, upstream_3m + upstream_3o),), size, jnp.bfloat16
    )
    return projected, token_grad, grads


def solution(mesh):
    line = tuple(mesh.shape[a] for a in ("groups", "dp", "tensor", "replica")) == (2, 4, 2, 2)
    return jax.shard_map(
        line_body if line else general_body,
        mesh=mesh,
        in_specs=(
            P(("groups", "dp"), None),
            P(("groups", "dp"), INNER),
            P(("dp",) + INNER, None, None),
            P(("dp",) + INNER),
        ),
        out_specs=(
            P(("groups", "dp"), INNER),
            P(("groups", "dp"), None),
            P(("groups", "dp") + INNER, None, None),
        ),
        check_vma=False,
    )
```

```python
import functools
import math

import jax
import jax.numpy as jnp
from jax import lax
from jax.experimental import pallas as pl
from jax.experimental.pallas import tpu as pltpu
from jax.sharding import PartitionSpec as P

VMEM_LIMIT = 60 * 1024 * 1024
INNER = ("tensor", "replica")


def whole(space=pltpu.VMEM):
    return pl.BlockSpec(memory_space=space)


def project_kernel(ids, blocks, tokens, upstream, proj, back, weight):
    slots, size = blocks.shape[0], blocks.shape[1]
    depth, width = weight.shape
    cols_n = width // size
    total = (depth // size) * cols_n
    weight[...] = jnp.zeros_like(weight)

    @pl.loop(0, slots)
    def place(s):
        b = ids[s]

        @pl.when(b < total)
        def put():
            r = pl.multiple_of((b // cols_n) * size, size)
            c = pl.multiple_of((b % cols_n) * size, size)
            weight[pl.ds(r, size), pl.ds(c, size)] = blocks[s]

    step = 256

    @pl.loop(0, width // step)
    def forward(n):
        c = pl.multiple_of(n * step, step)
        proj[:, pl.ds(c, step)] = jnp.dot(
            tokens[...], weight[:, pl.ds(c, step)], preferred_element_type=jnp.float32
        ).astype(proj.dtype)

    @pl.loop(0, depth // step)
    def backward(n):
        r = pl.multiple_of(n * step, step)
        back[:, pl.ds(r, step)] = lax.dot_general(
            upstream[...],
            weight[pl.ds(r, step), :],
            (((1,), (1,)), ((), ())),
            preferred_element_type=jnp.float32,
        ).astype(back.dtype)


def project(ids, blocks, tokens, upstream):
    rows, depth = tokens.shape
    width = upstream.shape[1]
    return pl.pallas_call(
        project_kernel,
        out_shape=(
            jax.ShapeDtypeStruct((rows, width), jnp.bfloat16),
            jax.ShapeDtypeStruct((rows, depth), jnp.bfloat16),
        ),
        in_specs=[whole(pltpu.SMEM), whole(), whole(), whole()],
        out_specs=(whole(), whole()),
        scratch_shapes=[pltpu.VMEM((depth, width), jnp.bfloat16)],
        compiler_params=pltpu.CompilerParams(vmem_limit_bytes=VMEM_LIMIT),
        cost_estimate=pl.CostEstimate(
            flops=4 * rows * depth * width,
            bytes_accessed=blocks.size * 2 + rows * (depth + width) * 4,
            transcendentals=0,
        ),
        name="project",
    )(ids, blocks, tokens, upstream)


def block_grad_kernel(ids, tokens, upstream, grads):
    slots, size = grads.shape[0], grads.shape[1]
    parts, slabs, _, part_width = tokens.shape
    cols_n = upstream.shape[2] // size
    per_part = part_width // size
    total = parts * per_part * cols_n

    @pl.loop(0, slots)
    def one(s):
        b = ids[s]

        @pl.when(b < total)
        def fill():
            row = b // cols_n
            part = row // per_part
            r = pl.multiple_of((row % per_part) * size, size)
            c = pl.multiple_of((b % cols_n) * size, size)
            acc = jnp.zeros((size, size), jnp.float32)
            for k in range(slabs):
                acc += lax.dot_general(
                    tokens[part, k, :, pl.ds(r, size)],
                    upstream[k, :, pl.ds(c, size)],
                    (((0,), (0,)), ((), ())),
                    preferred_element_type=jnp.float32,
                )
            grads[s] = acc.astype(grads.dtype)

        @pl.when(b >= total)
        def clear():
            grads[s] = jnp.zeros((size, size), grads.dtype)


def block_grads(ids, tokens, upstream, size):
    slots = ids.shape[0]
    parts, slabs, rows, part_width = tokens.shape
    return pl.pallas_call(
        block_grad_kernel,
        out_shape=jax.ShapeDtypeStruct((slots, size, size), jnp.bfloat16),
        in_specs=[whole(pltpu.SMEM), whole(), whole()],
        out_specs=whole(),
        compiler_params=pltpu.CompilerParams(vmem_limit_bytes=VMEM_LIMIT),
        cost_estimate=pl.CostEstimate(
            flops=2 * slots * slabs * rows * size * size,
            bytes_accessed=2 * (tokens.size + upstream.size + slots * size * size),
            transcendentals=0,
        ),
        name="block_grads",
    )(ids, tokens, upstream)


def general_body(tokens, upstream, blocks, block_ids):
    size = blocks.shape[1]
    all_blocks = lax.all_gather(blocks, "dp", axis=0, tiled=True)
    all_ids = lax.all_gather(block_ids, "dp", axis=0, tiled=True)
    proj, back = project(all_ids, all_blocks, tokens, upstream)
    terms = block_grads(all_ids, tokens[None, None], upstream[None], size)
    grads = lax.psum_scatter(terms, "dp", scatter_dimension=0, tiled=True)
    return proj, lax.psum(back, INNER), grads


def place_blocks(ids, first, blocks, weight, slots):
    size = blocks.shape[1]
    depth, width = weight.shape
    cols_n = width // size
    total = (depth // size) * cols_n

    @pl.loop(0, slots)
    def place(s):
        b = ids[first + s]

        @pl.when(b < total)
        def put():
            r = pl.multiple_of((b // cols_n) * size, size)
            c = pl.multiple_of((b % cols_n) * size, size)
            weight[pl.ds(r, size), pl.ds(c, size)] = blocks[s]


def place_kernel(place_of, ids_0, ids_1, ids_2, ids_3, own, near_a, far_a, far_b, end_a, weight):
    is_middle, half = place_of[0], place_of[1]
    half_slots = far_b.shape[0] - 1
    mine, other = half * half_slots, (1 - half) * half_slots

    @pl.when(is_middle == 1)
    def work():
        weight[...] = jnp.zeros_like(weight)
        place_blocks(ids_0, 0, own, weight, own.shape[0])
        place_blocks(ids_1, mine, near_a, weight, half_slots)
        place_blocks(ids_2, mine, far_a, weight, half_slots)
        place_blocks(ids_2, other, far_b, weight, half_slots)
        place_blocks(ids_3, mine, end_a, weight, half_slots)


def place_first(place_of, ids, pieces, depth, width):
    return pl.pallas_call(
        place_kernel,
        out_shape=jax.ShapeDtypeStruct((depth, width), jnp.bfloat16),
        in_specs=[whole(pltpu.SMEM)] * 5 + [whole()] * 5,
        out_specs=whole(),
        compiler_params=pltpu.CompilerParams(vmem_limit_bytes=VMEM_LIMIT),
        cost_estimate=pl.CostEstimate(
            flops=0, bytes_accessed=depth * width * 4, transcendentals=0
        ),
        name="place_first",
    )(place_of, *ids, *pieces)


def backward_rows(place_of, upstream, weight, keep, give):
    depth = weight.shape[0]
    step = 256
    per_part = keep.shape[2] // step
    at_replica = place_of[3]

    @pl.loop(0, depth // step)
    def backward(n):
        r = pl.multiple_of(n * step, step)
        part = n // per_part
        at = pl.multiple_of((n % per_part) * step, step)
        result = lax.dot_general(
            upstream[...],
            weight[pl.ds(r, step), :],
            (((1,), (1,)), ((), ())),
            preferred_element_type=jnp.float32,
        ).astype(keep.dtype)

        @pl.when(part % 2 == at_replica)
        def mine():
            keep[part // 2, :, pl.ds(at, step)] = result

        @pl.when(part % 2 != at_replica)
        def theirs():
            give[part // 2, :, pl.ds(at, step)] = result


def finish_kernel(
    place_of, ids_1, ids_3, partial, near_b, end_b, upstream, weight, keep, give,
    held, sem_in, sem_out,
):
    half_slots = near_b.shape[0]
    other = (1 - place_of[1]) * half_slots

    @pl.when(place_of[0] == 1)
    def work():
        load = pltpu.make_async_copy(partial, held, sem_in)
        load.start()
        load.wait()
        place_blocks(ids_1, other, near_b, held, half_slots)
        place_blocks(ids_3, other, end_b, held, half_slots)
        store = pltpu.make_async_copy(held, weight, sem_out)
        store.start()
        backward_rows(place_of, upstream, held, keep, give)
        store.wait()


def finish_weight(place_of, ids_1, ids_3, partial, near_b, end_b, upstream):
    depth, width = partial.shape
    rows = upstream.shape[0]
    half = jax.ShapeDtypeStruct((2, rows, depth // 4), jnp.bfloat16)
    return pl.pallas_call(
        finish_kernel,
        out_shape=(jax.ShapeDtypeStruct((depth, width), jnp.bfloat16), half, half),
        in_specs=[whole(pltpu.SMEM)] * 3 + [whole(pl.ANY)] + [whole()] * 3,
        out_specs=(whole(pl.ANY), whole(), whole()),
        scratch_shapes=[
            pltpu.VMEM((depth, width), jnp.bfloat16),
            pltpu.SemaphoreType.DMA,
            pltpu.SemaphoreType.DMA,
        ],
        compiler_params=pltpu.CompilerParams(vmem_limit_bytes=VMEM_LIMIT),
        cost_estimate=pl.CostEstimate(
            flops=2 * rows * depth * width,
            bytes_accessed=depth * width * 4 + rows * (depth + width) * 2,
            transcendentals=0,
        ),
        name="finish_weight",
    )(place_of, ids_1, ids_3, partial, near_b, end_b, upstream)


def backward_kernel(place_of, weight, upstream, keep, give):
    @pl.when(place_of[0] == 1)
    def work():
        backward_rows(place_of, upstream, weight, keep, give)


def project_back(place_of, weight, upstream):
    depth, width = weight.shape
    rows = upstream.shape[0]
    half = jax.ShapeDtypeStruct((2, rows, depth // 4), jnp.bfloat16)
    return pl.pallas_call(
        backward_kernel,
        out_shape=(half, half),
        in_specs=[whole(pltpu.SMEM)] + [whole()] * 2,
        out_specs=(whole(),) * 2,
        compiler_params=pltpu.CompilerParams(vmem_limit_bytes=VMEM_LIMIT),
        cost_estimate=pl.CostEstimate(
            flops=2 * rows * depth * width,
            bytes_accessed=depth * width * 2 + rows * (depth + width) * 2,
            transcendentals=0,
        ),
        name="project_back",
    )(place_of, weight, upstream)


def forward_kernel(place_of, weight, tokens, end_tokens, proj, end_proj):
    width = weight.shape[1]
    parts, rows, part_width = end_tokens.shape
    step = 256

    @pl.when(place_of[0] == 1)
    def work():
        @pl.loop(0, width // step)
        def forward(n):
            c = pl.multiple_of(n * step, step)
            acc = jnp.zeros((rows, step), jnp.float32)
            for q in range(parts):
                acc += jnp.dot(
                    end_tokens[q],
                    weight[q * part_width : (q + 1) * part_width, pl.ds(c, step)],
                    preferred_element_type=jnp.float32,
                )
            end_proj[:, pl.ds(c, step)] = acc.astype(end_proj.dtype)
            proj[:, pl.ds(c, step)] = jnp.dot(
                tokens[...], weight[:, pl.ds(c, step)], preferred_element_type=jnp.float32
            ).astype(proj.dtype)


def project_forward(place_of, weight, tokens, end_tokens):
    depth, width = weight.shape
    rows = tokens.shape[0]
    out = jax.ShapeDtypeStruct((rows, width), jnp.bfloat16)
    return pl.pallas_call(
        forward_kernel,
        out_shape=(out, out),
        in_specs=[whole(pltpu.SMEM)] + [whole()] * 3,
        out_specs=(whole(),) * 2,
        compiler_params=pltpu.CompilerParams(vmem_limit_bytes=VMEM_LIMIT),
        cost_estimate=pl.CostEstimate(
            flops=4 * rows * depth * width,
            bytes_accessed=depth * width * 2 + rows * (depth + width) * 4,
            transcendentals=0,
        ),
        name="project_forward",
    )(place_of, weight, tokens, end_tokens)


def split_kernel(place_of, keep, got, own, give):
    x = place_of[2]
    for ref, at in ((own, x), (give, 1 - x)):
        ref[...] = (keep[at].astype(jnp.float32) + got[at].astype(jnp.float32)).astype(ref.dtype)


def add_split(place_of, keep, got):
    out = jax.ShapeDtypeStruct(keep.shape[1:], keep.dtype)
    return pl.pallas_call(
        split_kernel,
        out_shape=(out, out),
        in_specs=[whole(pltpu.SMEM), whole(), whole()],
        out_specs=(whole(), whole()),
        compiler_params=pltpu.CompilerParams(vmem_limit_bytes=VMEM_LIMIT),
        cost_estimate=pl.CostEstimate(
            flops=keep.size, bytes_accessed=keep.size * 6, transcendentals=0
        ),
        name="add_split",
    )(place_of, keep, got)


def assemble_kernel(place_of, own, by_core, by_tensor, by_both, full):
    x, c = place_of[2], place_of[3]
    width = own.shape[1]
    for ref, xx, cc in (
        (own, x, c), (by_core, x, 1 - c), (by_tensor, 1 - x, c), (by_both, 1 - x, 1 - c)
    ):
        at = pl.multiple_of((xx * 2 + cc) * width, width)
        full[:, pl.ds(at, width)] = ref[...]


def assemble(place_of, quarters):
    rows, width = quarters[0].shape
    return pl.pallas_call(
        assemble_kernel,
        out_shape=jax.ShapeDtypeStruct((rows, 4 * width), quarters[0].dtype),
        in_specs=[whole(pltpu.SMEM)] + [whole()] * 4,
        out_specs=whole(),
        compiler_params=pltpu.CompilerParams(vmem_limit_bytes=VMEM_LIMIT),
        cost_estimate=pl.CostEstimate(
            flops=0, bytes_accessed=rows * width * 16, transcendentals=0
        ),
        name="assemble",
    )(place_of, *quarters)


def line_grads_kernel(pairs_n, has_start, parted, ids, *refs):
    refs = list(refs)
    start = refs.pop(0) if has_start else None
    pairs = [(refs[2 * k], refs[2 * k + 1]) for k in range(pairs_n)]
    grads = refs[2 * pairs_n]
    slots, size = grads.shape[0], grads.shape[1]
    cols_n = pairs[0][1].shape[1] // size
    rows_n = math.prod(pairs[0][0].shape[::2] if parted[0] else pairs[0][0].shape[1:]) // size
    per_part = pairs[0][0].shape[-1] // size
    total = rows_n * cols_n

    @pl.loop(0, slots)
    def one(s):
        b = ids[s]

        @pl.when(b < total)
        def fill():
            row = b // cols_n
            part = row // per_part
            r = pl.multiple_of((row % per_part) * size, size)
            c = pl.multiple_of((b % cols_n) * size, size)
            acc = start[s] if has_start else jnp.zeros((size, size), jnp.float32)
            for (x, d), cut in zip(pairs, parted):
                acc += lax.dot_general(
                    x[part, :, pl.ds(r, size)] if cut else x[:, pl.ds(r, size)],
                    d[:, pl.ds(c, size)],
                    (((0,), (0,)), ((), ())),
                    preferred_element_type=jnp.float32,
                )
            grads[s] = acc.astype(grads.dtype)

        @pl.when(b >= total)
        def clear():
            grads[s] = jnp.zeros((size, size), grads.dtype)


def line_grads(ids, start, pairs, size, out_dtype):
    slots = ids.shape[0]
    rows = pairs[0][1].shape[0]
    flat = [a for pair in pairs for a in pair]
    starts = [] if start is None else [start]
    return pl.pallas_call(
        functools.partial(
            line_grads_kernel,
            len(pairs),
            start is not None,
            tuple(x.ndim == 3 for x, _ in pairs),
        ),
        out_shape=jax.ShapeDtypeStruct((slots, size, size), out_dtype),
        in_specs=[whole(pltpu.SMEM)] + [whole()] * (len(starts) + len(flat)),
        out_specs=whole(),
        compiler_params=pltpu.CompilerParams(vmem_limit_bytes=VMEM_LIMIT),
        cost_estimate=pl.CostEstimate(
            flops=4 * len(pairs) * slots * rows * size * size,
            bytes_accessed=sum(2 * a.size for a in flat) + 4 * slots * size * size,
            transcendentals=0,
        ),
        name="line_grads",
    )(ids, *starts, *flat)


INWARD = ((0, 1), (3, 2))
OUTWARD = ((1, 0), (2, 3))
MIDDLE = ((1, 2), (2, 1))
SWAP = ((0, 1), (1, 0))


def ids_block(block_ids, size):
    rows = size * size // block_ids.shape[0]
    return jnp.broadcast_to(block_ids, (rows, block_ids.shape[0])).reshape(1, size, size)


def ids_of(piece, slots):
    return piece[-1, 0, :slots].astype(jnp.int32)


def line_body(tokens, upstream, blocks, block_ids):
    slots, size = blocks.shape[0], blocks.shape[1]
    rows, depth = tokens.shape
    width = upstream.shape[1]
    half_slots = slots // 2
    part_width = depth // 4
    at_z, half = lax.axis_index("dp"), lax.axis_index("groups")
    at_tensor, at_replica = lax.axis_index("tensor"), lax.axis_index("replica")
    middle = (at_z == 1) | (at_z == 2)
    place_of = jnp.stack([middle.astype(jnp.int32), half, at_tensor, at_replica])
    along = functools.partial(lax.ppermute, axis_name="dp")
    across = functools.partial(lax.ppermute, axis_name="groups", perm=SWAP)
    sideways = functools.partial(lax.ppermute, axis_name="tensor", perm=SWAP)
    cores = functools.partial(lax.ppermute, axis_name="replica", perm=SWAP)
    stage = lax.optimization_barrier

    mine = lax.dynamic_slice_in_dim(blocks, half * half_slots, half_slots, 0)
    other = lax.dynamic_slice_in_dim(blocks, (1 - half) * half_slots, half_slots, 0)
    mine = jnp.concatenate([mine, ids_block(block_ids, size).astype(jnp.bfloat16)])
    part = lax.dynamic_slice_in_dim(tokens, lax.axis_index(INNER) * part_width, part_width, 1)
    both = jnp.concatenate([part, upstream])
    mine, other, both = stage((mine, other, both))

    near_a = along(mine, perm=INWARD)
    far_a = along(mine, perm=MIDDLE)
    both_1o = along(both, perm=OUTWARD)
    grads = line_grads(block_ids, None, ((tokens, upstream),), size, jnp.float32)
    near_a, far_a, both_1o, grads, both_s, other = stage(
        (near_a, far_a, both_1o, grads, both, other)
    )

    both_1i = along(both_s, perm=INWARD)
    end_a = along(near_a, perm=MIDDLE)
    far_b = across(far_a)
    both_1i, end_a, far_b, both_s, other = stage((both_1i, end_a, far_b, both_s, other))
    tokens_1 = lax.all_gather(both_1i[:rows] + both_1o[:rows], INNER)
    upstream_1 = both_1i[rows:] + both_1o[rows:]

    near_b = along(other, perm=INWARD)
    both_2m = along(both_s, perm=MIDDLE)
    end_b = across(end_a)
    ids_1, ids_2, ids_3 = (ids_of(piece, slots) for piece in (near_a, far_a, end_a))
    partial = place_first(
        place_of, (block_ids, ids_1, ids_2, ids_3), (blocks, near_a, far_a, far_b, end_a), depth, width
    )
    near_b, both_2m, end_b, partial, both_1i = stage((near_b, both_2m, end_b, partial, both_1i))

    both_3m = along(both_1i, perm=MIDDLE)
    both_2o = along(both_2m, perm=OUTWARD)
    weight, keep, give = finish_weight(
        place_of, ids_1, ids_3, partial, near_b, end_b, upstream_1
    )
    end_keep, end_give = add_split(place_of, keep, cores(give))
    end_got = sideways(end_give)
    own_keep, own_give = project_back(place_of, weight, upstream)
    both_3m, both_2o, end_got, own_keep, own_give = stage(
        (both_3m, both_2o, end_got, own_keep, own_give)
    )
    sum_out = along(end_keep + end_got, perm=OUTWARD)
    tokens_2 = lax.all_gather(both_2m[:rows] + both_2o[:rows], INNER)
    upstream_2 = both_2m[rows:] + both_2o[rows:]
    token_3o = along(both_3m[:rows], perm=OUTWARD)
    own_keep, own_give = add_split(place_of, own_keep, cores(own_give))
    own_sum = own_keep + sideways(own_give)
    proj, end_proj = project_forward(place_of, weight, tokens, tokens_1)
    sum_out, own_sum, token_3o, proj, end_proj = stage(
        (sum_out, own_sum, token_3o, proj, end_proj)
    )
    tokens_3 = lax.all_gather(both_3m[:rows] + token_3o, INNER)
    quarter = jnp.where(middle, own_sum, sum_out)
    by_tensor, by_core = sideways(quarter), cores(quarter)
    proj_out = along(end_proj, perm=OUTWARD)
    upstream_3o = along(both_3m[rows:], perm=OUTWARD)
    upstream_3 = both_3m[rows:] + upstream_3o
    grads = line_grads(block_ids, grads, ((tokens_1, upstream_1),), size, jnp.float32)
    by_tensor, by_core, grads = stage((by_tensor, by_core, grads))
    by_both = cores(by_tensor)
    projected = jnp.where(middle, proj, proj_out)
    grads = line_grads(block_ids, grads, ((tokens_2, upstream_2),), size, jnp.float32)
    token_grad = assemble(place_of, (quarter, by_core, by_tensor, by_both))
    grads = line_grads(block_ids, grads, ((tokens_3, upstream_3),), size, jnp.bfloat16)
    return projected, token_grad, grads


def solution(mesh):
    line = tuple(mesh.shape[a] for a in ("groups", "dp", "tensor", "replica")) == (2, 4, 2, 2)
    return jax.shard_map(
        line_body if line else general_body,
        mesh=mesh,
        in_specs=(
            P(("groups", "dp"), None),
            P(("groups", "dp"), INNER),
            P(("dp",) + INNER, None, None),
            P(("dp",) + INNER),
        ),
        out_specs=(
            P(("groups", "dp"), INNER),
            P(("groups", "dp"), None),
            P(("groups", "dp") + INNER, None, None),
        ),
        check_vma=False,
    )
```

```python
import functools
import math

import jax
import jax.numpy as jnp
from jax import lax
from jax.experimental import pallas as pl
from jax.experimental.pallas import tpu as pltpu
from jax.sharding import PartitionSpec as P

VMEM_LIMIT = 60 * 1024 * 1024
INNER = ("tensor", "replica")


def whole(space=pltpu.VMEM):
    return pl.BlockSpec(memory_space=space)


def project_kernel(ids, blocks, tokens, upstream, proj, back, weight):
    slots, size = blocks.shape[0], blocks.shape[1]
    depth, width = weight.shape
    cols_n = width // size
    total = (depth // size) * cols_n
    weight[...] = jnp.zeros_like(weight)

    @pl.loop(0, slots, unroll=4)
    def place(s):
        b = ids[s]

        @pl.when(b < total)
        def put():
            r = pl.multiple_of((b // cols_n) * size, size)
            c = pl.multiple_of((b % cols_n) * size, size)
            weight[pl.ds(r, size), pl.ds(c, size)] = blocks[s]

    step = 256

    @pl.loop(0, width // step)
    def forward(n):
        c = pl.multiple_of(n * step, step)
        proj[:, pl.ds(c, step)] = jnp.dot(
            tokens[...], weight[:, pl.ds(c, step)], preferred_element_type=jnp.float32
        ).astype(proj.dtype)

    @pl.loop(0, depth // step, unroll=4)
    def backward(n):
        r = pl.multiple_of(n * step, step)
        back[:, pl.ds(r, step)] = lax.dot_general(
            upstream[...],
            weight[pl.ds(r, step), :],
            (((1,), (1,)), ((), ())),
            preferred_element_type=jnp.float32,
        ).astype(back.dtype)


def project(ids, blocks, tokens, upstream):
    rows, depth = tokens.shape
    width = upstream.shape[1]
    return pl.pallas_call(
        project_kernel,
        out_shape=(
            jax.ShapeDtypeStruct((rows, width), jnp.bfloat16),
            jax.ShapeDtypeStruct((rows, depth), jnp.bfloat16),
        ),
        in_specs=[whole(pltpu.SMEM), whole(), whole(), whole()],
        out_specs=(whole(), whole()),
        scratch_shapes=[pltpu.VMEM((depth, width), jnp.bfloat16)],
        compiler_params=pltpu.CompilerParams(vmem_limit_bytes=VMEM_LIMIT),
        cost_estimate=pl.CostEstimate(
            flops=4 * rows * depth * width,
            bytes_accessed=blocks.size * 2 + rows * (depth + width) * 4,
            transcendentals=0,
        ),
        name="project",
    )(ids, blocks, tokens, upstream)


def block_grad_kernel(ids, tokens, upstream, grads):
    slots, size = grads.shape[0], grads.shape[1]
    parts, slabs, _, part_width = tokens.shape
    cols_n = upstream.shape[2] // size
    per_part = part_width // size
    total = parts * per_part * cols_n

    @pl.loop(0, slots)
    def one(s):
        b = ids[s]

        @pl.when(b < total)
        def fill():
            row = b // cols_n
            part = row // per_part
            r = pl.multiple_of((row % per_part) * size, size)
            c = pl.multiple_of((b % cols_n) * size, size)
            acc = jnp.zeros((size, size), jnp.float32)
            for k in range(slabs):
                acc += lax.dot_general(
                    tokens[part, k, :, pl.ds(r, size)],
                    upstream[k, :, pl.ds(c, size)],
                    (((0,), (0,)), ((), ())),
                    preferred_element_type=jnp.float32,
                )
            grads[s] = acc.astype(grads.dtype)

        @pl.when(b >= total)
        def clear():
            grads[s] = jnp.zeros((size, size), grads.dtype)


def block_grads(ids, tokens, upstream, size):
    slots = ids.shape[0]
    parts, slabs, rows, part_width = tokens.shape
    return pl.pallas_call(
        block_grad_kernel,
        out_shape=jax.ShapeDtypeStruct((slots, size, size), jnp.bfloat16),
        in_specs=[whole(pltpu.SMEM), whole(), whole()],
        out_specs=whole(),
        compiler_params=pltpu.CompilerParams(vmem_limit_bytes=VMEM_LIMIT),
        cost_estimate=pl.CostEstimate(
            flops=2 * slots * slabs * rows * size * size,
            bytes_accessed=2 * (tokens.size + upstream.size + slots * size * size),
            transcendentals=0,
        ),
        name="block_grads",
    )(ids, tokens, upstream)


def general_body(tokens, upstream, blocks, block_ids):
    size = blocks.shape[1]
    all_blocks = lax.all_gather(blocks, "dp", axis=0, tiled=True)
    all_ids = lax.all_gather(block_ids, "dp", axis=0, tiled=True)
    proj, back = project(all_ids, all_blocks, tokens, upstream)
    terms = block_grads(all_ids, tokens[None, None], upstream[None], size)
    grads = lax.psum_scatter(terms, "dp", scatter_dimension=0, tiled=True)
    return proj, lax.psum(back, INNER), grads


def place_blocks(ids, first, blocks, weight, slots):
    size = blocks.shape[1]
    depth, width = weight.shape
    cols_n = width // size
    total = (depth // size) * cols_n

    @pl.loop(0, slots, unroll=4)
    def place(s):
        b = ids[first + s]

        @pl.when(b < total)
        def put():
            r = pl.multiple_of((b // cols_n) * size, size)
            c = pl.multiple_of((b % cols_n) * size, size)
            weight[pl.ds(r, size), pl.ds(c, size)] = blocks[s]


def place_kernel(place_of, ids_0, ids_1, ids_2, ids_3, own, near_a, far_a, far_b, end_a, weight):
    is_middle, half = place_of[0], place_of[1]
    half_slots = far_b.shape[0] - 1
    mine, other = half * half_slots, (1 - half) * half_slots

    @pl.when(is_middle == 1)
    def work():
        weight[...] = jnp.zeros_like(weight)
        place_blocks(ids_0, 0, own, weight, own.shape[0])
        place_blocks(ids_1, mine, near_a, weight, half_slots)
        place_blocks(ids_2, mine, far_a, weight, half_slots)
        place_blocks(ids_2, other, far_b, weight, half_slots)
        place_blocks(ids_3, mine, end_a, weight, half_slots)


def place_first(place_of, ids, pieces, depth, width):
    return pl.pallas_call(
        place_kernel,
        out_shape=jax.ShapeDtypeStruct((depth, width), jnp.bfloat16),
        in_specs=[whole(pltpu.SMEM)] * 5 + [whole()] * 5,
        out_specs=whole(),
        compiler_params=pltpu.CompilerParams(vmem_limit_bytes=VMEM_LIMIT),
        cost_estimate=pl.CostEstimate(
            flops=0, bytes_accessed=depth * width * 4, transcendentals=0
        ),
        name="place_first",
    )(place_of, *ids, *pieces)


def backward_rows(place_of, sources, weight, keep, give):
    depth = weight.shape[0]
    step = 256
    per_part = keep.shape[3] // step
    at_replica = place_of[3]

    @pl.loop(0, depth // step, unroll=2)
    def backward(n):
        r = pl.multiple_of(n * step, step)
        part = n // per_part
        at = pl.multiple_of((n % per_part) * step, step)
        for k, source in enumerate(sources):
            result = lax.dot_general(
                source[...],
                weight[pl.ds(r, step), :],
                (((1,), (1,)), ((), ())),
                preferred_element_type=jnp.float32,
            ).astype(keep.dtype)

            @pl.when(part % 2 == at_replica)
            def mine():
                keep[k, part // 2, :, pl.ds(at, step)] = result

            @pl.when(part % 2 != at_replica)
            def theirs():
                give[k, part // 2, :, pl.ds(at, step)] = result


def finish_kernel(
    place_of, ids_1, ids_3, partial, near_b, end_b, end_upstream, upstream, weight, keep, give,
    held, sem_in, sem_out,
):
    half_slots = near_b.shape[0]
    other = (1 - place_of[1]) * half_slots

    @pl.when(place_of[0] == 1)
    def work():
        load = pltpu.make_async_copy(partial, held, sem_in)
        load.start()
        load.wait()
        place_blocks(ids_1, other, near_b, held, half_slots)
        place_blocks(ids_3, other, end_b, held, half_slots)
        store = pltpu.make_async_copy(held, weight, sem_out)
        store.start()
        backward_rows(place_of, (end_upstream, upstream), held, keep, give)
        store.wait()


def finish_weight(place_of, ids_1, ids_3, partial, near_b, end_b, end_upstream, upstream):
    depth, width = partial.shape
    rows = upstream.shape[0]
    half = jax.ShapeDtypeStruct((2, 2, rows, depth // 4), jnp.bfloat16)
    return pl.pallas_call(
        finish_kernel,
        out_shape=(jax.ShapeDtypeStruct((depth, width), jnp.bfloat16), half, half),
        in_specs=[whole(pltpu.SMEM)] * 3 + [whole(pl.ANY)] + [whole()] * 4,
        out_specs=(whole(pl.ANY), whole(), whole()),
        scratch_shapes=[
            pltpu.VMEM((depth, width), jnp.bfloat16),
            pltpu.SemaphoreType.DMA,
            pltpu.SemaphoreType.DMA,
        ],
        compiler_params=pltpu.CompilerParams(vmem_limit_bytes=VMEM_LIMIT),
        cost_estimate=pl.CostEstimate(
            flops=4 * rows * depth * width,
            bytes_accessed=depth * width * 4 + rows * (depth + width) * 4,
            transcendentals=0,
        ),
        name="finish_weight",
    )(place_of, ids_1, ids_3, partial, near_b, end_b, end_upstream, upstream)


def forward_kernel(place_of, weight, tokens, end_tokens, proj, end_proj):
    width = weight.shape[1]
    parts, rows, part_width = end_tokens.shape
    step = 256

    @pl.when(place_of[0] == 1)
    def work():
        @pl.loop(0, width // step, unroll=2)
        def forward(n):
            c = pl.multiple_of(n * step, step)
            acc = jnp.zeros((rows, step), jnp.float32)
            for q in range(parts):
                acc += jnp.dot(
                    end_tokens[q],
                    weight[q * part_width : (q + 1) * part_width, pl.ds(c, step)],
                    preferred_element_type=jnp.float32,
                )
            end_proj[:, pl.ds(c, step)] = acc.astype(end_proj.dtype)
            proj[:, pl.ds(c, step)] = jnp.dot(
                tokens[...], weight[:, pl.ds(c, step)], preferred_element_type=jnp.float32
            ).astype(proj.dtype)


def project_forward(place_of, weight, tokens, end_tokens):
    depth, width = weight.shape
    rows = tokens.shape[0]
    out = jax.ShapeDtypeStruct((rows, width), jnp.bfloat16)
    return pl.pallas_call(
        forward_kernel,
        out_shape=(out, out),
        in_specs=[whole(pltpu.SMEM)] + [whole()] * 3,
        out_specs=(whole(),) * 2,
        compiler_params=pltpu.CompilerParams(vmem_limit_bytes=VMEM_LIMIT),
        cost_estimate=pl.CostEstimate(
            flops=4 * rows * depth * width,
            bytes_accessed=depth * width * 2 + rows * (depth + width) * 4,
            transcendentals=0,
        ),
        name="project_forward",
    )(place_of, weight, tokens, end_tokens)


def split_kernel(place_of, keep, got, *outs):
    x = place_of[2]
    for n, ref in enumerate(outs):
        k, at = n // 2, (x, 1 - x)[n % 2]
        total = keep[k, at].astype(jnp.float32) + got[k, at].astype(jnp.float32)
        ref[...] = total.astype(ref.dtype)


def add_split(place_of, keep, got):
    out = jax.ShapeDtypeStruct(keep.shape[2:], keep.dtype)
    return pl.pallas_call(
        split_kernel,
        out_shape=(out,) * 4,
        in_specs=[whole(pltpu.SMEM), whole(), whole()],
        out_specs=(whole(),) * 4,
        compiler_params=pltpu.CompilerParams(vmem_limit_bytes=VMEM_LIMIT),
        cost_estimate=pl.CostEstimate(
            flops=keep.size, bytes_accessed=keep.size * 6, transcendentals=0
        ),
        name="add_split",
    )(place_of, keep, got)


def assemble_kernel(place_of, own, by_core, by_tensor, by_both, full):
    x, c = place_of[2], place_of[3]
    width = own.shape[1]
    for ref, xx, cc in (
        (own, x, c), (by_core, x, 1 - c), (by_tensor, 1 - x, c), (by_both, 1 - x, 1 - c)
    ):
        at = pl.multiple_of((xx * 2 + cc) * width, width)
        full[:, pl.ds(at, width)] = ref[...]


def assemble(place_of, quarters):
    rows, width = quarters[0].shape
    return pl.pallas_call(
        assemble_kernel,
        out_shape=jax.ShapeDtypeStruct((rows, 4 * width), quarters[0].dtype),
        in_specs=[whole(pltpu.SMEM)] + [whole()] * 4,
        out_specs=whole(),
        compiler_params=pltpu.CompilerParams(vmem_limit_bytes=VMEM_LIMIT),
        cost_estimate=pl.CostEstimate(
            flops=0, bytes_accessed=rows * width * 16, transcendentals=0
        ),
        name="assemble",
    )(place_of, *quarters)


def line_grads_kernel(pairs_n, has_start, parted, ids, *refs):
    refs = list(refs)
    start = refs.pop(0) if has_start else None
    pairs = [(refs[2 * k], refs[2 * k + 1]) for k in range(pairs_n)]
    grads = refs[2 * pairs_n]
    slots, size = grads.shape[0], grads.shape[1]
    cols_n = pairs[0][1].shape[1] // size
    rows_n = math.prod(pairs[0][0].shape[::2] if parted[0] else pairs[0][0].shape[1:]) // size
    per_part = pairs[0][0].shape[-1] // size
    total = rows_n * cols_n

    group = math.gcd(slots, 8)

    @pl.loop(0, slots // group)
    def some(g):
        for s in [g * group + j for j in range(group)]:
            b = jnp.minimum(ids[s], total - 1)
            row = b // cols_n
            part = row // per_part
            r = pl.multiple_of((row % per_part) * size, size)
            c = pl.multiple_of((b % cols_n) * size, size)
            acc = start[s] if has_start else jnp.zeros((size, size), jnp.float32)
            for (x, d), cut in zip(pairs, parted):
                acc += lax.dot_general(
                    x[part, :, pl.ds(r, size)] if cut else x[:, pl.ds(r, size)],
                    d[:, pl.ds(c, size)],
                    (((0,), (0,)), ((), ())),
                    preferred_element_type=jnp.float32,
                )
            grads[s] = jnp.where(ids[s] < total, acc, 0.0).astype(grads.dtype)


def line_grads(ids, start, pairs, size, out_dtype):
    slots = ids.shape[0]
    rows = pairs[0][1].shape[0]
    flat = [a for pair in pairs for a in pair]
    starts = [] if start is None else [start]
    return pl.pallas_call(
        functools.partial(
            line_grads_kernel,
            len(pairs),
            start is not None,
            tuple(x.ndim == 3 for x, _ in pairs),
        ),
        out_shape=jax.ShapeDtypeStruct((slots, size, size), out_dtype),
        in_specs=[whole(pltpu.SMEM)] + [whole()] * (len(starts) + len(flat)),
        out_specs=whole(),
        compiler_params=pltpu.CompilerParams(vmem_limit_bytes=VMEM_LIMIT),
        cost_estimate=pl.CostEstimate(
            flops=4 * len(pairs) * slots * rows * size * size,
            bytes_accessed=sum(2 * a.size for a in flat) + 4 * slots * size * size,
            transcendentals=0,
        ),
        name="line_grads",
    )(ids, *starts, *flat)


INWARD = ((0, 1), (3, 2))
OUTWARD = ((1, 0), (2, 3))
PAIRS = INWARD + OUTWARD
MIDDLE = ((1, 2), (2, 1))
SWAP = ((0, 1), (1, 0))


def ids_block(block_ids, size):
    rows = size * size // block_ids.shape[0]
    return jnp.broadcast_to(block_ids, (rows, block_ids.shape[0])).reshape(1, size, size)


def ids_of(piece, slots):
    return piece[-1, 0, :slots].astype(jnp.int32)


def line_body(tokens, upstream, blocks, block_ids):
    slots, size = blocks.shape[0], blocks.shape[1]
    rows, depth = tokens.shape
    width = upstream.shape[1]
    half_slots = slots // 2
    part_width = depth // 4
    at_z, half = lax.axis_index("dp"), lax.axis_index("groups")
    at_tensor, at_replica = lax.axis_index("tensor"), lax.axis_index("replica")
    middle = (at_z == 1) | (at_z == 2)
    place_of = jnp.stack([middle.astype(jnp.int32), half, at_tensor, at_replica])
    along = functools.partial(lax.ppermute, axis_name="dp")
    across = functools.partial(lax.ppermute, axis_name="groups", perm=SWAP)
    sideways = functools.partial(lax.ppermute, axis_name="tensor", perm=SWAP)
    cores = functools.partial(lax.ppermute, axis_name="replica", perm=SWAP)
    stage = lax.optimization_barrier

    mine = lax.dynamic_slice_in_dim(blocks, half * half_slots, half_slots, 0)
    other = lax.dynamic_slice_in_dim(blocks, (1 - half) * half_slots, half_slots, 0)
    mine = jnp.concatenate([mine, ids_block(block_ids, size).astype(jnp.bfloat16)])
    part = lax.dynamic_slice_in_dim(tokens, lax.axis_index(INNER) * part_width, part_width, 1)
    both = jnp.concatenate([part, upstream])
    mine, other, both = stage((mine, other, both))

    near_a = along(mine, perm=INWARD)
    far_a = along(mine, perm=MIDDLE)
    grads = line_grads(block_ids, None, ((tokens, upstream),), size, jnp.float32)
    near_a, far_a, grads, both, other = stage((near_a, far_a, grads, both, other))

    end_a = along(near_a, perm=MIDDLE)
    both_1 = along(both, perm=PAIRS)
    far_b = across(far_a)
    both_1, end_a, far_b, both, other = stage((both_1, end_a, far_b, both, other))
    tokens_1 = lax.all_gather(both_1[:rows], INNER)
    upstream_1 = both_1[rows:]

    near_b = along(other, perm=INWARD)
    both_2m = along(both, perm=MIDDLE)
    end_b = across(end_a)
    ids_1, ids_2, ids_3 = (ids_of(piece, slots) for piece in (near_a, far_a, end_a))
    partial = place_first(
        place_of, (block_ids, ids_1, ids_2, ids_3), (blocks, near_a, far_a, far_b, end_a), depth, width
    )
    near_b, both_2m, end_b, partial, both_1, tokens_1 = stage(
        (near_b, both_2m, end_b, partial, both_1, tokens_1)
    )

    both_3m = along(both_1, perm=MIDDLE)
    both_2o = along(both_2m, perm=OUTWARD)
    weight, keep, give = finish_weight(
        place_of, ids_1, ids_3, partial, near_b, end_b, upstream_1, upstream
    )
    end_keep, end_give, own_keep, own_give = add_split(place_of, keep, cores(give))
    end_got = sideways(end_give)
    proj, end_proj = project_forward(place_of, weight, tokens, tokens_1)
    end_got, own_give, both_3m, both_2o, proj, end_proj = stage(
        (end_got, own_give, both_3m, both_2o, proj, end_proj)
    )
    sum_out = along(end_keep + end_got, perm=OUTWARD)
    own_got = sideways(own_give)
    token_3o = along(both_3m[:rows], perm=OUTWARD)
    tokens_2 = lax.all_gather(both_2m[:rows] + both_2o[:rows], INNER)
    upstream_2 = both_2m[rows:] + both_2o[rows:]
    grads = line_grads(block_ids, grads, ((tokens_1, upstream_1),), size, jnp.float32)
    sum_out, own_got, token_3o, grads = stage((sum_out, own_got, token_3o, grads))
    own_sum = own_keep + own_got
    tokens_3 = lax.all_gather(both_3m[:rows] + token_3o, INNER)
    quarter = jnp.where(middle, own_sum, sum_out)
    by_tensor, by_core = sideways(quarter), cores(quarter)
    proj_out = along(end_proj, perm=OUTWARD)
    upstream_3o = along(both_3m[rows:], perm=OUTWARD)
    upstream_3 = both_3m[rows:] + upstream_3o
    by_tensor, by_core = stage((by_tensor, by_core))
    by_both = cores(by_tensor)
    projected = jnp.where(middle, proj, proj_out)
    grads = line_grads(block_ids, grads, ((tokens_2, upstream_2),), size, jnp.float32)
    token_grad = assemble(place_of, (quarter, by_core, by_tensor, by_both))
    grads = line_grads(block_ids, grads, ((tokens_3, upstream_3),), size, jnp.bfloat16)
    return projected, token_grad, grads


def solution(mesh):
    line = tuple(mesh.shape[a] for a in ("groups", "dp", "tensor", "replica")) == (2, 4, 2, 2)
    return jax.shard_map(
        line_body if line else general_body,
        mesh=mesh,
        in_specs=(
            P(("groups", "dp"), None),
            P(("groups", "dp"), INNER),
            P(("dp",) + INNER, None, None),
            P(("dp",) + INNER),
        ),
        out_specs=(
            P(("groups", "dp"), INNER),
            P(("groups", "dp"), None),
            P(("groups", "dp") + INNER, None, None),
        ),
        check_vma=False,
    )
```

```python
import functools
import math

import jax
import jax.numpy as jnp
from jax import lax
from jax.experimental import pallas as pl
from jax.experimental.pallas import tpu as pltpu
from jax.sharding import PartitionSpec as P

VMEM_LIMIT = 60 * 1024 * 1024
INNER = ("tensor", "replica")


def whole(space=pltpu.VMEM):
    return pl.BlockSpec(memory_space=space)


def project_kernel(ids, blocks, tokens, upstream, proj, back, weight):
    slots, size = blocks.shape[0], blocks.shape[1]
    depth, width = weight.shape
    cols_n = width // size
    total = (depth // size) * cols_n
    weight[...] = jnp.zeros_like(weight)

    @pl.loop(0, slots, unroll=4)
    def place(s):
        b = ids[s]

        @pl.when(b < total)
        def put():
            r = pl.multiple_of((b // cols_n) * size, size)
            c = pl.multiple_of((b % cols_n) * size, size)
            weight[pl.ds(r, size), pl.ds(c, size)] = blocks[s]

    step = 256

    @pl.loop(0, width // step)
    def forward(n):
        c = pl.multiple_of(n * step, step)
        proj[:, pl.ds(c, step)] = jnp.dot(
            tokens[...], weight[:, pl.ds(c, step)], preferred_element_type=jnp.float32
        ).astype(proj.dtype)

    @pl.loop(0, depth // step, unroll=4)
    def backward(n):
        r = pl.multiple_of(n * step, step)
        back[:, pl.ds(r, step)] = lax.dot_general(
            upstream[...],
            weight[pl.ds(r, step), :],
            (((1,), (1,)), ((), ())),
            preferred_element_type=jnp.float32,
        ).astype(back.dtype)


def project(ids, blocks, tokens, upstream):
    rows, depth = tokens.shape
    width = upstream.shape[1]
    return pl.pallas_call(
        project_kernel,
        out_shape=(
            jax.ShapeDtypeStruct((rows, width), jnp.bfloat16),
            jax.ShapeDtypeStruct((rows, depth), jnp.bfloat16),
        ),
        in_specs=[whole(pltpu.SMEM), whole(), whole(), whole()],
        out_specs=(whole(), whole()),
        scratch_shapes=[pltpu.VMEM((depth, width), jnp.bfloat16)],
        compiler_params=pltpu.CompilerParams(vmem_limit_bytes=VMEM_LIMIT),
        cost_estimate=pl.CostEstimate(
            flops=4 * rows * depth * width,
            bytes_accessed=blocks.size * 2 + rows * (depth + width) * 4,
            transcendentals=0,
        ),
        name="project",
    )(ids, blocks, tokens, upstream)


def block_grad_kernel(ids, tokens, upstream, grads):
    slots, size = grads.shape[0], grads.shape[1]
    parts, slabs, _, part_width = tokens.shape
    cols_n = upstream.shape[2] // size
    per_part = part_width // size
    total = parts * per_part * cols_n

    @pl.loop(0, slots)
    def one(s):
        b = ids[s]

        @pl.when(b < total)
        def fill():
            row = b // cols_n
            part = row // per_part
            r = pl.multiple_of((row % per_part) * size, size)
            c = pl.multiple_of((b % cols_n) * size, size)
            acc = jnp.zeros((size, size), jnp.float32)
            for k in range(slabs):
                acc += lax.dot_general(
                    tokens[part, k, :, pl.ds(r, size)],
                    upstream[k, :, pl.ds(c, size)],
                    (((0,), (0,)), ((), ())),
                    preferred_element_type=jnp.float32,
                )
            grads[s] = acc.astype(grads.dtype)

        @pl.when(b >= total)
        def clear():
            grads[s] = jnp.zeros((size, size), grads.dtype)


def block_grads(ids, tokens, upstream, size):
    slots = ids.shape[0]
    parts, slabs, rows, part_width = tokens.shape
    return pl.pallas_call(
        block_grad_kernel,
        out_shape=jax.ShapeDtypeStruct((slots, size, size), jnp.bfloat16),
        in_specs=[whole(pltpu.SMEM), whole(), whole()],
        out_specs=whole(),
        compiler_params=pltpu.CompilerParams(vmem_limit_bytes=VMEM_LIMIT),
        cost_estimate=pl.CostEstimate(
            flops=2 * slots * slabs * rows * size * size,
            bytes_accessed=2 * (tokens.size + upstream.size + slots * size * size),
            transcendentals=0,
        ),
        name="block_grads",
    )(ids, tokens, upstream)


def general_body(tokens, upstream, blocks, block_ids):
    size = blocks.shape[1]
    all_blocks = lax.all_gather(blocks, "dp", axis=0, tiled=True)
    all_ids = lax.all_gather(block_ids, "dp", axis=0, tiled=True)
    proj, back = project(all_ids, all_blocks, tokens, upstream)
    terms = block_grads(all_ids, tokens[None, None], upstream[None], size)
    grads = lax.psum_scatter(terms, "dp", scatter_dimension=0, tiled=True)
    return proj, lax.psum(back, INNER), grads


def place_blocks(ids, first, blocks, weight, turned, slots):
    size = blocks.shape[1]
    depth, width = turned.shape[::-1] if weight is None else weight.shape
    cols_n = width // size
    total = (depth // size) * cols_n

    @pl.loop(0, slots, unroll=4)
    def place(s):
        b = ids[first + s]

        @pl.when(b < total)
        def put():
            r = pl.multiple_of((b // cols_n) * size, size)
            c = pl.multiple_of((b % cols_n) * size, size)
            if weight is not None:
                weight[pl.ds(r, size), pl.ds(c, size)] = blocks[s]
            if turned is not None:
                turned[pl.ds(c, size), pl.ds(r, size)] = blocks[s].T


def place_kernel(
    place_of, ids_0, ids_1, ids_2, ids_3, own, near_a, far_a, far_b, end_a, weight, turned
):
    is_middle, half = place_of[0], place_of[1]
    half_slots = far_b.shape[0] - 1
    mine, other = half * half_slots, (1 - half) * half_slots

    @pl.when(is_middle == 1)
    def work():
        weight[...] = jnp.zeros_like(weight)
        turned[...] = jnp.zeros_like(turned)
        place_blocks(ids_0, 0, own, weight, turned, own.shape[0])
        place_blocks(ids_1, mine, near_a, weight, turned, half_slots)
        place_blocks(ids_2, mine, far_a, weight, turned, half_slots)
        place_blocks(ids_2, other, far_b, weight, turned, half_slots)
        place_blocks(ids_3, mine, end_a, weight, turned, half_slots)


def place_first(place_of, ids, pieces, depth, width):
    return pl.pallas_call(
        place_kernel,
        out_shape=(
            jax.ShapeDtypeStruct((depth, width), jnp.bfloat16),
            jax.ShapeDtypeStruct((width, depth), jnp.bfloat16),
        ),
        in_specs=[whole(pltpu.SMEM)] * 5 + [whole()] * 5,
        out_specs=(whole(), whole()),
        compiler_params=pltpu.CompilerParams(vmem_limit_bytes=VMEM_LIMIT),
        cost_estimate=pl.CostEstimate(
            flops=0, bytes_accessed=depth * width * 6, transcendentals=0
        ),
        name="place_first",
    )(place_of, *ids, *pieces)


def back_kernel(
    place_of, ids_1, ids_3, partial, near_b, end_b, all_upstream, upstream, keep, give,
    held, sources, sem,
):
    half_slots = near_b.shape[0]
    other = (1 - place_of[1]) * half_slots
    rows, width = upstream.shape
    depth = held.shape[1]
    step = 256
    per_part = keep.shape[3] // step

    @pl.when(place_of[0] == 1)
    def work():
        load = pltpu.make_async_copy(partial, held, sem)
        load.start()
        sources[:rows] = all_upstream[place_of[5]]
        sources[rows:] = upstream[...]
        load.wait()
        place_blocks(ids_1, other, near_b, None, held, half_slots)
        place_blocks(ids_3, other, end_b, None, held, half_slots)

        def column(part, target, x):
            @pl.loop(0, per_part, unroll=2)
            def backward(n):
                at = pl.multiple_of(n * step, step)
                result = jnp.dot(
                    sources[...],
                    held[:, pl.ds(pl.multiple_of(part * per_part * step + at, step), step)],
                    preferred_element_type=jnp.float32,
                ).astype(target.dtype)
                target[0, x, :, pl.ds(at, step)] = result[:rows]
                target[1, x, :, pl.ds(at, step)] = result[rows:]

        for x in range(2):
            column(2 * x + place_of[3], keep, x)
            column(2 * x + 1 - place_of[3], give, x)


def project_back(place_of, ids_1, ids_3, partial, near_b, end_b, all_upstream, upstream):
    width, depth = partial.shape
    rows = upstream.shape[0]
    half = jax.ShapeDtypeStruct((2, 2, rows, depth // 4), jnp.bfloat16)
    return pl.pallas_call(
        back_kernel,
        out_shape=(half, half),
        in_specs=[whole(pltpu.SMEM)] * 3 + [whole(pl.ANY)] + [whole()] * 4,
        out_specs=(whole(), whole()),
        scratch_shapes=[
            pltpu.VMEM((width, depth), jnp.bfloat16),
            pltpu.VMEM((2 * rows, width), jnp.bfloat16),
            pltpu.SemaphoreType.DMA,
        ],
        compiler_params=pltpu.CompilerParams(vmem_limit_bytes=VMEM_LIMIT),
        cost_estimate=pl.CostEstimate(
            flops=4 * rows * depth * width,
            bytes_accessed=depth * width * 2 + rows * (depth + width) * 4,
            transcendentals=0,
        ),
        name="project_back",
    )(place_of, ids_1, ids_3, partial, near_b, end_b, all_upstream, upstream)


def forward_kernel(
    place_of, ids_1, ids_3, partial, near_b, end_b, tokens, gathered, proj, end_proj, held, sem
):
    half_slots = near_b.shape[0]
    other = (1 - place_of[1]) * half_slots
    depth, width = held.shape
    parts, _, rows, part_width = gathered.shape
    step = 256

    @pl.when(place_of[0] == 1)
    def work():
        load = pltpu.make_async_copy(partial, held, sem)
        load.start()
        load.wait()
        place_blocks(ids_1, other, near_b, held, None, half_slots)
        place_blocks(ids_3, other, end_b, held, None, half_slots)

        @pl.loop(0, width // step, unroll=2)
        def forward(n):
            c = pl.multiple_of(n * step, step)
            acc = jnp.zeros((rows, step), jnp.float32)
            for q in range(parts):
                acc += jnp.dot(
                    gathered[q, place_of[4]],
                    held[q * part_width : (q + 1) * part_width, pl.ds(c, step)],
                    preferred_element_type=jnp.float32,
                )
            end_proj[:, pl.ds(c, step)] = acc.astype(end_proj.dtype)
            proj[:, pl.ds(c, step)] = jnp.dot(
                tokens[...], held[:, pl.ds(c, step)], preferred_element_type=jnp.float32
            ).astype(proj.dtype)


def project_forward(place_of, ids_1, ids_3, partial, near_b, end_b, tokens, gathered):
    depth, width = partial.shape
    rows = tokens.shape[0]
    out = jax.ShapeDtypeStruct((rows, width), jnp.bfloat16)
    return pl.pallas_call(
        forward_kernel,
        out_shape=(out, out),
        in_specs=[whole(pltpu.SMEM)] * 3 + [whole(pl.ANY)] + [whole()] * 4,
        out_specs=(whole(),) * 2,
        scratch_shapes=[pltpu.VMEM((depth, width), jnp.bfloat16), pltpu.SemaphoreType.DMA],
        compiler_params=pltpu.CompilerParams(vmem_limit_bytes=VMEM_LIMIT),
        cost_estimate=pl.CostEstimate(
            flops=4 * rows * depth * width,
            bytes_accessed=depth * width * 2 + rows * (depth + width) * 4,
            transcendentals=0,
        ),
        name="project_forward",
    )(place_of, ids_1, ids_3, partial, near_b, end_b, tokens, gathered)


def others_kernel(place_of, quarters, others):
    count = quarters.shape[0]
    for j in range(count - 1):
        others[j] = quarters[lax.rem(place_of[6] + 1 + j, count)]


def other_slabs(place_of, quarters):
    return pl.pallas_call(
        others_kernel,
        out_shape=jax.ShapeDtypeStruct((quarters.shape[0] - 1,) + quarters.shape[1:], quarters.dtype),
        in_specs=[whole(pltpu.SMEM), whole()],
        out_specs=whole(),
        compiler_params=pltpu.CompilerParams(vmem_limit_bytes=VMEM_LIMIT),
        cost_estimate=pl.CostEstimate(
            flops=0, bytes_accessed=quarters.size * 4, transcendentals=0
        ),
        name="other_slabs",
    )(place_of, quarters)


def split_kernel(place_of, keep, got, *outs):
    x = place_of[2]
    for n, ref in enumerate(outs):
        k, at = n // 2, (x, 1 - x)[n % 2]
        total = keep[k, at].astype(jnp.float32) + got[k, at].astype(jnp.float32)
        ref[...] = total.astype(ref.dtype)


def add_split(place_of, keep, got):
    out = jax.ShapeDtypeStruct(keep.shape[2:], keep.dtype)
    return pl.pallas_call(
        split_kernel,
        out_shape=(out,) * 4,
        in_specs=[whole(pltpu.SMEM), whole(), whole()],
        out_specs=(whole(),) * 4,
        compiler_params=pltpu.CompilerParams(vmem_limit_bytes=VMEM_LIMIT),
        cost_estimate=pl.CostEstimate(
            flops=keep.size, bytes_accessed=keep.size * 6, transcendentals=0
        ),
        name="add_split",
    )(place_of, keep, got)


def assemble_kernel(place_of, own, by_core, by_tensor, by_both, full):
    x, c = place_of[2], place_of[3]
    width = own.shape[1]
    for ref, xx, cc in (
        (own, x, c), (by_core, x, 1 - c), (by_tensor, 1 - x, c), (by_both, 1 - x, 1 - c)
    ):
        at = pl.multiple_of((xx * 2 + cc) * width, width)
        full[:, pl.ds(at, width)] = ref[...]


def assemble(place_of, quarters):
    rows, width = quarters[0].shape
    return pl.pallas_call(
        assemble_kernel,
        out_shape=jax.ShapeDtypeStruct((rows, 4 * width), quarters[0].dtype),
        in_specs=[whole(pltpu.SMEM)] + [whole()] * 4,
        out_specs=whole(),
        compiler_params=pltpu.CompilerParams(vmem_limit_bytes=VMEM_LIMIT),
        cost_estimate=pl.CostEstimate(
            flops=0, bytes_accessed=rows * width * 16, transcendentals=0
        ),
        name="assemble",
    )(place_of, *quarters)


def line_grads_kernel(place_of, ids, tokens, upstream, gathered, all_upstream, grads):
    slots, size = grads.shape[0], grads.shape[1]
    cols_n = upstream.shape[1] // size
    total = (tokens.shape[1] // size) * cols_n
    parts, others_n, _, part_width = gathered.shape
    per_part = part_width // size
    group = math.gcd(slots, 8)
    contract = (((0,), (0,)), ((), ()))

    @pl.loop(0, slots // group)
    def some(g):
        for s in [g * group + j for j in range(group)]:
            b = jnp.minimum(ids[s], total - 1)
            row = b // cols_n
            part = row // per_part
            at = pl.ds(pl.multiple_of((row % per_part) * size, size), size)
            c = pl.ds(pl.multiple_of((b % cols_n) * size, size), size)
            acc = lax.dot_general(
                tokens[:, pl.ds(pl.multiple_of(row * size, size), size)],
                upstream[:, c],
                contract,
                preferred_element_type=jnp.float32,
            )
            for j in range(others_n):
                slab = lax.rem(place_of[6] + 1 + j, others_n + 1)
                acc += lax.dot_general(
                    gathered[part, j, :, at],
                    all_upstream[slab, :, c],
                    contract,
                    preferred_element_type=jnp.float32,
                )
            grads[s] = jnp.where(ids[s] < total, acc, 0.0).astype(grads.dtype)


def line_grads(place_of, ids, tokens, upstream, gathered, all_upstream, size):
    slots = ids.shape[0]
    rows = upstream.shape[0]
    return pl.pallas_call(
        line_grads_kernel,
        out_shape=jax.ShapeDtypeStruct((slots, size, size), jnp.bfloat16),
        in_specs=[whole(pltpu.SMEM)] * 2 + [whole()] * 4,
        out_specs=whole(),
        compiler_params=pltpu.CompilerParams(vmem_limit_bytes=VMEM_LIMIT),
        cost_estimate=pl.CostEstimate(
            flops=8 * slots * rows * size * size,
            bytes_accessed=2 * (4 * tokens.size + 5 * upstream.size + slots * size * size),
            transcendentals=0,
        ),
        name="line_grads",
    )(place_of, ids, tokens, upstream, gathered, all_upstream)


INWARD = ((0, 1), (3, 2))
OUTWARD = ((1, 0), (2, 3))
MIDDLE = ((1, 2), (2, 1))
SWAP = ((0, 1), (1, 0))


def ids_block(block_ids, size):
    rows = size * size // block_ids.shape[0]
    return jnp.broadcast_to(block_ids, (rows, block_ids.shape[0])).reshape(1, size, size)


def ids_of(piece, slots):
    return piece[-1, 0, :slots].astype(jnp.int32)


def line_body(tokens, upstream, blocks, block_ids):
    slots, size = blocks.shape[0], blocks.shape[1]
    depth, width = tokens.shape[1], upstream.shape[1]
    half_slots = slots // 2
    part_width = depth // 4
    at_z, half = lax.axis_index("dp"), lax.axis_index("groups")
    at_tensor, at_replica = lax.axis_index("tensor"), lax.axis_index("replica")
    middle = (at_z == 1) | (at_z == 2)
    end = jnp.where(at_z == 1, 0, 3)
    place_of = jnp.stack(
        [middle.astype(jnp.int32), half, at_tensor, at_replica, (end + 3 - at_z) % 4, end, at_z]
    )
    along = functools.partial(lax.ppermute, axis_name="dp")
    across = functools.partial(lax.ppermute, axis_name="groups", perm=SWAP)
    sideways = functools.partial(lax.ppermute, axis_name="tensor", perm=SWAP)
    cores = functools.partial(lax.ppermute, axis_name="replica", perm=SWAP)
    stage = lax.optimization_barrier

    mine = lax.dynamic_slice_in_dim(blocks, half * half_slots, half_slots, 0)
    other = lax.dynamic_slice_in_dim(blocks, (1 - half) * half_slots, half_slots, 0)
    mine = jnp.concatenate([mine, ids_block(block_ids, size).astype(jnp.bfloat16)])
    part = lax.dynamic_slice_in_dim(tokens, lax.axis_index(INNER) * part_width, part_width, 1)
    all_upstream = lax.all_gather(upstream, "dp")
    quarters = lax.all_gather(part, "dp")
    mine, other = stage((mine, other))

    near_a = along(mine, perm=INWARD)
    far_a = along(mine, perm=MIDDLE)
    near_a, far_a, other = stage((near_a, far_a, other))

    end_a = along(near_a, perm=MIDDLE)
    far_b = across(far_a)
    end_a, far_b, other = stage((end_a, far_b, other))

    near_b = along(other, perm=INWARD)
    end_b = across(end_a)
    ids_1, ids_2, ids_3 = (ids_of(piece, slots) for piece in (near_a, far_a, end_a))
    partial, turned = place_first(
        place_of, (block_ids, ids_1, ids_2, ids_3), (blocks, near_a, far_a, far_b, end_a), depth, width
    )
    near_b, end_b, partial, turned = stage((near_b, end_b, partial, turned))

    gathered = lax.all_gather(other_slabs(place_of, quarters), INNER)
    last = (near_b, end_b)
    keep, give = project_back(place_of, ids_1, ids_3, turned, *last, all_upstream, upstream)
    end_keep, end_give, own_keep, own_give = add_split(place_of, keep, cores(give))
    end_got, own_give = stage((sideways(end_give), own_give))
    sum_out = along(end_keep + end_got, perm=OUTWARD)
    own_got = sideways(own_give)
    sum_out, own_got = stage((sum_out, own_got))
    quarter = jnp.where(middle, own_keep + own_got, sum_out)
    by_tensor, by_core = stage((sideways(quarter), cores(quarter)))
    by_both = cores(by_tensor)
    token_grad = assemble(place_of, (quarter, by_core, by_tensor, by_both))
    proj, end_proj = project_forward(place_of, ids_1, ids_3, partial, *last, tokens, gathered)
    projected = jnp.where(middle, proj, along(end_proj, perm=OUTWARD))
    grads = line_grads(place_of, block_ids, tokens, upstream, gathered, all_upstream, size)
    return projected, token_grad, grads


def solution(mesh):
    line = tuple(mesh.shape[a] for a in ("groups", "dp", "tensor", "replica")) == (2, 4, 2, 2)
    return jax.shard_map(
        line_body if line else general_body,
        mesh=mesh,
        in_specs=(
            P(("groups", "dp"), None),
            P(("groups", "dp"), INNER),
            P(("dp",) + INNER, None, None),
            P(("dp",) + INNER),
        ),
        out_specs=(
            P(("groups", "dp"), INNER),
            P(("groups", "dp"), None),
            P(("groups", "dp") + INNER, None, None),
        ),
        check_vma=False,
    )
```

```python
import functools
import math

import jax
import jax.numpy as jnp
from jax import lax
from jax.experimental import pallas as pl
from jax.experimental.pallas import tpu as pltpu
from jax.sharding import PartitionSpec as P

VMEM_LIMIT = 60 * 1024 * 1024
INNER = ("tensor", "replica")


def whole(space=pltpu.VMEM):
    return pl.BlockSpec(memory_space=space)


def project_kernel(ids, blocks, tokens, upstream, proj, back, weight):
    slots, size = blocks.shape[0], blocks.shape[1]
    depth, width = weight.shape
    cols_n = width // size
    total = (depth // size) * cols_n
    weight[...] = jnp.zeros_like(weight)

    @pl.loop(0, slots, unroll=4)
    def place(s):
        b = ids[s]

        @pl.when(b < total)
        def put():
            r = pl.multiple_of((b // cols_n) * size, size)
            c = pl.multiple_of((b % cols_n) * size, size)
            weight[pl.ds(r, size), pl.ds(c, size)] = blocks[s]

    step = 256

    @pl.loop(0, width // step)
    def forward(n):
        c = pl.multiple_of(n * step, step)
        proj[:, pl.ds(c, step)] = jnp.dot(
            tokens[...], weight[:, pl.ds(c, step)], preferred_element_type=jnp.float32
        ).astype(proj.dtype)

    @pl.loop(0, depth // step, unroll=4)
    def backward(n):
        r = pl.multiple_of(n * step, step)
        back[:, pl.ds(r, step)] = lax.dot_general(
            upstream[...],
            weight[pl.ds(r, step), :],
            (((1,), (1,)), ((), ())),
            preferred_element_type=jnp.float32,
        ).astype(back.dtype)


def project(ids, blocks, tokens, upstream):
    rows, depth = tokens.shape
    width = upstream.shape[1]
    return pl.pallas_call(
        project_kernel,
        out_shape=(
            jax.ShapeDtypeStruct((rows, width), jnp.bfloat16),
            jax.ShapeDtypeStruct((rows, depth), jnp.bfloat16),
        ),
        in_specs=[whole(pltpu.SMEM), whole(), whole(), whole()],
        out_specs=(whole(), whole()),
        scratch_shapes=[pltpu.VMEM((depth, width), jnp.bfloat16)],
        compiler_params=pltpu.CompilerParams(vmem_limit_bytes=VMEM_LIMIT),
        cost_estimate=pl.CostEstimate(
            flops=4 * rows * depth * width,
            bytes_accessed=blocks.size * 2 + rows * (depth + width) * 4,
            transcendentals=0,
        ),
        name="project",
    )(ids, blocks, tokens, upstream)


def block_grad_kernel(ids, tokens, upstream, grads):
    slots, size = grads.shape[0], grads.shape[1]
    parts, slabs, _, part_width = tokens.shape
    cols_n = upstream.shape[2] // size
    per_part = part_width // size
    total = parts * per_part * cols_n

    @pl.loop(0, slots)
    def one(s):
        b = ids[s]

        @pl.when(b < total)
        def fill():
            row = b // cols_n
            part = row // per_part
            r = pl.multiple_of((row % per_part) * size, size)
            c = pl.multiple_of((b % cols_n) * size, size)
            acc = jnp.zeros((size, size), jnp.float32)
            for k in range(slabs):
                acc += lax.dot_general(
                    tokens[part, k, :, pl.ds(r, size)],
                    upstream[k, :, pl.ds(c, size)],
                    (((0,), (0,)), ((), ())),
                    preferred_element_type=jnp.float32,
                )
            grads[s] = acc.astype(grads.dtype)

        @pl.when(b >= total)
        def clear():
            grads[s] = jnp.zeros((size, size), grads.dtype)


def block_grads(ids, tokens, upstream, size):
    slots = ids.shape[0]
    parts, slabs, rows, part_width = tokens.shape
    return pl.pallas_call(
        block_grad_kernel,
        out_shape=jax.ShapeDtypeStruct((slots, size, size), jnp.bfloat16),
        in_specs=[whole(pltpu.SMEM), whole(), whole()],
        out_specs=whole(),
        compiler_params=pltpu.CompilerParams(vmem_limit_bytes=VMEM_LIMIT),
        cost_estimate=pl.CostEstimate(
            flops=2 * slots * slabs * rows * size * size,
            bytes_accessed=2 * (tokens.size + upstream.size + slots * size * size),
            transcendentals=0,
        ),
        name="block_grads",
    )(ids, tokens, upstream)


def general_body(tokens, upstream, blocks, block_ids):
    size = blocks.shape[1]
    all_blocks = lax.all_gather(blocks, "dp", axis=0, tiled=True)
    all_ids = lax.all_gather(block_ids, "dp", axis=0, tiled=True)
    proj, back = project(all_ids, all_blocks, tokens, upstream)
    terms = block_grads(all_ids, tokens[None, None], upstream[None], size)
    grads = lax.psum_scatter(terms, "dp", scatter_dimension=0, tiled=True)
    return proj, lax.psum(back, INNER), grads


def place_blocks(ids, first, blocks, weight, turned, slots):
    size = blocks.shape[1]
    depth, width = turned.shape[::-1] if weight is None else weight.shape
    cols_n = width // size
    total = (depth // size) * cols_n

    @pl.loop(0, slots, unroll=4)
    def place(s):
        b = ids[first + s]

        @pl.when(b < total)
        def put():
            r = pl.multiple_of((b // cols_n) * size, size)
            c = pl.multiple_of((b % cols_n) * size, size)
            if weight is not None:
                weight[pl.ds(r, size), pl.ds(c, size)] = blocks[s]
            if turned is not None:
                turned[pl.ds(c, size), pl.ds(r, size)] = blocks[s].T


def place_kernel(
    place_of, ids_0, ids_1, ids_2, ids_3, own, near_a, far_a, far_b, end_a, weight, turned
):
    is_middle, half = place_of[0], place_of[1]
    half_slots = far_b.shape[0] - 1
    mine, other = half * half_slots, (1 - half) * half_slots

    @pl.when(is_middle == 1)
    def work():
        weight[...] = jnp.zeros_like(weight)
        turned[...] = jnp.zeros_like(turned)
        place_blocks(ids_0, 0, own, weight, turned, own.shape[0])
        place_blocks(ids_1, mine, near_a, weight, turned, half_slots)
        place_blocks(ids_2, mine, far_a, weight, turned, half_slots)
        place_blocks(ids_2, other, far_b, weight, turned, half_slots)
        place_blocks(ids_3, mine, end_a, weight, turned, half_slots)


def place_first(place_of, ids, pieces, depth, width):
    return pl.pallas_call(
        place_kernel,
        out_shape=(
            jax.ShapeDtypeStruct((depth, width), jnp.bfloat16),
            jax.ShapeDtypeStruct((width, depth), jnp.bfloat16),
        ),
        in_specs=[whole(pltpu.SMEM)] * 5 + [whole()] * 5,
        out_specs=(whole(), whole()),
        compiler_params=pltpu.CompilerParams(vmem_limit_bytes=VMEM_LIMIT),
        cost_estimate=pl.CostEstimate(
            flops=0, bytes_accessed=depth * width * 6, transcendentals=0
        ),
        name="place_first",
    )(place_of, *ids, *pieces)


def back_kernel(
    place_of, ids_1, ids_3, partial, near_b, end_b, end_upstream, upstream,
    end_keep, own_keep, own_give, end_give_0, end_give_1, held, sources, sem,
):
    half_slots = near_b.shape[0]
    other = (1 - place_of[1]) * half_slots
    rows, width = upstream.shape
    step = 256
    per_part = end_keep.shape[2] // step

    @pl.when(place_of[0] == 1)
    def work():
        load = pltpu.make_async_copy(partial, held, sem)
        load.start()
        sources[:rows] = end_upstream[...]
        sources[rows:] = upstream[...]
        load.wait()
        place_blocks(ids_1, other, near_b, None, held, half_slots)
        place_blocks(ids_3, other, end_b, None, held, half_slots)

        def column(part, end_target, own_target):
            @pl.loop(0, per_part, unroll=2)
            def backward(n):
                at = pl.multiple_of(n * step, step)
                result = jnp.dot(
                    sources[...],
                    held[:, pl.ds(pl.multiple_of(part * per_part * step + at, step), step)],
                    preferred_element_type=jnp.float32,
                ).astype(own_target.dtype)
                end_target[:, pl.ds(at, step)] = result[:rows]
                own_target[:, pl.ds(at, step)] = result[rows:]

        for x, end_give in enumerate((end_give_0, end_give_1)):
            column(2 * x + place_of[3], end_keep.at[x], own_keep.at[x])
            column(2 * x + 1 - place_of[3], end_give, own_give.at[x])


def project_back(place_of, ids_1, ids_3, partial, near_b, end_b, end_upstream, upstream):
    width, depth = partial.shape
    rows = upstream.shape[0]
    quarter = jax.ShapeDtypeStruct((rows, depth // 4), jnp.bfloat16)
    half = jax.ShapeDtypeStruct((2, rows, depth // 4), jnp.bfloat16)
    return pl.pallas_call(
        back_kernel,
        out_shape=(half, half, half, quarter, quarter),
        in_specs=[whole(pltpu.SMEM)] * 3 + [whole(pl.ANY)] + [whole()] * 4,
        out_specs=(whole(),) * 5,
        scratch_shapes=[
            pltpu.VMEM((width, depth), jnp.bfloat16),
            pltpu.VMEM((2 * rows, width), jnp.bfloat16),
            pltpu.SemaphoreType.DMA,
        ],
        compiler_params=pltpu.CompilerParams(vmem_limit_bytes=VMEM_LIMIT),
        cost_estimate=pl.CostEstimate(
            flops=4 * rows * depth * width,
            bytes_accessed=depth * width * 2 + rows * (depth + width) * 4,
            transcendentals=0,
        ),
        name="project_back",
    )(place_of, ids_1, ids_3, partial, near_b, end_b, end_upstream, upstream)


def forward_kernel(
    place_of, ids_1, ids_3, partial, near_b, end_b, tokens, gathered, proj, end_proj, held, sem
):
    half_slots = near_b.shape[0]
    other = (1 - place_of[1]) * half_slots
    depth, width = held.shape
    parts, rows, part_width = gathered.shape
    step = 256

    @pl.when(place_of[0] == 1)
    def work():
        load = pltpu.make_async_copy(partial, held, sem)
        load.start()
        load.wait()
        place_blocks(ids_1, other, near_b, held, None, half_slots)
        place_blocks(ids_3, other, end_b, held, None, half_slots)

        @pl.loop(0, width // step, unroll=2)
        def forward(n):
            c = pl.multiple_of(n * step, step)
            acc = jnp.zeros((rows, step), jnp.float32)
            for q in range(parts):
                acc += jnp.dot(
                    gathered[q],
                    held[q * part_width : (q + 1) * part_width, pl.ds(c, step)],
                    preferred_element_type=jnp.float32,
                )
            end_proj[:, pl.ds(c, step)] = acc.astype(end_proj.dtype)
            proj[:, pl.ds(c, step)] = jnp.dot(
                tokens[...], held[:, pl.ds(c, step)], preferred_element_type=jnp.float32
            ).astype(proj.dtype)


def project_forward(place_of, ids_1, ids_3, partial, near_b, end_b, tokens, gathered):
    depth, width = partial.shape
    rows = tokens.shape[0]
    out = jax.ShapeDtypeStruct((rows, width), jnp.bfloat16)
    return pl.pallas_call(
        forward_kernel,
        out_shape=(out, out),
        in_specs=[whole(pltpu.SMEM)] * 3 + [whole(pl.ANY)] + [whole()] * 4,
        out_specs=(whole(),) * 2,
        scratch_shapes=[pltpu.VMEM((depth, width), jnp.bfloat16), pltpu.SemaphoreType.DMA],
        compiler_params=pltpu.CompilerParams(vmem_limit_bytes=VMEM_LIMIT),
        cost_estimate=pl.CostEstimate(
            flops=4 * rows * depth * width,
            bytes_accessed=depth * width * 2 + rows * (depth + width) * 4,
            transcendentals=0,
        ),
        name="project_forward",
    )(place_of, ids_1, ids_3, partial, near_b, end_b, tokens, gathered)


def split_kernel(place_of, keep, *refs):
    x = place_of[2]
    own, give = refs[-2:]
    got = refs[:-2] if len(refs) > 3 else (refs[0].at[0], refs[0].at[1])
    for at in range(2):
        total = (keep[at].astype(jnp.float32) + got[at][...].astype(jnp.float32)).astype(own.dtype)

        @pl.when(x == at)
        def mine():
            own[...] = total

        @pl.when(x != at)
        def theirs():
            give[...] = total


def add_split(place_of, keep, *got):
    out = jax.ShapeDtypeStruct(keep.shape[1:], keep.dtype)
    return pl.pallas_call(
        split_kernel,
        out_shape=(out, out),
        in_specs=[whole(pltpu.SMEM), whole()] + [whole()] * len(got),
        out_specs=(whole(), whole()),
        compiler_params=pltpu.CompilerParams(vmem_limit_bytes=VMEM_LIMIT),
        cost_estimate=pl.CostEstimate(
            flops=keep.size, bytes_accessed=keep.size * 6, transcendentals=0
        ),
        name="add_split",
    )(place_of, keep, *got)


def assemble_kernel(place_of, own, by_core, by_tensor, by_both, full):
    x, c = place_of[2], place_of[3]
    width = own.shape[1]
    for ref, xx, cc in (
        (own, x, c), (by_core, x, 1 - c), (by_tensor, 1 - x, c), (by_both, 1 - x, 1 - c)
    ):
        at = pl.multiple_of((xx * 2 + cc) * width, width)
        full[:, pl.ds(at, width)] = ref[...]


def assemble(place_of, quarters):
    rows, width = quarters[0].shape
    return pl.pallas_call(
        assemble_kernel,
        out_shape=jax.ShapeDtypeStruct((rows, 4 * width), quarters[0].dtype),
        in_specs=[whole(pltpu.SMEM)] + [whole()] * 4,
        out_specs=whole(),
        compiler_params=pltpu.CompilerParams(vmem_limit_bytes=VMEM_LIMIT),
        cost_estimate=pl.CostEstimate(
            flops=0, bytes_accessed=rows * width * 16, transcendentals=0
        ),
        name="assemble",
    )(place_of, *quarters)


def line_grads_kernel(pairs_n, ids, *refs):
    pairs = [(refs[2 * k], refs[2 * k + 1]) for k in range(pairs_n)]
    grads = refs[-1]
    start = refs[2 * pairs_n] if len(refs) > 2 * pairs_n + 1 else None
    slots, size = grads.shape[0], grads.shape[1]
    first = pairs[0][0]
    cols_n = pairs[0][1].shape[1] // size
    rows_n = first.shape[-1] // size * (first.shape[0] if len(first.shape) == 3 else 1)
    total = rows_n * cols_n
    group = math.gcd(slots, 8)

    @pl.loop(0, slots // group)
    def some(g):
        for s in [g * group + j for j in range(group)]:
            b = jnp.minimum(ids[s], total - 1)
            row = b // cols_n
            c = pl.ds(pl.multiple_of((b % cols_n) * size, size), size)
            acc = jnp.zeros((size, size), jnp.float32) if start is None else start[s]
            for x, d in pairs:
                per_part = x.shape[-1] // size
                at = pl.ds(pl.multiple_of((row % per_part) * size, size), size)
                acc += lax.dot_general(
                    x[row // per_part, :, at] if len(x.shape) == 3 else x[:, at],
                    d[:, c],
                    (((0,), (0,)), ((), ())),
                    preferred_element_type=jnp.float32,
                )
            grads[s] = jnp.where(ids[s] < total, acc, 0.0).astype(grads.dtype)


def line_grads(ids, pairs, start, size, out_dtype):
    slots = ids.shape[0]
    rows = pairs[0][1].shape[0]
    flat = [a for pair in pairs for a in pair] + ([] if start is None else [start])
    return pl.pallas_call(
        functools.partial(line_grads_kernel, len(pairs)),
        out_shape=jax.ShapeDtypeStruct((slots, size, size), out_dtype),
        in_specs=[whole(pltpu.SMEM)] + [whole()] * len(flat),
        out_specs=whole(),
        compiler_params=pltpu.CompilerParams(vmem_limit_bytes=VMEM_LIMIT),
        cost_estimate=pl.CostEstimate(
            flops=2 * len(pairs) * slots * rows * size * size,
            bytes_accessed=sum(2 * a.size for a in flat) + 4 * slots * size * size,
            transcendentals=0,
        ),
        name="line_grads",
    )(ids, *flat)


INWARD = ((0, 1), (3, 2))
OUTWARD = ((1, 0), (2, 3))
PAIRS = INWARD + OUTWARD
MIDDLE = ((1, 2), (2, 1))
SWAP = ((0, 1), (1, 0))


def ids_block(block_ids, size):
    rows = size * size // block_ids.shape[0]
    return jnp.broadcast_to(block_ids, (rows, block_ids.shape[0])).reshape(1, size, size)


def ids_of(piece, slots):
    return piece[-1, 0, :slots].astype(jnp.int32)


def line_body(tokens, upstream, blocks, block_ids):
    slots, size = blocks.shape[0], blocks.shape[1]
    rows, depth = tokens.shape
    width = upstream.shape[1]
    half_slots = slots // 2
    part_width = depth // 4
    at_z, half = lax.axis_index("dp"), lax.axis_index("groups")
    at_tensor, at_replica = lax.axis_index("tensor"), lax.axis_index("replica")
    middle = (at_z == 1) | (at_z == 2)
    place_of = jnp.stack([middle.astype(jnp.int32), half, at_tensor, at_replica])
    along = functools.partial(lax.ppermute, axis_name="dp")
    across = functools.partial(lax.ppermute, axis_name="groups", perm=SWAP)
    sideways = functools.partial(lax.ppermute, axis_name="tensor", perm=SWAP)
    cores = functools.partial(lax.ppermute, axis_name="replica", perm=SWAP)
    stage = lax.optimization_barrier

    mine = lax.dynamic_slice_in_dim(blocks, half * half_slots, half_slots, 0)
    other = lax.dynamic_slice_in_dim(blocks, (1 - half) * half_slots, half_slots, 0)
    mine = jnp.concatenate([mine, ids_block(block_ids, size).astype(jnp.bfloat16)])
    part = lax.dynamic_slice_in_dim(tokens, lax.axis_index(INNER) * part_width, part_width, 1)
    both = jnp.concatenate([part, upstream])
    mine, other, both = stage((mine, other, both))

    near_a = along(mine, perm=INWARD)
    far_a = along(mine, perm=MIDDLE)
    near_a, far_a, both, other = stage((near_a, far_a, both, other))

    end_a = along(near_a, perm=MIDDLE)
    far_b = across(far_a)
    both_1 = along(both, perm=PAIRS)
    both_1, end_a, far_b, both, other = stage((both_1, end_a, far_b, both, other))
    upstream_1 = both_1[rows:]

    near_b = along(other, perm=INWARD)
    end_b = across(end_a)
    both_2m = along(both, perm=MIDDLE)
    tokens_1 = lax.all_gather(both_1[:rows], INNER)
    ids_1, ids_2, ids_3 = (ids_of(piece, slots) for piece in (near_a, far_a, end_a))
    partial, turned = place_first(
        place_of, (block_ids, ids_1, ids_2, ids_3), (blocks, near_a, far_a, far_b, end_a), depth, width
    )
    near_b, end_b, both_2m, both_1, tokens_1, partial, turned = stage(
        (near_b, end_b, both_2m, both_1, tokens_1, partial, turned)
    )

    both_3m = along(both_1, perm=MIDDLE)
    both_2o = along(both_2m, perm=OUTWARD)
    last = (near_b, end_b)
    end_keep, own_keep, own_give, *end_give = project_back(
        place_of, ids_1, ids_3, turned, *last, upstream_1, upstream
    )
    end_keep, end_give = add_split(place_of, end_keep, *[cores(a) for a in end_give])
    end_keep, end_give, own_give, both_3m, both_2o = stage(
        (end_keep, end_give, own_give, both_3m, both_2o)
    )

    end_got = sideways(end_give)
    own_keep, own_give = add_split(place_of, own_keep, cores(own_give))
    both_3o = along(both_3m, perm=OUTWARD)
    tokens_2 = lax.all_gather(both_2m[:rows] + both_2o[:rows], INNER)
    upstream_2 = both_2m[rows:] + both_2o[rows:]
    end_got, own_give, own_keep = stage((end_got, own_give, own_keep))

    sum_out = along(end_keep + end_got, perm=OUTWARD)
    own_got = sideways(own_give)
    proj, end_proj = project_forward(place_of, ids_1, ids_3, partial, *last, tokens, tokens_1)
    sum_out, own_got, both_3o, proj, end_proj = stage((sum_out, own_got, both_3o, proj, end_proj))

    tokens_3 = lax.all_gather(both_3m[:rows] + both_3o[:rows], INNER)
    upstream_3 = both_3m[rows:] + both_3o[rows:]
    quarter = jnp.where(middle, own_keep + own_got, sum_out)
    proj_out = along(end_proj, perm=OUTWARD)
    pairs = ((tokens, upstream), (tokens_1, upstream_1), (tokens_2, upstream_2))
    grads = line_grads(block_ids, pairs, None, size, jnp.float32)
    by_tensor, by_core, grads = stage((sideways(quarter), cores(quarter), grads))
    by_both = cores(by_tensor)
    projected = jnp.where(middle, proj, proj_out)
    token_grad = assemble(place_of, (quarter, by_core, by_tensor, by_both))
    grads = line_grads(block_ids, ((tokens_3, upstream_3),), grads, size, jnp.bfloat16)
    return projected, token_grad, grads


def solution(mesh):
    line = tuple(mesh.shape[a] for a in ("groups", "dp", "tensor", "replica")) == (2, 4, 2, 2)
    return jax.shard_map(
        line_body if line else general_body,
        mesh=mesh,
        in_specs=(
            P(("groups", "dp"), None),
            P(("groups", "dp"), INNER),
            P(("dp",) + INNER, None, None),
            P(("dp",) + INNER),
        ),
        out_specs=(
            P(("groups", "dp"), INNER),
            P(("groups", "dp"), None),
            P(("groups", "dp") + INNER, None, None),
        ),
        check_vma=False,
    )
```

```python
import functools
import math

import jax
import jax.numpy as jnp
from jax import lax
from jax.experimental import pallas as pl
from jax.experimental.pallas import tpu as pltpu
from jax.sharding import PartitionSpec as P

VMEM_LIMIT = 60 * 1024 * 1024
INNER = ("tensor", "replica")


def whole(space=pltpu.VMEM):
    return pl.BlockSpec(memory_space=space)


def project_kernel(ids, blocks, tokens, upstream, proj, back, weight):
    slots, size = blocks.shape[0], blocks.shape[1]
    depth, width = weight.shape
    cols_n = width // size
    total = (depth // size) * cols_n
    weight[...] = jnp.zeros_like(weight)

    @pl.loop(0, slots, unroll=4)
    def place(s):
        b = ids[s]

        @pl.when(b < total)
        def put():
            r = pl.multiple_of((b // cols_n) * size, size)
            c = pl.multiple_of((b % cols_n) * size, size)
            weight[pl.ds(r, size), pl.ds(c, size)] = blocks[s]

    step = 256

    @pl.loop(0, width // step)
    def forward(n):
        c = pl.multiple_of(n * step, step)
        proj[:, pl.ds(c, step)] = jnp.dot(
            tokens[...], weight[:, pl.ds(c, step)], preferred_element_type=jnp.float32
        ).astype(proj.dtype)

    @pl.loop(0, depth // step, unroll=4)
    def backward(n):
        r = pl.multiple_of(n * step, step)
        back[:, pl.ds(r, step)] = lax.dot_general(
            upstream[...],
            weight[pl.ds(r, step), :],
            (((1,), (1,)), ((), ())),
            preferred_element_type=jnp.float32,
        ).astype(back.dtype)


def project(ids, blocks, tokens, upstream):
    rows, depth = tokens.shape
    width = upstream.shape[1]
    return pl.pallas_call(
        project_kernel,
        out_shape=(
            jax.ShapeDtypeStruct((rows, width), jnp.bfloat16),
            jax.ShapeDtypeStruct((rows, depth), jnp.bfloat16),
        ),
        in_specs=[whole(pltpu.SMEM), whole(), whole(), whole()],
        out_specs=(whole(), whole()),
        scratch_shapes=[pltpu.VMEM((depth, width), jnp.bfloat16)],
        compiler_params=pltpu.CompilerParams(vmem_limit_bytes=VMEM_LIMIT),
        cost_estimate=pl.CostEstimate(
            flops=4 * rows * depth * width,
            bytes_accessed=blocks.size * 2 + rows * (depth + width) * 4,
            transcendentals=0,
        ),
        name="project",
    )(ids, blocks, tokens, upstream)


def block_grad_kernel(ids, tokens, upstream, grads):
    slots, size = grads.shape[0], grads.shape[1]
    parts, slabs, _, part_width = tokens.shape
    cols_n = upstream.shape[2] // size
    per_part = part_width // size
    total = parts * per_part * cols_n

    @pl.loop(0, slots)
    def one(s):
        b = ids[s]

        @pl.when(b < total)
        def fill():
            row = b // cols_n
            part = row // per_part
            r = pl.multiple_of((row % per_part) * size, size)
            c = pl.multiple_of((b % cols_n) * size, size)
            acc = jnp.zeros((size, size), jnp.float32)
            for k in range(slabs):
                acc += lax.dot_general(
                    tokens[part, k, :, pl.ds(r, size)],
                    upstream[k, :, pl.ds(c, size)],
                    (((0,), (0,)), ((), ())),
                    preferred_element_type=jnp.float32,
                )
            grads[s] = acc.astype(grads.dtype)

        @pl.when(b >= total)
        def clear():
            grads[s] = jnp.zeros((size, size), grads.dtype)


def block_grads(ids, tokens, upstream, size):
    slots = ids.shape[0]
    parts, slabs, rows, part_width = tokens.shape
    return pl.pallas_call(
        block_grad_kernel,
        out_shape=jax.ShapeDtypeStruct((slots, size, size), jnp.bfloat16),
        in_specs=[whole(pltpu.SMEM), whole(), whole()],
        out_specs=whole(),
        compiler_params=pltpu.CompilerParams(vmem_limit_bytes=VMEM_LIMIT),
        cost_estimate=pl.CostEstimate(
            flops=2 * slots * slabs * rows * size * size,
            bytes_accessed=2 * (tokens.size + upstream.size + slots * size * size),
            transcendentals=0,
        ),
        name="block_grads",
    )(ids, tokens, upstream)


def general_body(tokens, upstream, blocks, block_ids):
    size = blocks.shape[1]
    all_blocks = lax.all_gather(blocks, "dp", axis=0, tiled=True)
    all_ids = lax.all_gather(block_ids, "dp", axis=0, tiled=True)
    proj, back = project(all_ids, all_blocks, tokens, upstream)
    terms = block_grads(all_ids, tokens[None, None], upstream[None], size)
    grads = lax.psum_scatter(terms, "dp", scatter_dimension=0, tiled=True)
    return proj, lax.psum(back, INNER), grads


def place_blocks(ids, first, blocks, weight, turned, slots):
    size = blocks.shape[1]
    depth, width = turned.shape[::-1] if weight is None else weight.shape
    cols_n = width // size
    total = (depth // size) * cols_n

    @pl.loop(0, slots, unroll=4)
    def place(s):
        b = ids[first + s]

        @pl.when(b < total)
        def put():
            r = pl.multiple_of((b // cols_n) * size, size)
            c = pl.multiple_of((b % cols_n) * size, size)
            if weight is not None:
                weight[pl.ds(r, size), pl.ds(c, size)] = blocks[s]
            if turned is not None:
                turned[pl.ds(c, size), pl.ds(r, size)] = blocks[s].T


def place_kernel(
    place_of, ids_0, ids_1, ids_2, ids_3, own, near_a, far_a, far_b, end_a, weight, turned
):
    is_middle, half = place_of[0], place_of[1]
    half_slots = far_b.shape[0] - 1
    mine, other = half * half_slots, (1 - half) * half_slots

    @pl.when(is_middle == 1)
    def work():
        weight[...] = jnp.zeros_like(weight)
        turned[...] = jnp.zeros_like(turned)
        place_blocks(ids_0, 0, own, weight, turned, own.shape[0])
        place_blocks(ids_1, mine, near_a, weight, turned, half_slots)
        place_blocks(ids_2, mine, far_a, weight, turned, half_slots)
        place_blocks(ids_2, other, far_b, weight, turned, half_slots)
        place_blocks(ids_3, mine, end_a, weight, turned, half_slots)


def place_first(place_of, ids, pieces, depth, width):
    return pl.pallas_call(
        place_kernel,
        out_shape=(
            jax.ShapeDtypeStruct((depth, width), jnp.bfloat16),
            jax.ShapeDtypeStruct((width, depth), jnp.bfloat16),
        ),
        in_specs=[whole(pltpu.SMEM)] * 5 + [whole()] * 5,
        out_specs=(whole(), whole()),
        compiler_params=pltpu.CompilerParams(vmem_limit_bytes=VMEM_LIMIT),
        cost_estimate=pl.CostEstimate(
            flops=0, bytes_accessed=depth * width * 6, transcendentals=0
        ),
        name="place_first",
    )(place_of, *ids, *pieces)


def back_kernel(
    place_of, ids_1, ids_3, partial, near_b, end_b, two_upstream,
    end_keep, own_keep, own_give, end_give_0, end_give_1, held, sources, sem,
):
    half_slots = near_b.shape[0]
    other = (1 - place_of[1]) * half_slots
    rows, width = two_upstream.shape[1:]
    step = 256
    per_part = end_keep.shape[2] // step

    @pl.when(place_of[0] == 1)
    def work():
        load = pltpu.make_async_copy(partial, held, sem)
        load.start()
        sources[:rows] = two_upstream[1]
        sources[rows:] = two_upstream[0]
        load.wait()
        place_blocks(ids_1, other, near_b, None, held, half_slots)
        place_blocks(ids_3, other, end_b, None, held, half_slots)

        def column(part, end_target, own_target):
            @pl.loop(0, per_part, unroll=2)
            def backward(n):
                at = pl.multiple_of(n * step, step)
                result = jnp.dot(
                    sources[...],
                    held[:, pl.ds(pl.multiple_of(part * per_part * step + at, step), step)],
                    preferred_element_type=jnp.float32,
                ).astype(own_target.dtype)
                end_target[:, pl.ds(at, step)] = result[:rows]
                own_target[:, pl.ds(at, step)] = result[rows:]

        for x, end_give in enumerate((end_give_0, end_give_1)):
            column(2 * x + place_of[3], end_keep.at[x], own_keep.at[x])
            column(2 * x + 1 - place_of[3], end_give, own_give.at[x])


def project_back(place_of, ids_1, ids_3, partial, near_b, end_b, two_upstream):
    width, depth = partial.shape
    rows = two_upstream.shape[1]
    quarter = jax.ShapeDtypeStruct((rows, depth // 4), jnp.bfloat16)
    half = jax.ShapeDtypeStruct((2, rows, depth // 4), jnp.bfloat16)
    return pl.pallas_call(
        back_kernel,
        out_shape=(half, half, half, quarter, quarter),
        in_specs=[whole(pltpu.SMEM)] * 3 + [whole(pl.ANY)] + [whole()] * 3,
        out_specs=(whole(),) * 5,
        scratch_shapes=[
            pltpu.VMEM((width, depth), jnp.bfloat16),
            pltpu.VMEM((2 * rows, width), jnp.bfloat16),
            pltpu.SemaphoreType.DMA,
        ],
        compiler_params=pltpu.CompilerParams(vmem_limit_bytes=VMEM_LIMIT),
        cost_estimate=pl.CostEstimate(
            flops=4 * rows * depth * width,
            bytes_accessed=depth * width * 2 + rows * (depth + width) * 4,
            transcendentals=0,
        ),
        name="project_back",
    )(place_of, ids_1, ids_3, partial, near_b, end_b, two_upstream)


def forward_kernel(
    place_of, ids_1, ids_3, partial, near_b, end_b, tokens, gathered, proj, end_proj, held, sem
):
    half_slots = near_b.shape[0]
    other = (1 - place_of[1]) * half_slots
    depth, width = held.shape
    parts, rows, part_width = gathered.shape
    step = 256

    @pl.when(place_of[0] == 1)
    def work():
        load = pltpu.make_async_copy(partial, held, sem)
        load.start()
        load.wait()
        place_blocks(ids_1, other, near_b, held, None, half_slots)
        place_blocks(ids_3, other, end_b, held, None, half_slots)

        @pl.loop(0, width // step, unroll=2)
        def forward(n):
            c = pl.multiple_of(n * step, step)
            acc = jnp.zeros((rows, step), jnp.float32)
            for q in range(parts):
                acc += jnp.dot(
                    gathered[q],
                    held[q * part_width : (q + 1) * part_width, pl.ds(c, step)],
                    preferred_element_type=jnp.float32,
                )
            end_proj[:, pl.ds(c, step)] = acc.astype(end_proj.dtype)
            proj[:, pl.ds(c, step)] = jnp.dot(
                tokens[...], held[:, pl.ds(c, step)], preferred_element_type=jnp.float32
            ).astype(proj.dtype)


def project_forward(place_of, ids_1, ids_3, partial, near_b, end_b, tokens, gathered):
    depth, width = partial.shape
    rows = tokens.shape[0]
    out = jax.ShapeDtypeStruct((rows, width), jnp.bfloat16)
    return pl.pallas_call(
        forward_kernel,
        out_shape=(out, out),
        in_specs=[whole(pltpu.SMEM)] * 3 + [whole(pl.ANY)] + [whole()] * 4,
        out_specs=(whole(),) * 2,
        scratch_shapes=[pltpu.VMEM((depth, width), jnp.bfloat16), pltpu.SemaphoreType.DMA],
        compiler_params=pltpu.CompilerParams(vmem_limit_bytes=VMEM_LIMIT),
        cost_estimate=pl.CostEstimate(
            flops=4 * rows * depth * width,
            bytes_accessed=depth * width * 2 + rows * (depth + width) * 4,
            transcendentals=0,
        ),
        name="project_forward",
    )(place_of, ids_1, ids_3, partial, near_b, end_b, tokens, gathered)


def split_kernel(place_of, keep, *refs):
    x = place_of[2]
    own, give = refs[-2:]
    got = refs[:-2] if len(refs) > 3 else (refs[0].at[0], refs[0].at[1])
    for at in range(2):
        total = (keep[at].astype(jnp.float32) + got[at][...].astype(jnp.float32)).astype(own.dtype)

        @pl.when(x == at)
        def mine():
            own[...] = total

        @pl.when(x != at)
        def theirs():
            give[...] = total


def add_split(place_of, keep, *got):
    out = jax.ShapeDtypeStruct(keep.shape[1:], keep.dtype)
    return pl.pallas_call(
        split_kernel,
        out_shape=(out, out),
        in_specs=[whole(pltpu.SMEM), whole()] + [whole()] * len(got),
        out_specs=(whole(), whole()),
        compiler_params=pltpu.CompilerParams(vmem_limit_bytes=VMEM_LIMIT),
        cost_estimate=pl.CostEstimate(
            flops=keep.size, bytes_accessed=keep.size * 6, transcendentals=0
        ),
        name="add_split",
    )(place_of, keep, *got)


def assemble_kernel(place_of, own, by_core, by_tensor, by_both, full):
    x, c = place_of[2], place_of[3]
    width = own.shape[1]
    for ref, xx, cc in (
        (own, x, c), (by_core, x, 1 - c), (by_tensor, 1 - x, c), (by_both, 1 - x, 1 - c)
    ):
        at = pl.multiple_of((xx * 2 + cc) * width, width)
        full[:, pl.ds(at, width)] = ref[...]


def assemble(place_of, quarters):
    rows, width = quarters[0].shape
    return pl.pallas_call(
        assemble_kernel,
        out_shape=jax.ShapeDtypeStruct((rows, 4 * width), quarters[0].dtype),
        in_specs=[whole(pltpu.SMEM)] + [whole()] * 4,
        out_specs=whole(),
        compiler_params=pltpu.CompilerParams(vmem_limit_bytes=VMEM_LIMIT),
        cost_estimate=pl.CostEstimate(
            flops=0, bytes_accessed=rows * width * 16, transcendentals=0
        ),
        name="assemble",
    )(place_of, *quarters)


def line_grads_kernel(pairs_n, total, ids, *refs):
    pairs = [(refs[2 * k], refs[2 * k + 1]) for k in range(pairs_n)]
    grads = refs[-1]
    start = refs[2 * pairs_n] if len(refs) > 2 * pairs_n + 1 else None
    slots, size = grads.shape[0], grads.shape[1]
    group = math.gcd(slots, 8)

    @pl.loop(0, slots // group)
    def some(g):
        for s in [g * group + j for j in range(group)]:
            b = jnp.minimum(ids[s], total - 1)
            acc = jnp.zeros((size, size), jnp.float32) if start is None else start[s]
            for x, d in pairs:
                cols_n = d.shape[-1] // size
                row = b // cols_n
                per_part = x.shape[-1] // size
                at = pl.ds(pl.multiple_of((row % per_part) * size, size), size)
                c = pl.ds(pl.multiple_of((b % cols_n) * size, size), size)
                if len(x.shape) == 2:
                    operands = [(x[:, at], d[:, c])]
                elif len(x.shape) == 3:
                    operands = [(x[row // per_part, :, at], d[:, c])]
                else:
                    operands = [(x[row // per_part, k, :, at], d[k, :, c]) for k in range(x.shape[1])]
                for left, right in operands:
                    acc += lax.dot_general(
                        left,
                        right,
                        (((0,), (0,)), ((), ())),
                        preferred_element_type=jnp.float32,
                    )
            grads[s] = jnp.where(ids[s] < total, acc, 0.0).astype(grads.dtype)


def line_grads(ids, total, pairs, start, size, out_dtype):
    slots = ids.shape[0]
    flat = [a for pair in pairs for a in pair] + ([] if start is None else [start])
    return pl.pallas_call(
        functools.partial(line_grads_kernel, len(pairs), total),
        out_shape=jax.ShapeDtypeStruct((slots, size, size), out_dtype),
        in_specs=[whole(pltpu.SMEM)] + [whole()] * len(flat),
        out_specs=whole(),
        compiler_params=pltpu.CompilerParams(vmem_limit_bytes=VMEM_LIMIT),
        cost_estimate=pl.CostEstimate(
            flops=1024 * len(pairs) * slots * size * size,
            bytes_accessed=sum(2 * a.size for a in flat) + 4 * slots * size * size,
            transcendentals=0,
        ),
        name="line_grads",
    )(ids, *flat)


INWARD = ((0, 1), (3, 2))
OUTWARD = ((1, 0), (2, 3))
PAIRS = INWARD + OUTWARD
MIDDLE = ((1, 2), (2, 1))
SWAP = ((0, 1), (1, 0))


def ids_block(block_ids, size):
    rows = size * size // block_ids.shape[0]
    return jnp.broadcast_to(block_ids, (rows, block_ids.shape[0])).reshape(1, size, size)


def ids_of(piece, slots):
    return piece[-1, 0, :slots].astype(jnp.int32)


def line_body(tokens, upstream, blocks, block_ids):
    slots, size = blocks.shape[0], blocks.shape[1]
    rows, depth = tokens.shape
    width = upstream.shape[1]
    half_slots = slots // 2
    part_width = depth // 4
    at_z, half = lax.axis_index("dp"), lax.axis_index("groups")
    at_tensor, at_replica = lax.axis_index("tensor"), lax.axis_index("replica")
    middle = (at_z == 1) | (at_z == 2)
    place_of = jnp.stack([middle.astype(jnp.int32), half, at_tensor, at_replica])
    along = functools.partial(lax.ppermute, axis_name="dp")
    across = functools.partial(
        lax.ppermute, axis_name=("groups", "dp"), perm=((1, 5), (5, 1), (2, 6), (6, 2))
    )
    middle_swap = ((2, 3), (3, 2), (4, 5), (5, 4))
    sideways = functools.partial(lax.ppermute, axis_name=("dp", "tensor"), perm=middle_swap)
    cores = functools.partial(lax.ppermute, axis_name=("dp", "replica"), perm=middle_swap)
    everywhere = functools.partial(lax.ppermute, axis_name="tensor", perm=SWAP)
    all_cores = functools.partial(lax.ppermute, axis_name="replica", perm=SWAP)
    total = (depth // size) * (width // size)
    stage = lax.optimization_barrier

    mine = lax.dynamic_slice_in_dim(blocks, half * half_slots, half_slots, 0)
    other = lax.dynamic_slice_in_dim(blocks, (1 - half) * half_slots, half_slots, 0)
    mine = jnp.concatenate([mine, ids_block(block_ids, size).astype(jnp.bfloat16)])
    part = lax.dynamic_slice_in_dim(tokens, lax.axis_index(INNER) * part_width, part_width, 1)
    both = jnp.concatenate([part, upstream])
    mine, other, both = stage((mine, other, both))

    near_a = along(mine, perm=INWARD)
    far_a = along(mine, perm=MIDDLE)
    near_a, far_a, both, part, other = stage((near_a, far_a, both, part, other))

    end_a = along(near_a, perm=MIDDLE)
    far_b = across(far_a)
    both_1 = along(both, perm=PAIRS)
    both_1, end_a, far_b, part, other = stage((both_1, end_a, far_b, part, other))
    part_1, upstream_1 = both_1[:rows], both_1[rows:]

    near_b = along(other, perm=INWARD)
    end_b = across(end_a)
    far_parts_m = along(jnp.stack([part, part_1]), perm=MIDDLE)
    tokens_1 = lax.all_gather(part_1, INNER)
    ids_1, ids_2, ids_3 = (ids_of(piece, slots) for piece in (near_a, far_a, end_a))
    partial, turned = place_first(
        place_of, (block_ids, ids_1, ids_2, ids_3), (blocks, near_a, far_a, far_b, end_a), depth, width
    )
    two_upstream = jnp.stack([upstream, upstream_1])
    near_b, end_b, far_parts_m, two_upstream, tokens_1, partial, turned = stage(
        (near_b, end_b, far_parts_m, two_upstream, tokens_1, partial, turned)
    )

    far_parts_o = along(far_parts_m, perm=OUTWARD)
    far_upstream_m = along(two_upstream, perm=MIDDLE)
    last = (near_b, end_b)
    end_keep, own_keep, own_give, *end_give = project_back(
        place_of, ids_1, ids_3, turned, *last, two_upstream
    )
    end_keep, end_give = add_split(place_of, end_keep, *[cores(a) for a in end_give])
    end_keep, end_give, own_give, far_parts_o, far_upstream_m = stage(
        (end_keep, end_give, own_give, far_parts_o, far_upstream_m)
    )

    end_got = sideways(end_give)
    own_keep, own_give = add_split(place_of, own_keep, cores(own_give))
    far_upstream_o = along(far_upstream_m, perm=OUTWARD)
    far_tokens = lax.all_gather(far_parts_m + far_parts_o, INNER)
    pairs = ((tokens, upstream), (tokens_1, upstream_1))
    grads = line_grads(block_ids, total, pairs, None, size, jnp.float32)
    end_got, own_give, own_keep, grads = stage((end_got, own_give, own_keep, grads))

    sum_out = along(end_keep + end_got, perm=OUTWARD)
    own_got = sideways(own_give)
    proj, end_proj = project_forward(place_of, ids_1, ids_3, partial, *last, tokens, tokens_1)
    sum_out, own_got, far_upstream_o, proj, end_proj = stage(
        (sum_out, own_got, far_upstream_o, proj, end_proj)
    )

    quarter = jnp.where(middle, own_keep + own_got, sum_out)
    proj_out = along(end_proj, perm=OUTWARD)
    pairs = ((far_tokens, far_upstream_m + far_upstream_o),)
    grads = line_grads(block_ids, total, pairs, grads, size, jnp.bfloat16)
    by_tensor, by_core, grads = stage((everywhere(quarter), all_cores(quarter), grads))
    by_both = all_cores(by_tensor)
    projected = jnp.where(middle, proj, proj_out)
    token_grad = assemble(place_of, (quarter, by_core, by_tensor, by_both))
    return projected, token_grad, grads


def solution(mesh):
    line = tuple(mesh.shape[a] for a in ("groups", "dp", "tensor", "replica")) == (2, 4, 2, 2)
    return jax.shard_map(
        line_body if line else general_body,
        mesh=mesh,
        in_specs=(
            P(("groups", "dp"), None),
            P(("groups", "dp"), INNER),
            P(("dp",) + INNER, None, None),
            P(("dp",) + INNER),
        ),
        out_specs=(
            P(("groups", "dp"), INNER),
            P(("groups", "dp"), None),
            P(("groups", "dp") + INNER, None, None),
        ),
        check_vma=False,
    )
```

```python
import functools
import math

import jax
import jax.numpy as jnp
from jax import lax
from jax.experimental import pallas as pl
from jax.experimental.pallas import tpu as pltpu
from jax.sharding import PartitionSpec as P

VMEM_LIMIT = 60 * 1024 * 1024
INNER = ("tensor", "replica")


def whole(space=pltpu.VMEM):
    return pl.BlockSpec(memory_space=space)


def project_kernel(ids, blocks, tokens, upstream, proj, back, weight):
    slots, size = blocks.shape[0], blocks.shape[1]
    depth, width = weight.shape
    cols_n = width // size
    total = (depth // size) * cols_n
    weight[...] = jnp.zeros_like(weight)

    @pl.loop(0, slots, unroll=4)
    def place(s):
        b = ids[s]

        @pl.when(b < total)
        def put():
            r = pl.multiple_of((b // cols_n) * size, size)
            c = pl.multiple_of((b % cols_n) * size, size)
            weight[pl.ds(r, size), pl.ds(c, size)] = blocks[s]

    step = 256

    @pl.loop(0, width // step)
    def forward(n):
        c = pl.multiple_of(n * step, step)
        proj[:, pl.ds(c, step)] = jnp.dot(
            tokens[...], weight[:, pl.ds(c, step)], preferred_element_type=jnp.float32
        ).astype(proj.dtype)

    @pl.loop(0, depth // step, unroll=4)
    def backward(n):
        r = pl.multiple_of(n * step, step)
        back[:, pl.ds(r, step)] = lax.dot_general(
            upstream[...],
            weight[pl.ds(r, step), :],
            (((1,), (1,)), ((), ())),
            preferred_element_type=jnp.float32,
        ).astype(back.dtype)


def project(ids, blocks, tokens, upstream):
    rows, depth = tokens.shape
    width = upstream.shape[1]
    return pl.pallas_call(
        project_kernel,
        out_shape=(
            jax.ShapeDtypeStruct((rows, width), jnp.bfloat16),
            jax.ShapeDtypeStruct((rows, depth), jnp.bfloat16),
        ),
        in_specs=[whole(pltpu.SMEM), whole(), whole(), whole()],
        out_specs=(whole(), whole()),
        scratch_shapes=[pltpu.VMEM((depth, width), jnp.bfloat16)],
        compiler_params=pltpu.CompilerParams(vmem_limit_bytes=VMEM_LIMIT),
        cost_estimate=pl.CostEstimate(
            flops=4 * rows * depth * width,
            bytes_accessed=blocks.size * 2 + rows * (depth + width) * 4,
            transcendentals=0,
        ),
        name="project",
    )(ids, blocks, tokens, upstream)


def block_grad_kernel(ids, tokens, upstream, grads):
    slots, size = grads.shape[0], grads.shape[1]
    parts, slabs, _, part_width = tokens.shape
    cols_n = upstream.shape[2] // size
    per_part = part_width // size
    total = parts * per_part * cols_n

    @pl.loop(0, slots)
    def one(s):
        b = ids[s]

        @pl.when(b < total)
        def fill():
            row = b // cols_n
            part = row // per_part
            r = pl.multiple_of((row % per_part) * size, size)
            c = pl.multiple_of((b % cols_n) * size, size)
            acc = jnp.zeros((size, size), jnp.float32)
            for k in range(slabs):
                acc += lax.dot_general(
                    tokens[part, k, :, pl.ds(r, size)],
                    upstream[k, :, pl.ds(c, size)],
                    (((0,), (0,)), ((), ())),
                    preferred_element_type=jnp.float32,
                )
            grads[s] = acc.astype(grads.dtype)

        @pl.when(b >= total)
        def clear():
            grads[s] = jnp.zeros((size, size), grads.dtype)


def block_grads(ids, tokens, upstream, size):
    slots = ids.shape[0]
    parts, slabs, rows, part_width = tokens.shape
    return pl.pallas_call(
        block_grad_kernel,
        out_shape=jax.ShapeDtypeStruct((slots, size, size), jnp.bfloat16),
        in_specs=[whole(pltpu.SMEM), whole(), whole()],
        out_specs=whole(),
        compiler_params=pltpu.CompilerParams(vmem_limit_bytes=VMEM_LIMIT),
        cost_estimate=pl.CostEstimate(
            flops=2 * slots * slabs * rows * size * size,
            bytes_accessed=2 * (tokens.size + upstream.size + slots * size * size),
            transcendentals=0,
        ),
        name="block_grads",
    )(ids, tokens, upstream)


def general_body(tokens, upstream, blocks, block_ids):
    size = blocks.shape[1]
    all_blocks = lax.all_gather(blocks, "dp", axis=0, tiled=True)
    all_ids = lax.all_gather(block_ids, "dp", axis=0, tiled=True)
    proj, back = project(all_ids, all_blocks, tokens, upstream)
    terms = block_grads(all_ids, tokens[None, None], upstream[None], size)
    grads = lax.psum_scatter(terms, "dp", scatter_dimension=0, tiled=True)
    return proj, lax.psum(back, INNER), grads


def place_blocks(ids, first, blocks, weight, turned, slots):
    size = blocks.shape[1]
    depth, width = turned.shape[::-1] if weight is None else weight.shape
    cols_n = width // size
    total = (depth // size) * cols_n

    @pl.loop(0, slots, unroll=4)
    def place(s):
        b = ids[first + s]

        @pl.when(b < total)
        def put():
            r = pl.multiple_of((b // cols_n) * size, size)
            c = pl.multiple_of((b % cols_n) * size, size)
            if weight is not None:
                weight[pl.ds(r, size), pl.ds(c, size)] = blocks[s]
            if turned is not None:
                turned[pl.ds(c, size), pl.ds(r, size)] = blocks[s].T


def place_kernel(place_of, ids_0, ids_1, ids_2, ids_3, own, near_a, far_a, far_b, end_a, turned):
    is_middle, half = place_of[0], place_of[1]
    half_slots = far_b.shape[0] - 1
    mine, other = half * half_slots, (1 - half) * half_slots

    @pl.when(is_middle == 1)
    def work():
        turned[...] = jnp.zeros_like(turned)
        place_blocks(ids_0, 0, own, None, turned, own.shape[0])
        place_blocks(ids_1, mine, near_a, None, turned, half_slots)
        place_blocks(ids_2, mine, far_a, None, turned, half_slots)
        place_blocks(ids_2, other, far_b, None, turned, half_slots)
        place_blocks(ids_3, mine, end_a, None, turned, half_slots)


def place_first(place_of, ids, pieces, depth, width):
    return pl.pallas_call(
        place_kernel,
        out_shape=jax.ShapeDtypeStruct((width, depth), jnp.bfloat16),
        in_specs=[whole(pltpu.SMEM)] * 5 + [whole()] * 5,
        out_specs=whole(),
        compiler_params=pltpu.CompilerParams(vmem_limit_bytes=VMEM_LIMIT),
        cost_estimate=pl.CostEstimate(
            flops=0, bytes_accessed=depth * width * 4, transcendentals=0
        ),
        name="place_first",
    )(place_of, *ids, *pieces)


def back_kernel(
    place_of, ids_1, ids_3, partial, near_b, end_b, end_upstream, upstream,
    end_keep, own_keep, own_give, end_give_0, end_give_1, held, sources, sem,
):
    half_slots = near_b.shape[0]
    other = (1 - place_of[1]) * half_slots
    rows, width = upstream.shape
    step = 256
    per_part = end_keep.shape[2] // step

    @pl.when(place_of[0] == 1)
    def work():
        load = pltpu.make_async_copy(partial, held, sem)
        load.start()
        sources[:rows] = end_upstream[...]
        sources[rows:] = upstream[...]
        load.wait()
        place_blocks(ids_1, other, near_b, None, held, half_slots)
        place_blocks(ids_3, other, end_b, None, held, half_slots)

        def column(part, end_target, own_target):
            @pl.loop(0, per_part, unroll=2)
            def backward(n):
                at = pl.multiple_of(n * step, step)
                result = jnp.dot(
                    sources[...],
                    held[:, pl.ds(pl.multiple_of(part * per_part * step + at, step), step)],
                    preferred_element_type=jnp.float32,
                ).astype(own_target.dtype)
                end_target[:, pl.ds(at, step)] = result[:rows]
                own_target[:, pl.ds(at, step)] = result[rows:]

        for x, end_give in enumerate((end_give_0, end_give_1)):
            column(2 * x + place_of[3], end_keep.at[x], own_keep.at[x])
            column(2 * x + 1 - place_of[3], end_give, own_give.at[x])


def project_back(place_of, ids_1, ids_3, partial, near_b, end_b, end_upstream, upstream):
    width, depth = partial.shape
    rows = upstream.shape[0]
    quarter = jax.ShapeDtypeStruct((rows, depth // 4), jnp.bfloat16)
    half = jax.ShapeDtypeStruct((2, rows, depth // 4), jnp.bfloat16)
    return pl.pallas_call(
        back_kernel,
        out_shape=(half, half, half, quarter, quarter),
        in_specs=[whole(pltpu.SMEM)] * 3 + [whole(pl.ANY)] + [whole()] * 4,
        out_specs=(whole(),) * 5,
        scratch_shapes=[
            pltpu.VMEM((width, depth), jnp.bfloat16),
            pltpu.VMEM((2 * rows, width), jnp.bfloat16),
            pltpu.SemaphoreType.DMA,
        ],
        compiler_params=pltpu.CompilerParams(vmem_limit_bytes=VMEM_LIMIT),
        cost_estimate=pl.CostEstimate(
            flops=4 * rows * depth * width,
            bytes_accessed=depth * width * 2 + rows * (depth + width) * 4,
            transcendentals=0,
        ),
        name="project_back",
    )(place_of, ids_1, ids_3, partial, near_b, end_b, end_upstream, upstream)


def forward_kernel(
    place_of, ids_0, ids_1, ids_2, ids_3, own, near_a, near_b, far_a, far_b, end_a, end_b,
    tokens, end_tokens, proj, end_proj, weight,
):
    half_slots = near_b.shape[0]
    mine, other = place_of[1] * half_slots, (1 - place_of[1]) * half_slots
    width = weight.shape[1]
    parts, rows, part_width = end_tokens.shape
    step = 256

    @pl.when(place_of[0] == 1)
    def work():
        weight[...] = jnp.zeros_like(weight)
        place_blocks(ids_0, 0, own, weight, None, own.shape[0])
        for ids, a, b in ((ids_1, near_a, near_b), (ids_2, far_a, far_b), (ids_3, end_a, end_b)):
            place_blocks(ids, mine, a, weight, None, half_slots)
            place_blocks(ids, other, b, weight, None, half_slots)

        @pl.loop(0, width // step, unroll=2)
        def forward(n):
            c = pl.multiple_of(n * step, step)
            acc = jnp.zeros((rows, step), jnp.float32)
            for q in range(parts):
                acc += jnp.dot(
                    end_tokens[q],
                    weight[q * part_width : (q + 1) * part_width, pl.ds(c, step)],
                    preferred_element_type=jnp.float32,
                )
            end_proj[:, pl.ds(c, step)] = acc.astype(end_proj.dtype)
            proj[:, pl.ds(c, step)] = jnp.dot(
                tokens[...], weight[:, pl.ds(c, step)], preferred_element_type=jnp.float32
            ).astype(proj.dtype)


def project_forward(place_of, ids, pieces, tokens, end_tokens, width):
    rows, depth = tokens.shape
    out = jax.ShapeDtypeStruct((rows, width), jnp.bfloat16)
    return pl.pallas_call(
        forward_kernel,
        out_shape=(out, out),
        in_specs=[whole(pltpu.SMEM)] * 5 + [whole()] * 9,
        out_specs=(whole(),) * 2,
        scratch_shapes=[pltpu.VMEM((depth, width), jnp.bfloat16)],
        compiler_params=pltpu.CompilerParams(vmem_limit_bytes=VMEM_LIMIT),
        cost_estimate=pl.CostEstimate(
            flops=4 * rows * depth * width,
            bytes_accessed=depth * width * 2 + rows * (depth + width) * 4,
            transcendentals=0,
        ),
        name="project_forward",
    )(place_of, *ids, *pieces, tokens, end_tokens)


def split_kernel(place_of, keep, *refs):
    x = place_of[2]
    own, give = refs[-2:]
    got = refs[:-2] if len(refs) > 3 else (refs[0].at[0], refs[0].at[1])
    for at in range(2):
        total = (keep[at].astype(jnp.float32) + got[at][...].astype(jnp.float32)).astype(own.dtype)

        @pl.when(x == at)
        def mine():
            own[...] = total

        @pl.when(x != at)
        def theirs():
            give[...] = total


def add_split(place_of, keep, *got):
    out = jax.ShapeDtypeStruct(keep.shape[1:], keep.dtype)
    return pl.pallas_call(
        split_kernel,
        out_shape=(out, out),
        in_specs=[whole(pltpu.SMEM), whole()] + [whole()] * len(got),
        out_specs=(whole(), whole()),
        compiler_params=pltpu.CompilerParams(vmem_limit_bytes=VMEM_LIMIT),
        cost_estimate=pl.CostEstimate(
            flops=keep.size, bytes_accessed=keep.size * 6, transcendentals=0
        ),
        name="add_split",
    )(place_of, keep, *got)


def assemble_kernel(place_of, own, by_core, by_tensor, by_both, full):
    x, c = place_of[2], place_of[3]
    width = own.shape[1]
    for ref, xx, cc in (
        (own, x, c), (by_core, x, 1 - c), (by_tensor, 1 - x, c), (by_both, 1 - x, 1 - c)
    ):
        at = pl.multiple_of((xx * 2 + cc) * width, width)
        full[:, pl.ds(at, width)] = ref[...]


def assemble(place_of, quarters):
    rows, width = quarters[0].shape
    return pl.pallas_call(
        assemble_kernel,
        out_shape=jax.ShapeDtypeStruct((rows, 4 * width), quarters[0].dtype),
        in_specs=[whole(pltpu.SMEM)] + [whole()] * 4,
        out_specs=whole(),
        compiler_params=pltpu.CompilerParams(vmem_limit_bytes=VMEM_LIMIT),
        cost_estimate=pl.CostEstimate(
            flops=0, bytes_accessed=rows * width * 16, transcendentals=0
        ),
        name="assemble",
    )(place_of, *quarters)


def line_grads_kernel(
    place_of, ids, tokens, upstream, tokens_1, upstream_1, tokens_2, upstream_2m, upstream_2o,
    mine_3, theirs_3, upstream_3m, upstream_3o, grads, tokens_3, upstream_2, upstream_3,
):
    slots, size = grads.shape[0], grads.shape[1]
    cols_n = upstream.shape[1] // size
    total = (tokens.shape[1] // size) * cols_n
    per_part = tokens_1.shape[2] // size
    group = math.gcd(slots, 8)
    tokens_3[place_of[3]] = mine_3[...]
    tokens_3[1 - place_of[3]] = theirs_3[...]
    upstream_2[...] = upstream_2m[...] + upstream_2o[...]
    upstream_3[...] = upstream_3m[...] + upstream_3o[...]

    @pl.loop(0, slots // group)
    def some(g):
        for s in [g * group + j for j in range(group)]:
            b = jnp.minimum(ids[s], total - 1)
            row = b // cols_n
            part = row // per_part
            whole_at = pl.ds(pl.multiple_of(row * size, size), size)
            at = pl.ds(pl.multiple_of((row % per_part) * size, size), size)
            c = pl.ds(pl.multiple_of((b % cols_n) * size, size), size)
            acc = jnp.zeros((size, size), jnp.float32)
            for left, right in (
                (tokens[:, whole_at], upstream),
                (tokens_1[part, :, at], upstream_1),
                (tokens_2[part, :, at], upstream_2),
                (tokens_3[part // 2, part % 2, :, at], upstream_3),
            ):
                acc += lax.dot_general(
                    left,
                    right[:, c],
                    (((0,), (0,)), ((), ())),
                    preferred_element_type=jnp.float32,
                )
            grads[s] = jnp.where(ids[s] < total, acc, 0.0).astype(grads.dtype)


def line_grads(place_of, ids, operands, size):
    slots = ids.shape[0]
    rows, width = operands[1].shape
    half = operands[7].shape
    return pl.pallas_call(
        line_grads_kernel,
        out_shape=jax.ShapeDtypeStruct((slots, size, size), jnp.bfloat16),
        in_specs=[whole(pltpu.SMEM)] * 2 + [whole()] * len(operands),
        out_specs=whole(),
        scratch_shapes=[pltpu.VMEM((2,) + half, jnp.bfloat16)]
        + [pltpu.VMEM((rows, width), jnp.bfloat16)] * 2,
        compiler_params=pltpu.CompilerParams(vmem_limit_bytes=VMEM_LIMIT),
        cost_estimate=pl.CostEstimate(
            flops=8 * slots * rows * size * size,
            bytes_accessed=2 * sum(a.size for a in operands) + 2 * slots * size * size,
            transcendentals=0,
        ),
        name="line_grads",
    )(place_of, ids, *operands)


INWARD = ((0, 1), (3, 2))
OUTWARD = ((1, 0), (2, 3))
PAIRS = INWARD + OUTWARD
MIDDLE = ((1, 2), (2, 1))
SWAP = ((0, 1), (1, 0))


def ids_block(block_ids, size):
    rows = size * size // block_ids.shape[0]
    return jnp.broadcast_to(block_ids, (rows, block_ids.shape[0])).reshape(1, size, size)


def ids_of(piece, slots):
    return piece[-1, 0, :slots].astype(jnp.int32)


def line_body(tokens, upstream, blocks, block_ids):
    slots, size = blocks.shape[0], blocks.shape[1]
    rows, depth = tokens.shape
    width = upstream.shape[1]
    half_slots = slots // 2
    part_width = depth // 4
    at_z, half = lax.axis_index("dp"), lax.axis_index("groups")
    at_tensor, at_replica = lax.axis_index("tensor"), lax.axis_index("replica")
    middle = (at_z == 1) | (at_z == 2)
    place_of = jnp.stack([middle.astype(jnp.int32), half, at_tensor, at_replica])
    along = functools.partial(lax.ppermute, axis_name="dp")
    across = functools.partial(
        lax.ppermute, axis_name=("groups", "dp"), perm=((1, 5), (5, 1), (2, 6), (6, 2))
    )
    middle_swap = ((2, 3), (3, 2), (4, 5), (5, 4))
    sideways = functools.partial(lax.ppermute, axis_name=("dp", "tensor"), perm=middle_swap)
    cores = functools.partial(lax.ppermute, axis_name=("dp", "replica"), perm=middle_swap)
    everywhere = functools.partial(lax.ppermute, axis_name="tensor", perm=SWAP)
    all_cores = functools.partial(lax.ppermute, axis_name="replica", perm=SWAP)
    stage = lax.optimization_barrier

    mine = lax.dynamic_slice_in_dim(blocks, half * half_slots, half_slots, 0)
    mine = jnp.concatenate([mine, ids_block(block_ids, size).astype(jnp.bfloat16)])
    (mine,) = stage((mine,))

    near_a = along(mine, perm=INWARD)
    far_a = along(mine, perm=MIDDLE)
    other = lax.dynamic_slice_in_dim(blocks, (1 - half) * half_slots, half_slots, 0)
    part = lax.dynamic_slice_in_dim(tokens, lax.axis_index(INNER) * part_width, part_width, 1)
    both = jnp.concatenate([part, upstream])
    near_a, far_a, both, other = stage((near_a, far_a, both, other))

    end_a = along(near_a, perm=MIDDLE)
    far_b = across(far_a)
    both_1 = along(both, perm=PAIRS)
    both_1, end_a, far_b, both, other = stage((both_1, end_a, far_b, both, other))

    near_b = along(other, perm=INWARD)
    end_b = across(end_a)
    both_2m = along(both, perm=MIDDLE)
    upstream_1 = both_1[rows:]
    tokens_1 = lax.all_gather(both_1[:rows], INNER)
    ids = (block_ids,) + tuple(ids_of(piece, slots) for piece in (near_a, far_a, end_a))
    turned = place_first(place_of, ids, (blocks, near_a, far_a, far_b, end_a), depth, width)
    half_1 = lax.dynamic_slice_in_dim(tokens_1, 2 * at_replica, 2, 0)
    near_b, end_b, both_2m, upstream_1, tokens_1, half_1, turned = stage(
        (near_b, end_b, both_2m, upstream_1, tokens_1, half_1, turned)
    )

    half_3m = along(half_1, perm=MIDDLE)
    both_2o = along(both_2m, perm=OUTWARD)
    end_keep, own_keep, own_give, *end_give = project_back(
        place_of, ids[1], ids[3], turned, near_b, end_b, upstream_1, upstream
    )
    end_keep, end_give = add_split(place_of, end_keep, *[cores(a) for a in end_give])
    end_keep, end_give, own_give, half_3m, both_2o = stage(
        (end_keep, end_give, own_give, half_3m, both_2o)
    )

    end_got = sideways(end_give)
    half_3o = along(half_3m, perm=OUTWARD)
    upstream_3m = along(upstream_1, perm=MIDDLE)
    own_keep, own_give = add_split(place_of, own_keep, cores(own_give))
    part_2 = both_2m[:rows] + both_2o[:rows]
    end_got, own_give, own_keep, part_2, upstream_3m = stage(
        (end_got, own_give, own_keep, part_2, upstream_3m)
    )

    sum_out = along(end_keep + end_got, perm=OUTWARD)
    own_got = sideways(own_give)
    tokens_2 = lax.all_gather(part_2, INNER)
    pieces = (blocks, near_a, near_b, far_a, far_b, end_a, end_b)
    proj, end_proj = project_forward(place_of, ids, pieces, tokens, tokens_1, width)
    upstream_3o = along(upstream_3m, perm=OUTWARD)
    sum_out, own_got, half_3o, upstream_3o, proj, end_proj = stage(
        (sum_out, own_got, half_3o, upstream_3o, proj, end_proj)
    )

    quarter = jnp.where(middle, own_keep + own_got, sum_out)
    by_tensor, by_core = everywhere(quarter), all_cores(quarter)
    proj_out = along(end_proj, perm=OUTWARD)
    half_3 = half_3m + half_3o
    operands = (
        tokens, upstream, tokens_1, upstream_1, tokens_2, both_2m[rows:], both_2o[rows:],
        half_3, all_cores(half_3), upstream_3m, upstream_3o,
    )
    grads = line_grads(place_of, block_ids, operands, size)
    by_tensor, by_core, grads = stage((by_tensor, by_core, grads))
    by_both = all_cores(by_tensor)
    projected = jnp.where(middle, proj, proj_out)
    token_grad = assemble(place_of, (quarter, by_core, by_tensor, by_both))
    return projected, token_grad, grads


def solution(mesh):
    line = tuple(mesh.shape[a] for a in ("groups", "dp", "tensor", "replica")) == (2, 4, 2, 2)
    return jax.shard_map(
        line_body if line else general_body,
        mesh=mesh,
        in_specs=(
            P(("groups", "dp"), None),
            P(("groups", "dp"), INNER),
            P(("dp",) + INNER, None, None),
            P(("dp",) + INNER),
        ),
        out_specs=(
            P(("groups", "dp"), INNER),
            P(("groups", "dp"), None),
            P(("groups", "dp") + INNER, None, None),
        ),
        check_vma=False,
    )
```

```python
import functools
import math

import jax
import jax.numpy as jnp
from jax import lax
from jax.experimental import pallas as pl
from jax.experimental.pallas import tpu as pltpu
from jax.sharding import PartitionSpec as P

VMEM_LIMIT = 60 * 1024 * 1024
INNER = ("tensor", "replica")


def whole(space=pltpu.VMEM):
    return pl.BlockSpec(memory_space=space)


def project_kernel(ids, blocks, tokens, upstream, proj, back, weight):
    slots, size = blocks.shape[0], blocks.shape[1]
    depth, width = weight.shape
    cols_n = width // size
    total = (depth // size) * cols_n
    weight[...] = jnp.zeros_like(weight)

    @pl.loop(0, slots, unroll=4)
    def place(s):
        b = ids[s]

        @pl.when(b < total)
        def put():
            r = pl.multiple_of((b // cols_n) * size, size)
            c = pl.multiple_of((b % cols_n) * size, size)
            weight[pl.ds(r, size), pl.ds(c, size)] = blocks[s]

    step = 256

    @pl.loop(0, width // step)
    def forward(n):
        c = pl.multiple_of(n * step, step)
        proj[:, pl.ds(c, step)] = jnp.dot(
            tokens[...], weight[:, pl.ds(c, step)], preferred_element_type=jnp.float32
        ).astype(proj.dtype)

    @pl.loop(0, depth // step, unroll=4)
    def backward(n):
        r = pl.multiple_of(n * step, step)
        back[:, pl.ds(r, step)] = lax.dot_general(
            upstream[...],
            weight[pl.ds(r, step), :],
            (((1,), (1,)), ((), ())),
            preferred_element_type=jnp.float32,
        ).astype(back.dtype)


def project(ids, blocks, tokens, upstream):
    rows, depth = tokens.shape
    width = upstream.shape[1]
    return pl.pallas_call(
        project_kernel,
        out_shape=(
            jax.ShapeDtypeStruct((rows, width), jnp.bfloat16),
            jax.ShapeDtypeStruct((rows, depth), jnp.bfloat16),
        ),
        in_specs=[whole(pltpu.SMEM), whole(), whole(), whole()],
        out_specs=(whole(), whole()),
        scratch_shapes=[pltpu.VMEM((depth, width), jnp.bfloat16)],
        compiler_params=pltpu.CompilerParams(vmem_limit_bytes=VMEM_LIMIT),
        cost_estimate=pl.CostEstimate(
            flops=4 * rows * depth * width,
            bytes_accessed=blocks.size * 2 + rows * (depth + width) * 4,
            transcendentals=0,
        ),
        name="project",
    )(ids, blocks, tokens, upstream)


def block_grad_kernel(ids, tokens, upstream, grads):
    slots, size = grads.shape[0], grads.shape[1]
    parts, slabs, _, part_width = tokens.shape
    cols_n = upstream.shape[2] // size
    per_part = part_width // size
    total = parts * per_part * cols_n

    @pl.loop(0, slots)
    def one(s):
        b = ids[s]

        @pl.when(b < total)
        def fill():
            row = b // cols_n
            part = row // per_part
            r = pl.multiple_of((row % per_part) * size, size)
            c = pl.multiple_of((b % cols_n) * size, size)
            acc = jnp.zeros((size, size), jnp.float32)
            for k in range(slabs):
                acc += lax.dot_general(
                    tokens[part, k, :, pl.ds(r, size)],
                    upstream[k, :, pl.ds(c, size)],
                    (((0,), (0,)), ((), ())),
                    preferred_element_type=jnp.float32,
                )
            grads[s] = acc.astype(grads.dtype)

        @pl.when(b >= total)
        def clear():
            grads[s] = jnp.zeros((size, size), grads.dtype)


def block_grads(ids, tokens, upstream, size):
    slots = ids.shape[0]
    parts, slabs, rows, part_width = tokens.shape
    return pl.pallas_call(
        block_grad_kernel,
        out_shape=jax.ShapeDtypeStruct((slots, size, size), jnp.bfloat16),
        in_specs=[whole(pltpu.SMEM), whole(), whole()],
        out_specs=whole(),
        compiler_params=pltpu.CompilerParams(vmem_limit_bytes=VMEM_LIMIT),
        cost_estimate=pl.CostEstimate(
            flops=2 * slots * slabs * rows * size * size,
            bytes_accessed=2 * (tokens.size + upstream.size + slots * size * size),
            transcendentals=0,
        ),
        name="block_grads",
    )(ids, tokens, upstream)


def general_body(tokens, upstream, blocks, block_ids):
    size = blocks.shape[1]
    all_blocks = lax.all_gather(blocks, "dp", axis=0, tiled=True)
    all_ids = lax.all_gather(block_ids, "dp", axis=0, tiled=True)
    proj, back = project(all_ids, all_blocks, tokens, upstream)
    terms = block_grads(all_ids, tokens[None, None], upstream[None], size)
    grads = lax.psum_scatter(terms, "dp", scatter_dimension=0, tiled=True)
    return proj, lax.psum(back, INNER), grads


def place_blocks(ids, first, blocks, weight, turned, slots):
    size = blocks.shape[1]
    depth, width = turned.shape[::-1] if weight is None else weight.shape
    cols_n = width // size
    total = (depth // size) * cols_n

    @pl.loop(0, slots, unroll=4)
    def place(s):
        b = ids[first + s]

        @pl.when(b < total)
        def put():
            r = pl.multiple_of((b // cols_n) * size, size)
            c = pl.multiple_of((b % cols_n) * size, size)
            if weight is not None:
                weight[pl.ds(r, size), pl.ds(c, size)] = blocks[s]
            if turned is not None:
                turned[pl.ds(c, size), pl.ds(r, size)] = blocks[s].T


def place_kernel(place_of, ids_0, ids_1, ids_2, ids_3, own, near_a, far_a, far_b, end_a, turned):
    is_middle, half = place_of[0], place_of[1]
    half_slots = far_b.shape[0] - 1
    mine, other = half * half_slots, (1 - half) * half_slots

    @pl.when(is_middle == 1)
    def work():
        turned[...] = jnp.zeros_like(turned)
        place_blocks(ids_0, 0, own, None, turned, own.shape[0])
        place_blocks(ids_1, mine, near_a, None, turned, half_slots)
        place_blocks(ids_2, mine, far_a, None, turned, half_slots)
        place_blocks(ids_2, other, far_b, None, turned, half_slots)
        place_blocks(ids_3, mine, end_a, None, turned, half_slots)


def place_first(place_of, ids, pieces, depth, width):
    return pl.pallas_call(
        place_kernel,
        out_shape=jax.ShapeDtypeStruct((width, depth), jnp.bfloat16),
        in_specs=[whole(pltpu.SMEM)] * 5 + [whole()] * 5,
        out_specs=whole(),
        compiler_params=pltpu.CompilerParams(vmem_limit_bytes=VMEM_LIMIT),
        cost_estimate=pl.CostEstimate(
            flops=0, bytes_accessed=depth * width * 4, transcendentals=0
        ),
        name="place_first",
    )(place_of, *ids, *pieces)


def plain_kernel(place_of, ids_0, ids_1, ids_2, own, near_a, far_a, weight):
    half_slots = near_a.shape[0] - 1
    mine = place_of[1] * half_slots

    @pl.when(place_of[0] == 1)
    def work():
        weight[...] = jnp.zeros_like(weight)
        place_blocks(ids_0, 0, own, weight, None, own.shape[0])
        place_blocks(ids_1, mine, near_a, weight, None, half_slots)
        place_blocks(ids_2, mine, far_a, weight, None, half_slots)


def place_plain(place_of, ids, pieces, depth, width):
    return pl.pallas_call(
        plain_kernel,
        out_shape=jax.ShapeDtypeStruct((depth, width), jnp.bfloat16),
        in_specs=[whole(pltpu.SMEM)] * 4 + [whole()] * 3,
        out_specs=whole(),
        compiler_params=pltpu.CompilerParams(vmem_limit_bytes=VMEM_LIMIT),
        cost_estimate=pl.CostEstimate(
            flops=0, bytes_accessed=depth * width * 3, transcendentals=0
        ),
        name="place_plain",
    )(place_of, *ids, *pieces)


def back_kernel(
    place_of, ids_1, ids_3, partial, near_b, end_b, two_upstream,
    end_keep, own_keep, own_give, end_give_0, end_give_1, held, sources, sem,
):
    half_slots = near_b.shape[0]
    other = (1 - place_of[1]) * half_slots
    rows, width = two_upstream.shape[1:]
    step = 256
    per_part = end_keep.shape[2] // step

    @pl.when(place_of[0] == 1)
    def work():
        load = pltpu.make_async_copy(partial, held, sem)
        load.start()
        sources[:rows] = two_upstream[1]
        sources[rows:] = two_upstream[0]
        load.wait()
        place_blocks(ids_1, other, near_b, None, held, half_slots)
        place_blocks(ids_3, other, end_b, None, held, half_slots)

        def column(part, end_target, own_target):
            @pl.loop(0, per_part, unroll=2)
            def backward(n):
                at = pl.multiple_of(n * step, step)
                result = jnp.dot(
                    sources[...],
                    held[:, pl.ds(pl.multiple_of(part * per_part * step + at, step), step)],
                    preferred_element_type=jnp.float32,
                ).astype(own_target.dtype)
                end_target[:, pl.ds(at, step)] = result[:rows]
                own_target[:, pl.ds(at, step)] = result[rows:]

        for x, end_give in enumerate((end_give_0, end_give_1)):
            column(2 * x + place_of[3], end_keep.at[x], own_keep.at[x])
            column(2 * x + 1 - place_of[3], end_give, own_give.at[x])


def project_back(place_of, ids_1, ids_3, partial, near_b, end_b, two_upstream):
    width, depth = partial.shape
    rows = two_upstream.shape[1]
    quarter = jax.ShapeDtypeStruct((rows, depth // 4), jnp.bfloat16)
    half = jax.ShapeDtypeStruct((2, rows, depth // 4), jnp.bfloat16)
    return pl.pallas_call(
        back_kernel,
        out_shape=(half, half, half, quarter, quarter),
        in_specs=[whole(pltpu.SMEM)] * 3 + [whole(pl.ANY)] + [whole()] * 3,
        out_specs=(whole(),) * 5,
        scratch_shapes=[
            pltpu.VMEM((width, depth), jnp.bfloat16),
            pltpu.VMEM((2 * rows, width), jnp.bfloat16),
            pltpu.SemaphoreType.DMA,
        ],
        compiler_params=pltpu.CompilerParams(vmem_limit_bytes=VMEM_LIMIT),
        cost_estimate=pl.CostEstimate(
            flops=4 * rows * depth * width,
            bytes_accessed=depth * width * 2 + rows * (depth + width) * 4,
            transcendentals=0,
        ),
        name="project_back",
    )(place_of, ids_1, ids_3, partial, near_b, end_b, two_upstream)


def forward_kernel(
    place_of, ids_1, ids_2, ids_3, partial, near_b, far_b, end_a, end_b,
    tokens, end_tokens, proj, end_proj, weight, sem,
):
    half_slots = near_b.shape[0]
    mine, other = place_of[1] * half_slots, (1 - place_of[1]) * half_slots
    width = weight.shape[1]
    parts, rows, part_width = end_tokens.shape
    step = 256

    @pl.when(place_of[0] == 1)
    def work():
        load = pltpu.make_async_copy(partial, weight, sem)
        load.start()
        load.wait()
        place_blocks(ids_1, other, near_b, weight, None, half_slots)
        place_blocks(ids_2, other, far_b, weight, None, half_slots)
        place_blocks(ids_3, mine, end_a, weight, None, half_slots)
        place_blocks(ids_3, other, end_b, weight, None, half_slots)

        @pl.loop(0, width // step, unroll=2)
        def forward(n):
            c = pl.multiple_of(n * step, step)
            acc = jnp.zeros((rows, step), jnp.float32)
            for q in range(parts):
                acc += jnp.dot(
                    end_tokens[q],
                    weight[q * part_width : (q + 1) * part_width, pl.ds(c, step)],
                    preferred_element_type=jnp.float32,
                )
            end_proj[:, pl.ds(c, step)] = acc.astype(end_proj.dtype)
            proj[:, pl.ds(c, step)] = jnp.dot(
                tokens[...], weight[:, pl.ds(c, step)], preferred_element_type=jnp.float32
            ).astype(proj.dtype)


def project_forward(place_of, ids, partial, pieces, tokens, end_tokens):
    rows, depth = tokens.shape
    width = partial.shape[1]
    out = jax.ShapeDtypeStruct((rows, width), jnp.bfloat16)
    return pl.pallas_call(
        forward_kernel,
        out_shape=(out, out),
        in_specs=[whole(pltpu.SMEM)] * 4 + [whole(pl.ANY)] + [whole()] * 6,
        out_specs=(whole(),) * 2,
        scratch_shapes=[pltpu.VMEM((depth, width), jnp.bfloat16), pltpu.SemaphoreType.DMA],
        compiler_params=pltpu.CompilerParams(vmem_limit_bytes=VMEM_LIMIT),
        cost_estimate=pl.CostEstimate(flops=0, bytes_accessed=0, transcendentals=0),
        name="project_forward",
    )(place_of, *ids, partial, *pieces, tokens, end_tokens)


def split_kernel(place_of, keep, *refs):
    x = place_of[2]
    own, give = refs[-2:]
    got = refs[:-2] if len(refs) > 3 else (refs[0].at[0], refs[0].at[1])
    for at in range(2):
        total = (keep[at].astype(jnp.float32) + got[at][...].astype(jnp.float32)).astype(own.dtype)

        @pl.when(x == at)
        def mine():
            own[...] = total

        @pl.when(x != at)
        def theirs():
            give[...] = total


def add_split(place_of, keep, *got):
    out = jax.ShapeDtypeStruct(keep.shape[1:], keep.dtype)
    return pl.pallas_call(
        split_kernel,
        out_shape=(out, out),
        in_specs=[whole(pltpu.SMEM), whole()] + [whole()] * len(got),
        out_specs=(whole(), whole()),
        compiler_params=pltpu.CompilerParams(vmem_limit_bytes=VMEM_LIMIT),
        cost_estimate=pl.CostEstimate(
            flops=keep.size, bytes_accessed=keep.size * 6, transcendentals=0
        ),
        name="add_split",
    )(place_of, keep, *got)


def assemble_kernel(place_of, own, by_core, by_tensor, by_both, full):
    x, c = place_of[2], place_of[3]
    width = own.shape[1]
    for ref, xx, cc in (
        (own, x, c), (by_core, x, 1 - c), (by_tensor, 1 - x, c), (by_both, 1 - x, 1 - c)
    ):
        at = pl.multiple_of((xx * 2 + cc) * width, width)
        full[:, pl.ds(at, width)] = ref[...]


def assemble(place_of, quarters):
    rows, width = quarters[0].shape
    return pl.pallas_call(
        assemble_kernel,
        out_shape=jax.ShapeDtypeStruct((rows, 4 * width), quarters[0].dtype),
        in_specs=[whole(pltpu.SMEM)] + [whole()] * 4,
        out_specs=whole(),
        compiler_params=pltpu.CompilerParams(vmem_limit_bytes=VMEM_LIMIT),
        cost_estimate=pl.CostEstimate(
            flops=0, bytes_accessed=rows * width * 16, transcendentals=0
        ),
        name="assemble",
    )(place_of, *quarters)


def line_grads_kernel(
    place_of, ids, tokens, tokens_1, own_far, core_far, side_far, both_far,
    two_upstream, far_upstream_m, far_upstream_o, grads, far, turned,
):
    slots, size = grads.shape[0], grads.shape[1]
    parts, rows, part_width = tokens_1.shape
    cols_n = two_upstream.shape[2] // size
    total = parts * (part_width // size) * cols_n
    per_part = part_width // size
    group = math.gcd(slots, 8)
    x, c = place_of[2], place_of[3]
    for ref, xx, cc in (
        (own_far, x, c), (core_far, x, 1 - c), (side_far, 1 - x, c), (both_far, 1 - x, 1 - c)
    ):
        far[2 * xx + cc] = ref[...]

    @pl.loop(0, cols_n)
    def turn(n):
        at = pl.ds(pl.multiple_of(n * size, size), size)
        for k in range(2):
            turned[k, at, :] = two_upstream[k, :, at].T
            turned[2 + k, at, :] = (far_upstream_m[k, :, at] + far_upstream_o[k, :, at]).T

    @pl.loop(0, slots // group)
    def some(g):
        for s in [g * group + j for j in range(group)]:
            b = jnp.minimum(ids[s], total - 1)
            row = b // cols_n
            part = row // per_part
            whole_at = pl.ds(pl.multiple_of(row * size, size), size)
            at = pl.ds(pl.multiple_of((row % per_part) * size, size), size)
            col = pl.ds(pl.multiple_of((b % cols_n) * size, size), size)
            acc = jnp.zeros((size, size), jnp.float32)
            for k, right in enumerate(
                (tokens[:, whole_at], tokens_1[part, :, at], far[part, 0, :, at], far[part, 1, :, at])
            ):
                acc += jnp.dot(turned[k, col, :], right, preferred_element_type=jnp.float32)
            grads[s] = jnp.where(ids[s] < total, acc.T, 0.0).astype(grads.dtype)


def line_grads(place_of, ids, operands, size):
    slots = ids.shape[0]
    rows, depth = operands[0].shape
    width = operands[-1].shape[2]
    return pl.pallas_call(
        line_grads_kernel,
        out_shape=jax.ShapeDtypeStruct((slots, size, size), jnp.bfloat16),
        in_specs=[whole(pltpu.SMEM)] * 2 + [whole()] * len(operands),
        out_specs=whole(),
        scratch_shapes=[
            pltpu.VMEM((4, 2, rows, depth // 4), jnp.bfloat16),
            pltpu.VMEM((4, width, rows), jnp.bfloat16),
        ],
        compiler_params=pltpu.CompilerParams(vmem_limit_bytes=VMEM_LIMIT),
        cost_estimate=pl.CostEstimate(
            flops=8 * slots * rows * size * size,
            bytes_accessed=2 * sum(a.size for a in operands) + 2 * slots * size * size,
            transcendentals=0,
        ),
        name="line_grads",
    )(place_of, ids, *operands)


INWARD = ((0, 1), (3, 2))
OUTWARD = ((1, 0), (2, 3))
PAIRS = INWARD + OUTWARD
MIDDLE = ((1, 2), (2, 1))
SWAP = ((0, 1), (1, 0))


def ids_block(block_ids, size):
    rows = size * size // block_ids.shape[0]
    return jnp.broadcast_to(block_ids, (rows, block_ids.shape[0])).reshape(1, size, size)


def ids_of(piece, slots):
    return piece[-1, 0, :slots].astype(jnp.int32)


def line_body(tokens, upstream, blocks, block_ids):
    slots, size = blocks.shape[0], blocks.shape[1]
    rows, depth = tokens.shape
    width = upstream.shape[1]
    half_slots = slots // 2
    part_width = depth // 4
    at_z, half = lax.axis_index("dp"), lax.axis_index("groups")
    at_tensor, at_replica = lax.axis_index("tensor"), lax.axis_index("replica")
    middle = (at_z == 1) | (at_z == 2)
    place_of = jnp.stack([middle.astype(jnp.int32), half, at_tensor, at_replica])
    along = functools.partial(lax.ppermute, axis_name="dp")
    across = functools.partial(
        lax.ppermute, axis_name=("groups", "dp"), perm=((1, 5), (5, 1), (2, 6), (6, 2))
    )
    middle_swap = ((2, 3), (3, 2), (4, 5), (5, 4))
    sideways = functools.partial(lax.ppermute, axis_name=("dp", "tensor"), perm=middle_swap)
    cores = functools.partial(lax.ppermute, axis_name=("dp", "replica"), perm=middle_swap)
    end_sideways = functools.partial(
        lax.ppermute, axis_name=("dp", "tensor"), perm=((0, 1), (1, 0), (6, 7), (7, 6))
    )
    everywhere = functools.partial(lax.ppermute, axis_name="tensor", perm=SWAP)
    all_cores = functools.partial(lax.ppermute, axis_name="replica", perm=SWAP)
    stage = lax.optimization_barrier

    mine = lax.dynamic_slice_in_dim(blocks, half * half_slots, half_slots, 0)
    mine = jnp.concatenate([mine, ids_block(block_ids, size).astype(jnp.bfloat16)])
    (mine,) = stage((mine,))

    near_a = along(mine, perm=INWARD)
    far_a = along(mine, perm=MIDDLE)
    other = lax.dynamic_slice_in_dim(blocks, (1 - half) * half_slots, half_slots, 0)
    part = lax.dynamic_slice_in_dim(tokens, lax.axis_index(INNER) * part_width, part_width, 1)
    near_a, far_a, part, other = stage((near_a, far_a, part, other))

    end_a = along(near_a, perm=MIDDLE)
    far_b = across(far_a)
    part_1 = along(part, perm=PAIRS)
    upstream_1 = along(upstream, perm=PAIRS)
    ids_1, ids_2 = ids_of(near_a, slots), ids_of(far_a, slots)
    plain = place_plain(place_of, (block_ids, ids_1, ids_2), (blocks, near_a, far_a), depth, width)
    part_1, upstream_1, end_a, far_b, part, other, plain = stage(
        (part_1, upstream_1, end_a, far_b, part, other, plain)
    )

    near_b = along(other, perm=INWARD)
    end_b = across(end_a)
    part_2m = along(part, perm=MIDDLE)
    part_3m = along(part_1, perm=MIDDLE)
    tokens_1 = lax.all_gather(part_1, INNER)
    two_upstream = jnp.stack([upstream, upstream_1])
    ids_3 = ids_of(end_a, slots)
    turned = place_first(
        place_of, (block_ids, ids_1, ids_2, ids_3), (blocks, near_a, far_a, far_b, end_a), depth, width
    )
    near_b, end_b, part_2m, part_3m, two_upstream, tokens_1, turned = stage(
        (near_b, end_b, part_2m, part_3m, two_upstream, tokens_1, turned)
    )

    far_m = jnp.stack([part_2m, part_3m])
    far_o = along(far_m, perm=OUTWARD)
    far_upstream_m = along(two_upstream, perm=MIDDLE)
    side_m = sideways(far_m)
    end_keep, own_keep, own_give, *end_give = project_back(
        place_of, ids_1, ids_3, turned, near_b, end_b, two_upstream
    )
    end_keep, end_give = add_split(place_of, end_keep, *[cores(a) for a in end_give])
    end_keep, end_give, own_give, far_o, far_upstream_m, side_m = stage(
        (end_keep, end_give, own_give, far_o, far_upstream_m, side_m)
    )

    end_got = sideways(end_give)
    side_o = end_sideways(far_o)
    far_upstream_o = along(far_upstream_m, perm=OUTWARD)
    own_keep, own_give = add_split(place_of, own_keep, cores(own_give))
    own_far = far_m + far_o
    core_far = all_cores(own_far)
    end_got, own_give, own_keep, core_far, own_far = stage(
        (end_got, own_give, own_keep, core_far, own_far)
    )

    sum_out = along(end_keep + end_got, perm=OUTWARD)
    own_got = sideways(own_give)
    proj, end_proj = project_forward(
        place_of, (ids_1, ids_2, ids_3), plain, (near_b, far_b, end_a, end_b), tokens, tokens_1
    )
    sum_out, own_got, side_o, far_upstream_o, proj, end_proj = stage(
        (sum_out, own_got, side_o, far_upstream_o, proj, end_proj)
    )

    side_far = side_m + side_o
    both_far = all_cores(side_far)
    quarter = jnp.where(middle, own_keep + own_got, sum_out)
    by_tensor, by_core = everywhere(quarter), all_cores(quarter)
    proj_out = along(end_proj, perm=OUTWARD)
    operands = (
        tokens, tokens_1, own_far, core_far, side_far, both_far,
        two_upstream, far_upstream_m, far_upstream_o,
    )
    grads = line_grads(place_of, block_ids, operands, size)
    by_tensor, by_core, grads = stage((by_tensor, by_core, grads))
    by_both = all_cores(by_tensor)
    projected = jnp.where(middle, proj, proj_out)
    token_grad = assemble(place_of, (quarter, by_core, by_tensor, by_both))
    return projected, token_grad, grads


def solution(mesh):
    line = tuple(mesh.shape[a] for a in ("groups", "dp", "tensor", "replica")) == (2, 4, 2, 2)
    return jax.shard_map(
        line_body if line else general_body,
        mesh=mesh,
        in_specs=(
            P(("groups", "dp"), None),
            P(("groups", "dp"), INNER),
            P(("dp",) + INNER, None, None),
            P(("dp",) + INNER),
        ),
        out_specs=(
            P(("groups", "dp"), INNER),
            P(("groups", "dp"), None),
            P(("groups", "dp") + INNER, None, None),
        ),
        check_vma=False,
    )
```

```python
import functools
import math

import jax
import jax.numpy as jnp
from jax import lax
from jax.experimental import pallas as pl
from jax.experimental.pallas import tpu as pltpu
from jax.sharding import PartitionSpec as P

VMEM_LIMIT = 60 * 1024 * 1024
INNER = ("tensor", "replica")


def whole(space=pltpu.VMEM):
    return pl.BlockSpec(memory_space=space)


def project_kernel(ids, blocks, tokens, upstream, proj, back, weight):
    slots, size = blocks.shape[0], blocks.shape[1]
    depth, width = weight.shape
    cols_n = width // size
    total = (depth // size) * cols_n
    weight[...] = jnp.zeros_like(weight)

    @pl.loop(0, slots, unroll=4)
    def place(s):
        b = ids[s]

        @pl.when(b < total)
        def put():
            r = pl.multiple_of((b // cols_n) * size, size)
            c = pl.multiple_of((b % cols_n) * size, size)
            weight[pl.ds(r, size), pl.ds(c, size)] = blocks[s]

    step = 256

    @pl.loop(0, width // step)
    def forward(n):
        c = pl.multiple_of(n * step, step)
        proj[:, pl.ds(c, step)] = jnp.dot(
            tokens[...], weight[:, pl.ds(c, step)], preferred_element_type=jnp.float32
        ).astype(proj.dtype)

    @pl.loop(0, depth // step, unroll=4)
    def backward(n):
        r = pl.multiple_of(n * step, step)
        back[:, pl.ds(r, step)] = lax.dot_general(
            upstream[...],
            weight[pl.ds(r, step), :],
            (((1,), (1,)), ((), ())),
            preferred_element_type=jnp.float32,
        ).astype(back.dtype)


def project(ids, blocks, tokens, upstream):
    rows, depth = tokens.shape
    width = upstream.shape[1]
    return pl.pallas_call(
        project_kernel,
        out_shape=(
            jax.ShapeDtypeStruct((rows, width), jnp.bfloat16),
            jax.ShapeDtypeStruct((rows, depth), jnp.bfloat16),
        ),
        in_specs=[whole(pltpu.SMEM), whole(), whole(), whole()],
        out_specs=(whole(), whole()),
        scratch_shapes=[pltpu.VMEM((depth, width), jnp.bfloat16)],
        compiler_params=pltpu.CompilerParams(vmem_limit_bytes=VMEM_LIMIT),
        cost_estimate=pl.CostEstimate(
            flops=4 * rows * depth * width,
            bytes_accessed=blocks.size * 2 + rows * (depth + width) * 4,
            transcendentals=0,
        ),
        name="project",
    )(ids, blocks, tokens, upstream)


def block_grad_kernel(ids, tokens, upstream, grads):
    slots, size = grads.shape[0], grads.shape[1]
    parts, slabs, _, part_width = tokens.shape
    cols_n = upstream.shape[2] // size
    per_part = part_width // size
    total = parts * per_part * cols_n

    @pl.loop(0, slots)
    def one(s):
        b = ids[s]

        @pl.when(b < total)
        def fill():
            row = b // cols_n
            part = row // per_part
            r = pl.multiple_of((row % per_part) * size, size)
            c = pl.multiple_of((b % cols_n) * size, size)
            acc = jnp.zeros((size, size), jnp.float32)
            for k in range(slabs):
                acc += lax.dot_general(
                    tokens[part, k, :, pl.ds(r, size)],
                    upstream[k, :, pl.ds(c, size)],
                    (((0,), (0,)), ((), ())),
                    preferred_element_type=jnp.float32,
                )
            grads[s] = acc.astype(grads.dtype)

        @pl.when(b >= total)
        def clear():
            grads[s] = jnp.zeros((size, size), grads.dtype)


def block_grads(ids, tokens, upstream, size):
    slots = ids.shape[0]
    parts, slabs, rows, part_width = tokens.shape
    return pl.pallas_call(
        block_grad_kernel,
        out_shape=jax.ShapeDtypeStruct((slots, size, size), jnp.bfloat16),
        in_specs=[whole(pltpu.SMEM), whole(), whole()],
        out_specs=whole(),
        compiler_params=pltpu.CompilerParams(vmem_limit_bytes=VMEM_LIMIT),
        cost_estimate=pl.CostEstimate(
            flops=2 * slots * slabs * rows * size * size,
            bytes_accessed=2 * (tokens.size + upstream.size + slots * size * size),
            transcendentals=0,
        ),
        name="block_grads",
    )(ids, tokens, upstream)


def general_body(tokens, upstream, blocks, block_ids):
    size = blocks.shape[1]
    all_blocks = lax.all_gather(blocks, "dp", axis=0, tiled=True)
    all_ids = lax.all_gather(block_ids, "dp", axis=0, tiled=True)
    proj, back = project(all_ids, all_blocks, tokens, upstream)
    terms = block_grads(all_ids, tokens[None, None], upstream[None], size)
    grads = lax.psum_scatter(terms, "dp", scatter_dimension=0, tiled=True)
    return proj, lax.psum(back, INNER), grads


def place_blocks(ids, first, blocks, weight, turned, slots):
    size = blocks.shape[1]
    depth, width = turned.shape[::-1] if weight is None else weight.shape
    cols_n = width // size
    total = (depth // size) * cols_n

    @pl.loop(0, slots, unroll=4)
    def place(s):
        b = ids[first + s]

        @pl.when(b < total)
        def put():
            r = pl.multiple_of((b // cols_n) * size, size)
            c = pl.multiple_of((b % cols_n) * size, size)
            if weight is not None:
                weight[pl.ds(r, size), pl.ds(c, size)] = blocks[s]
            if turned is not None:
                turned[pl.ds(c, size), pl.ds(r, size)] = blocks[s].T


def place_kernel(
    place_of, ids_0, ids_1, ids_2, ids_3, own, near_a, far_a, far_b, end_a, weight, turned
):
    is_middle, half = place_of[0], place_of[1]
    half_slots = far_b.shape[0] - 1
    mine, other = half * half_slots, (1 - half) * half_slots

    @pl.when(is_middle == 1)
    def work():
        weight[...] = jnp.zeros_like(weight)
        turned[...] = jnp.zeros_like(turned)
        place_blocks(ids_0, 0, own, weight, turned, own.shape[0])
        place_blocks(ids_1, mine, near_a, weight, turned, half_slots)
        place_blocks(ids_2, mine, far_a, weight, turned, half_slots)
        place_blocks(ids_2, other, far_b, weight, turned, half_slots)
        place_blocks(ids_3, mine, end_a, weight, turned, half_slots)


def place_first(place_of, ids, pieces, depth, width):
    return pl.pallas_call(
        place_kernel,
        out_shape=(
            jax.ShapeDtypeStruct((depth, width), jnp.bfloat16),
            jax.ShapeDtypeStruct((width, depth), jnp.bfloat16),
        ),
        in_specs=[whole(pltpu.SMEM)] * 5 + [whole()] * 5,
        out_specs=(whole(), whole()),
        compiler_params=pltpu.CompilerParams(vmem_limit_bytes=VMEM_LIMIT),
        cost_estimate=pl.CostEstimate(
            flops=0, bytes_accessed=depth * width * 6, transcendentals=0
        ),
        name="place_first",
    )(place_of, *ids, *pieces)


def back_kernel(
    place_of, ids_1, ids_3, partial, near_b, end_b, end_upstream, upstream,
    end_keep, own_keep, own_give, end_give_0, end_give_1, held, sources, sem,
):
    half_slots = near_b.shape[0]
    other = (1 - place_of[1]) * half_slots
    rows, width = upstream.shape
    step = 256
    per_part = end_keep.shape[2] // step

    @pl.when(place_of[0] == 1)
    def work():
        load = pltpu.make_async_copy(partial, held, sem)
        load.start()
        sources[:rows] = end_upstream[...]
        sources[rows:] = upstream[...]
        load.wait()
        place_blocks(ids_1, other, near_b, None, held, half_slots)
        place_blocks(ids_3, other, end_b, None, held, half_slots)

        def column(part, end_target, own_target):
            @pl.loop(0, per_part, unroll=2)
            def backward(n):
                at = pl.multiple_of(n * step, step)
                result = jnp.dot(
                    sources[...],
                    held[:, pl.ds(pl.multiple_of(part * per_part * step + at, step), step)],
                    preferred_element_type=jnp.float32,
                ).astype(own_target.dtype)
                end_target[:, pl.ds(at, step)] = result[:rows]
                own_target[:, pl.ds(at, step)] = result[rows:]

        for x, end_give in enumerate((end_give_0, end_give_1)):
            column(2 * x + place_of[3], end_keep.at[x], own_keep.at[x])
            column(2 * x + 1 - place_of[3], end_give, own_give.at[x])


def project_back(place_of, ids_1, ids_3, partial, near_b, end_b, end_upstream, upstream):
    width, depth = partial.shape
    rows = upstream.shape[0]
    quarter = jax.ShapeDtypeStruct((rows, depth // 4), jnp.bfloat16)
    half = jax.ShapeDtypeStruct((2, rows, depth // 4), jnp.bfloat16)
    return pl.pallas_call(
        back_kernel,
        out_shape=(half, half, half, quarter, quarter),
        in_specs=[whole(pltpu.SMEM)] * 3 + [whole(pl.ANY)] + [whole()] * 4,
        out_specs=(whole(),) * 5,
        scratch_shapes=[
            pltpu.VMEM((width, depth), jnp.bfloat16),
            pltpu.VMEM((2 * rows, width), jnp.bfloat16),
            pltpu.SemaphoreType.DMA,
        ],
        compiler_params=pltpu.CompilerParams(vmem_limit_bytes=VMEM_LIMIT),
        cost_estimate=pl.CostEstimate(
            flops=4 * rows * depth * width,
            bytes_accessed=depth * width * 2 + rows * (depth + width) * 4,
            transcendentals=0,
        ),
        name="project_back",
    )(place_of, ids_1, ids_3, partial, near_b, end_b, end_upstream, upstream)


def forward_kernel(place_of, ids_1, ids_3, partial, near_b, end_b, tokens, proj, held, sem):
    half_slots = near_b.shape[0]
    other = (1 - place_of[1]) * half_slots
    width = held.shape[1]
    rows = proj.shape[0]
    step = 256

    @pl.when(place_of[0] == 1)
    def work():
        load = pltpu.make_async_copy(partial, held, sem)
        load.start()
        load.wait()
        place_blocks(ids_1, other, near_b, held, None, half_slots)
        place_blocks(ids_3, other, end_b, held, None, half_slots)

        @pl.loop(0, width // step, unroll=2)
        def forward(n):
            c = pl.ds(pl.multiple_of(n * step, step), step)
            if len(tokens.shape) == 2:
                acc = jnp.dot(tokens[...], held[:, c], preferred_element_type=jnp.float32)
            else:
                part_width = tokens.shape[2]
                acc = jnp.zeros((rows, step), jnp.float32)
                for q in range(tokens.shape[0]):
                    acc += jnp.dot(
                        tokens[q],
                        held[q * part_width : (q + 1) * part_width, c],
                        preferred_element_type=jnp.float32,
                    )
            proj[:, c] = acc.astype(proj.dtype)


def project_forward(place_of, ids_1, ids_3, partial, near_b, end_b, tokens):
    depth, width = partial.shape
    rows = tokens.shape[-2]
    return pl.pallas_call(
        forward_kernel,
        out_shape=jax.ShapeDtypeStruct((rows, width), jnp.bfloat16),
        in_specs=[whole(pltpu.SMEM)] * 3 + [whole(pl.ANY)] + [whole()] * 3,
        out_specs=whole(),
        scratch_shapes=[pltpu.VMEM((depth, width), jnp.bfloat16), pltpu.SemaphoreType.DMA],
        compiler_params=pltpu.CompilerParams(vmem_limit_bytes=VMEM_LIMIT),
        cost_estimate=pl.CostEstimate(
            flops=2 * rows * depth * width,
            bytes_accessed=depth * width * 2 + rows * (depth + width) * 2,
            transcendentals=0,
        ),
        name="project_forward",
    )(place_of, ids_1, ids_3, partial, near_b, end_b, tokens)


def split_kernel(place_of, keep, *refs):
    x = place_of[2]
    own, give = refs[-2:]
    got = refs[:-2] if len(refs) > 3 else (refs[0].at[0], refs[0].at[1])
    for at in range(2):
        total = (keep[at].astype(jnp.float32) + got[at][...].astype(jnp.float32)).astype(own.dtype)

        @pl.when(x == at)
        def mine():
            own[...] = total

        @pl.when(x != at)
        def theirs():
            give[...] = total


def add_split(place_of, keep, *got):
    out = jax.ShapeDtypeStruct(keep.shape[1:], keep.dtype)
    return pl.pallas_call(
        split_kernel,
        out_shape=(out, out),
        in_specs=[whole(pltpu.SMEM), whole()] + [whole()] * len(got),
        out_specs=(whole(), whole()),
        compiler_params=pltpu.CompilerParams(vmem_limit_bytes=VMEM_LIMIT),
        cost_estimate=pl.CostEstimate(
            flops=keep.size, bytes_accessed=keep.size * 6, transcendentals=0
        ),
        name="add_split",
    )(place_of, keep, *got)


def assemble_kernel(place_of, own, by_core, by_tensor, by_both, full):
    x, c = place_of[2], place_of[3]
    width = own.shape[1]
    for ref, xx, cc in (
        (own, x, c), (by_core, x, 1 - c), (by_tensor, 1 - x, c), (by_both, 1 - x, 1 - c)
    ):
        at = pl.multiple_of((xx * 2 + cc) * width, width)
        full[:, pl.ds(at, width)] = ref[...]


def assemble(place_of, quarters):
    rows, width = quarters[0].shape
    return pl.pallas_call(
        assemble_kernel,
        out_shape=jax.ShapeDtypeStruct((rows, 4 * width), quarters[0].dtype),
        in_specs=[whole(pltpu.SMEM)] + [whole()] * 4,
        out_specs=whole(),
        compiler_params=pltpu.CompilerParams(vmem_limit_bytes=VMEM_LIMIT),
        cost_estimate=pl.CostEstimate(
            flops=0, bytes_accessed=rows * width * 16, transcendentals=0
        ),
        name="assemble",
    )(place_of, *quarters)


def line_grads_kernel(kinds, place_of, ids, *refs):
    refs = list(refs)
    scratch = [refs.pop() for kind in kinds if kind == "split"]
    grads = refs.pop()
    pairs = []
    for kind in kinds:
        if kind == "split":
            mine, theirs, target = refs.pop(0), refs.pop(0), scratch.pop()
            for x in range(2):
                target[2 * x + place_of[3]] = mine[x]
                target[2 * x + 1 - place_of[3]] = theirs[x]
            pairs.append((target, refs.pop(0)))
        else:
            pairs.append((refs.pop(0), refs.pop(0)))
    start = refs.pop(0) if refs else None
    slots, size = grads.shape[0], grads.shape[1]
    first, cols_n = pairs[0][0], pairs[0][1].shape[1] // size
    total = math.prod(first.shape) // first.shape[-2] // size * cols_n
    group = math.gcd(slots, 8)

    @pl.loop(0, slots // group)
    def some(g):
        for s in [g * group + j for j in range(group)]:
            b = jnp.minimum(ids[s], total - 1)
            row = b // cols_n
            c = pl.ds(pl.multiple_of((b % cols_n) * size, size), size)
            acc = jnp.zeros((size, size), jnp.float32) if start is None else start[s]
            for x, d in pairs:
                per_part = x.shape[-1] // size
                at = pl.ds(pl.multiple_of((row % per_part) * size, size), size)
                acc += lax.dot_general(
                    x[row // per_part, :, at] if len(x.shape) == 3 else x[:, at],
                    d[:, c],
                    (((0,), (0,)), ((), ())),
                    preferred_element_type=jnp.float32,
                )
            grads[s] = jnp.where(ids[s] < total, acc, 0.0).astype(grads.dtype)


def line_grads(place_of, ids, pairs, start, size, out_dtype):
    slots = ids.shape[0]
    kinds = tuple("split" if len(p) == 3 else "plain" for p in pairs)
    flat = [a for p in pairs for a in p] + ([] if start is None else [start])
    split = [
        pltpu.VMEM((4,) + p[0].shape[1:], jnp.bfloat16) for p in pairs if len(p) == 3
    ]
    return pl.pallas_call(
        functools.partial(line_grads_kernel, kinds),
        out_shape=jax.ShapeDtypeStruct((slots, size, size), out_dtype),
        in_specs=[whole(pltpu.SMEM)] * 2 + [whole()] * len(flat),
        out_specs=whole(),
        scratch_shapes=split,
        compiler_params=pltpu.CompilerParams(vmem_limit_bytes=VMEM_LIMIT),
        cost_estimate=pl.CostEstimate(
            flops=512 * len(pairs) * slots * size * size,
            bytes_accessed=sum(2 * a.size for a in flat) + 4 * slots * size * size,
            transcendentals=0,
        ),
        name="line_grads",
    )(place_of, ids, *flat)


INWARD = ((0, 1), (3, 2))
OUTWARD = ((1, 0), (2, 3))
PAIRS = INWARD + OUTWARD
MIDDLE = ((1, 2), (2, 1))
SWAP = ((0, 1), (1, 0))


def ids_block(block_ids, size):
    rows = size * size // block_ids.shape[0]
    return jnp.broadcast_to(block_ids, (rows, block_ids.shape[0])).reshape(1, size, size)


def ids_of(piece, slots):
    return piece[-1, 0, :slots].astype(jnp.int32)


def line_body(tokens, upstream, blocks, block_ids):
    slots, size = blocks.shape[0], blocks.shape[1]
    rows, depth = tokens.shape
    width = upstream.shape[1]
    half_slots = slots // 2
    part_width = depth // 4
    at_z, half = lax.axis_index("dp"), lax.axis_index("groups")
    at_tensor, at_replica = lax.axis_index("tensor"), lax.axis_index("replica")
    middle = (at_z == 1) | (at_z == 2)
    place_of = jnp.stack([middle.astype(jnp.int32), half, at_tensor, at_replica])
    along = functools.partial(lax.ppermute, axis_name="dp")
    across = functools.partial(
        lax.ppermute, axis_name=("groups", "dp"), perm=((1, 5), (5, 1), (2, 6), (6, 2))
    )
    middle_swap = ((2, 3), (3, 2), (4, 5), (5, 4))
    sideways = functools.partial(lax.ppermute, axis_name=("dp", "tensor"), perm=middle_swap)
    cores = functools.partial(lax.ppermute, axis_name=("dp", "replica"), perm=middle_swap)
    everywhere = functools.partial(lax.ppermute, axis_name="tensor", perm=SWAP)
    all_cores = functools.partial(lax.ppermute, axis_name="replica", perm=SWAP)
    stage = lax.optimization_barrier

    mine = lax.dynamic_slice_in_dim(blocks, half * half_slots, half_slots, 0)
    other = lax.dynamic_slice_in_dim(blocks, (1 - half) * half_slots, half_slots, 0)
    mine = jnp.concatenate([mine, ids_block(block_ids, size).astype(jnp.bfloat16)])
    part = lax.dynamic_slice_in_dim(tokens, lax.axis_index(INNER) * part_width, part_width, 1)
    both = jnp.concatenate([part, upstream])
    mine, other, both = stage((mine, other, both))

    near_a = along(mine, perm=INWARD)
    far_a = along(mine, perm=MIDDLE)
    near_a, far_a, both, other = stage((near_a, far_a, both, other))

    end_a = along(near_a, perm=MIDDLE)
    far_b = across(far_a)
    both_1 = along(both, perm=PAIRS)
    both_1, end_a, far_b, both, other = stage((both_1, end_a, far_b, both, other))
    upstream_1 = both_1[rows:]

    near_b = along(other, perm=INWARD)
    end_b = across(end_a)
    both_2m = along(both, perm=MIDDLE)
    tokens_1 = lax.all_gather(both_1[:rows], INNER)
    ids_1, ids_2, ids_3 = (ids_of(piece, slots) for piece in (near_a, far_a, end_a))
    partial, turned = place_first(
        place_of, (block_ids, ids_1, ids_2, ids_3), (blocks, near_a, far_a, far_b, end_a), depth, width
    )
    near_b, end_b, both_2m, both_1, tokens_1, partial, turned = stage(
        (near_b, end_b, both_2m, both_1, tokens_1, partial, turned)
    )

    both_3m = along(both_1, perm=MIDDLE)
    both_2o = along(both_2m, perm=OUTWARD)
    last = (near_b, end_b)
    end_keep, own_keep, own_give, *end_give = project_back(
        place_of, ids_1, ids_3, turned, *last, upstream_1, upstream
    )
    end_keep, end_give = add_split(place_of, end_keep, *[cores(a) for a in end_give])
    end_keep, end_give, own_give, both_3m, both_2o = stage(
        (end_keep, end_give, own_give, both_3m, both_2o)
    )

    end_got = sideways(end_give)
    own_keep, own_give = add_split(place_of, own_keep, cores(own_give))
    both_3o = along(both_3m, perm=OUTWARD)
    end_proj = project_forward(place_of, ids_1, ids_3, partial, *last, tokens_1)
    end_got, own_give, own_keep, end_proj, both_2o = stage(
        (end_got, own_give, own_keep, end_proj, both_2o)
    )

    sum_out = along(end_keep + end_got, perm=OUTWARD)
    own_got = sideways(own_give)
    side_2 = lax.all_gather(both_2m[:rows] + both_2o[:rows], "tensor")
    upstream_2 = both_2m[rows:] + both_2o[rows:]
    proj = project_forward(place_of, ids_1, ids_3, partial, *last, tokens)
    sum_out, own_got, both_3o, proj = stage((sum_out, own_got, both_3o, proj))

    side_3 = lax.all_gather(both_3m[:rows] + both_3o[:rows], "tensor")
    upstream_3 = both_3m[rows:] + both_3o[rows:]
    quarter = jnp.where(middle, own_keep + own_got, sum_out)
    proj_out = along(end_proj, perm=OUTWARD)
    pairs = ((tokens, upstream), (tokens_1, upstream_1))
    grads = line_grads(place_of, block_ids, pairs, None, size, jnp.float32)
    by_tensor, by_core, grads, side_2, side_3 = stage(
        (everywhere(quarter), all_cores(quarter), grads, side_2, side_3)
    )
    by_both = all_cores(by_tensor)
    projected = jnp.where(middle, proj, proj_out)
    token_grad = assemble(place_of, (quarter, by_core, by_tensor, by_both))
    pairs = ((side_2, all_cores(side_2), upstream_2), (side_3, all_cores(side_3), upstream_3))
    grads = line_grads(place_of, block_ids, pairs, grads, size, jnp.bfloat16)
    return projected, token_grad, grads


def solution(mesh):
    line = tuple(mesh.shape[a] for a in ("groups", "dp", "tensor", "replica")) == (2, 4, 2, 2)
    return jax.shard_map(
        line_body if line else general_body,
        mesh=mesh,
        in_specs=(
            P(("groups", "dp"), None),
            P(("groups", "dp"), INNER),
            P(("dp",) + INNER, None, None),
            P(("dp",) + INNER),
        ),
        out_specs=(
            P(("groups", "dp"), INNER),
            P(("groups", "dp"), None),
            P(("groups", "dp") + INNER, None, None),
        ),
        check_vma=False,
    )
```

```python
import functools
import math

import jax
import jax.numpy as jnp
from jax import lax
from jax.experimental import pallas as pl
from jax.experimental.pallas import tpu as pltpu
from jax.sharding import PartitionSpec as P

VMEM_LIMIT = 60 * 1024 * 1024
INNER = ("tensor", "replica")
FREE = pl.CostEstimate(flops=0, bytes_accessed=0, transcendentals=0)


def whole(space=pltpu.VMEM):
    return pl.BlockSpec(memory_space=space)


def project_kernel(ids, blocks, tokens, upstream, proj, back, weight):
    slots, size = blocks.shape[0], blocks.shape[1]
    depth, width = weight.shape
    cols_n = width // size
    total = (depth // size) * cols_n
    weight[...] = jnp.zeros_like(weight)

    @pl.loop(0, slots, unroll=4)
    def place(s):
        b = ids[s]

        @pl.when(b < total)
        def put():
            r = pl.multiple_of((b // cols_n) * size, size)
            c = pl.multiple_of((b % cols_n) * size, size)
            weight[pl.ds(r, size), pl.ds(c, size)] = blocks[s]

    step = 256

    @pl.loop(0, width // step)
    def forward(n):
        c = pl.multiple_of(n * step, step)
        proj[:, pl.ds(c, step)] = jnp.dot(
            tokens[...], weight[:, pl.ds(c, step)], preferred_element_type=jnp.float32
        ).astype(proj.dtype)

    @pl.loop(0, depth // step, unroll=4)
    def backward(n):
        r = pl.multiple_of(n * step, step)
        back[:, pl.ds(r, step)] = lax.dot_general(
            upstream[...],
            weight[pl.ds(r, step), :],
            (((1,), (1,)), ((), ())),
            preferred_element_type=jnp.float32,
        ).astype(back.dtype)


def project(ids, blocks, tokens, upstream):
    rows, depth = tokens.shape
    width = upstream.shape[1]
    return pl.pallas_call(
        project_kernel,
        out_shape=(
            jax.ShapeDtypeStruct((rows, width), jnp.bfloat16),
            jax.ShapeDtypeStruct((rows, depth), jnp.bfloat16),
        ),
        in_specs=[whole(pltpu.SMEM), whole(), whole(), whole()],
        out_specs=(whole(), whole()),
        scratch_shapes=[pltpu.VMEM((depth, width), jnp.bfloat16)],
        compiler_params=pltpu.CompilerParams(vmem_limit_bytes=VMEM_LIMIT),
        cost_estimate=FREE,
        name="project",
    )(ids, blocks, tokens, upstream)


def block_grad_kernel(ids, tokens, upstream, grads):
    slots, size = grads.shape[0], grads.shape[1]
    parts, slabs, _, part_width = tokens.shape
    cols_n = upstream.shape[2] // size
    per_part = part_width // size
    total = parts * per_part * cols_n

    @pl.loop(0, slots)
    def one(s):
        b = ids[s]

        @pl.when(b < total)
        def fill():
            row = b // cols_n
            part = row // per_part
            r = pl.multiple_of((row % per_part) * size, size)
            c = pl.multiple_of((b % cols_n) * size, size)
            acc = jnp.zeros((size, size), jnp.float32)
            for k in range(slabs):
                acc += lax.dot_general(
                    tokens[part, k, :, pl.ds(r, size)],
                    upstream[k, :, pl.ds(c, size)],
                    (((0,), (0,)), ((), ())),
                    preferred_element_type=jnp.float32,
                )
            grads[s] = acc.astype(grads.dtype)

        @pl.when(b >= total)
        def clear():
            grads[s] = jnp.zeros((size, size), grads.dtype)


def block_grads(ids, tokens, upstream, size):
    slots = ids.shape[0]
    parts, slabs, rows, part_width = tokens.shape
    return pl.pallas_call(
        block_grad_kernel,
        out_shape=jax.ShapeDtypeStruct((slots, size, size), jnp.bfloat16),
        in_specs=[whole(pltpu.SMEM), whole(), whole()],
        out_specs=whole(),
        compiler_params=pltpu.CompilerParams(vmem_limit_bytes=VMEM_LIMIT),
        cost_estimate=FREE,
        name="block_grads",
    )(ids, tokens, upstream)


def general_body(tokens, upstream, blocks, block_ids):
    size = blocks.shape[1]
    all_blocks = lax.all_gather(blocks, "dp", axis=0, tiled=True)
    all_ids = lax.all_gather(block_ids, "dp", axis=0, tiled=True)
    proj, back = project(all_ids, all_blocks, tokens, upstream)
    terms = block_grads(all_ids, tokens[None, None], upstream[None], size)
    grads = lax.psum_scatter(terms, "dp", scatter_dimension=0, tiled=True)
    return proj, lax.psum(back, INNER), grads


def place_blocks(ids, first, blocks, weight, turned, slots):
    size = blocks.shape[1]
    depth, width = turned.shape[::-1] if weight is None else weight.shape
    cols_n = width // size
    total = (depth // size) * cols_n

    @pl.loop(0, slots, unroll=4)
    def place(s):
        b = ids[first + s]

        @pl.when(b < total)
        def put():
            r = pl.multiple_of((b // cols_n) * size, size)
            c = pl.multiple_of((b % cols_n) * size, size)
            if weight is not None:
                weight[pl.ds(r, size), pl.ds(c, size)] = blocks[s]
            if turned is not None:
                turned[pl.ds(c, size), pl.ds(r, size)] = blocks[s].T


def place_kernel(place_of, ids_0, ids_1, ids_2, ids_3, own, near_a, far_a, far_b, end_a, turned):
    is_middle, half = place_of[0], place_of[1]
    half_slots = far_b.shape[0] - 1
    mine, other = half * half_slots, (1 - half) * half_slots

    @pl.when(is_middle == 1)
    def work():
        turned[...] = jnp.zeros_like(turned)
        place_blocks(ids_0, 0, own, None, turned, own.shape[0])
        place_blocks(ids_1, mine, near_a, None, turned, half_slots)
        place_blocks(ids_2, mine, far_a, None, turned, half_slots)
        place_blocks(ids_2, other, far_b, None, turned, half_slots)
        place_blocks(ids_3, mine, end_a, None, turned, half_slots)


def place_first(place_of, ids, pieces, depth, width):
    return pl.pallas_call(
        place_kernel,
        out_shape=jax.ShapeDtypeStruct((width, depth), jnp.bfloat16),
        in_specs=[whole(pltpu.SMEM)] * 5 + [whole()] * 5,
        out_specs=whole(),
        compiler_params=pltpu.CompilerParams(vmem_limit_bytes=VMEM_LIMIT),
        cost_estimate=FREE,
        name="place_first",
    )(place_of, *ids, *pieces)


def plain_kernel(place_of, ids_0, ids_1, ids_2, own, near_a, far_a, weight):
    half_slots = near_a.shape[0] - 1
    mine = place_of[1] * half_slots

    @pl.when(place_of[0] == 1)
    def work():
        weight[...] = jnp.zeros_like(weight)
        place_blocks(ids_0, 0, own, weight, None, own.shape[0])
        place_blocks(ids_1, mine, near_a, weight, None, half_slots)
        place_blocks(ids_2, mine, far_a, weight, None, half_slots)


def place_plain(place_of, ids, pieces, depth, width):
    return pl.pallas_call(
        plain_kernel,
        out_shape=jax.ShapeDtypeStruct((depth, width), jnp.bfloat16),
        in_specs=[whole(pltpu.SMEM)] * 4 + [whole()] * 3,
        out_specs=whole(),
        compiler_params=pltpu.CompilerParams(vmem_limit_bytes=VMEM_LIMIT),
        cost_estimate=FREE,
        name="place_plain",
    )(place_of, *ids, *pieces)


def back_kernel(
    place_of, ids_1, ids_3, partial, near_b, end_b, end_upstream, upstream,
    end_keep, own_keep, own_give, end_give_0, end_give_1, held, sources, sem,
):
    half_slots = near_b.shape[0]
    other = (1 - place_of[1]) * half_slots
    rows, width = upstream.shape
    step = 256
    per_part = end_keep.shape[2] // step

    @pl.when(place_of[0] == 1)
    def work():
        load = pltpu.make_async_copy(partial, held, sem)
        load.start()
        sources[:rows] = end_upstream[...]
        sources[rows:] = upstream[...]
        load.wait()
        place_blocks(ids_1, other, near_b, None, held, half_slots)
        place_blocks(ids_3, other, end_b, None, held, half_slots)

        def column(part, end_target, own_target):
            @pl.loop(0, per_part, unroll=2)
            def backward(n):
                at = pl.multiple_of(n * step, step)
                result = jnp.dot(
                    sources[...],
                    held[:, pl.ds(pl.multiple_of(part * per_part * step + at, step), step)],
                    preferred_element_type=jnp.float32,
                ).astype(own_target.dtype)
                end_target[:, pl.ds(at, step)] = result[:rows]
                own_target[:, pl.ds(at, step)] = result[rows:]

        for x, end_give in enumerate((end_give_0, end_give_1)):
            column(2 * x + place_of[3], end_keep.at[x], own_keep.at[x])
            column(2 * x + 1 - place_of[3], end_give, own_give.at[x])


def project_back(place_of, ids_1, ids_3, partial, near_b, end_b, end_upstream, upstream):
    width, depth = partial.shape
    rows = upstream.shape[0]
    quarter = jax.ShapeDtypeStruct((rows, depth // 4), jnp.bfloat16)
    half = jax.ShapeDtypeStruct((2, rows, depth // 4), jnp.bfloat16)
    return pl.pallas_call(
        back_kernel,
        out_shape=(half, half, half, quarter, quarter),
        in_specs=[whole(pltpu.SMEM)] * 3 + [whole(pl.ANY)] + [whole()] * 4,
        out_specs=(whole(),) * 5,
        scratch_shapes=[
            pltpu.VMEM((width, depth), jnp.bfloat16),
            pltpu.VMEM((2 * rows, width), jnp.bfloat16),
            pltpu.SemaphoreType.DMA,
        ],
        compiler_params=pltpu.CompilerParams(vmem_limit_bytes=VMEM_LIMIT),
        cost_estimate=FREE,
        name="project_back",
    )(place_of, ids_1, ids_3, partial, near_b, end_b, end_upstream, upstream)


def forward_kernel(
    place_of, ids_1, ids_2, ids_3, partial, near_b, far_b, end_a, end_b,
    tokens, end_tokens, proj, end_proj, weight, sem,
):
    half_slots = near_b.shape[0]
    mine, other = place_of[1] * half_slots, (1 - place_of[1]) * half_slots
    width = weight.shape[1]
    parts, rows, part_width = end_tokens.shape
    step = 256

    @pl.when(place_of[0] == 1)
    def work():
        load = pltpu.make_async_copy(partial, weight, sem)
        load.start()
        load.wait()
        place_blocks(ids_1, other, near_b, weight, None, half_slots)
        place_blocks(ids_2, other, far_b, weight, None, half_slots)
        place_blocks(ids_3, mine, end_a, weight, None, half_slots)
        place_blocks(ids_3, other, end_b, weight, None, half_slots)

        @pl.loop(0, width // step, unroll=2)
        def forward(n):
            c = pl.multiple_of(n * step, step)
            acc = jnp.zeros((rows, step), jnp.float32)
            for q in range(parts):
                acc += jnp.dot(
                    end_tokens[q],
                    weight[q * part_width : (q + 1) * part_width, pl.ds(c, step)],
                    preferred_element_type=jnp.float32,
                )
            end_proj[:, pl.ds(c, step)] = acc.astype(end_proj.dtype)
            proj[:, pl.ds(c, step)] = jnp.dot(
                tokens[...], weight[:, pl.ds(c, step)], preferred_element_type=jnp.float32
            ).astype(proj.dtype)


def project_forward(place_of, ids, partial, pieces, tokens, end_tokens):
    rows, depth = tokens.shape
    width = partial.shape[1]
    out = jax.ShapeDtypeStruct((rows, width), jnp.bfloat16)
    return pl.pallas_call(
        forward_kernel,
        out_shape=(out, out),
        in_specs=[whole(pltpu.SMEM)] * 4 + [whole(pl.ANY)] + [whole()] * 6,
        out_specs=(whole(),) * 2,
        scratch_shapes=[pltpu.VMEM((depth, width), jnp.bfloat16), pltpu.SemaphoreType.DMA],
        compiler_params=pltpu.CompilerParams(vmem_limit_bytes=VMEM_LIMIT),
        cost_estimate=FREE,
        name="project_forward",
    )(place_of, *ids, partial, *pieces, tokens, end_tokens)


def split_kernel(place_of, keep, *refs):
    x = place_of[2]
    own, give = refs[-2:]
    got = refs[:-2] if len(refs) > 3 else (refs[0].at[0], refs[0].at[1])
    for at in range(2):
        total = (keep[at].astype(jnp.float32) + got[at][...].astype(jnp.float32)).astype(own.dtype)

        @pl.when(x == at)
        def mine():
            own[...] = total

        @pl.when(x != at)
        def theirs():
            give[...] = total


def add_split(place_of, keep, *got):
    out = jax.ShapeDtypeStruct(keep.shape[1:], keep.dtype)
    return pl.pallas_call(
        split_kernel,
        out_shape=(out, out),
        in_specs=[whole(pltpu.SMEM), whole()] + [whole()] * len(got),
        out_specs=(whole(), whole()),
        compiler_params=pltpu.CompilerParams(vmem_limit_bytes=VMEM_LIMIT),
        cost_estimate=FREE,
        name="add_split",
    )(place_of, keep, *got)


def assemble_kernel(place_of, own, by_core, by_tensor, by_both, full):
    x, c = place_of[2], place_of[3]
    width = own.shape[1]
    for ref, xx, cc in (
        (own, x, c), (by_core, x, 1 - c), (by_tensor, 1 - x, c), (by_both, 1 - x, 1 - c)
    ):
        at = pl.multiple_of((xx * 2 + cc) * width, width)
        full[:, pl.ds(at, width)] = ref[...]


def assemble(place_of, quarters):
    rows, width = quarters[0].shape
    return pl.pallas_call(
        assemble_kernel,
        out_shape=jax.ShapeDtypeStruct((rows, 4 * width), quarters[0].dtype),
        in_specs=[whole(pltpu.SMEM)] + [whole()] * 4,
        out_specs=whole(),
        compiler_params=pltpu.CompilerParams(vmem_limit_bytes=VMEM_LIMIT),
        cost_estimate=FREE,
        name="assemble",
    )(place_of, *quarters)


def line_grads_kernel(pairs_n, ids, *refs):
    pairs = [(refs[2 * k], refs[2 * k + 1]) for k in range(pairs_n)]
    grads = refs[-1]
    start = refs[2 * pairs_n] if len(refs) > 2 * pairs_n + 1 else None
    slots, size = grads.shape[0], grads.shape[1]
    first = pairs[0][0]
    cols_n = pairs[0][1].shape[1] // size
    rows_n = first.shape[-1] // size * (first.shape[0] if len(first.shape) == 3 else 1)
    total = rows_n * cols_n
    group = math.gcd(slots, 8)

    @pl.loop(0, slots // group)
    def some(g):
        for s in [g * group + j for j in range(group)]:
            b = jnp.minimum(ids[s], total - 1)
            row = b // cols_n
            c = pl.ds(pl.multiple_of((b % cols_n) * size, size), size)
            acc = jnp.zeros((size, size), jnp.float32) if start is None else start[s]
            for x, d in pairs:
                per_part = x.shape[-1] // size
                at = pl.ds(pl.multiple_of((row % per_part) * size, size), size)
                acc += lax.dot_general(
                    x[row // per_part, :, at] if len(x.shape) == 3 else x[:, at],
                    d[:, c],
                    (((0,), (0,)), ((), ())),
                    preferred_element_type=jnp.float32,
                )
            grads[s] = jnp.where(ids[s] < total, acc, 0.0).astype(grads.dtype)


def line_grads(ids, pairs, start, size, out_dtype):
    slots = ids.shape[0]
    rows = pairs[0][1].shape[0]
    flat = [a for pair in pairs for a in pair] + ([] if start is None else [start])
    return pl.pallas_call(
        functools.partial(line_grads_kernel, len(pairs)),
        out_shape=jax.ShapeDtypeStruct((slots, size, size), out_dtype),
        in_specs=[whole(pltpu.SMEM)] + [whole()] * len(flat),
        out_specs=whole(),
        compiler_params=pltpu.CompilerParams(vmem_limit_bytes=VMEM_LIMIT),
        cost_estimate=FREE,
        name="line_grads",
    )(ids, *flat)


INWARD = ((0, 1), (3, 2))
OUTWARD = ((1, 0), (2, 3))
PAIRS = INWARD + OUTWARD
MIDDLE = ((1, 2), (2, 1))
SWAP = ((0, 1), (1, 0))


def ids_block(block_ids, size):
    rows = size * size // block_ids.shape[0]
    return jnp.broadcast_to(block_ids, (rows, block_ids.shape[0])).reshape(1, size, size)


def ids_of(piece, slots):
    return piece[-1, 0, :slots].astype(jnp.int32)


def line_body(tokens, upstream, blocks, block_ids):
    slots, size = blocks.shape[0], blocks.shape[1]
    rows, depth = tokens.shape
    width = upstream.shape[1]
    half_slots = slots // 2
    part_width = depth // 4
    at_z, half = lax.axis_index("dp"), lax.axis_index("groups")
    at_tensor, at_replica = lax.axis_index("tensor"), lax.axis_index("replica")
    middle = (at_z == 1) | (at_z == 2)
    place_of = jnp.stack([middle.astype(jnp.int32), half, at_tensor, at_replica])
    along = functools.partial(lax.ppermute, axis_name="dp")
    across = functools.partial(
        lax.ppermute, axis_name=("groups", "dp"), perm=((1, 5), (5, 1), (2, 6), (6, 2))
    )
    middle_swap = ((2, 3), (3, 2), (4, 5), (5, 4))
    sideways = functools.partial(lax.ppermute, axis_name=("dp", "tensor"), perm=middle_swap)
    cores = functools.partial(lax.ppermute, axis_name=("dp", "replica"), perm=middle_swap)
    end_sideways = functools.partial(
        lax.ppermute, axis_name=("dp", "tensor"), perm=((0, 1), (1, 0), (6, 7), (7, 6))
    )
    everywhere = functools.partial(lax.ppermute, axis_name="tensor", perm=SWAP)
    all_cores = functools.partial(lax.ppermute, axis_name="replica", perm=SWAP)
    stage = lax.optimization_barrier

    mine = lax.dynamic_slice_in_dim(blocks, half * half_slots, half_slots, 0)
    mine = jnp.concatenate([mine, ids_block(block_ids, size).astype(jnp.bfloat16)])
    (mine,) = stage((mine,))

    near_a = along(mine, perm=INWARD)
    far_a = along(mine, perm=MIDDLE)
    other = lax.dynamic_slice_in_dim(blocks, (1 - half) * half_slots, half_slots, 0)
    part = lax.dynamic_slice_in_dim(tokens, lax.axis_index(INNER) * part_width, part_width, 1)
    both = jnp.concatenate([part, upstream])
    near_a, far_a, both, other = stage((near_a, far_a, both, other))

    end_a = along(near_a, perm=MIDDLE)
    far_b = across(far_a)
    both_1 = along(both, perm=PAIRS)
    ids_1, ids_2 = ids_of(near_a, slots), ids_of(far_a, slots)
    plain = place_plain(place_of, (block_ids, ids_1, ids_2), (blocks, near_a, far_a), depth, width)
    both_1, end_a, far_b, both, other, plain = stage((both_1, end_a, far_b, both, other, plain))

    near_b = along(other, perm=INWARD)
    end_b = across(end_a)
    both_2m = along(both, perm=MIDDLE)
    upstream_1 = both_1[rows:]
    tokens_1 = lax.all_gather(both_1[:rows], INNER)
    ids_3 = ids_of(end_a, slots)
    turned = place_first(
        place_of, (block_ids, ids_1, ids_2, ids_3), (blocks, near_a, far_a, far_b, end_a), depth, width
    )
    near_b, end_b, both_2m, both_1, upstream_1, tokens_1, turned = stage(
        (near_b, end_b, both_2m, both_1, upstream_1, tokens_1, turned)
    )

    both_3m = along(both_1, perm=MIDDLE)
    both_2o = along(both_2m, perm=OUTWARD)
    end_keep, own_keep, own_give, *end_give = project_back(
        place_of, ids_1, ids_3, turned, near_b, end_b, upstream_1, upstream
    )
    end_keep, end_give = add_split(place_of, end_keep, *[cores(a) for a in end_give])
    end_keep, end_give, own_give, both_3m, both_2o = stage(
        (end_keep, end_give, own_give, both_3m, both_2o)
    )

    end_got = sideways(end_give)
    both_3o = along(both_3m, perm=OUTWARD)
    own_keep, own_give = add_split(place_of, own_keep, cores(own_give))
    tokens_2 = lax.all_gather(both_2m[:rows] + both_2o[:rows], INNER)
    upstream_2 = both_2m[rows:] + both_2o[rows:]
    proj, end_proj = project_forward(
        place_of, (ids_1, ids_2, ids_3), plain, (near_b, far_b, end_a, end_b), tokens, tokens_1
    )
    end_got, own_give, own_keep, proj, end_proj = stage(
        (end_got, own_give, own_keep, proj, end_proj)
    )

    sum_out = along(end_keep + end_got, perm=OUTWARD)
    own_got = sideways(own_give)
    part_3, upstream_1 = stage((both_3m[:rows] + both_3o[:rows], upstream_1))
    tokens_3 = lax.all_gather(part_3, INNER)
    upstream_3 = both_3m[rows:] + both_3o[rows:]
    pairs = ((tokens, upstream), (tokens_1, upstream_1))
    grads = line_grads(block_ids, pairs, None, size, jnp.float32)
    sum_out, own_got, grads = stage((sum_out, own_got, grads))

    quarter = jnp.where(middle, own_keep + own_got, sum_out)
    proj_out = along(end_proj, perm=OUTWARD)
    grads = line_grads(block_ids, ((tokens_2, upstream_2),), grads, size, jnp.float32)
    by_tensor, by_core, grads = stage((everywhere(quarter), all_cores(quarter), grads))
    by_both = all_cores(by_tensor)
    projected = jnp.where(middle, proj, proj_out)
    token_grad = assemble(place_of, (quarter, by_core, by_tensor, by_both))
    grads = line_grads(block_ids, ((tokens_3, upstream_3),), grads, size, jnp.bfloat16)
    return projected, token_grad, grads


def solution(mesh):
    line = tuple(mesh.shape[a] for a in ("groups", "dp", "tensor", "replica")) == (2, 4, 2, 2)
    return jax.shard_map(
        line_body if line else general_body,
        mesh=mesh,
        in_specs=(
            P(("groups", "dp"), None),
            P(("groups", "dp"), INNER),
            P(("dp",) + INNER, None, None),
            P(("dp",) + INNER),
        ),
        out_specs=(
            P(("groups", "dp"), INNER),
            P(("groups", "dp"), None),
            P(("groups", "dp") + INNER, None, None),
        ),
        check_vma=False,
    )
```

```python
import functools
import math

import jax
import jax.numpy as jnp
from jax import lax
from jax.experimental import pallas as pl
from jax.experimental.pallas import tpu as pltpu
from jax.sharding import PartitionSpec as P

VMEM_LIMIT = 60 * 1024 * 1024
INNER = ("tensor", "replica")
FREE = pl.CostEstimate(flops=0, bytes_accessed=0, transcendentals=0)


def whole(space=pltpu.VMEM):
    return pl.BlockSpec(memory_space=space)


def project_kernel(ids, blocks, tokens, upstream, proj, back, weight):
    slots, size = blocks.shape[0], blocks.shape[1]
    depth, width = weight.shape
    cols_n = width // size
    total = (depth // size) * cols_n
    weight[...] = jnp.zeros_like(weight)

    @pl.loop(0, slots, unroll=4)
    def place(s):
        b = ids[s]

        @pl.when(b < total)
        def put():
            r = pl.multiple_of((b // cols_n) * size, size)
            c = pl.multiple_of((b % cols_n) * size, size)
            weight[pl.ds(r, size), pl.ds(c, size)] = blocks[s]

    step = 256

    @pl.loop(0, width // step)
    def forward(n):
        c = pl.multiple_of(n * step, step)
        proj[:, pl.ds(c, step)] = jnp.dot(
            tokens[...], weight[:, pl.ds(c, step)], preferred_element_type=jnp.float32
        ).astype(proj.dtype)

    @pl.loop(0, depth // step, unroll=4)
    def backward(n):
        r = pl.multiple_of(n * step, step)
        back[:, pl.ds(r, step)] = lax.dot_general(
            upstream[...],
            weight[pl.ds(r, step), :],
            (((1,), (1,)), ((), ())),
            preferred_element_type=jnp.float32,
        ).astype(back.dtype)


def project(ids, blocks, tokens, upstream):
    rows, depth = tokens.shape
    width = upstream.shape[1]
    return pl.pallas_call(
        project_kernel,
        out_shape=(
            jax.ShapeDtypeStruct((rows, width), jnp.bfloat16),
            jax.ShapeDtypeStruct((rows, depth), jnp.bfloat16),
        ),
        in_specs=[whole(pltpu.SMEM), whole(), whole(), whole()],
        out_specs=(whole(), whole()),
        scratch_shapes=[pltpu.VMEM((depth, width), jnp.bfloat16)],
        compiler_params=pltpu.CompilerParams(vmem_limit_bytes=VMEM_LIMIT),
        cost_estimate=FREE,
        name="project",
    )(ids, blocks, tokens, upstream)


def block_grad_kernel(ids, tokens, upstream, grads):
    slots, size = grads.shape[0], grads.shape[1]
    parts, slabs, _, part_width = tokens.shape
    cols_n = upstream.shape[2] // size
    per_part = part_width // size
    total = parts * per_part * cols_n

    @pl.loop(0, slots)
    def one(s):
        b = ids[s]

        @pl.when(b < total)
        def fill():
            row = b // cols_n
            part = row // per_part
            r = pl.multiple_of((row % per_part) * size, size)
            c = pl.multiple_of((b % cols_n) * size, size)
            acc = jnp.zeros((size, size), jnp.float32)
            for k in range(slabs):
                acc += lax.dot_general(
                    tokens[part, k, :, pl.ds(r, size)],
                    upstream[k, :, pl.ds(c, size)],
                    (((0,), (0,)), ((), ())),
                    preferred_element_type=jnp.float32,
                )
            grads[s] = acc.astype(grads.dtype)

        @pl.when(b >= total)
        def clear():
            grads[s] = jnp.zeros((size, size), grads.dtype)


def block_grads(ids, tokens, upstream, size):
    slots = ids.shape[0]
    parts, slabs, rows, part_width = tokens.shape
    return pl.pallas_call(
        block_grad_kernel,
        out_shape=jax.ShapeDtypeStruct((slots, size, size), jnp.bfloat16),
        in_specs=[whole(pltpu.SMEM), whole(), whole()],
        out_specs=whole(),
        compiler_params=pltpu.CompilerParams(vmem_limit_bytes=VMEM_LIMIT),
        cost_estimate=FREE,
        name="block_grads",
    )(ids, tokens, upstream)


def general_body(tokens, upstream, blocks, block_ids):
    size = blocks.shape[1]
    all_blocks = lax.all_gather(blocks, "dp", axis=0, tiled=True)
    all_ids = lax.all_gather(block_ids, "dp", axis=0, tiled=True)
    proj, back = project(all_ids, all_blocks, tokens, upstream)
    terms = block_grads(all_ids, tokens[None, None], upstream[None], size)
    grads = lax.psum_scatter(terms, "dp", scatter_dimension=0, tiled=True)
    return proj, lax.psum(back, INNER), grads


def place_blocks(ids, first, blocks, weight, turned, slots):
    size = blocks.shape[1]
    depth, width = turned.shape[::-1] if weight is None else weight.shape
    cols_n = width // size
    total = (depth // size) * cols_n

    @pl.loop(0, slots, unroll=4)
    def place(s):
        b = ids[first + s]

        @pl.when(b < total)
        def put():
            r = pl.multiple_of((b // cols_n) * size, size)
            c = pl.multiple_of((b % cols_n) * size, size)
            if weight is not None:
                weight[pl.ds(r, size), pl.ds(c, size)] = blocks[s]
            if turned is not None:
                turned[pl.ds(c, size), pl.ds(r, size)] = blocks[s].T


def place_kernel(place_of, ids_0, ids_1, ids_2, ids_3, own, near_a, far_a, far_b, end_a, turned):
    is_middle, half = place_of[0], place_of[1]
    half_slots = far_b.shape[0] - 1
    mine, other = half * half_slots, (1 - half) * half_slots

    @pl.when(is_middle == 1)
    def work():
        turned[...] = jnp.zeros_like(turned)
        place_blocks(ids_0, 0, own, None, turned, own.shape[0])
        place_blocks(ids_1, mine, near_a, None, turned, half_slots)
        place_blocks(ids_2, mine, far_a, None, turned, half_slots)
        place_blocks(ids_2, other, far_b, None, turned, half_slots)
        place_blocks(ids_3, mine, end_a, None, turned, half_slots)


def place_first(place_of, ids, pieces, depth, width):
    return pl.pallas_call(
        place_kernel,
        out_shape=jax.ShapeDtypeStruct((width, depth), jnp.bfloat16),
        in_specs=[whole(pltpu.SMEM)] * 5 + [whole()] * 5,
        out_specs=whole(),
        compiler_params=pltpu.CompilerParams(vmem_limit_bytes=VMEM_LIMIT),
        cost_estimate=FREE,
        name="place_first",
    )(place_of, *ids, *pieces)


def plain_kernel(place_of, ids_0, ids_1, ids_2, own, near_a, far_a, weight):
    half_slots = near_a.shape[0] - 1
    mine = place_of[1] * half_slots

    @pl.when(place_of[0] == 1)
    def work():
        weight[...] = jnp.zeros_like(weight)
        place_blocks(ids_0, 0, own, weight, None, own.shape[0])
        place_blocks(ids_1, mine, near_a, weight, None, half_slots)
        place_blocks(ids_2, mine, far_a, weight, None, half_slots)


def place_plain(place_of, ids, pieces, depth, width):
    return pl.pallas_call(
        plain_kernel,
        out_shape=jax.ShapeDtypeStruct((depth, width), jnp.bfloat16),
        in_specs=[whole(pltpu.SMEM)] * 4 + [whole()] * 3,
        out_specs=whole(),
        compiler_params=pltpu.CompilerParams(vmem_limit_bytes=VMEM_LIMIT),
        cost_estimate=FREE,
        name="place_plain",
    )(place_of, *ids, *pieces)


def back_kernel(
    place_of, ids_1, ids_3, partial, near_b, end_b, end_upstream, upstream,
    end_keep, own_keep, own_give, end_give_0, end_give_1, held, sources, sem,
):
    half_slots = near_b.shape[0]
    other = (1 - place_of[1]) * half_slots
    rows, width = upstream.shape
    step = 256
    per_part = end_keep.shape[2] // step

    @pl.when(place_of[0] == 1)
    def work():
        load = pltpu.make_async_copy(partial, held, sem)
        load.start()
        sources[:rows] = end_upstream[...]
        sources[rows:] = upstream[...]
        load.wait()
        place_blocks(ids_1, other, near_b, None, held, half_slots)
        place_blocks(ids_3, other, end_b, None, held, half_slots)

        def column(part, end_target, own_target):
            @pl.loop(0, per_part, unroll=2)
            def backward(n):
                at = pl.multiple_of(n * step, step)
                result = jnp.dot(
                    sources[...],
                    held[:, pl.ds(pl.multiple_of(part * per_part * step + at, step), step)],
                    preferred_element_type=jnp.float32,
                ).astype(own_target.dtype)
                end_target[:, pl.ds(at, step)] = result[:rows]
                own_target[:, pl.ds(at, step)] = result[rows:]

        for x, end_give in enumerate((end_give_0, end_give_1)):
            column(2 * x + place_of[3], end_keep.at[x], own_keep.at[x])
            column(2 * x + 1 - place_of[3], end_give, own_give.at[x])


def project_back(place_of, ids_1, ids_3, partial, near_b, end_b, end_upstream, upstream):
    width, depth = partial.shape
    rows = upstream.shape[0]
    quarter = jax.ShapeDtypeStruct((rows, depth // 4), jnp.bfloat16)
    half = jax.ShapeDtypeStruct((2, rows, depth // 4), jnp.bfloat16)
    return pl.pallas_call(
        back_kernel,
        out_shape=(half, half, half, quarter, quarter),
        in_specs=[whole(pltpu.SMEM)] * 3 + [whole(pl.ANY)] + [whole()] * 4,
        out_specs=(whole(),) * 5,
        scratch_shapes=[
            pltpu.VMEM((width, depth), jnp.bfloat16),
            pltpu.VMEM((2 * rows, width), jnp.bfloat16),
            pltpu.SemaphoreType.DMA,
        ],
        compiler_params=pltpu.CompilerParams(vmem_limit_bytes=VMEM_LIMIT),
        cost_estimate=FREE,
        name="project_back",
    )(place_of, ids_1, ids_3, partial, near_b, end_b, end_upstream, upstream)


def forward_kernel(
    place_of, ids_1, ids_2, ids_3, partial, near_b, far_b, end_a, end_b,
    tokens, end_tokens, proj, end_proj, weight, sem,
):
    half_slots = near_b.shape[0]
    mine, other = place_of[1] * half_slots, (1 - place_of[1]) * half_slots
    width = weight.shape[1]
    parts, rows, part_width = end_tokens.shape
    step = 256

    @pl.when(place_of[0] == 1)
    def work():
        load = pltpu.make_async_copy(partial, weight, sem)
        load.start()
        load.wait()
        place_blocks(ids_1, other, near_b, weight, None, half_slots)
        place_blocks(ids_2, other, far_b, weight, None, half_slots)
        place_blocks(ids_3, mine, end_a, weight, None, half_slots)
        place_blocks(ids_3, other, end_b, weight, None, half_slots)

        @pl.loop(0, width // step, unroll=2)
        def forward(n):
            c = pl.multiple_of(n * step, step)
            acc = jnp.zeros((rows, step), jnp.float32)
            for q in range(parts):
                acc += jnp.dot(
                    end_tokens[q],
                    weight[q * part_width : (q + 1) * part_width, pl.ds(c, step)],
                    preferred_element_type=jnp.float32,
                )
            end_proj[:, pl.ds(c, step)] = acc.astype(end_proj.dtype)
            proj[:, pl.ds(c, step)] = jnp.dot(
                tokens[...], weight[:, pl.ds(c, step)], preferred_element_type=jnp.float32
            ).astype(proj.dtype)


def project_forward(place_of, ids, partial, pieces, tokens, end_tokens):
    rows, depth = tokens.shape
    width = partial.shape[1]
    out = jax.ShapeDtypeStruct((rows, width), jnp.bfloat16)
    return pl.pallas_call(
        forward_kernel,
        out_shape=(out, out),
        in_specs=[whole(pltpu.SMEM)] * 4 + [whole(pl.ANY)] + [whole()] * 6,
        out_specs=(whole(),) * 2,
        scratch_shapes=[pltpu.VMEM((depth, width), jnp.bfloat16), pltpu.SemaphoreType.DMA],
        compiler_params=pltpu.CompilerParams(vmem_limit_bytes=VMEM_LIMIT),
        cost_estimate=FREE,
        name="project_forward",
    )(place_of, *ids, partial, *pieces, tokens, end_tokens)


def split_kernel(place_of, keep, *refs):
    x = place_of[2]
    own, give = refs[-2:]
    got = refs[:-2] if len(refs) > 3 else (refs[0].at[0], refs[0].at[1])
    for at in range(2):
        total = (keep[at].astype(jnp.float32) + got[at][...].astype(jnp.float32)).astype(own.dtype)

        @pl.when(x == at)
        def mine():
            own[...] = total

        @pl.when(x != at)
        def theirs():
            give[...] = total


def add_split(place_of, keep, *got):
    out = jax.ShapeDtypeStruct(keep.shape[1:], keep.dtype)
    return pl.pallas_call(
        split_kernel,
        out_shape=(out, out),
        in_specs=[whole(pltpu.SMEM), whole()] + [whole()] * len(got),
        out_specs=(whole(), whole()),
        compiler_params=pltpu.CompilerParams(vmem_limit_bytes=VMEM_LIMIT),
        cost_estimate=FREE,
        name="add_split",
    )(place_of, keep, *got)


def assemble_kernel(place_of, own, by_core, by_tensor, by_both, full):
    x, c = place_of[2], place_of[3]
    width = own.shape[1]
    for ref, xx, cc in (
        (own, x, c), (by_core, x, 1 - c), (by_tensor, 1 - x, c), (by_both, 1 - x, 1 - c)
    ):
        at = pl.multiple_of((xx * 2 + cc) * width, width)
        full[:, pl.ds(at, width)] = ref[...]


def assemble(place_of, quarters):
    rows, width = quarters[0].shape
    return pl.pallas_call(
        assemble_kernel,
        out_shape=jax.ShapeDtypeStruct((rows, 4 * width), quarters[0].dtype),
        in_specs=[whole(pltpu.SMEM)] + [whole()] * 4,
        out_specs=whole(),
        compiler_params=pltpu.CompilerParams(vmem_limit_bytes=VMEM_LIMIT),
        cost_estimate=FREE,
        name="assemble",
    )(place_of, *quarters)


def line_grads_kernel(pairs_n, ids, *refs):
    pairs = [(refs[2 * k], refs[2 * k + 1]) for k in range(pairs_n)]
    grads = refs[-1]
    start = refs[2 * pairs_n] if len(refs) > 2 * pairs_n + 1 else None
    slots, size = grads.shape[0], grads.shape[1]
    first = pairs[0][0]
    cols_n = pairs[0][1].shape[1] // size
    rows_n = first.shape[-1] // size * (first.shape[0] if len(first.shape) == 3 else 1)
    total = rows_n * cols_n
    group = math.gcd(slots, 8)

    @pl.loop(0, slots // group)
    def some(g):
        for s in [g * group + j for j in range(group)]:
            b = jnp.minimum(ids[s], total - 1)
            row = b // cols_n
            c = pl.ds(pl.multiple_of((b % cols_n) * size, size), size)
            acc = jnp.zeros((size, size), jnp.float32) if start is None else start[s]
            for x, d in pairs:
                per_part = x.shape[-1] // size
                at = pl.ds(pl.multiple_of((row % per_part) * size, size), size)
                acc += lax.dot_general(
                    x[row // per_part, :, at] if len(x.shape) == 3 else x[:, at],
                    d[:, c],
                    (((0,), (0,)), ((), ())),
                    preferred_element_type=jnp.float32,
                )
            grads[s] = jnp.where(ids[s] < total, acc, 0.0).astype(grads.dtype)


def line_grads(ids, pairs, start, size, out_dtype):
    slots = ids.shape[0]
    rows = pairs[0][1].shape[0]
    flat = [a for pair in pairs for a in pair] + ([] if start is None else [start])
    return pl.pallas_call(
        functools.partial(line_grads_kernel, len(pairs)),
        out_shape=jax.ShapeDtypeStruct((slots, size, size), out_dtype),
        in_specs=[whole(pltpu.SMEM)] + [whole()] * len(flat),
        out_specs=whole(),
        compiler_params=pltpu.CompilerParams(vmem_limit_bytes=VMEM_LIMIT),
        cost_estimate=FREE,
        name="line_grads",
    )(ids, *flat)


INWARD = ((0, 1), (3, 2))
OUTWARD = ((1, 0), (2, 3))
PAIRS = INWARD + OUTWARD
MIDDLE = ((1, 2), (2, 1))
SWAP = ((0, 1), (1, 0))


def ids_block(block_ids, size):
    rows = size * size // block_ids.shape[0]
    return jnp.broadcast_to(block_ids, (rows, block_ids.shape[0])).reshape(1, size, size)


def ids_of(piece, slots):
    return piece[-1, 0, :slots].astype(jnp.int32)


def line_body(tokens, upstream, blocks, block_ids):
    slots, size = blocks.shape[0], blocks.shape[1]
    rows, depth = tokens.shape
    width = upstream.shape[1]
    half_slots = slots // 2
    part_width = depth // 4
    at_z, half = lax.axis_index("dp"), lax.axis_index("groups")
    at_tensor, at_replica = lax.axis_index("tensor"), lax.axis_index("replica")
    middle = (at_z == 1) | (at_z == 2)
    place_of = jnp.stack([middle.astype(jnp.int32), half, at_tensor, at_replica])
    along = functools.partial(lax.ppermute, axis_name="dp")
    across = functools.partial(
        lax.ppermute, axis_name=("groups", "dp"), perm=((1, 5), (5, 1), (2, 6), (6, 2))
    )
    middle_swap = ((2, 3), (3, 2), (4, 5), (5, 4))
    sideways = functools.partial(lax.ppermute, axis_name=("dp", "tensor"), perm=middle_swap)
    cores = functools.partial(lax.ppermute, axis_name=("dp", "replica"), perm=middle_swap)
    end_sideways = functools.partial(
        lax.ppermute, axis_name=("dp", "tensor"), perm=((0, 1), (1, 0), (6, 7), (7, 6))
    )
    everywhere = functools.partial(lax.ppermute, axis_name="tensor", perm=SWAP)
    all_cores = functools.partial(lax.ppermute, axis_name="replica", perm=SWAP)
    stage = lax.optimization_barrier

    mine = lax.dynamic_slice_in_dim(blocks, half * half_slots, half_slots, 0)
    mine = jnp.concatenate([mine, ids_block(block_ids, size).astype(jnp.bfloat16)])
    (mine,) = stage((mine,))

    near_a = along(mine, perm=INWARD)
    far_a = along(mine, perm=MIDDLE)
    other = lax.dynamic_slice_in_dim(blocks, (1 - half) * half_slots, half_slots, 0)
    part = lax.dynamic_slice_in_dim(tokens, lax.axis_index(INNER) * part_width, part_width, 1)
    both = jnp.concatenate([part, upstream])
    near_a, far_a, both, other = stage((near_a, far_a, both, other))

    end_a = along(near_a, perm=MIDDLE)
    far_b = across(far_a)
    both_1 = along(both, perm=PAIRS)
    ids_1, ids_2 = ids_of(near_a, slots), ids_of(far_a, slots)
    plain = place_plain(place_of, (block_ids, ids_1, ids_2), (blocks, near_a, far_a), depth, width)
    both_1, end_a, far_b, both, other, plain = stage((both_1, end_a, far_b, both, other, plain))

    near_b = along(other, perm=INWARD)
    end_b = across(end_a)
    both_2m = along(both, perm=MIDDLE)
    upstream_1 = both_1[rows:]
    tokens_1 = lax.all_gather(both_1[:rows], INNER)
    ids_3 = ids_of(end_a, slots)
    turned = place_first(
        place_of, (block_ids, ids_1, ids_2, ids_3), (blocks, near_a, far_a, far_b, end_a), depth, width
    )
    near_b, end_b, both_2m, both_1, upstream_1, tokens_1, turned = stage(
        (near_b, end_b, both_2m, both_1, upstream_1, tokens_1, turned)
    )

    both_3m = along(both_1, perm=MIDDLE)
    both_2o = along(both_2m, perm=OUTWARD)
    end_keep, own_keep, own_give, *end_give = project_back(
        place_of, ids_1, ids_3, turned, near_b, end_b, upstream_1, upstream
    )
    end_keep, end_give = add_split(place_of, end_keep, *[cores(a) for a in end_give])
    end_keep, end_give, own_give, both_3m, both_2o = stage(
        (end_keep, end_give, own_give, both_3m, both_2o)
    )

    end_got = sideways(end_give)
    both_3o = along(both_3m, perm=OUTWARD)
    own_keep, own_give = add_split(place_of, own_keep, cores(own_give))
    tokens_2 = lax.all_gather(both_2m[:rows] + both_2o[:rows], INNER)
    upstream_2 = both_2m[rows:] + both_2o[rows:]
    proj, end_proj = project_forward(
        place_of, (ids_1, ids_2, ids_3), plain, (near_b, far_b, end_a, end_b), tokens, tokens_1
    )
    end_got, own_give, own_keep, both_3o, proj, end_proj = stage(
        (end_got, own_give, own_keep, both_3o, proj, end_proj)
    )

    sum_out = along(end_keep + end_got, perm=OUTWARD)
    own_got = sideways(own_give)
    tokens_3 = lax.all_gather(both_3m[:rows] + both_3o[:rows], INNER)
    upstream_3 = both_3m[rows:] + both_3o[rows:]
    pairs = ((tokens, upstream), (tokens_1, upstream_1))
    grads = line_grads(block_ids, pairs, None, size, jnp.float32)
    sum_out, own_got, grads = stage((sum_out, own_got, grads))

    quarter = jnp.where(middle, own_keep + own_got, sum_out)
    proj_out = along(end_proj, perm=OUTWARD)
    grads = line_grads(block_ids, ((tokens_2, upstream_2),), grads, size, jnp.float32)
    by_tensor, by_core, grads = stage((everywhere(quarter), all_cores(quarter), grads))
    by_both = all_cores(by_tensor)
    projected = jnp.where(middle, proj, proj_out)
    token_grad = assemble(place_of, (quarter, by_core, by_tensor, by_both))
    grads = line_grads(block_ids, ((tokens_3, upstream_3),), grads, size, jnp.bfloat16)
    return projected, token_grad, grads


def solution(mesh):
    line = tuple(mesh.shape[a] for a in ("groups", "dp", "tensor", "replica")) == (2, 4, 2, 2)
    return jax.shard_map(
        line_body if line else general_body,
        mesh=mesh,
        in_specs=(
            P(("groups", "dp"), None),
            P(("groups", "dp"), INNER),
            P(("dp",) + INNER, None, None),
            P(("dp",) + INNER),
        ),
        out_specs=(
            P(("groups", "dp"), INNER),
            P(("groups", "dp"), None),
            P(("groups", "dp") + INNER, None, None),
        ),
        check_vma=False,
    )
```

```python
import functools
import math

import jax
import jax.numpy as jnp
from jax import lax
from jax.experimental import pallas as pl
from jax.experimental.pallas import tpu as pltpu
from jax.sharding import PartitionSpec as P

VMEM_LIMIT = 60 * 1024 * 1024
INNER = ("tensor", "replica")


def whole(space=pltpu.VMEM):
    return pl.BlockSpec(memory_space=space)


def project_kernel(ids, blocks, tokens, upstream, proj, back, weight):
    slots, size = blocks.shape[0], blocks.shape[1]
    depth, width = weight.shape
    cols_n = width // size
    total = (depth // size) * cols_n
    weight[...] = jnp.zeros_like(weight)

    @pl.loop(0, slots, unroll=4)
    def place(s):
        b = ids[s]

        @pl.when(b < total)
        def put():
            r = pl.multiple_of((b // cols_n) * size, size)
            c = pl.multiple_of((b % cols_n) * size, size)
            weight[pl.ds(r, size), pl.ds(c, size)] = blocks[s]

    step = 256

    @pl.loop(0, width // step)
    def forward(n):
        c = pl.multiple_of(n * step, step)
        proj[:, pl.ds(c, step)] = jnp.dot(
            tokens[...], weight[:, pl.ds(c, step)], preferred_element_type=jnp.float32
        ).astype(proj.dtype)

    @pl.loop(0, depth // step, unroll=4)
    def backward(n):
        r = pl.multiple_of(n * step, step)
        back[:, pl.ds(r, step)] = lax.dot_general(
            upstream[...],
            weight[pl.ds(r, step), :],
            (((1,), (1,)), ((), ())),
            preferred_element_type=jnp.float32,
        ).astype(back.dtype)


def project(ids, blocks, tokens, upstream):
    rows, depth = tokens.shape
    width = upstream.shape[1]
    return pl.pallas_call(
        project_kernel,
        out_shape=(
            jax.ShapeDtypeStruct((rows, width), jnp.bfloat16),
            jax.ShapeDtypeStruct((rows, depth), jnp.bfloat16),
        ),
        in_specs=[whole(pltpu.SMEM), whole(), whole(), whole()],
        out_specs=(whole(), whole()),
        scratch_shapes=[pltpu.VMEM((depth, width), jnp.bfloat16)],
        compiler_params=pltpu.CompilerParams(vmem_limit_bytes=VMEM_LIMIT),
        cost_estimate=pl.CostEstimate(
            flops=4 * rows * depth * width,
            bytes_accessed=blocks.size * 2 + rows * (depth + width) * 4,
            transcendentals=0,
        ),
        name="project",
    )(ids, blocks, tokens, upstream)


def block_grad_kernel(ids, tokens, upstream, grads):
    slots, size = grads.shape[0], grads.shape[1]
    parts, slabs, _, part_width = tokens.shape
    cols_n = upstream.shape[2] // size
    per_part = part_width // size
    total = parts * per_part * cols_n

    @pl.loop(0, slots)
    def one(s):
        b = ids[s]

        @pl.when(b < total)
        def fill():
            row = b // cols_n
            part = row // per_part
            r = pl.multiple_of((row % per_part) * size, size)
            c = pl.multiple_of((b % cols_n) * size, size)
            acc = jnp.zeros((size, size), jnp.float32)
            for k in range(slabs):
                acc += lax.dot_general(
                    tokens[part, k, :, pl.ds(r, size)],
                    upstream[k, :, pl.ds(c, size)],
                    (((0,), (0,)), ((), ())),
                    preferred_element_type=jnp.float32,
                )
            grads[s] = acc.astype(grads.dtype)

        @pl.when(b >= total)
        def clear():
            grads[s] = jnp.zeros((size, size), grads.dtype)


def block_grads(ids, tokens, upstream, size):
    slots = ids.shape[0]
    parts, slabs, rows, part_width = tokens.shape
    return pl.pallas_call(
        block_grad_kernel,
        out_shape=jax.ShapeDtypeStruct((slots, size, size), jnp.bfloat16),
        in_specs=[whole(pltpu.SMEM), whole(), whole()],
        out_specs=whole(),
        compiler_params=pltpu.CompilerParams(vmem_limit_bytes=VMEM_LIMIT),
        cost_estimate=pl.CostEstimate(
            flops=2 * slots * slabs * rows * size * size,
            bytes_accessed=2 * (tokens.size + upstream.size + slots * size * size),
            transcendentals=0,
        ),
        name="block_grads",
    )(ids, tokens, upstream)


def general_body(tokens, upstream, blocks, block_ids):
    size = blocks.shape[1]
    all_blocks = lax.all_gather(blocks, "dp", axis=0, tiled=True)
    all_ids = lax.all_gather(block_ids, "dp", axis=0, tiled=True)
    proj, back = project(all_ids, all_blocks, tokens, upstream)
    terms = block_grads(all_ids, tokens[None, None], upstream[None], size)
    grads = lax.psum_scatter(terms, "dp", scatter_dimension=0, tiled=True)
    return proj, lax.psum(back, INNER), grads


def place_blocks(ids, first, blocks, weight, turned, slots):
    size = blocks.shape[1]
    depth, width = turned.shape[::-1] if weight is None else weight.shape
    cols_n = width // size
    total = (depth // size) * cols_n

    @pl.loop(0, slots, unroll=4)
    def place(s):
        b = ids[first + s]

        @pl.when(b < total)
        def put():
            r = pl.multiple_of((b // cols_n) * size, size)
            c = pl.multiple_of((b % cols_n) * size, size)
            if weight is not None:
                weight[pl.ds(r, size), pl.ds(c, size)] = blocks[s]
            if turned is not None:
                turned[pl.ds(c, size), pl.ds(r, size)] = blocks[s].T


def place_kernel(
    place_of, ids_0, ids_1, ids_2, ids_3, own, near_a, far_a, far_b, end_a, weight, turned
):
    is_middle, half = place_of[0], place_of[1]
    half_slots = far_b.shape[0] - 1
    mine, other = half * half_slots, (1 - half) * half_slots

    @pl.when(is_middle == 1)
    def work():
        weight[...] = jnp.zeros_like(weight)
        turned[...] = jnp.zeros_like(turned)
        place_blocks(ids_0, 0, own, weight, turned, own.shape[0])
        place_blocks(ids_1, mine, near_a, weight, turned, half_slots)
        place_blocks(ids_2, mine, far_a, weight, turned, half_slots)
        place_blocks(ids_2, other, far_b, weight, turned, half_slots)
        place_blocks(ids_3, mine, end_a, weight, turned, half_slots)


def place_first(place_of, ids, pieces, depth, width):
    return pl.pallas_call(
        place_kernel,
        out_shape=(
            jax.ShapeDtypeStruct((depth, width), jnp.bfloat16),
            jax.ShapeDtypeStruct((width, depth), jnp.bfloat16),
        ),
        in_specs=[whole(pltpu.SMEM)] * 5 + [whole()] * 5,
        out_specs=(whole(), whole()),
        compiler_params=pltpu.CompilerParams(vmem_limit_bytes=VMEM_LIMIT),
        cost_estimate=pl.CostEstimate(
            flops=0, bytes_accessed=depth * width * 6, transcendentals=0
        ),
        name="place_first",
    )(place_of, *ids, *pieces)


def back_kernel(
    place_of, ids_1, ids_3, partial, near_b, end_b, end_upstream, upstream,
    end_keep, own_keep, own_give, end_give_0, end_give_1, held, sources, sem,
):
    half_slots = near_b.shape[0]
    other = (1 - place_of[1]) * half_slots
    rows, width = upstream.shape
    step = 256
    per_part = end_keep.shape[2] // step

    @pl.when(place_of[0] == 1)
    def work():
        load = pltpu.make_async_copy(partial, held, sem)
        load.start()
        sources[:rows] = end_upstream[...]
        sources[rows:] = upstream[...]
        load.wait()
        place_blocks(ids_1, other, near_b, None, held, half_slots)
        place_blocks(ids_3, other, end_b, None, held, half_slots)

        def column(part, end_target, own_target):
            @pl.loop(0, per_part, unroll=2)
            def backward(n):
                at = pl.multiple_of(n * step, step)
                result = jnp.dot(
                    sources[...],
                    held[:, pl.ds(pl.multiple_of(part * per_part * step + at, step), step)],
                    preferred_element_type=jnp.float32,
                ).astype(own_target.dtype)
                end_target[:, pl.ds(at, step)] = result[:rows]
                own_target[:, pl.ds(at, step)] = result[rows:]

        for x, end_give in enumerate((end_give_0, end_give_1)):
            column(2 * x + place_of[3], end_keep.at[x], own_keep.at[x])
            column(2 * x + 1 - place_of[3], end_give, own_give.at[x])


def project_back(place_of, ids_1, ids_3, partial, near_b, end_b, end_upstream, upstream):
    width, depth = partial.shape
    rows = upstream.shape[0]
    quarter = jax.ShapeDtypeStruct((rows, depth // 4), jnp.bfloat16)
    half = jax.ShapeDtypeStruct((2, rows, depth // 4), jnp.bfloat16)
    return pl.pallas_call(
        back_kernel,
        out_shape=(half, half, half, quarter, quarter),
        in_specs=[whole(pltpu.SMEM)] * 3 + [whole(pl.ANY)] + [whole()] * 4,
        out_specs=(whole(),) * 5,
        scratch_shapes=[
            pltpu.VMEM((width, depth), jnp.bfloat16),
            pltpu.VMEM((2 * rows, width), jnp.bfloat16),
            pltpu.SemaphoreType.DMA,
        ],
        compiler_params=pltpu.CompilerParams(vmem_limit_bytes=VMEM_LIMIT),
        cost_estimate=pl.CostEstimate(
            flops=4 * rows * depth * width,
            bytes_accessed=depth * width * 2 + rows * (depth + width) * 4,
            transcendentals=0,
        ),
        name="project_back",
    )(place_of, ids_1, ids_3, partial, near_b, end_b, end_upstream, upstream)


def forward_kernel(
    place_of, ids_1, ids_3, partial, near_b, end_b, tokens, gathered, proj, end_proj, held, sem
):
    half_slots = near_b.shape[0]
    other = (1 - place_of[1]) * half_slots
    depth, width = held.shape
    parts, rows, part_width = gathered.shape
    step = 256

    @pl.when(place_of[0] == 1)
    def work():
        load = pltpu.make_async_copy(partial, held, sem)
        load.start()
        load.wait()
        place_blocks(ids_1, other, near_b, held, None, half_slots)
        place_blocks(ids_3, other, end_b, held, None, half_slots)

        @pl.loop(0, width // step, unroll=2)
        def forward(n):
            c = pl.multiple_of(n * step, step)
            acc = jnp.zeros((rows, step), jnp.float32)
            for q in range(parts):
                acc += jnp.dot(
                    gathered[q],
                    held[q * part_width : (q + 1) * part_width, pl.ds(c, step)],
                    preferred_element_type=jnp.float32,
                )
            end_proj[:, pl.ds(c, step)] = acc.astype(end_proj.dtype)
            proj[:, pl.ds(c, step)] = jnp.dot(
                tokens[...], held[:, pl.ds(c, step)], preferred_element_type=jnp.float32
            ).astype(proj.dtype)


def project_forward(place_of, ids_1, ids_3, partial, near_b, end_b, tokens, gathered):
    depth, width = partial.shape
    rows = tokens.shape[0]
    out = jax.ShapeDtypeStruct((rows, width), jnp.bfloat16)
    return pl.pallas_call(
        forward_kernel,
        out_shape=(out, out),
        in_specs=[whole(pltpu.SMEM)] * 3 + [whole(pl.ANY)] + [whole()] * 4,
        out_specs=(whole(),) * 2,
        scratch_shapes=[pltpu.VMEM((depth, width), jnp.bfloat16), pltpu.SemaphoreType.DMA],
        compiler_params=pltpu.CompilerParams(vmem_limit_bytes=VMEM_LIMIT),
        cost_estimate=pl.CostEstimate(
            flops=4 * rows * depth * width,
            bytes_accessed=depth * width * 2 + rows * (depth + width) * 4,
            transcendentals=0,
        ),
        name="project_forward",
    )(place_of, ids_1, ids_3, partial, near_b, end_b, tokens, gathered)


def split_kernel(place_of, keep, *refs):
    x = place_of[2]
    own, give = refs[-2:]
    got = refs[:-2] if len(refs) > 3 else (refs[0].at[0], refs[0].at[1])
    for at in range(2):
        total = (keep[at].astype(jnp.float32) + got[at][...].astype(jnp.float32)).astype(own.dtype)

        @pl.when(x == at)
        def mine():
            own[...] = total

        @pl.when(x != at)
        def theirs():
            give[...] = total


def add_split(place_of, keep, *got):
    out = jax.ShapeDtypeStruct(keep.shape[1:], keep.dtype)
    return pl.pallas_call(
        split_kernel,
        out_shape=(out, out),
        in_specs=[whole(pltpu.SMEM), whole()] + [whole()] * len(got),
        out_specs=(whole(), whole()),
        compiler_params=pltpu.CompilerParams(vmem_limit_bytes=VMEM_LIMIT),
        cost_estimate=pl.CostEstimate(
            flops=keep.size, bytes_accessed=keep.size * 6, transcendentals=0
        ),
        name="add_split",
    )(place_of, keep, *got)


def assemble_kernel(place_of, own, by_core, by_tensor, by_both, full):
    x, c = place_of[2], place_of[3]
    width = own.shape[1]
    for ref, xx, cc in (
        (own, x, c), (by_core, x, 1 - c), (by_tensor, 1 - x, c), (by_both, 1 - x, 1 - c)
    ):
        at = pl.multiple_of((xx * 2 + cc) * width, width)
        full[:, pl.ds(at, width)] = ref[...]


def assemble(place_of, quarters):
    rows, width = quarters[0].shape
    return pl.pallas_call(
        assemble_kernel,
        out_shape=jax.ShapeDtypeStruct((rows, 4 * width), quarters[0].dtype),
        in_specs=[whole(pltpu.SMEM)] + [whole()] * 4,
        out_specs=whole(),
        compiler_params=pltpu.CompilerParams(vmem_limit_bytes=VMEM_LIMIT),
        cost_estimate=pl.CostEstimate(
            flops=0, bytes_accessed=rows * width * 16, transcendentals=0
        ),
        name="assemble",
    )(place_of, *quarters)


def line_grads_kernel(pairs_n, ids, *refs):
    pairs = [(refs[2 * k], refs[2 * k + 1]) for k in range(pairs_n)]
    grads = refs[-1]
    start = refs[2 * pairs_n] if len(refs) > 2 * pairs_n + 1 else None
    slots, size = grads.shape[0], grads.shape[1]
    first = pairs[0][0]
    cols_n = pairs[0][1].shape[1] // size
    rows_n = first.shape[-1] // size * (first.shape[0] if len(first.shape) == 3 else 1)
    total = rows_n * cols_n
    group = math.gcd(slots, 8)

    @pl.loop(0, slots // group)
    def some(g):
        for s in [g * group + j for j in range(group)]:
            b = jnp.minimum(ids[s], total - 1)
            row = b // cols_n
            c = pl.ds(pl.multiple_of((b % cols_n) * size, size), size)
            acc = jnp.zeros((size, size), jnp.float32) if start is None else start[s].astype(jnp.float32)
            for x, d in pairs:
                per_part = x.shape[-1] // size
                at = pl.ds(pl.multiple_of((row % per_part) * size, size), size)
                acc += lax.dot_general(
                    x[row // per_part, :, at] if len(x.shape) == 3 else x[:, at],
                    d[:, c],
                    (((0,), (0,)), ((), ())),
                    preferred_element_type=jnp.float32,
                )
            grads[s] = jnp.where(ids[s] < total, acc, 0.0).astype(grads.dtype)


def line_grads(ids, pairs, start, size):
    slots = ids.shape[0]
    rows = pairs[0][1].shape[0]
    flat = [a for pair in pairs for a in pair] + ([] if start is None else [start])
    return pl.pallas_call(
        functools.partial(line_grads_kernel, len(pairs)),
        out_shape=jax.ShapeDtypeStruct((slots, size, size), jnp.bfloat16),
        in_specs=[whole(pltpu.SMEM)] + [whole()] * len(flat),
        out_specs=whole(),
        compiler_params=pltpu.CompilerParams(vmem_limit_bytes=VMEM_LIMIT),
        cost_estimate=pl.CostEstimate(
            flops=2 * len(pairs) * slots * rows * size * size,
            bytes_accessed=sum(2 * a.size for a in flat) + 4 * slots * size * size,
            transcendentals=0,
        ),
        name="line_grads",
    )(ids, *flat)


INWARD = ((0, 1), (3, 2))
OUTWARD = ((1, 0), (2, 3))
PAIRS = INWARD + OUTWARD
MIDDLE = ((1, 2), (2, 1))
SWAP = ((0, 1), (1, 0))


def ids_block(block_ids, size):
    rows = size * size // block_ids.shape[0]
    return jnp.broadcast_to(block_ids, (rows, block_ids.shape[0])).reshape(1, size, size)


def ids_of(piece, slots):
    return piece[-1, 0, :slots].astype(jnp.int32)


def line_body(tokens, upstream, blocks, block_ids):
    slots, size = blocks.shape[0], blocks.shape[1]
    rows, depth = tokens.shape
    width = upstream.shape[1]
    half_slots = slots // 2
    part_width = depth // 4
    at_z, half = lax.axis_index("dp"), lax.axis_index("groups")
    at_tensor, at_replica = lax.axis_index("tensor"), lax.axis_index("replica")
    middle = (at_z == 1) | (at_z == 2)
    place_of = jnp.stack([middle.astype(jnp.int32), half, at_tensor, at_replica])
    along = functools.partial(lax.ppermute, axis_name="dp")
    across = functools.partial(lax.ppermute, axis_name="groups", perm=SWAP)
    sideways = functools.partial(lax.ppermute, axis_name="tensor", perm=SWAP)
    cores = functools.partial(lax.ppermute, axis_name="replica", perm=SWAP)
    stage = lax.optimization_barrier

    mine = lax.dynamic_slice_in_dim(blocks, half * half_slots, half_slots, 0)
    other = lax.dynamic_slice_in_dim(blocks, (1 - half) * half_slots, half_slots, 0)
    mine = jnp.concatenate([mine, ids_block(block_ids, size).astype(jnp.bfloat16)])
    part = lax.dynamic_slice_in_dim(tokens, lax.axis_index(INNER) * part_width, part_width, 1)
    both = jnp.concatenate([part, upstream])
    mine, other, both = stage((mine, other, both))

    near_a = along(mine, perm=INWARD)
    far_a = along(mine, perm=MIDDLE)
    near_a, far_a, both, other = stage((near_a, far_a, both, other))

    end_a = along(near_a, perm=MIDDLE)
    far_b = across(far_a)
    both_1 = along(both, perm=PAIRS)
    both_1, end_a, far_b, both, other = stage((both_1, end_a, far_b, both, other))
    upstream_1 = both_1[rows:]

    near_b = along(other, perm=INWARD)
    end_b = across(end_a)
    both_2m = along(both, perm=MIDDLE)
    tokens_1 = lax.all_gather(both_1[:rows], INNER)
    ids_1, ids_2, ids_3 = (ids_of(piece, slots) for piece in (near_a, far_a, end_a))
    partial, turned = place_first(
        place_of, (block_ids, ids_1, ids_2, ids_3), (blocks, near_a, far_a, far_b, end_a), depth, width
    )
    near_b, end_b, both_2m, both_1, tokens_1, partial, turned = stage(
        (near_b, end_b, both_2m, both_1, tokens_1, partial, turned)
    )

    both_3m = along(both_1, perm=MIDDLE)
    both_2o = along(both_2m, perm=OUTWARD)
    last = (near_b, end_b)
    end_keep, own_keep, own_give, *end_give = project_back(
        place_of, ids_1, ids_3, turned, *last, upstream_1, upstream
    )
    end_keep, end_give = add_split(place_of, end_keep, *[cores(a) for a in end_give])
    end_keep, end_give, own_give, both_3m, both_2o = stage(
        (end_keep, end_give, own_give, both_3m, both_2o)
    )

    end_got = sideways(end_give)
    own_keep, own_give = add_split(place_of, own_keep, cores(own_give))
    both_3o = along(both_3m, perm=OUTWARD)
    tokens_2 = lax.all_gather(both_2m[:rows] + both_2o[:rows], INNER)
    upstream_2 = both_2m[rows:] + both_2o[rows:]
    pairs = ((tokens, upstream), (tokens_1, upstream_1))
    grads = line_grads(block_ids, pairs, None, size)
    end_got, own_give, own_keep, grads = stage((end_got, own_give, own_keep, grads))

    sum_out = along(end_keep + end_got, perm=OUTWARD)
    own_got = sideways(own_give)
    proj, end_proj = project_forward(place_of, ids_1, ids_3, partial, *last, tokens, tokens_1)
    sum_out, own_got, both_3o, proj, end_proj = stage((sum_out, own_got, both_3o, proj, end_proj))

    tokens_3 = lax.all_gather(both_3m[:rows] + both_3o[:rows], INNER)
    upstream_3 = both_3m[rows:] + both_3o[rows:]
    quarter = jnp.where(middle, own_keep + own_got, sum_out)
    proj_out = along(end_proj, perm=OUTWARD)
    grads = line_grads(block_ids, ((tokens_2, upstream_2),), grads, size)
    by_tensor, by_core, grads = stage((sideways(quarter), cores(quarter), grads))
    by_both = cores(by_tensor)
    projected = jnp.where(middle, proj, proj_out)
    token_grad = assemble(place_of, (quarter, by_core, by_tensor, by_both))
    grads = line_grads(block_ids, ((tokens_3, upstream_3),), grads, size)
    return projected, token_grad, grads


def solution(mesh):
    line = tuple(mesh.shape[a] for a in ("groups", "dp", "tensor", "replica")) == (2, 4, 2, 2)
    return jax.shard_map(
        line_body if line else general_body,
        mesh=mesh,
        in_specs=(
            P(("groups", "dp"), None),
            P(("groups", "dp"), INNER),
            P(("dp",) + INNER, None, None),
            P(("dp",) + INNER),
        ),
        out_specs=(
            P(("groups", "dp"), INNER),
            P(("groups", "dp"), None),
            P(("groups", "dp") + INNER, None, None),
        ),
        check_vma=False,
    )
```

```python
import functools
import math

import jax
import jax.numpy as jnp
from jax import lax
from jax.experimental import pallas as pl
from jax.experimental.pallas import tpu as pltpu
from jax.sharding import PartitionSpec as P

VMEM_LIMIT = 60 * 1024 * 1024
INNER = ("tensor", "replica")


def whole(space=pltpu.VMEM):
    return pl.BlockSpec(memory_space=space)


def project_kernel(ids, blocks, tokens, upstream, proj, back, weight):
    slots, size = blocks.shape[0], blocks.shape[1]
    depth, width = weight.shape
    cols_n = width // size
    total = (depth // size) * cols_n
    weight[...] = jnp.zeros_like(weight)

    @pl.loop(0, slots, unroll=4)
    def place(s):
        b = ids[s]

        @pl.when(b < total)
        def put():
            r = pl.multiple_of((b // cols_n) * size, size)
            c = pl.multiple_of((b % cols_n) * size, size)
            weight[pl.ds(r, size), pl.ds(c, size)] = blocks[s]

    step = 256

    @pl.loop(0, width // step)
    def forward(n):
        c = pl.multiple_of(n * step, step)
        proj[:, pl.ds(c, step)] = jnp.dot(
            tokens[...], weight[:, pl.ds(c, step)], preferred_element_type=jnp.float32
        ).astype(proj.dtype)

    @pl.loop(0, depth // step, unroll=4)
    def backward(n):
        r = pl.multiple_of(n * step, step)
        back[:, pl.ds(r, step)] = lax.dot_general(
            upstream[...],
            weight[pl.ds(r, step), :],
            (((1,), (1,)), ((), ())),
            preferred_element_type=jnp.float32,
        ).astype(back.dtype)


def project(ids, blocks, tokens, upstream):
    rows, depth = tokens.shape
    width = upstream.shape[1]
    return pl.pallas_call(
        project_kernel,
        out_shape=(
            jax.ShapeDtypeStruct((rows, width), jnp.bfloat16),
            jax.ShapeDtypeStruct((rows, depth), jnp.bfloat16),
        ),
        in_specs=[whole(pltpu.SMEM), whole(), whole(), whole()],
        out_specs=(whole(), whole()),
        scratch_shapes=[pltpu.VMEM((depth, width), jnp.bfloat16)],
        compiler_params=pltpu.CompilerParams(vmem_limit_bytes=VMEM_LIMIT),
        cost_estimate=pl.CostEstimate(
            flops=4 * rows * depth * width,
            bytes_accessed=blocks.size * 2 + rows * (depth + width) * 4,
            transcendentals=0,
        ),
        name="project",
    )(ids, blocks, tokens, upstream)


def block_grad_kernel(ids, tokens, upstream, grads):
    slots, size = grads.shape[0], grads.shape[1]
    parts, slabs, _, part_width = tokens.shape
    cols_n = upstream.shape[2] // size
    per_part = part_width // size
    total = parts * per_part * cols_n

    @pl.loop(0, slots)
    def one(s):
        b = ids[s]

        @pl.when(b < total)
        def fill():
            row = b // cols_n
            part = row // per_part
            r = pl.multiple_of((row % per_part) * size, size)
            c = pl.multiple_of((b % cols_n) * size, size)
            acc = jnp.zeros((size, size), jnp.float32)
            for k in range(slabs):
                acc += lax.dot_general(
                    tokens[part, k, :, pl.ds(r, size)],
                    upstream[k, :, pl.ds(c, size)],
                    (((0,), (0,)), ((), ())),
                    preferred_element_type=jnp.float32,
                )
            grads[s] = acc.astype(grads.dtype)

        @pl.when(b >= total)
        def clear():
            grads[s] = jnp.zeros((size, size), grads.dtype)


def block_grads(ids, tokens, upstream, size):
    slots = ids.shape[0]
    parts, slabs, rows, part_width = tokens.shape
    return pl.pallas_call(
        block_grad_kernel,
        out_shape=jax.ShapeDtypeStruct((slots, size, size), jnp.bfloat16),
        in_specs=[whole(pltpu.SMEM), whole(), whole()],
        out_specs=whole(),
        compiler_params=pltpu.CompilerParams(vmem_limit_bytes=VMEM_LIMIT),
        cost_estimate=pl.CostEstimate(
            flops=2 * slots * slabs * rows * size * size,
            bytes_accessed=2 * (tokens.size + upstream.size + slots * size * size),
            transcendentals=0,
        ),
        name="block_grads",
    )(ids, tokens, upstream)


def general_body(tokens, upstream, blocks, block_ids):
    size = blocks.shape[1]
    all_blocks = lax.all_gather(blocks, "dp", axis=0, tiled=True)
    all_ids = lax.all_gather(block_ids, "dp", axis=0, tiled=True)
    proj, back = project(all_ids, all_blocks, tokens, upstream)
    terms = block_grads(all_ids, tokens[None, None], upstream[None], size)
    grads = lax.psum_scatter(terms, "dp", scatter_dimension=0, tiled=True)
    return proj, lax.psum(back, INNER), grads


def place_blocks(ids, first, blocks, weight, turned, slots):
    size = blocks.shape[1]
    depth, width = turned.shape[::-1] if weight is None else weight.shape
    cols_n = width // size
    total = (depth // size) * cols_n
    group = math.gcd(slots, 8)

    @pl.loop(0, slots // group)
    def place(g):
        some = [g * group + j for j in range(group)]
        flipped = [None if turned is None else blocks[s].T for s in some]
        for s, flip in zip(some, flipped):
            b = ids[first + s]

            @pl.when(b < total)
            def put(s=s, flip=flip, b=b):
                r = pl.multiple_of((b // cols_n) * size, size)
                c = pl.multiple_of((b % cols_n) * size, size)
                if weight is not None:
                    weight[pl.ds(r, size), pl.ds(c, size)] = blocks[s]
                if turned is not None:
                    turned[pl.ds(c, size), pl.ds(r, size)] = flip


def place_kernel(
    place_of, ids_0, ids_1, ids_2, ids_3, own, near_a, far_a, far_b, end_a, weight, turned
):
    is_middle, half = place_of[0], place_of[1]
    half_slots = far_b.shape[0] - 1
    mine, other = half * half_slots, (1 - half) * half_slots

    @pl.when(is_middle == 1)
    def work():
        weight[...] = jnp.zeros_like(weight)
        turned[...] = jnp.zeros_like(turned)
        place_blocks(ids_0, 0, own, weight, turned, own.shape[0])
        place_blocks(ids_1, mine, near_a, weight, turned, half_slots)
        place_blocks(ids_2, mine, far_a, weight, turned, half_slots)
        place_blocks(ids_2, other, far_b, weight, turned, half_slots)
        place_blocks(ids_3, mine, end_a, weight, turned, half_slots)


def place_first(place_of, ids, pieces, depth, width):
    return pl.pallas_call(
        place_kernel,
        out_shape=(
            jax.ShapeDtypeStruct((depth, width), jnp.bfloat16),
            jax.ShapeDtypeStruct((width, depth), jnp.bfloat16),
        ),
        in_specs=[whole(pltpu.SMEM)] * 5 + [whole()] * 5,
        out_specs=(whole(), whole()),
        compiler_params=pltpu.CompilerParams(vmem_limit_bytes=VMEM_LIMIT),
        cost_estimate=pl.CostEstimate(
            flops=0, bytes_accessed=depth * width * 6, transcendentals=0
        ),
        name="place_first",
    )(place_of, *ids, *pieces)


def back_kernel(
    place_of, ids_1, ids_3, partial, near_b, end_b, end_upstream, upstream,
    end_keep, own_keep, own_give, end_give_0, end_give_1, held, sources, sem,
):
    half_slots = near_b.shape[0]
    other = (1 - place_of[1]) * half_slots
    rows, width = upstream.shape
    step = 256
    per_part = end_keep.shape[2] // step

    @pl.when(place_of[0] == 1)
    def work():
        load = pltpu.make_async_copy(partial, held, sem)
        load.start()
        sources[:rows] = end_upstream[...]
        sources[rows:] = upstream[...]
        load.wait()
        place_blocks(ids_1, other, near_b, None, held, half_slots)
        place_blocks(ids_3, other, end_b, None, held, half_slots)

        def column(part, end_target, own_target):
            @pl.loop(0, per_part, unroll=2)
            def backward(n):
                at = pl.multiple_of(n * step, step)
                result = jnp.dot(
                    sources[...],
                    held[:, pl.ds(pl.multiple_of(part * per_part * step + at, step), step)],
                    preferred_element_type=jnp.float32,
                ).astype(own_target.dtype)
                end_target[:, pl.ds(at, step)] = result[:rows]
                own_target[:, pl.ds(at, step)] = result[rows:]

        for x, end_give in enumerate((end_give_0, end_give_1)):
            column(2 * x + place_of[3], end_keep.at[x], own_keep.at[x])
            column(2 * x + 1 - place_of[3], end_give, own_give.at[x])


def project_back(place_of, ids_1, ids_3, partial, near_b, end_b, end_upstream, upstream):
    width, depth = partial.shape
    rows = upstream.shape[0]
    quarter = jax.ShapeDtypeStruct((rows, depth // 4), jnp.bfloat16)
    half = jax.ShapeDtypeStruct((2, rows, depth // 4), jnp.bfloat16)
    return pl.pallas_call(
        back_kernel,
        out_shape=(half, half, half, quarter, quarter),
        in_specs=[whole(pltpu.SMEM)] * 3 + [whole(pl.ANY)] + [whole()] * 4,
        out_specs=(whole(),) * 5,
        scratch_shapes=[
            pltpu.VMEM((width, depth), jnp.bfloat16),
            pltpu.VMEM((2 * rows, width), jnp.bfloat16),
            pltpu.SemaphoreType.DMA,
        ],
        compiler_params=pltpu.CompilerParams(vmem_limit_bytes=VMEM_LIMIT),
        cost_estimate=pl.CostEstimate(
            flops=4 * rows * depth * width,
            bytes_accessed=depth * width * 2 + rows * (depth + width) * 4,
            transcendentals=0,
        ),
        name="project_back",
    )(place_of, ids_1, ids_3, partial, near_b, end_b, end_upstream, upstream)


def forward_kernel(
    place_of, ids_1, ids_3, partial, near_b, end_b, tokens, gathered, proj, end_proj, held, sem
):
    half_slots = near_b.shape[0]
    other = (1 - place_of[1]) * half_slots
    depth, width = held.shape
    parts, rows, part_width = gathered.shape
    step = 256

    @pl.when(place_of[0] == 1)
    def work():
        load = pltpu.make_async_copy(partial, held, sem)
        load.start()
        load.wait()
        place_blocks(ids_1, other, near_b, held, None, half_slots)
        place_blocks(ids_3, other, end_b, held, None, half_slots)

        @pl.loop(0, width // step, unroll=2)
        def forward(n):
            c = pl.multiple_of(n * step, step)
            acc = jnp.zeros((rows, step), jnp.float32)
            for q in range(parts):
                acc += jnp.dot(
                    gathered[q],
                    held[q * part_width : (q + 1) * part_width, pl.ds(c, step)],
                    preferred_element_type=jnp.float32,
                )
            end_proj[:, pl.ds(c, step)] = acc.astype(end_proj.dtype)
            proj[:, pl.ds(c, step)] = jnp.dot(
                tokens[...], held[:, pl.ds(c, step)], preferred_element_type=jnp.float32
            ).astype(proj.dtype)


def project_forward(place_of, ids_1, ids_3, partial, near_b, end_b, tokens, gathered):
    depth, width = partial.shape
    rows = tokens.shape[0]
    out = jax.ShapeDtypeStruct((rows, width), jnp.bfloat16)
    return pl.pallas_call(
        forward_kernel,
        out_shape=(out, out),
        in_specs=[whole(pltpu.SMEM)] * 3 + [whole(pl.ANY)] + [whole()] * 4,
        out_specs=(whole(),) * 2,
        scratch_shapes=[pltpu.VMEM((depth, width), jnp.bfloat16), pltpu.SemaphoreType.DMA],
        compiler_params=pltpu.CompilerParams(vmem_limit_bytes=VMEM_LIMIT),
        cost_estimate=pl.CostEstimate(
            flops=4 * rows * depth * width,
            bytes_accessed=depth * width * 2 + rows * (depth + width) * 4,
            transcendentals=0,
        ),
        name="project_forward",
    )(place_of, ids_1, ids_3, partial, near_b, end_b, tokens, gathered)


def split_kernel(place_of, keep, *refs):
    x = place_of[2]
    own, give = refs[-2:]
    got = refs[:-2] if len(refs) > 3 else (refs[0].at[0], refs[0].at[1])
    for at in range(2):
        total = (keep[at].astype(jnp.float32) + got[at][...].astype(jnp.float32)).astype(own.dtype)

        @pl.when(x == at)
        def mine():
            own[...] = total

        @pl.when(x != at)
        def theirs():
            give[...] = total


def add_split(place_of, keep, *got):
    out = jax.ShapeDtypeStruct(keep.shape[1:], keep.dtype)
    return pl.pallas_call(
        split_kernel,
        out_shape=(out, out),
        in_specs=[whole(pltpu.SMEM), whole()] + [whole()] * len(got),
        out_specs=(whole(), whole()),
        compiler_params=pltpu.CompilerParams(vmem_limit_bytes=VMEM_LIMIT),
        cost_estimate=pl.CostEstimate(
            flops=keep.size, bytes_accessed=keep.size * 6, transcendentals=0
        ),
        name="add_split",
    )(place_of, keep, *got)


def assemble_kernel(place_of, own, by_core, by_tensor, by_both, full):
    x, c = place_of[2], place_of[3]
    width = own.shape[1]
    for ref, xx, cc in (
        (own, x, c), (by_core, x, 1 - c), (by_tensor, 1 - x, c), (by_both, 1 - x, 1 - c)
    ):
        at = pl.multiple_of((xx * 2 + cc) * width, width)
        full[:, pl.ds(at, width)] = ref[...]


def assemble(place_of, quarters):
    rows, width = quarters[0].shape
    return pl.pallas_call(
        assemble_kernel,
        out_shape=jax.ShapeDtypeStruct((rows, 4 * width), quarters[0].dtype),
        in_specs=[whole(pltpu.SMEM)] + [whole()] * 4,
        out_specs=whole(),
        compiler_params=pltpu.CompilerParams(vmem_limit_bytes=VMEM_LIMIT),
        cost_estimate=pl.CostEstimate(
            flops=0, bytes_accessed=rows * width * 16, transcendentals=0
        ),
        name="assemble",
    )(place_of, *quarters)


def line_grads_kernel(pairs_n, ids, *refs):
    refs = list(refs)
    pairs = []
    for k in range(pairs_n):
        x, d = refs.pop(0), refs.pop(0)
        if d.shape[0] > x.shape[-2]:
            rows, other = x.shape[-2], refs.pop(0)
            total_d = refs.pop()
            total_d[...] = d[rows:] + other[rows:]
            d = total_d
        pairs.append((x, d))
    start = refs.pop(0) if len(refs) == 2 else None
    (grads,) = refs
    slots, size = grads.shape[0], grads.shape[1]
    first = pairs[0][0]
    cols_n = pairs[0][1].shape[1] // size
    rows_n = first.shape[-1] // size * (first.shape[0] if len(first.shape) == 3 else 1)
    total = rows_n * cols_n
    group = math.gcd(slots, 8)

    @pl.loop(0, slots // group)
    def some(g):
        for s in [g * group + j for j in range(group)]:
            b = jnp.minimum(ids[s], total - 1)
            row = b // cols_n
            c = pl.ds(pl.multiple_of((b % cols_n) * size, size), size)
            acc = jnp.zeros((size, size), jnp.float32) if start is None else start[s].astype(jnp.float32)
            for x, d in pairs:
                per_part = x.shape[-1] // size
                at = pl.ds(pl.multiple_of((row % per_part) * size, size), size)
                acc += lax.dot_general(
                    x[row // per_part, :, at] if len(x.shape) == 3 else x[:, at],
                    d[:, c],
                    (((0,), (0,)), ((), ())),
                    preferred_element_type=jnp.float32,
                )
            grads[s] = jnp.where(ids[s] < total, acc, 0.0).astype(grads.dtype)


def line_grads(ids, pairs, start, size):
    slots = ids.shape[0]
    flat = [a for pair in pairs for a in pair] + ([] if start is None else [start])
    sums = [
        pltpu.VMEM((p[0].shape[-2], p[1].shape[1]), jnp.bfloat16) for p in pairs if len(p) == 3
    ]
    return pl.pallas_call(
        functools.partial(line_grads_kernel, len(pairs)),
        out_shape=jax.ShapeDtypeStruct((slots, size, size), jnp.bfloat16),
        in_specs=[whole(pltpu.SMEM)] + [whole()] * len(flat),
        out_specs=whole(),
        scratch_shapes=sums,
        compiler_params=pltpu.CompilerParams(vmem_limit_bytes=VMEM_LIMIT),
        cost_estimate=pl.CostEstimate(
            flops=512 * len(pairs) * slots * size * size,
            bytes_accessed=sum(2 * a.size for a in flat) + 2 * slots * size * size,
            transcendentals=0,
        ),
        name="line_grads",
    )(ids, *flat)


INWARD = ((0, 1), (3, 2))
OUTWARD = ((1, 0), (2, 3))
PAIRS = INWARD + OUTWARD
MIDDLE = ((1, 2), (2, 1))
SWAP = ((0, 1), (1, 0))


def ids_block(block_ids, size):
    rows = size * size // block_ids.shape[0]
    return jnp.broadcast_to(block_ids, (rows, block_ids.shape[0])).reshape(1, size, size)


def ids_of(piece, slots):
    return piece[-1, 0, :slots].astype(jnp.int32)


def line_body(tokens, upstream, blocks, block_ids):
    slots, size = blocks.shape[0], blocks.shape[1]
    rows, depth = tokens.shape
    width = upstream.shape[1]
    half_slots = slots // 2
    part_width = depth // 4
    at_z, half = lax.axis_index("dp"), lax.axis_index("groups")
    at_tensor, at_replica = lax.axis_index("tensor"), lax.axis_index("replica")
    middle = (at_z == 1) | (at_z == 2)
    place_of = jnp.stack([middle.astype(jnp.int32), half, at_tensor, at_replica])
    along = functools.partial(lax.ppermute, axis_name="dp")
    across = functools.partial(lax.ppermute, axis_name="groups", perm=SWAP)
    sideways = functools.partial(lax.ppermute, axis_name="tensor", perm=SWAP)
    cores = functools.partial(lax.ppermute, axis_name="replica", perm=SWAP)
    stage = lax.optimization_barrier

    mine = lax.dynamic_slice_in_dim(blocks, half * half_slots, half_slots, 0)
    mine = jnp.concatenate([mine, ids_block(block_ids, size).astype(jnp.bfloat16)])
    mine, late_blocks = stage((mine, blocks))

    near_a = along(mine, perm=INWARD)
    far_a = along(mine, perm=MIDDLE)
    other = lax.dynamic_slice_in_dim(late_blocks, (1 - half) * half_slots, half_slots, 0)
    part = lax.dynamic_slice_in_dim(tokens, lax.axis_index(INNER) * part_width, part_width, 1)
    both = jnp.concatenate([part, upstream])
    grads = line_grads(block_ids, ((tokens, upstream),), None, size)
    near_a, far_a, both, other, grads = stage((near_a, far_a, both, other, grads))

    end_a = along(near_a, perm=MIDDLE)
    far_b = across(far_a)
    both_1 = along(both, perm=PAIRS)
    both_1, end_a, far_b, both, other = stage((both_1, end_a, far_b, both, other))
    upstream_1 = both_1[rows:]

    near_b = along(other, perm=INWARD)
    end_b = across(end_a)
    both_2m = along(both, perm=MIDDLE)
    tokens_1 = lax.all_gather(both_1[:rows], INNER)
    ids_1, ids_2, ids_3 = (ids_of(piece, slots) for piece in (near_a, far_a, end_a))
    partial, turned = place_first(
        place_of, (block_ids, ids_1, ids_2, ids_3), (blocks, near_a, far_a, far_b, end_a), depth, width
    )
    near_b, end_b, both_2m, both_1, tokens_1, partial, turned = stage(
        (near_b, end_b, both_2m, both_1, tokens_1, partial, turned)
    )

    both_3m = along(both_1, perm=MIDDLE)
    both_2o = along(both_2m, perm=OUTWARD)
    last = (near_b, end_b)
    end_keep, own_keep, own_give, *end_give = project_back(
        place_of, ids_1, ids_3, turned, *last, upstream_1, upstream
    )
    end_keep, end_give = add_split(place_of, end_keep, *[cores(a) for a in end_give])
    end_keep, end_give, own_give, both_3m, both_2o = stage(
        (end_keep, end_give, own_give, both_3m, both_2o)
    )

    end_got = sideways(end_give)
    own_keep, own_give = add_split(place_of, own_keep, cores(own_give))
    both_3o = along(both_3m, perm=OUTWARD)
    tokens_2 = lax.all_gather(both_2m[:rows] + both_2o[:rows], INNER)
    grads = line_grads(block_ids, ((tokens_1, upstream_1),), grads, size)
    end_got, own_give, own_keep, grads = stage((end_got, own_give, own_keep, grads))

    sum_out = along(end_keep + end_got, perm=OUTWARD)
    own_got = sideways(own_give)
    proj, end_proj = project_forward(place_of, ids_1, ids_3, partial, *last, tokens, tokens_1)
    sum_out, own_got, both_3o, proj, end_proj = stage((sum_out, own_got, both_3o, proj, end_proj))

    tokens_3 = lax.all_gather(both_3m[:rows] + both_3o[:rows], INNER)
    quarter = jnp.where(middle, own_keep + own_got, sum_out)
    proj_out = along(end_proj, perm=OUTWARD)
    grads = line_grads(block_ids, ((tokens_2, both_2m, both_2o),), grads, size)
    by_tensor, by_core, grads = stage((sideways(quarter), cores(quarter), grads))
    by_both = cores(by_tensor)
    projected = jnp.where(middle, proj, proj_out)
    token_grad = assemble(place_of, (quarter, by_core, by_tensor, by_both))
    grads = line_grads(block_ids, ((tokens_3, both_3m, both_3o),), grads, size)
    return projected, token_grad, grads


def solution(mesh):
    line = tuple(mesh.shape[a] for a in ("groups", "dp", "tensor", "replica")) == (2, 4, 2, 2)
    return jax.shard_map(
        line_body if line else general_body,
        mesh=mesh,
        in_specs=(
            P(("groups", "dp"), None),
            P(("groups", "dp"), INNER),
            P(("dp",) + INNER, None, None),
            P(("dp",) + INNER),
        ),
        out_specs=(
            P(("groups", "dp"), INNER),
            P(("groups", "dp"), None),
            P(("groups", "dp") + INNER, None, None),
        ),
        check_vma=False,
    )
```

```python
import functools
import math

import jax
import jax.numpy as jnp
from jax import lax
from jax.experimental import pallas as pl
from jax.experimental.pallas import tpu as pltpu
from jax.sharding import PartitionSpec as P

VMEM_LIMIT = 60 * 1024 * 1024
INNER = ("tensor", "replica")


def whole(space=pltpu.VMEM):
    return pl.BlockSpec(memory_space=space)


def project_kernel(ids, blocks, tokens, upstream, proj, back, weight):
    slots, size = blocks.shape[0], blocks.shape[1]
    depth, width = weight.shape
    cols_n = width // size
    total = (depth // size) * cols_n
    weight[...] = jnp.zeros_like(weight)

    @pl.loop(0, slots, unroll=4)
    def place(s):
        b = ids[s]

        @pl.when(b < total)
        def put():
            r = pl.multiple_of((b // cols_n) * size, size)
            c = pl.multiple_of((b % cols_n) * size, size)
            weight[pl.ds(r, size), pl.ds(c, size)] = blocks[s]

    step = 256

    @pl.loop(0, width // step)
    def forward(n):
        c = pl.multiple_of(n * step, step)
        proj[:, pl.ds(c, step)] = jnp.dot(
            tokens[...], weight[:, pl.ds(c, step)], preferred_element_type=jnp.float32
        ).astype(proj.dtype)

    @pl.loop(0, depth // step, unroll=4)
    def backward(n):
        r = pl.multiple_of(n * step, step)
        back[:, pl.ds(r, step)] = lax.dot_general(
            upstream[...],
            weight[pl.ds(r, step), :],
            (((1,), (1,)), ((), ())),
            preferred_element_type=jnp.float32,
        ).astype(back.dtype)


def project(ids, blocks, tokens, upstream):
    rows, depth = tokens.shape
    width = upstream.shape[1]
    return pl.pallas_call(
        project_kernel,
        out_shape=(
            jax.ShapeDtypeStruct((rows, width), jnp.bfloat16),
            jax.ShapeDtypeStruct((rows, depth), jnp.bfloat16),
        ),
        in_specs=[whole(pltpu.SMEM), whole(), whole(), whole()],
        out_specs=(whole(), whole()),
        scratch_shapes=[pltpu.VMEM((depth, width), jnp.bfloat16)],
        compiler_params=pltpu.CompilerParams(vmem_limit_bytes=VMEM_LIMIT),
        cost_estimate=pl.CostEstimate(
            flops=4 * rows * depth * width,
            bytes_accessed=blocks.size * 2 + rows * (depth + width) * 4,
            transcendentals=0,
        ),
        name="project",
    )(ids, blocks, tokens, upstream)


def block_grad_kernel(ids, tokens, upstream, grads):
    slots, size = grads.shape[0], grads.shape[1]
    parts, slabs, _, part_width = tokens.shape
    cols_n = upstream.shape[2] // size
    per_part = part_width // size
    total = parts * per_part * cols_n

    @pl.loop(0, slots)
    def one(s):
        b = ids[s]

        @pl.when(b < total)
        def fill():
            row = b // cols_n
            part = row // per_part
            r = pl.multiple_of((row % per_part) * size, size)
            c = pl.multiple_of((b % cols_n) * size, size)
            acc = jnp.zeros((size, size), jnp.float32)
            for k in range(slabs):
                acc += lax.dot_general(
                    tokens[part, k, :, pl.ds(r, size)],
                    upstream[k, :, pl.ds(c, size)],
                    (((0,), (0,)), ((), ())),
                    preferred_element_type=jnp.float32,
                )
            grads[s] = acc.astype(grads.dtype)

        @pl.when(b >= total)
        def clear():
            grads[s] = jnp.zeros((size, size), grads.dtype)


def block_grads(ids, tokens, upstream, size):
    slots = ids.shape[0]
    parts, slabs, rows, part_width = tokens.shape
    return pl.pallas_call(
        block_grad_kernel,
        out_shape=jax.ShapeDtypeStruct((slots, size, size), jnp.bfloat16),
        in_specs=[whole(pltpu.SMEM), whole(), whole()],
        out_specs=whole(),
        compiler_params=pltpu.CompilerParams(vmem_limit_bytes=VMEM_LIMIT),
        cost_estimate=pl.CostEstimate(
            flops=2 * slots * slabs * rows * size * size,
            bytes_accessed=2 * (tokens.size + upstream.size + slots * size * size),
            transcendentals=0,
        ),
        name="block_grads",
    )(ids, tokens, upstream)


def general_body(tokens, upstream, blocks, block_ids):
    size = blocks.shape[1]
    all_blocks = lax.all_gather(blocks, "dp", axis=0, tiled=True)
    all_ids = lax.all_gather(block_ids, "dp", axis=0, tiled=True)
    proj, back = project(all_ids, all_blocks, tokens, upstream)
    terms = block_grads(all_ids, tokens[None, None], upstream[None], size)
    grads = lax.psum_scatter(terms, "dp", scatter_dimension=0, tiled=True)
    return proj, lax.psum(back, INNER), grads


def place_blocks(ids, first, blocks, weight, turned, slots):
    size = blocks.shape[1]
    depth, width = turned.shape[::-1] if weight is None else weight.shape
    cols_n = width // size
    total = (depth // size) * cols_n
    group = math.gcd(slots, 8)

    @pl.loop(0, slots // group)
    def place(g):
        some = [g * group + j for j in range(group)]
        flipped = [None if turned is None else blocks[s].T for s in some]
        for s, flip in zip(some, flipped):
            b = ids[first + s]

            @pl.when(b < total)
            def put(s=s, flip=flip, b=b):
                r = pl.multiple_of((b // cols_n) * size, size)
                c = pl.multiple_of((b % cols_n) * size, size)
                if weight is not None:
                    weight[pl.ds(r, size), pl.ds(c, size)] = blocks[s]
                if turned is not None:
                    turned[pl.ds(c, size), pl.ds(r, size)] = flip


def place_kernel(
    place_of, ids_0, ids_1, ids_2, ids_3, own, near_a, far_a, far_b, end_a, weight, turned
):
    is_middle, half = place_of[0], place_of[1]
    half_slots = far_b.shape[0] - 1
    mine, other = half * half_slots, (1 - half) * half_slots

    @pl.when(is_middle == 1)
    def work():
        weight[...] = jnp.zeros_like(weight)
        turned[...] = jnp.zeros_like(turned)
        place_blocks(ids_0, 0, own, weight, turned, own.shape[0])
        place_blocks(ids_1, mine, near_a, weight, turned, half_slots)
        place_blocks(ids_2, mine, far_a, weight, turned, half_slots)
        place_blocks(ids_2, other, far_b, weight, turned, half_slots)
        place_blocks(ids_3, mine, end_a, weight, turned, half_slots)


def place_first(place_of, ids, pieces, depth, width):
    return pl.pallas_call(
        place_kernel,
        out_shape=(
            jax.ShapeDtypeStruct((depth, width), jnp.bfloat16),
            jax.ShapeDtypeStruct((width, depth), jnp.bfloat16),
        ),
        in_specs=[whole(pltpu.SMEM)] * 5 + [whole()] * 5,
        out_specs=(whole(), whole()),
        compiler_params=pltpu.CompilerParams(vmem_limit_bytes=VMEM_LIMIT),
        cost_estimate=pl.CostEstimate(
            flops=0, bytes_accessed=depth * width * 6, transcendentals=0
        ),
        name="place_first",
    )(place_of, *ids, *pieces)


def back_kernel(
    place_of, ids_1, ids_3, partial, near_b, end_b, end_upstream, upstream,
    end_keep, own_keep, own_give, end_give_0, end_give_1, held, sources, sem,
):
    half_slots = near_b.shape[0]
    other = (1 - place_of[1]) * half_slots
    rows, width = upstream.shape
    step = 256
    per_part = end_keep.shape[2] // step

    @pl.when(place_of[0] == 1)
    def work():
        load = pltpu.make_async_copy(partial, held, sem)
        load.start()
        sources[:rows] = end_upstream[...]
        sources[rows:] = upstream[...]
        load.wait()
        place_blocks(ids_1, other, near_b, None, held, half_slots)
        place_blocks(ids_3, other, end_b, None, held, half_slots)

        def column(part, end_target, own_target):
            @pl.loop(0, per_part, unroll=2)
            def backward(n):
                at = pl.multiple_of(n * step, step)
                result = jnp.dot(
                    sources[...],
                    held[:, pl.ds(pl.multiple_of(part * per_part * step + at, step), step)],
                    preferred_element_type=jnp.float32,
                ).astype(own_target.dtype)
                end_target[:, pl.ds(at, step)] = result[:rows]
                own_target[:, pl.ds(at, step)] = result[rows:]

        for x, end_give in enumerate((end_give_0, end_give_1)):
            column(2 * x + place_of[3], end_keep.at[x], own_keep.at[x])
            column(2 * x + 1 - place_of[3], end_give, own_give.at[x])


def project_back(place_of, ids_1, ids_3, partial, near_b, end_b, end_upstream, upstream):
    width, depth = partial.shape
    rows = upstream.shape[0]
    quarter = jax.ShapeDtypeStruct((rows, depth // 4), jnp.bfloat16)
    half = jax.ShapeDtypeStruct((2, rows, depth // 4), jnp.bfloat16)
    return pl.pallas_call(
        back_kernel,
        out_shape=(half, half, half, quarter, quarter),
        in_specs=[whole(pltpu.SMEM)] * 3 + [whole(pl.ANY)] + [whole()] * 4,
        out_specs=(whole(),) * 5,
        scratch_shapes=[
            pltpu.VMEM((width, depth), jnp.bfloat16),
            pltpu.VMEM((2 * rows, width), jnp.bfloat16),
            pltpu.SemaphoreType.DMA,
        ],
        compiler_params=pltpu.CompilerParams(vmem_limit_bytes=VMEM_LIMIT),
        cost_estimate=pl.CostEstimate(
            flops=4 * rows * depth * width,
            bytes_accessed=depth * width * 2 + rows * (depth + width) * 4,
            transcendentals=0,
        ),
        name="project_back",
    )(place_of, ids_1, ids_3, partial, near_b, end_b, end_upstream, upstream)


def forward_kernel(
    place_of, ids_1, ids_3, partial, near_b, end_b, tokens, gathered, proj, end_proj, held, sem
):
    half_slots = near_b.shape[0]
    other = (1 - place_of[1]) * half_slots
    depth, width = held.shape
    parts, rows, part_width = gathered.shape
    step = 256

    @pl.when(place_of[0] == 1)
    def work():
        load = pltpu.make_async_copy(partial, held, sem)
        load.start()
        load.wait()
        place_blocks(ids_1, other, near_b, held, None, half_slots)
        place_blocks(ids_3, other, end_b, held, None, half_slots)

        @pl.loop(0, width // step, unroll=2)
        def forward(n):
            c = pl.multiple_of(n * step, step)
            acc = jnp.zeros((rows, step), jnp.float32)
            for q in range(parts):
                acc += jnp.dot(
                    gathered[q],
                    held[q * part_width : (q + 1) * part_width, pl.ds(c, step)],
                    preferred_element_type=jnp.float32,
                )
            end_proj[:, pl.ds(c, step)] = acc.astype(end_proj.dtype)
            proj[:, pl.ds(c, step)] = jnp.dot(
                tokens[...], held[:, pl.ds(c, step)], preferred_element_type=jnp.float32
            ).astype(proj.dtype)


def project_forward(place_of, ids_1, ids_3, partial, near_b, end_b, tokens, gathered):
    depth, width = partial.shape
    rows = tokens.shape[0]
    out = jax.ShapeDtypeStruct((rows, width), jnp.bfloat16)
    return pl.pallas_call(
        forward_kernel,
        out_shape=(out, out),
        in_specs=[whole(pltpu.SMEM)] * 3 + [whole(pl.ANY)] + [whole()] * 4,
        out_specs=(whole(),) * 2,
        scratch_shapes=[pltpu.VMEM((depth, width), jnp.bfloat16), pltpu.SemaphoreType.DMA],
        compiler_params=pltpu.CompilerParams(vmem_limit_bytes=VMEM_LIMIT),
        cost_estimate=pl.CostEstimate(
            flops=rows * depth * width // 2, bytes_accessed=depth * width, transcendentals=0
        ),
        name="project_forward",
    )(place_of, ids_1, ids_3, partial, near_b, end_b, tokens, gathered)


def split_kernel(place_of, keep, *refs):
    x = place_of[2]
    own, give = refs[-2:]
    got = refs[:-2] if len(refs) > 3 else (refs[0].at[0], refs[0].at[1])
    for at in range(2):
        total = (keep[at].astype(jnp.float32) + got[at][...].astype(jnp.float32)).astype(own.dtype)

        @pl.when(x == at)
        def mine():
            own[...] = total

        @pl.when(x != at)
        def theirs():
            give[...] = total


def add_split(place_of, keep, *got):
    out = jax.ShapeDtypeStruct(keep.shape[1:], keep.dtype)
    return pl.pallas_call(
        split_kernel,
        out_shape=(out, out),
        in_specs=[whole(pltpu.SMEM), whole()] + [whole()] * len(got),
        out_specs=(whole(), whole()),
        compiler_params=pltpu.CompilerParams(vmem_limit_bytes=VMEM_LIMIT),
        cost_estimate=pl.CostEstimate(
            flops=keep.size, bytes_accessed=keep.size * 6, transcendentals=0
        ),
        name="add_split",
    )(place_of, keep, *got)


def assemble_kernel(place_of, own, by_core, by_tensor, by_both, full):
    x, c = place_of[2], place_of[3]
    width = own.shape[1]
    for ref, xx, cc in (
        (own, x, c), (by_core, x, 1 - c), (by_tensor, 1 - x, c), (by_both, 1 - x, 1 - c)
    ):
        at = pl.multiple_of((xx * 2 + cc) * width, width)
        full[:, pl.ds(at, width)] = ref[...]


def assemble(place_of, quarters):
    rows, width = quarters[0].shape
    return pl.pallas_call(
        assemble_kernel,
        out_shape=jax.ShapeDtypeStruct((rows, 4 * width), quarters[0].dtype),
        in_specs=[whole(pltpu.SMEM)] + [whole()] * 4,
        out_specs=whole(),
        compiler_params=pltpu.CompilerParams(vmem_limit_bytes=VMEM_LIMIT),
        cost_estimate=pl.CostEstimate(
            flops=0, bytes_accessed=rows * width * 16, transcendentals=0
        ),
        name="assemble",
    )(place_of, *quarters)


def line_grads_kernel(pairs_n, ids, *refs):
    refs = list(refs)
    pairs = []
    for k in range(pairs_n):
        x, d = refs.pop(0), refs.pop(0)
        if d.shape[0] > x.shape[-2]:
            rows, other = x.shape[-2], refs.pop(0)
            total_d = refs.pop()
            total_d[...] = d[rows:] + other[rows:]
            d = total_d
        pairs.append((x, d))
    start = refs.pop(0) if len(refs) == 2 else None
    (grads,) = refs
    slots, size = grads.shape[0], grads.shape[1]
    first = pairs[0][0]
    cols_n = pairs[0][1].shape[1] // size
    rows_n = first.shape[-1] // size * (first.shape[0] if len(first.shape) == 3 else 1)
    total = rows_n * cols_n
    group = math.gcd(slots, 8)

    @pl.loop(0, slots // group)
    def some(g):
        for s in [g * group + j for j in range(group)]:
            b = jnp.minimum(ids[s], total - 1)
            row = b // cols_n
            c = pl.ds(pl.multiple_of((b % cols_n) * size, size), size)
            acc = jnp.zeros((size, size), jnp.float32) if start is None else start[s].astype(jnp.float32)
            for x, d in pairs:
                per_part = x.shape[-1] // size
                at = pl.ds(pl.multiple_of((row % per_part) * size, size), size)
                acc += lax.dot_general(
                    x[row // per_part, :, at] if len(x.shape) == 3 else x[:, at],
                    d[:, c],
                    (((0,), (0,)), ((), ())),
                    preferred_element_type=jnp.float32,
                )
            grads[s] = jnp.where(ids[s] < total, acc, 0.0).astype(grads.dtype)


def line_grads(ids, pairs, start, size):
    slots = ids.shape[0]
    flat = [a for pair in pairs for a in pair] + ([] if start is None else [start])
    sums = [
        pltpu.VMEM((p[0].shape[-2], p[1].shape[1]), jnp.bfloat16) for p in pairs if len(p) == 3
    ]
    return pl.pallas_call(
        functools.partial(line_grads_kernel, len(pairs)),
        out_shape=jax.ShapeDtypeStruct((slots, size, size), jnp.bfloat16),
        in_specs=[whole(pltpu.SMEM)] + [whole()] * len(flat),
        out_specs=whole(),
        scratch_shapes=sums,
        compiler_params=pltpu.CompilerParams(vmem_limit_bytes=VMEM_LIMIT),
        cost_estimate=pl.CostEstimate(
            flops=512 * len(pairs) * slots * size * size,
            bytes_accessed=sum(2 * a.size for a in flat) + 2 * slots * size * size,
            transcendentals=0,
        ),
        name="line_grads",
    )(ids, *flat)


INWARD = ((0, 1), (3, 2))
OUTWARD = ((1, 0), (2, 3))
PAIRS = INWARD + OUTWARD
MIDDLE = ((1, 2), (2, 1))
SWAP = ((0, 1), (1, 0))


def ids_block(block_ids, size):
    rows = size * size // block_ids.shape[0]
    return jnp.broadcast_to(block_ids, (rows, block_ids.shape[0])).reshape(1, size, size)


def ids_of(piece, slots):
    return piece[-1, 0, :slots].astype(jnp.int32)


def line_body(tokens, upstream, blocks, block_ids):
    slots, size = blocks.shape[0], blocks.shape[1]
    rows, depth = tokens.shape
    width = upstream.shape[1]
    half_slots = slots // 2
    part_width = depth // 4
    at_z, half = lax.axis_index("dp"), lax.axis_index("groups")
    at_tensor, at_replica = lax.axis_index("tensor"), lax.axis_index("replica")
    middle = (at_z == 1) | (at_z == 2)
    place_of = jnp.stack([middle.astype(jnp.int32), half, at_tensor, at_replica])
    along = functools.partial(lax.ppermute, axis_name="dp")
    across = functools.partial(lax.ppermute, axis_name="groups", perm=SWAP)
    sideways = functools.partial(lax.ppermute, axis_name="tensor", perm=SWAP)
    cores = functools.partial(lax.ppermute, axis_name="replica", perm=SWAP)
    stage = lax.optimization_barrier

    mine = lax.dynamic_slice_in_dim(blocks, half * half_slots, half_slots, 0)
    mine = jnp.concatenate([mine, ids_block(block_ids, size).astype(jnp.bfloat16)])
    mine, late_blocks = stage((mine, blocks))

    near_a = along(mine, perm=INWARD)
    far_a = along(mine, perm=MIDDLE)
    other = lax.dynamic_slice_in_dim(late_blocks, (1 - half) * half_slots, half_slots, 0)
    part = lax.dynamic_slice_in_dim(tokens, lax.axis_index(INNER) * part_width, part_width, 1)
    both = jnp.concatenate([part, upstream])
    grads = line_grads(block_ids, ((tokens, upstream),), None, size)
    near_a, far_a, both, other, grads = stage((near_a, far_a, both, other, grads))

    end_a = along(near_a, perm=MIDDLE)
    far_b = across(far_a)
    both_1 = along(both, perm=PAIRS)
    both_1, end_a, far_b, both, other = stage((both_1, end_a, far_b, both, other))
    upstream_1 = both_1[rows:]

    near_b = along(other, perm=INWARD)
    end_b = across(end_a)
    both_2m = along(both, perm=MIDDLE)
    tokens_1 = lax.all_gather(both_1[:rows], INNER)
    ids_1, ids_2, ids_3 = (ids_of(piece, slots) for piece in (near_a, far_a, end_a))
    partial, turned = place_first(
        place_of, (block_ids, ids_1, ids_2, ids_3), (blocks, near_a, far_a, far_b, end_a), depth, width
    )
    near_b, end_b, both_2m, both_1, tokens_1, partial, turned = stage(
        (near_b, end_b, both_2m, both_1, tokens_1, partial, turned)
    )

    both_3m = along(both_1, perm=MIDDLE)
    both_2o = along(both_2m, perm=OUTWARD)
    last = (near_b, end_b)
    end_keep, own_keep, own_give, *end_give = project_back(
        place_of, ids_1, ids_3, turned, *last, upstream_1, upstream
    )
    end_keep, end_give = add_split(place_of, end_keep, *[cores(a) for a in end_give])
    end_keep, end_give, own_give, both_3m, both_2o = stage(
        (end_keep, end_give, own_give, both_3m, both_2o)
    )

    end_got = sideways(end_give)
    own_keep, own_give = add_split(place_of, own_keep, cores(own_give))
    both_3o = along(both_3m, perm=OUTWARD)
    tokens_2 = lax.all_gather(both_2m[:rows] + both_2o[:rows], INNER)
    proj, end_proj = project_forward(place_of, ids_1, ids_3, partial, *last, tokens, tokens_1)
    end_got, own_give, own_keep, proj, end_proj = stage(
        (end_got, own_give, own_keep, proj, end_proj)
    )

    sum_out = along(end_keep + end_got, perm=OUTWARD)
    own_got = sideways(own_give)
    grads = line_grads(block_ids, ((tokens_1, upstream_1),), grads, size)
    sum_out, own_got, both_3o, grads = stage((sum_out, own_got, both_3o, grads))

    tokens_3 = lax.all_gather(both_3m[:rows] + both_3o[:rows], INNER)
    quarter = jnp.where(middle, own_keep + own_got, sum_out)
    proj_out = along(end_proj, perm=OUTWARD)
    grads = line_grads(block_ids, ((tokens_2, both_2m, both_2o),), grads, size)
    by_tensor, by_core, grads = stage((sideways(quarter), cores(quarter), grads))
    by_both = cores(by_tensor)
    projected = jnp.where(middle, proj, proj_out)
    token_grad = assemble(place_of, (quarter, by_core, by_tensor, by_both))
    grads = line_grads(block_ids, ((tokens_3, both_3m, both_3o),), grads, size)
    return projected, token_grad, grads


def solution(mesh):
    line = tuple(mesh.shape[a] for a in ("groups", "dp", "tensor", "replica")) == (2, 4, 2, 2)
    return jax.shard_map(
        line_body if line else general_body,
        mesh=mesh,
        in_specs=(
            P(("groups", "dp"), None),
            P(("groups", "dp"), INNER),
            P(("dp",) + INNER, None, None),
            P(("dp",) + INNER),
        ),
        out_specs=(
            P(("groups", "dp"), INNER),
            P(("groups", "dp"), None),
            P(("groups", "dp") + INNER, None, None),
        ),
        check_vma=False,
    )
```

```python
import functools
import math

import jax
import jax.numpy as jnp
from jax import lax
from jax.experimental import pallas as pl
from jax.experimental.pallas import tpu as pltpu
from jax.sharding import PartitionSpec as P

VMEM_LIMIT = 60 * 1024 * 1024
INNER = ("tensor", "replica")


def whole(space=pltpu.VMEM):
    return pl.BlockSpec(memory_space=space)


def project_kernel(ids, blocks, tokens, upstream, proj, back, weight):
    slots, size = blocks.shape[0], blocks.shape[1]
    depth, width = weight.shape
    cols_n = width // size
    total = (depth // size) * cols_n
    weight[...] = jnp.zeros_like(weight)

    @pl.loop(0, slots, unroll=4)
    def place(s):
        b = ids[s]

        @pl.when(b < total)
        def put():
            r = pl.multiple_of((b // cols_n) * size, size)
            c = pl.multiple_of((b % cols_n) * size, size)
            weight[pl.ds(r, size), pl.ds(c, size)] = blocks[s]

    step = 256

    @pl.loop(0, width // step)
    def forward(n):
        c = pl.multiple_of(n * step, step)
        proj[:, pl.ds(c, step)] = jnp.dot(
            tokens[...], weight[:, pl.ds(c, step)], preferred_element_type=jnp.float32
        ).astype(proj.dtype)

    @pl.loop(0, depth // step, unroll=4)
    def backward(n):
        r = pl.multiple_of(n * step, step)
        back[:, pl.ds(r, step)] = lax.dot_general(
            upstream[...],
            weight[pl.ds(r, step), :],
            (((1,), (1,)), ((), ())),
            preferred_element_type=jnp.float32,
        ).astype(back.dtype)


def project(ids, blocks, tokens, upstream):
    rows, depth = tokens.shape
    width = upstream.shape[1]
    return pl.pallas_call(
        project_kernel,
        out_shape=(
            jax.ShapeDtypeStruct((rows, width), jnp.bfloat16),
            jax.ShapeDtypeStruct((rows, depth), jnp.bfloat16),
        ),
        in_specs=[whole(pltpu.SMEM), whole(), whole(), whole()],
        out_specs=(whole(), whole()),
        scratch_shapes=[pltpu.VMEM((depth, width), jnp.bfloat16)],
        compiler_params=pltpu.CompilerParams(vmem_limit_bytes=VMEM_LIMIT),
        cost_estimate=pl.CostEstimate(
            flops=4 * rows * depth * width,
            bytes_accessed=blocks.size * 2 + rows * (depth + width) * 4,
            transcendentals=0,
        ),
        name="project",
    )(ids, blocks, tokens, upstream)


def block_grad_kernel(ids, tokens, upstream, grads):
    slots, size = grads.shape[0], grads.shape[1]
    parts, slabs, _, part_width = tokens.shape
    cols_n = upstream.shape[2] // size
    per_part = part_width // size
    total = parts * per_part * cols_n

    @pl.loop(0, slots)
    def one(s):
        b = ids[s]

        @pl.when(b < total)
        def fill():
            row = b // cols_n
            part = row // per_part
            r = pl.multiple_of((row % per_part) * size, size)
            c = pl.multiple_of((b % cols_n) * size, size)
            acc = jnp.zeros((size, size), jnp.float32)
            for k in range(slabs):
                acc += lax.dot_general(
                    tokens[part, k, :, pl.ds(r, size)],
                    upstream[k, :, pl.ds(c, size)],
                    (((0,), (0,)), ((), ())),
                    preferred_element_type=jnp.float32,
                )
            grads[s] = acc.astype(grads.dtype)

        @pl.when(b >= total)
        def clear():
            grads[s] = jnp.zeros((size, size), grads.dtype)


def block_grads(ids, tokens, upstream, size):
    slots = ids.shape[0]
    parts, slabs, rows, part_width = tokens.shape
    return pl.pallas_call(
        block_grad_kernel,
        out_shape=jax.ShapeDtypeStruct((slots, size, size), jnp.bfloat16),
        in_specs=[whole(pltpu.SMEM), whole(), whole()],
        out_specs=whole(),
        compiler_params=pltpu.CompilerParams(vmem_limit_bytes=VMEM_LIMIT),
        cost_estimate=pl.CostEstimate(
            flops=2 * slots * slabs * rows * size * size,
            bytes_accessed=2 * (tokens.size + upstream.size + slots * size * size),
            transcendentals=0,
        ),
        name="block_grads",
    )(ids, tokens, upstream)


def general_body(tokens, upstream, blocks, block_ids):
    size = blocks.shape[1]
    all_blocks = lax.all_gather(blocks, "dp", axis=0, tiled=True)
    all_ids = lax.all_gather(block_ids, "dp", axis=0, tiled=True)
    proj, back = project(all_ids, all_blocks, tokens, upstream)
    terms = block_grads(all_ids, tokens[None, None], upstream[None], size)
    grads = lax.psum_scatter(terms, "dp", scatter_dimension=0, tiled=True)
    return proj, lax.psum(back, INNER), grads


def place_blocks(ids, first, blocks, weight, turned, slots):
    size = blocks.shape[1]
    depth, width = turned.shape[::-1] if weight is None else weight.shape
    cols_n = width // size
    total = (depth // size) * cols_n
    group = math.gcd(slots, 8)

    @pl.loop(0, slots // group)
    def place(g):
        some = [g * group + j for j in range(group)]
        flipped = [None if turned is None else blocks[s].T for s in some]
        for s, flip in zip(some, flipped):
            b = ids[first + s]

            @pl.when(b < total)
            def put(s=s, flip=flip, b=b):
                r = pl.multiple_of((b // cols_n) * size, size)
                c = pl.multiple_of((b % cols_n) * size, size)
                if weight is not None:
                    weight[pl.ds(r, size), pl.ds(c, size)] = blocks[s]
                if turned is not None:
                    turned[pl.ds(c, size), pl.ds(r, size)] = flip


def place_kernel(
    place_of, ids_0, ids_1, ids_2, ids_3, own, near_a, far_a, far_b, end_a, weight, turned
):
    is_middle, half = place_of[0], place_of[1]
    half_slots = far_b.shape[0] - 1
    mine, other = half * half_slots, (1 - half) * half_slots

    @pl.when(is_middle == 1)
    def work():
        weight[...] = jnp.zeros_like(weight)
        turned[...] = jnp.zeros_like(turned)
        place_blocks(ids_0, 0, own, weight, turned, own.shape[0])
        place_blocks(ids_1, mine, near_a, weight, turned, half_slots)
        place_blocks(ids_2, mine, far_a, weight, turned, half_slots)
        place_blocks(ids_2, other, far_b, weight, turned, half_slots)
        place_blocks(ids_3, mine, end_a, weight, turned, half_slots)


def place_first(place_of, ids, pieces, depth, width):
    return pl.pallas_call(
        place_kernel,
        out_shape=(
            jax.ShapeDtypeStruct((depth, width), jnp.bfloat16),
            jax.ShapeDtypeStruct((width, depth), jnp.bfloat16),
        ),
        in_specs=[whole(pltpu.SMEM)] * 5 + [whole()] * 5,
        out_specs=(whole(), whole()),
        compiler_params=pltpu.CompilerParams(vmem_limit_bytes=VMEM_LIMIT),
        cost_estimate=pl.CostEstimate(
            flops=0, bytes_accessed=depth * width * 6, transcendentals=0
        ),
        name="place_first",
    )(place_of, *ids, *pieces)


def back_kernel(
    place_of, ids_1, ids_3, partial, near_b, end_b, end_upstream, upstream,
    end_keep, own_keep, own_give, end_give_0, end_give_1, held, sources, sem,
):
    half_slots = near_b.shape[0]
    other = (1 - place_of[1]) * half_slots
    rows, width = upstream.shape
    step = 256
    per_part = end_keep.shape[2] // step

    @pl.when(place_of[0] == 1)
    def work():
        load = pltpu.make_async_copy(partial, held, sem)
        load.start()
        sources[:rows] = end_upstream[...]
        sources[rows:] = upstream[...]
        load.wait()
        place_blocks(ids_1, other, near_b, None, held, half_slots)
        place_blocks(ids_3, other, end_b, None, held, half_slots)

        def column(part, end_target, own_target):
            @pl.loop(0, per_part, unroll=2)
            def backward(n):
                at = pl.multiple_of(n * step, step)
                result = jnp.dot(
                    sources[...],
                    held[:, pl.ds(pl.multiple_of(part * per_part * step + at, step), step)],
                    preferred_element_type=jnp.float32,
                ).astype(own_target.dtype)
                end_target[:, pl.ds(at, step)] = result[:rows]
                own_target[:, pl.ds(at, step)] = result[rows:]

        for x, end_give in enumerate((end_give_0, end_give_1)):
            column(2 * x + place_of[3], end_keep.at[x], own_keep.at[x])
            column(2 * x + 1 - place_of[3], end_give, own_give.at[x])


def project_back(place_of, ids_1, ids_3, partial, near_b, end_b, end_upstream, upstream):
    width, depth = partial.shape
    rows = upstream.shape[0]
    quarter = jax.ShapeDtypeStruct((rows, depth // 4), jnp.bfloat16)
    half = jax.ShapeDtypeStruct((2, rows, depth // 4), jnp.bfloat16)
    return pl.pallas_call(
        back_kernel,
        out_shape=(half, half, half, quarter, quarter),
        in_specs=[whole(pltpu.SMEM)] * 3 + [whole(pl.ANY)] + [whole()] * 4,
        out_specs=(whole(),) * 5,
        scratch_shapes=[
            pltpu.VMEM((width, depth), jnp.bfloat16),
            pltpu.VMEM((2 * rows, width), jnp.bfloat16),
            pltpu.SemaphoreType.DMA,
        ],
        compiler_params=pltpu.CompilerParams(vmem_limit_bytes=VMEM_LIMIT),
        cost_estimate=pl.CostEstimate(
            flops=4 * rows * depth * width,
            bytes_accessed=depth * width * 2 + rows * (depth + width) * 4,
            transcendentals=0,
        ),
        name="project_back",
    )(place_of, ids_1, ids_3, partial, near_b, end_b, end_upstream, upstream)


def forward_kernel(
    place_of, ids_1, ids_3, partial, near_b, end_b, tokens, gathered, proj, end_proj, held, sem
):
    half_slots = near_b.shape[0]
    other = (1 - place_of[1]) * half_slots
    depth, width = held.shape
    parts, rows, part_width = gathered.shape
    step = 256

    @pl.when(place_of[0] == 1)
    def work():
        load = pltpu.make_async_copy(partial, held, sem)
        load.start()
        load.wait()
        place_blocks(ids_1, other, near_b, held, None, half_slots)
        place_blocks(ids_3, other, end_b, held, None, half_slots)

        @pl.loop(0, width // step, unroll=2)
        def forward(n):
            c = pl.multiple_of(n * step, step)
            acc = jnp.zeros((rows, step), jnp.float32)
            for q in range(parts):
                acc += jnp.dot(
                    gathered[q],
                    held[q * part_width : (q + 1) * part_width, pl.ds(c, step)],
                    preferred_element_type=jnp.float32,
                )
            end_proj[:, pl.ds(c, step)] = acc.astype(end_proj.dtype)
            proj[:, pl.ds(c, step)] = jnp.dot(
                tokens[...], held[:, pl.ds(c, step)], preferred_element_type=jnp.float32
            ).astype(proj.dtype)


def project_forward(place_of, ids_1, ids_3, partial, near_b, end_b, tokens, gathered):
    depth, width = partial.shape
    rows = tokens.shape[0]
    out = jax.ShapeDtypeStruct((rows, width), jnp.bfloat16)
    return pl.pallas_call(
        forward_kernel,
        out_shape=(out, out),
        in_specs=[whole(pltpu.SMEM)] * 3 + [whole(pl.ANY)] + [whole()] * 4,
        out_specs=(whole(),) * 2,
        scratch_shapes=[pltpu.VMEM((depth, width), jnp.bfloat16), pltpu.SemaphoreType.DMA],
        compiler_params=pltpu.CompilerParams(vmem_limit_bytes=VMEM_LIMIT),
        cost_estimate=pl.CostEstimate(
            flops=rows * depth * width // 2, bytes_accessed=depth * width, transcendentals=0
        ),
        name="project_forward",
    )(place_of, ids_1, ids_3, partial, near_b, end_b, tokens, gathered)


def split_kernel(place_of, keep, *refs):
    x = place_of[2]
    own, give = refs[-2:]
    got = refs[:-2] if len(refs) > 3 else (refs[0].at[0], refs[0].at[1])
    for at in range(2):
        total = (keep[at].astype(jnp.float32) + got[at][...].astype(jnp.float32)).astype(own.dtype)

        @pl.when(x == at)
        def mine():
            own[...] = total

        @pl.when(x != at)
        def theirs():
            give[...] = total


def add_split(place_of, keep, *got):
    out = jax.ShapeDtypeStruct(keep.shape[1:], keep.dtype)
    return pl.pallas_call(
        split_kernel,
        out_shape=(out, out),
        in_specs=[whole(pltpu.SMEM), whole()] + [whole()] * len(got),
        out_specs=(whole(), whole()),
        compiler_params=pltpu.CompilerParams(vmem_limit_bytes=VMEM_LIMIT),
        cost_estimate=pl.CostEstimate(
            flops=keep.size, bytes_accessed=keep.size * 6, transcendentals=0
        ),
        name="add_split",
    )(place_of, keep, *got)


def assemble_kernel(place_of, own, by_core, by_tensor, by_both, full):
    x, c = place_of[2], place_of[3]
    width = own.shape[1]
    for ref, xx, cc in (
        (own, x, c), (by_core, x, 1 - c), (by_tensor, 1 - x, c), (by_both, 1 - x, 1 - c)
    ):
        at = pl.multiple_of((xx * 2 + cc) * width, width)
        full[:, pl.ds(at, width)] = ref[...]


def assemble(place_of, quarters):
    rows, width = quarters[0].shape
    return pl.pallas_call(
        assemble_kernel,
        out_shape=jax.ShapeDtypeStruct((rows, 4 * width), quarters[0].dtype),
        in_specs=[whole(pltpu.SMEM)] + [whole()] * 4,
        out_specs=whole(),
        compiler_params=pltpu.CompilerParams(vmem_limit_bytes=VMEM_LIMIT),
        cost_estimate=pl.CostEstimate(
            flops=0, bytes_accessed=rows * width * 16, transcendentals=0
        ),
        name="assemble",
    )(place_of, *quarters)


def line_grads_kernel(pairs_n, ids, *refs):
    refs = list(refs)
    pairs = []
    for k in range(pairs_n):
        x, d = refs.pop(0), refs.pop(0)
        if d.shape[0] > x.shape[-2]:
            rows, other = x.shape[-2], refs.pop(0)
            total_d = refs.pop()
            total_d[...] = d[rows:] + other[rows:]
            d = total_d
        pairs.append((x, d))
    start = refs.pop(0) if len(refs) == 2 else None
    (grads,) = refs
    slots, size = grads.shape[0], grads.shape[1]
    first = pairs[0][0]
    cols_n = pairs[0][1].shape[1] // size
    rows_n = first.shape[-1] // size * (first.shape[0] if len(first.shape) == 3 else 1)
    total = rows_n * cols_n
    group = math.gcd(slots, 8)

    @pl.loop(0, slots // group)
    def some(g):
        for s in [g * group + j for j in range(group)]:
            b = jnp.minimum(ids[s], total - 1)
            row = b // cols_n
            c = pl.ds(pl.multiple_of((b % cols_n) * size, size), size)
            acc = jnp.zeros((size, size), jnp.float32) if start is None else start[s].astype(jnp.float32)
            for x, d in pairs:
                per_part = x.shape[-1] // size
                at = pl.ds(pl.multiple_of((row % per_part) * size, size), size)
                acc += lax.dot_general(
                    x[row // per_part, :, at] if len(x.shape) == 3 else x[:, at],
                    d[:, c],
                    (((0,), (0,)), ((), ())),
                    preferred_element_type=jnp.float32,
                )
            grads[s] = jnp.where(ids[s] < total, acc, 0.0).astype(grads.dtype)


def line_grads(ids, pairs, start, size):
    slots = ids.shape[0]
    flat = [a for pair in pairs for a in pair] + ([] if start is None else [start])
    sums = [
        pltpu.VMEM((p[0].shape[-2], p[1].shape[1]), jnp.bfloat16) for p in pairs if len(p) == 3
    ]
    return pl.pallas_call(
        functools.partial(line_grads_kernel, len(pairs)),
        out_shape=jax.ShapeDtypeStruct((slots, size, size), jnp.bfloat16),
        in_specs=[whole(pltpu.SMEM)] + [whole()] * len(flat),
        out_specs=whole(),
        scratch_shapes=sums,
        compiler_params=pltpu.CompilerParams(vmem_limit_bytes=VMEM_LIMIT),
        cost_estimate=pl.CostEstimate(
            flops=512 * len(pairs) * slots * size * size,
            bytes_accessed=sum(2 * a.size for a in flat) + 2 * slots * size * size,
            transcendentals=0,
        ),
        name="line_grads",
    )(ids, *flat)


INWARD = ((0, 1), (3, 2))
OUTWARD = ((1, 0), (2, 3))
PAIRS = INWARD + OUTWARD
MIDDLE = ((1, 2), (2, 1))
SWAP = ((0, 1), (1, 0))


def ids_block(block_ids, size):
    rows = size * size // block_ids.shape[0]
    return jnp.broadcast_to(block_ids, (rows, block_ids.shape[0])).reshape(1, size, size)


def ids_of(piece, slots):
    return piece[-1, 0, :slots].astype(jnp.int32)


def line_body(tokens, upstream, blocks, block_ids):
    slots, size = blocks.shape[0], blocks.shape[1]
    rows, depth = tokens.shape
    width = upstream.shape[1]
    half_slots = slots // 2
    part_width = depth // 4
    at_z, half = lax.axis_index("dp"), lax.axis_index("groups")
    at_tensor, at_replica = lax.axis_index("tensor"), lax.axis_index("replica")
    middle = (at_z == 1) | (at_z == 2)
    place_of = jnp.stack([middle.astype(jnp.int32), half, at_tensor, at_replica])
    along = functools.partial(lax.ppermute, axis_name="dp")
    across = functools.partial(lax.ppermute, axis_name="groups", perm=SWAP)
    sideways = functools.partial(lax.ppermute, axis_name="tensor", perm=SWAP)
    cores = functools.partial(lax.ppermute, axis_name="replica", perm=SWAP)
    stage = lax.optimization_barrier

    mine = lax.dynamic_slice_in_dim(blocks, half * half_slots, half_slots, 0)
    mine = jnp.concatenate([mine, ids_block(block_ids, size).astype(jnp.bfloat16)])
    mine, late_blocks = stage((mine, blocks))

    near_a = along(mine, perm=INWARD)
    far_a = along(mine, perm=MIDDLE)
    other = lax.dynamic_slice_in_dim(late_blocks, (1 - half) * half_slots, half_slots, 0)
    part = lax.dynamic_slice_in_dim(tokens, lax.axis_index(INNER) * part_width, part_width, 1)
    both = jnp.concatenate([part, upstream])
    grads = line_grads(block_ids, ((tokens, upstream),), None, size)
    near_a, far_a, both, other, grads = stage((near_a, far_a, both, other, grads))

    end_a = along(near_a, perm=MIDDLE)
    far_b = across(far_a)
    both_1 = along(both, perm=PAIRS)
    both_1, end_a, far_b, both, other = stage((both_1, end_a, far_b, both, other))
    upstream_1 = both_1[rows:]

    near_b = along(other, perm=INWARD)
    end_b = across(end_a)
    both_2m = along(both, perm=MIDDLE)
    tokens_1 = lax.all_gather(both_1[:rows], INNER)
    ids_1, ids_2, ids_3 = (ids_of(piece, slots) for piece in (near_a, far_a, end_a))
    partial, turned = place_first(
        place_of, (block_ids, ids_1, ids_2, ids_3), (blocks, near_a, far_a, far_b, end_a), depth, width
    )
    near_b, end_b, both_2m, both_1, tokens_1, partial, turned = stage(
        (near_b, end_b, both_2m, both_1, tokens_1, partial, turned)
    )

    both_3m = along(both_1, perm=MIDDLE)
    both_2o = along(both_2m, perm=OUTWARD)
    last = (near_b, end_b)
    end_keep, own_keep, own_give, *end_give = project_back(
        place_of, ids_1, ids_3, turned, *last, upstream_1, upstream
    )
    end_keep, end_give = add_split(place_of, end_keep, *[cores(a) for a in end_give])
    end_keep, end_give, own_give, both_3m, both_2o = stage(
        (end_keep, end_give, own_give, both_3m, both_2o)
    )

    end_got = sideways(end_give)
    own_keep, own_give = add_split(place_of, own_keep, cores(own_give))
    both_3o = along(both_3m, perm=OUTWARD)
    tokens_2 = lax.all_gather(both_2m[:rows] + both_2o[:rows], INNER)
    proj, end_proj = project_forward(place_of, ids_1, ids_3, partial, *last, tokens, tokens_1)
    end_got, own_give, own_keep, proj, end_proj = stage(
        (end_got, own_give, own_keep, proj, end_proj)
    )

    sum_out = along(end_keep + end_got, perm=OUTWARD)
    own_got = sideways(own_give)
    part_3, upstream_1 = stage((both_3m[:rows] + both_3o[:rows], upstream_1))
    tokens_3 = lax.all_gather(part_3, INNER)
    grads = line_grads(block_ids, ((tokens_1, upstream_1),), grads, size)
    sum_out, own_got, grads = stage((sum_out, own_got, grads))

    quarter = jnp.where(middle, own_keep + own_got, sum_out)
    proj_out = along(end_proj, perm=OUTWARD)
    grads = line_grads(block_ids, ((tokens_2, both_2m, both_2o),), grads, size)
    by_tensor, by_core, grads = stage((sideways(quarter), cores(quarter), grads))
    by_both = cores(by_tensor)
    projected = jnp.where(middle, proj, proj_out)
    token_grad = assemble(place_of, (quarter, by_core, by_tensor, by_both))
    grads = line_grads(block_ids, ((tokens_3, both_3m, both_3o),), grads, size)
    return projected, token_grad, grads


def solution(mesh):
    line = tuple(mesh.shape[a] for a in ("groups", "dp", "tensor", "replica")) == (2, 4, 2, 2)
    return jax.shard_map(
        line_body if line else general_body,
        mesh=mesh,
        in_specs=(
            P(("groups", "dp"), None),
            P(("groups", "dp"), INNER),
            P(("dp",) + INNER, None, None),
            P(("dp",) + INNER),
        ),
        out_specs=(
            P(("groups", "dp"), INNER),
            P(("groups", "dp"), None),
            P(("groups", "dp") + INNER, None, None),
        ),
        check_vma=False,
    )
```

```python
import functools
import math

import jax
import jax.numpy as jnp
from jax import lax
from jax.experimental import pallas as pl
from jax.experimental.pallas import tpu as pltpu
from jax.sharding import PartitionSpec as P

VMEM_LIMIT = 60 * 1024 * 1024
INNER = ("tensor", "replica")


def whole(space=pltpu.VMEM):
    return pl.BlockSpec(memory_space=space)


def project_kernel(ids, blocks, tokens, upstream, proj, back, weight):
    slots, size = blocks.shape[0], blocks.shape[1]
    depth, width = weight.shape
    cols_n = width // size
    total = (depth // size) * cols_n
    weight[...] = jnp.zeros_like(weight)

    @pl.loop(0, slots, unroll=4)
    def place(s):
        b = ids[s]

        @pl.when(b < total)
        def put():
            r = pl.multiple_of((b // cols_n) * size, size)
            c = pl.multiple_of((b % cols_n) * size, size)
            weight[pl.ds(r, size), pl.ds(c, size)] = blocks[s]

    step = 256

    @pl.loop(0, width // step)
    def forward(n):
        c = pl.multiple_of(n * step, step)
        proj[:, pl.ds(c, step)] = jnp.dot(
            tokens[...], weight[:, pl.ds(c, step)], preferred_element_type=jnp.float32
        ).astype(proj.dtype)

    @pl.loop(0, depth // step, unroll=4)
    def backward(n):
        r = pl.multiple_of(n * step, step)
        back[:, pl.ds(r, step)] = lax.dot_general(
            upstream[...],
            weight[pl.ds(r, step), :],
            (((1,), (1,)), ((), ())),
            preferred_element_type=jnp.float32,
        ).astype(back.dtype)


def project(ids, blocks, tokens, upstream):
    rows, depth = tokens.shape
    width = upstream.shape[1]
    return pl.pallas_call(
        project_kernel,
        out_shape=(
            jax.ShapeDtypeStruct((rows, width), jnp.bfloat16),
            jax.ShapeDtypeStruct((rows, depth), jnp.bfloat16),
        ),
        in_specs=[whole(pltpu.SMEM), whole(), whole(), whole()],
        out_specs=(whole(), whole()),
        scratch_shapes=[pltpu.VMEM((depth, width), jnp.bfloat16)],
        compiler_params=pltpu.CompilerParams(vmem_limit_bytes=VMEM_LIMIT),
        cost_estimate=pl.CostEstimate(
            flops=4 * rows * depth * width,
            bytes_accessed=blocks.size * 2 + rows * (depth + width) * 4,
            transcendentals=0,
        ),
        name="project",
    )(ids, blocks, tokens, upstream)


def block_grad_kernel(ids, tokens, upstream, grads):
    slots, size = grads.shape[0], grads.shape[1]
    parts, slabs, _, part_width = tokens.shape
    cols_n = upstream.shape[2] // size
    per_part = part_width // size
    total = parts * per_part * cols_n

    @pl.loop(0, slots)
    def one(s):
        b = ids[s]

        @pl.when(b < total)
        def fill():
            row = b // cols_n
            part = row // per_part
            r = pl.multiple_of((row % per_part) * size, size)
            c = pl.multiple_of((b % cols_n) * size, size)
            acc = jnp.zeros((size, size), jnp.float32)
            for k in range(slabs):
                acc += lax.dot_general(
                    tokens[part, k, :, pl.ds(r, size)],
                    upstream[k, :, pl.ds(c, size)],
                    (((0,), (0,)), ((), ())),
                    preferred_element_type=jnp.float32,
                )
            grads[s] = acc.astype(grads.dtype)

        @pl.when(b >= total)
        def clear():
            grads[s] = jnp.zeros((size, size), grads.dtype)


def block_grads(ids, tokens, upstream, size):
    slots = ids.shape[0]
    parts, slabs, rows, part_width = tokens.shape
    return pl.pallas_call(
        block_grad_kernel,
        out_shape=jax.ShapeDtypeStruct((slots, size, size), jnp.bfloat16),
        in_specs=[whole(pltpu.SMEM), whole(), whole()],
        out_specs=whole(),
        compiler_params=pltpu.CompilerParams(vmem_limit_bytes=VMEM_LIMIT),
        cost_estimate=pl.CostEstimate(
            flops=2 * slots * slabs * rows * size * size,
            bytes_accessed=2 * (tokens.size + upstream.size + slots * size * size),
            transcendentals=0,
        ),
        name="block_grads",
    )(ids, tokens, upstream)


def general_body(tokens, upstream, blocks, block_ids):
    size = blocks.shape[1]
    all_blocks = lax.all_gather(blocks, "dp", axis=0, tiled=True)
    all_ids = lax.all_gather(block_ids, "dp", axis=0, tiled=True)
    proj, back = project(all_ids, all_blocks, tokens, upstream)
    terms = block_grads(all_ids, tokens[None, None], upstream[None], size)
    grads = lax.psum_scatter(terms, "dp", scatter_dimension=0, tiled=True)
    return proj, lax.psum(back, INNER), grads


def place_blocks(ids, first, blocks, weight, turned, slots):
    size = blocks.shape[1]
    depth, width = turned.shape[::-1] if weight is None else weight.shape
    cols_n = width // size
    total = (depth // size) * cols_n
    group = math.gcd(slots, 8)

    @pl.loop(0, slots // group)
    def place(g):
        some = [g * group + j for j in range(group)]
        flipped = [None if turned is None else blocks[s].T for s in some]
        for s, flip in zip(some, flipped):
            b = ids[first + s]

            @pl.when(b < total)
            def put(s=s, flip=flip, b=b):
                r = pl.multiple_of((b // cols_n) * size, size)
                c = pl.multiple_of((b % cols_n) * size, size)
                if weight is not None:
                    weight[pl.ds(r, size), pl.ds(c, size)] = blocks[s]
                if turned is not None:
                    turned[pl.ds(c, size), pl.ds(r, size)] = flip


def place_kernel(
    place_of, ids_0, ids_1, ids_2, ids_3, own, near_a, far_a, far_b, end_a, weight, turned
):
    is_middle, half = place_of[0], place_of[1]
    half_slots = far_b.shape[0] - 1
    mine, other = half * half_slots, (1 - half) * half_slots

    @pl.when(is_middle == 1)
    def work():
        weight[...] = jnp.zeros_like(weight)
        turned[...] = jnp.zeros_like(turned)
        place_blocks(ids_0, 0, own, weight, turned, own.shape[0])
        place_blocks(ids_1, mine, near_a, weight, turned, half_slots)
        place_blocks(ids_2, mine, far_a, weight, turned, half_slots)
        place_blocks(ids_2, other, far_b, weight, turned, half_slots)
        place_blocks(ids_3, mine, end_a, weight, turned, half_slots)


def place_first(place_of, ids, pieces, depth, width):
    return pl.pallas_call(
        place_kernel,
        out_shape=(
            jax.ShapeDtypeStruct((depth, width), jnp.bfloat16),
            jax.ShapeDtypeStruct((width, depth), jnp.bfloat16),
        ),
        in_specs=[whole(pltpu.SMEM)] * 5 + [whole()] * 5,
        out_specs=(whole(), whole()),
        compiler_params=pltpu.CompilerParams(vmem_limit_bytes=VMEM_LIMIT),
        cost_estimate=pl.CostEstimate(
            flops=0, bytes_accessed=depth * width * 6, transcendentals=0
        ),
        name="place_first",
    )(place_of, *ids, *pieces)


def back_kernel(
    place_of, ids_1, ids_3, partial, near_b, end_b, end_upstream, upstream,
    end_keep, own_keep, own_give, end_give_0, end_give_1, held, sources, sem,
):
    half_slots = near_b.shape[0]
    other = (1 - place_of[1]) * half_slots
    rows, width = upstream.shape
    step = 256
    per_part = end_keep.shape[2] // step

    @pl.when(place_of[0] == 1)
    def work():
        load = pltpu.make_async_copy(partial, held, sem)
        load.start()
        sources[:rows] = end_upstream[...]
        sources[rows:] = upstream[...]
        load.wait()
        place_blocks(ids_1, other, near_b, None, held, half_slots)
        place_blocks(ids_3, other, end_b, None, held, half_slots)

        def column(part, end_target, own_target):
            @pl.loop(0, per_part, unroll=2)
            def backward(n):
                at = pl.multiple_of(n * step, step)
                result = jnp.dot(
                    sources[...],
                    held[:, pl.ds(pl.multiple_of(part * per_part * step + at, step), step)],
                    preferred_element_type=jnp.float32,
                ).astype(own_target.dtype)
                end_target[:, pl.ds(at, step)] = result[:rows]
                own_target[:, pl.ds(at, step)] = result[rows:]

        for x, end_give in enumerate((end_give_0, end_give_1)):
            column(2 * x + place_of[3], end_keep.at[x], own_keep.at[x])
            column(2 * x + 1 - place_of[3], end_give, own_give.at[x])


def project_back(place_of, ids_1, ids_3, partial, near_b, end_b, end_upstream, upstream):
    width, depth = partial.shape
    rows = upstream.shape[0]
    quarter = jax.ShapeDtypeStruct((rows, depth // 4), jnp.bfloat16)
    half = jax.ShapeDtypeStruct((2, rows, depth // 4), jnp.bfloat16)
    return pl.pallas_call(
        back_kernel,
        out_shape=(half, half, half, quarter, quarter),
        in_specs=[whole(pltpu.SMEM)] * 3 + [whole(pl.ANY)] + [whole()] * 4,
        out_specs=(whole(),) * 5,
        scratch_shapes=[
            pltpu.VMEM((width, depth), jnp.bfloat16),
            pltpu.VMEM((2 * rows, width), jnp.bfloat16),
            pltpu.SemaphoreType.DMA,
        ],
        compiler_params=pltpu.CompilerParams(vmem_limit_bytes=VMEM_LIMIT),
        cost_estimate=pl.CostEstimate(
            flops=4 * rows * depth * width,
            bytes_accessed=depth * width * 2 + rows * (depth + width) * 4,
            transcendentals=0,
        ),
        name="project_back",
    )(place_of, ids_1, ids_3, partial, near_b, end_b, end_upstream, upstream)


def forward_kernel(
    place_of, ids_1, ids_3, partial, near_b, end_b, tokens, gathered, proj, end_proj, held, sem
):
    half_slots = near_b.shape[0]
    other = (1 - place_of[1]) * half_slots
    depth, width = held.shape
    parts, rows, part_width = gathered.shape
    step = 256

    @pl.when(place_of[0] == 1)
    def work():
        load = pltpu.make_async_copy(partial, held, sem)
        load.start()
        load.wait()
        place_blocks(ids_1, other, near_b, held, None, half_slots)
        place_blocks(ids_3, other, end_b, held, None, half_slots)

        @pl.loop(0, width // step, unroll=2)
        def forward(n):
            c = pl.multiple_of(n * step, step)
            acc = jnp.zeros((rows, step), jnp.float32)
            for q in range(parts):
                acc += jnp.dot(
                    gathered[q],
                    held[q * part_width : (q + 1) * part_width, pl.ds(c, step)],
                    preferred_element_type=jnp.float32,
                )
            end_proj[:, pl.ds(c, step)] = acc.astype(end_proj.dtype)
            proj[:, pl.ds(c, step)] = jnp.dot(
                tokens[...], held[:, pl.ds(c, step)], preferred_element_type=jnp.float32
            ).astype(proj.dtype)


def project_forward(place_of, ids_1, ids_3, partial, near_b, end_b, tokens, gathered):
    depth, width = partial.shape
    rows = tokens.shape[0]
    out = jax.ShapeDtypeStruct((rows, width), jnp.bfloat16)
    return pl.pallas_call(
        forward_kernel,
        out_shape=(out, out),
        in_specs=[whole(pltpu.SMEM)] * 3 + [whole(pl.ANY)] + [whole()] * 4,
        out_specs=(whole(),) * 2,
        scratch_shapes=[pltpu.VMEM((depth, width), jnp.bfloat16), pltpu.SemaphoreType.DMA],
        compiler_params=pltpu.CompilerParams(vmem_limit_bytes=VMEM_LIMIT),
        cost_estimate=pl.CostEstimate(
            flops=rows * depth * width // 2, bytes_accessed=depth * width, transcendentals=0
        ),
        name="project_forward",
    )(place_of, ids_1, ids_3, partial, near_b, end_b, tokens, gathered)


def split_kernel(place_of, keep, *refs):
    x = place_of[2]
    own, give = refs[-2:]
    got = refs[:-2] if len(refs) > 3 else (refs[0].at[0], refs[0].at[1])
    for at in range(2):
        total = (keep[at].astype(jnp.float32) + got[at][...].astype(jnp.float32)).astype(own.dtype)

        @pl.when(x == at)
        def mine():
            own[...] = total

        @pl.when(x != at)
        def theirs():
            give[...] = total


def add_split(place_of, keep, *got):
    out = jax.ShapeDtypeStruct(keep.shape[1:], keep.dtype)
    return pl.pallas_call(
        split_kernel,
        out_shape=(out, out),
        in_specs=[whole(pltpu.SMEM), whole()] + [whole()] * len(got),
        out_specs=(whole(), whole()),
        compiler_params=pltpu.CompilerParams(vmem_limit_bytes=VMEM_LIMIT),
        cost_estimate=pl.CostEstimate(
            flops=keep.size, bytes_accessed=keep.size * 6, transcendentals=0
        ),
        name="add_split",
    )(place_of, keep, *got)


def assemble_kernel(place_of, own, by_core, by_tensor, by_both, full):
    x, c = place_of[2], place_of[3]
    width = own.shape[1]
    for ref, xx, cc in (
        (own, x, c), (by_core, x, 1 - c), (by_tensor, 1 - x, c), (by_both, 1 - x, 1 - c)
    ):
        at = pl.multiple_of((xx * 2 + cc) * width, width)
        full[:, pl.ds(at, width)] = ref[...]


def assemble(place_of, quarters):
    rows, width = quarters[0].shape
    return pl.pallas_call(
        assemble_kernel,
        out_shape=jax.ShapeDtypeStruct((rows, 4 * width), quarters[0].dtype),
        in_specs=[whole(pltpu.SMEM)] + [whole()] * 4,
        out_specs=whole(),
        compiler_params=pltpu.CompilerParams(vmem_limit_bytes=VMEM_LIMIT),
        cost_estimate=pl.CostEstimate(
            flops=0, bytes_accessed=rows * width * 16, transcendentals=0
        ),
        name="assemble",
    )(place_of, *quarters)


def line_grads_kernel(pairs_n, ids, *refs):
    refs = list(refs)
    pairs = []
    for k in range(pairs_n):
        x, d = refs.pop(0), refs.pop(0)
        if d.shape[0] > x.shape[-2]:
            rows, other = x.shape[-2], refs.pop(0)
            total_d = refs.pop()
            total_d[...] = d[rows:] + other[other.shape[0] - rows :]
            d = total_d
        pairs.append((x, d))
    start = refs.pop(0) if len(refs) == 2 else None
    (grads,) = refs
    slots, size = grads.shape[0], grads.shape[1]
    first = pairs[0][0]
    cols_n = pairs[0][1].shape[1] // size
    rows_n = first.shape[-1] // size * (first.shape[0] if len(first.shape) == 3 else 1)
    total = rows_n * cols_n
    group = math.gcd(slots, 8)

    @pl.loop(0, slots // group)
    def some(g):
        for s in [g * group + j for j in range(group)]:
            b = jnp.minimum(ids[s], total - 1)
            row = b // cols_n
            c = pl.ds(pl.multiple_of((b % cols_n) * size, size), size)
            acc = jnp.zeros((size, size), jnp.float32) if start is None else start[s].astype(jnp.float32)
            for x, d in pairs:
                per_part = x.shape[-1] // size
                at = pl.ds(pl.multiple_of((row % per_part) * size, size), size)
                acc += lax.dot_general(
                    x[row // per_part, :, at] if len(x.shape) == 3 else x[:, at],
                    d[:, c],
                    (((0,), (0,)), ((), ())),
                    preferred_element_type=jnp.float32,
                )
            grads[s] = jnp.where(ids[s] < total, acc, 0.0).astype(grads.dtype)


def line_grads(ids, pairs, start, size):
    slots = ids.shape[0]
    flat = [a for pair in pairs for a in pair] + ([] if start is None else [start])
    sums = [
        pltpu.VMEM((p[0].shape[-2], p[1].shape[1]), jnp.bfloat16) for p in pairs if len(p) == 3
    ]
    return pl.pallas_call(
        functools.partial(line_grads_kernel, len(pairs)),
        out_shape=jax.ShapeDtypeStruct((slots, size, size), jnp.bfloat16),
        in_specs=[whole(pltpu.SMEM)] + [whole()] * len(flat),
        out_specs=whole(),
        scratch_shapes=sums,
        compiler_params=pltpu.CompilerParams(vmem_limit_bytes=VMEM_LIMIT),
        cost_estimate=pl.CostEstimate(
            flops=512 * len(pairs) * slots * size * size,
            bytes_accessed=sum(2 * a.size for a in flat) + 2 * slots * size * size,
            transcendentals=0,
        ),
        name="line_grads",
    )(ids, *flat)


INWARD = ((0, 1), (3, 2))
OUTWARD = ((1, 0), (2, 3))
PAIRS = INWARD + OUTWARD
MIDDLE = ((1, 2), (2, 1))
SWAP = ((0, 1), (1, 0))


def ids_block(block_ids, size):
    rows = size * size // block_ids.shape[0]
    return jnp.broadcast_to(block_ids, (rows, block_ids.shape[0])).reshape(1, size, size)


def ids_of(piece, slots):
    return piece[-1, 0, :slots].astype(jnp.int32)


def line_body(tokens, upstream, blocks, block_ids):
    slots, size = blocks.shape[0], blocks.shape[1]
    rows, depth = tokens.shape
    width = upstream.shape[1]
    half_slots = slots // 2
    part_width = depth // 4
    at_z, half = lax.axis_index("dp"), lax.axis_index("groups")
    at_tensor, at_replica = lax.axis_index("tensor"), lax.axis_index("replica")
    middle = (at_z == 1) | (at_z == 2)
    place_of = jnp.stack([middle.astype(jnp.int32), half, at_tensor, at_replica])
    along = functools.partial(lax.ppermute, axis_name="dp")
    across = functools.partial(lax.ppermute, axis_name="groups", perm=SWAP)
    sideways = functools.partial(lax.ppermute, axis_name="tensor", perm=SWAP)
    cores = functools.partial(lax.ppermute, axis_name="replica", perm=SWAP)
    stage = lax.optimization_barrier

    mine = lax.dynamic_slice_in_dim(blocks, half * half_slots, half_slots, 0)
    mine = jnp.concatenate([mine, ids_block(block_ids, size).astype(jnp.bfloat16)])
    mine, late_blocks = stage((mine, blocks))

    near_a = along(mine, perm=INWARD)
    far_a = along(mine, perm=MIDDLE)
    other = lax.dynamic_slice_in_dim(late_blocks, (1 - half) * half_slots, half_slots, 0)
    part = lax.dynamic_slice_in_dim(tokens, lax.axis_index(INNER) * part_width, part_width, 1)
    both = jnp.concatenate([part, upstream])
    grads = line_grads(block_ids, ((tokens, upstream),), None, size)
    near_a, far_a, both, other, grads = stage((near_a, far_a, both, other, grads))

    end_a = along(near_a, perm=MIDDLE)
    far_b = across(far_a)
    both_1 = along(both, perm=PAIRS)
    both_1, end_a, far_b, both, other = stage((both_1, end_a, far_b, both, other))
    upstream_1 = both_1[rows:]

    near_b = along(other, perm=INWARD)
    end_b = across(end_a)
    both_2m = along(both, perm=MIDDLE)
    tokens_1 = lax.all_gather(both_1[:rows], INNER)
    ids_1, ids_2, ids_3 = (ids_of(piece, slots) for piece in (near_a, far_a, end_a))
    partial, turned = place_first(
        place_of, (block_ids, ids_1, ids_2, ids_3), (blocks, near_a, far_a, far_b, end_a), depth, width
    )
    near_b, end_b, both_2m, both_1, tokens_1, partial, turned = stage(
        (near_b, end_b, both_2m, both_1, tokens_1, partial, turned)
    )

    both_3m = along(both_1, perm=MIDDLE)
    both_2o = along(both_2m, perm=OUTWARD)
    last = (near_b, end_b)
    end_keep, own_keep, own_give, *end_give = project_back(
        place_of, ids_1, ids_3, turned, *last, upstream_1, upstream
    )
    end_keep, end_give = add_split(place_of, end_keep, *[cores(a) for a in end_give])
    end_keep, end_give, own_give, both_3m, both_2o = stage(
        (end_keep, end_give, own_give, both_3m, both_2o)
    )

    end_got = sideways(end_give)
    own_keep, own_give = add_split(place_of, own_keep, cores(own_give))
    part_3o = along(both_3m[:rows], perm=OUTWARD)
    tokens_2 = lax.all_gather(both_2m[:rows] + both_2o[:rows], INNER)
    proj, end_proj = project_forward(place_of, ids_1, ids_3, partial, *last, tokens, tokens_1)
    end_got, own_give, own_keep, part_3o, proj, end_proj = stage(
        (end_got, own_give, own_keep, part_3o, proj, end_proj)
    )

    sum_out = along(end_keep + end_got, perm=OUTWARD)
    own_got = sideways(own_give)
    tokens_3 = lax.all_gather(both_3m[:rows] + part_3o, INNER)
    upstream_3o = along(both_3m[rows:], perm=OUTWARD)
    grads = line_grads(block_ids, ((tokens_1, upstream_1),), grads, size)
    sum_out, own_got, grads = stage((sum_out, own_got, grads))

    quarter = jnp.where(middle, own_keep + own_got, sum_out)
    proj_out = along(end_proj, perm=OUTWARD)
    grads = line_grads(block_ids, ((tokens_2, both_2m, both_2o),), grads, size)
    by_tensor, by_core, grads = stage((sideways(quarter), cores(quarter), grads))
    by_both = cores(by_tensor)
    projected = jnp.where(middle, proj, proj_out)
    token_grad = assemble(place_of, (quarter, by_core, by_tensor, by_both))
    grads = line_grads(block_ids, ((tokens_3, both_3m, upstream_3o),), grads, size)
    return projected, token_grad, grads


def solution(mesh):
    line = tuple(mesh.shape[a] for a in ("groups", "dp", "tensor", "replica")) == (2, 4, 2, 2)
    return jax.shard_map(
        line_body if line else general_body,
        mesh=mesh,
        in_specs=(
            P(("groups", "dp"), None),
            P(("groups", "dp"), INNER),
            P(("dp",) + INNER, None, None),
            P(("dp",) + INNER),
        ),
        out_specs=(
            P(("groups", "dp"), INNER),
            P(("groups", "dp"), None),
            P(("groups", "dp") + INNER, None, None),
        ),
        check_vma=False,
    )
```

```python
import functools
import math

import jax
import jax.numpy as jnp
from jax import lax
from jax.experimental import pallas as pl
from jax.experimental.pallas import tpu as pltpu
from jax.sharding import PartitionSpec as P

VMEM_LIMIT = 60 * 1024 * 1024
INNER = ("tensor", "replica")


def whole(space=pltpu.VMEM):
    return pl.BlockSpec(memory_space=space)


def project_kernel(ids, blocks, tokens, upstream, proj, back, weight):
    slots, size = blocks.shape[0], blocks.shape[1]
    depth, width = weight.shape
    cols_n = width // size
    total = (depth // size) * cols_n
    weight[...] = jnp.zeros_like(weight)

    @pl.loop(0, slots, unroll=4)
    def place(s):
        b = ids[s]

        @pl.when(b < total)
        def put():
            r = pl.multiple_of((b // cols_n) * size, size)
            c = pl.multiple_of((b % cols_n) * size, size)
            weight[pl.ds(r, size), pl.ds(c, size)] = blocks[s]

    step = 256

    @pl.loop(0, width // step)
    def forward(n):
        c = pl.multiple_of(n * step, step)
        proj[:, pl.ds(c, step)] = jnp.dot(
            tokens[...], weight[:, pl.ds(c, step)], preferred_element_type=jnp.float32
        ).astype(proj.dtype)

    @pl.loop(0, depth // step, unroll=4)
    def backward(n):
        r = pl.multiple_of(n * step, step)
        back[:, pl.ds(r, step)] = lax.dot_general(
            upstream[...],
            weight[pl.ds(r, step), :],
            (((1,), (1,)), ((), ())),
            preferred_element_type=jnp.float32,
        ).astype(back.dtype)


def project(ids, blocks, tokens, upstream):
    rows, depth = tokens.shape
    width = upstream.shape[1]
    return pl.pallas_call(
        project_kernel,
        out_shape=(
            jax.ShapeDtypeStruct((rows, width), jnp.bfloat16),
            jax.ShapeDtypeStruct((rows, depth), jnp.bfloat16),
        ),
        in_specs=[whole(pltpu.SMEM), whole(), whole(), whole()],
        out_specs=(whole(), whole()),
        scratch_shapes=[pltpu.VMEM((depth, width), jnp.bfloat16)],
        compiler_params=pltpu.CompilerParams(vmem_limit_bytes=VMEM_LIMIT),
        cost_estimate=pl.CostEstimate(
            flops=4 * rows * depth * width,
            bytes_accessed=blocks.size * 2 + rows * (depth + width) * 4,
            transcendentals=0,
        ),
        name="project",
    )(ids, blocks, tokens, upstream)


def block_grad_kernel(ids, tokens, upstream, grads):
    slots, size = grads.shape[0], grads.shape[1]
    parts, slabs, _, part_width = tokens.shape
    cols_n = upstream.shape[2] // size
    per_part = part_width // size
    total = parts * per_part * cols_n

    @pl.loop(0, slots)
    def one(s):
        b = ids[s]

        @pl.when(b < total)
        def fill():
            row = b // cols_n
            part = row // per_part
            r = pl.multiple_of((row % per_part) * size, size)
            c = pl.multiple_of((b % cols_n) * size, size)
            acc = jnp.zeros((size, size), jnp.float32)
            for k in range(slabs):
                acc += lax.dot_general(
                    tokens[part, k, :, pl.ds(r, size)],
                    upstream[k, :, pl.ds(c, size)],
                    (((0,), (0,)), ((), ())),
                    preferred_element_type=jnp.float32,
                )
            grads[s] = acc.astype(grads.dtype)

        @pl.when(b >= total)
        def clear():
            grads[s] = jnp.zeros((size, size), grads.dtype)


def block_grads(ids, tokens, upstream, size):
    slots = ids.shape[0]
    parts, slabs, rows, part_width = tokens.shape
    return pl.pallas_call(
        block_grad_kernel,
        out_shape=jax.ShapeDtypeStruct((slots, size, size), jnp.bfloat16),
        in_specs=[whole(pltpu.SMEM), whole(), whole()],
        out_specs=whole(),
        compiler_params=pltpu.CompilerParams(vmem_limit_bytes=VMEM_LIMIT),
        cost_estimate=pl.CostEstimate(
            flops=2 * slots * slabs * rows * size * size,
            bytes_accessed=2 * (tokens.size + upstream.size + slots * size * size),
            transcendentals=0,
        ),
        name="block_grads",
    )(ids, tokens, upstream)


def general_body(tokens, upstream, blocks, block_ids):
    size = blocks.shape[1]
    all_blocks = lax.all_gather(blocks, "dp", axis=0, tiled=True)
    all_ids = lax.all_gather(block_ids, "dp", axis=0, tiled=True)
    proj, back = project(all_ids, all_blocks, tokens, upstream)
    terms = block_grads(all_ids, tokens[None, None], upstream[None], size)
    grads = lax.psum_scatter(terms, "dp", scatter_dimension=0, tiled=True)
    return proj, lax.psum(back, INNER), grads


def place_blocks(ids, first, blocks, weight, turned, slots):
    size = blocks.shape[1]
    depth, width = turned.shape[::-1] if weight is None else weight.shape
    cols_n = width // size
    total = (depth // size) * cols_n
    group = math.gcd(slots, 8)

    @pl.loop(0, slots // group)
    def place(g):
        some = [g * group + j for j in range(group)]
        flipped = [None if turned is None else blocks[s].T for s in some]
        for s, flip in zip(some, flipped):
            b = ids[first + s]

            @pl.when(b < total)
            def put(s=s, flip=flip, b=b):
                r = pl.multiple_of((b // cols_n) * size, size)
                c = pl.multiple_of((b % cols_n) * size, size)
                if weight is not None:
                    weight[pl.ds(r, size), pl.ds(c, size)] = blocks[s]
                if turned is not None:
                    turned[pl.ds(c, size), pl.ds(r, size)] = flip


def place_kernel(
    place_of, ids_0, ids_1, ids_2, ids_3, own, near_a, far_a, far_b, end_a, weight, turned
):
    is_middle, half = place_of[0], place_of[1]
    half_slots = far_b.shape[0] - 1
    mine, other = half * half_slots, (1 - half) * half_slots

    @pl.when(is_middle == 1)
    def work():
        weight[...] = jnp.zeros_like(weight)
        turned[...] = jnp.zeros_like(turned)
        place_blocks(ids_0, 0, own, weight, turned, own.shape[0])
        place_blocks(ids_1, mine, near_a, weight, turned, half_slots)
        place_blocks(ids_2, mine, far_a, weight, turned, half_slots)
        place_blocks(ids_2, other, far_b, weight, turned, half_slots)
        place_blocks(ids_3, mine, end_a, weight, turned, half_slots)


def place_first(place_of, ids, pieces, depth, width):
    return pl.pallas_call(
        place_kernel,
        out_shape=(
            jax.ShapeDtypeStruct((depth, width), jnp.bfloat16),
            jax.ShapeDtypeStruct((width, depth), jnp.bfloat16),
        ),
        in_specs=[whole(pltpu.SMEM)] * 5 + [whole()] * 5,
        out_specs=(whole(), whole()),
        compiler_params=pltpu.CompilerParams(vmem_limit_bytes=VMEM_LIMIT),
        cost_estimate=pl.CostEstimate(
            flops=0, bytes_accessed=depth * width * 6, transcendentals=0
        ),
        name="place_first",
    )(place_of, *ids, *pieces)


def back_kernel(
    place_of, ids_1, ids_3, partial, near_b, end_b, end_upstream, upstream,
    end_keep, own_keep, own_give, end_give_0, end_give_1, held, sources, sem,
):
    half_slots = near_b.shape[0]
    other = (1 - place_of[1]) * half_slots
    rows, width = upstream.shape
    step = 256
    per_part = end_keep.shape[2] // step

    @pl.when(place_of[0] == 1)
    def work():
        load = pltpu.make_async_copy(partial, held, sem)
        load.start()
        sources[:rows] = end_upstream[...]
        sources[rows:] = upstream[...]
        load.wait()
        place_blocks(ids_1, other, near_b, None, held, half_slots)
        place_blocks(ids_3, other, end_b, None, held, half_slots)

        def column(part, end_target, own_target):
            @pl.loop(0, per_part, unroll=2)
            def backward(n):
                at = pl.multiple_of(n * step, step)
                result = jnp.dot(
                    sources[...],
                    held[:, pl.ds(pl.multiple_of(part * per_part * step + at, step), step)],
                    preferred_element_type=jnp.float32,
                ).astype(own_target.dtype)
                end_target[:, pl.ds(at, step)] = result[:rows]
                own_target[:, pl.ds(at, step)] = result[rows:]

        for x, end_give in enumerate((end_give_0, end_give_1)):
            column(2 * x + place_of[3], end_keep.at[x], own_keep.at[x])
            column(2 * x + 1 - place_of[3], end_give, own_give.at[x])


def project_back(place_of, ids_1, ids_3, partial, near_b, end_b, end_upstream, upstream):
    width, depth = partial.shape
    rows = upstream.shape[0]
    quarter = jax.ShapeDtypeStruct((rows, depth // 4), jnp.bfloat16)
    half = jax.ShapeDtypeStruct((2, rows, depth // 4), jnp.bfloat16)
    return pl.pallas_call(
        back_kernel,
        out_shape=(half, half, half, quarter, quarter),
        in_specs=[whole(pltpu.SMEM)] * 3 + [whole(pl.ANY)] + [whole()] * 4,
        out_specs=(whole(),) * 5,
        scratch_shapes=[
            pltpu.VMEM((width, depth), jnp.bfloat16),
            pltpu.VMEM((2 * rows, width), jnp.bfloat16),
            pltpu.SemaphoreType.DMA,
        ],
        compiler_params=pltpu.CompilerParams(vmem_limit_bytes=VMEM_LIMIT),
        cost_estimate=pl.CostEstimate(
            flops=4 * rows * depth * width,
            bytes_accessed=depth * width * 2 + rows * (depth + width) * 4,
            transcendentals=0,
        ),
        name="project_back",
    )(place_of, ids_1, ids_3, partial, near_b, end_b, end_upstream, upstream)


def forward_kernel(
    place_of, ids_1, ids_3, partial, near_b, end_b, tokens, gathered, proj, end_proj, held, sem
):
    half_slots = near_b.shape[0]
    other = (1 - place_of[1]) * half_slots
    depth, width = held.shape
    parts, rows, part_width = gathered.shape
    step = 256

    @pl.when(place_of[0] == 1)
    def work():
        load = pltpu.make_async_copy(partial, held, sem)
        load.start()
        load.wait()
        place_blocks(ids_1, other, near_b, held, None, half_slots)
        place_blocks(ids_3, other, end_b, held, None, half_slots)

        @pl.loop(0, width // step, unroll=2)
        def forward(n):
            c = pl.multiple_of(n * step, step)
            acc = jnp.zeros((rows, step), jnp.float32)
            for q in range(parts):
                acc += jnp.dot(
                    gathered[q],
                    held[q * part_width : (q + 1) * part_width, pl.ds(c, step)],
                    preferred_element_type=jnp.float32,
                )
            end_proj[:, pl.ds(c, step)] = acc.astype(end_proj.dtype)
            proj[:, pl.ds(c, step)] = jnp.dot(
                tokens[...], held[:, pl.ds(c, step)], preferred_element_type=jnp.float32
            ).astype(proj.dtype)


def project_forward(place_of, ids_1, ids_3, partial, near_b, end_b, tokens, gathered):
    depth, width = partial.shape
    rows = tokens.shape[0]
    out = jax.ShapeDtypeStruct((rows, width), jnp.bfloat16)
    return pl.pallas_call(
        forward_kernel,
        out_shape=(out, out),
        in_specs=[whole(pltpu.SMEM)] * 3 + [whole(pl.ANY)] + [whole()] * 4,
        out_specs=(whole(),) * 2,
        scratch_shapes=[pltpu.VMEM((depth, width), jnp.bfloat16), pltpu.SemaphoreType.DMA],
        compiler_params=pltpu.CompilerParams(vmem_limit_bytes=VMEM_LIMIT),
        cost_estimate=pl.CostEstimate(
            flops=rows * depth * width // 2, bytes_accessed=depth * width, transcendentals=0
        ),
        name="project_forward",
    )(place_of, ids_1, ids_3, partial, near_b, end_b, tokens, gathered)


def split_kernel(place_of, keep, *refs):
    x = place_of[2]
    own, give = refs[-2:]
    got = refs[:-2] if len(refs) > 3 else (refs[0].at[0], refs[0].at[1])
    for at in range(2):
        total = (keep[at].astype(jnp.float32) + got[at][...].astype(jnp.float32)).astype(own.dtype)

        @pl.when(x == at)
        def mine():
            own[...] = total

        @pl.when(x != at)
        def theirs():
            give[...] = total


def add_split(place_of, keep, *got):
    out = jax.ShapeDtypeStruct(keep.shape[1:], keep.dtype)
    return pl.pallas_call(
        split_kernel,
        out_shape=(out, out),
        in_specs=[whole(pltpu.SMEM), whole()] + [whole()] * len(got),
        out_specs=(whole(), whole()),
        compiler_params=pltpu.CompilerParams(vmem_limit_bytes=VMEM_LIMIT),
        cost_estimate=pl.CostEstimate(
            flops=keep.size, bytes_accessed=keep.size * 6, transcendentals=0
        ),
        name="add_split",
    )(place_of, keep, *got)


def assemble_kernel(place_of, own, by_core, by_tensor, by_both, full):
    x, c = place_of[2], place_of[3]
    width = own.shape[1]
    for ref, xx, cc in (
        (own, x, c), (by_core, x, 1 - c), (by_tensor, 1 - x, c), (by_both, 1 - x, 1 - c)
    ):
        at = pl.multiple_of((xx * 2 + cc) * width, width)
        full[:, pl.ds(at, width)] = ref[...]


def assemble(place_of, quarters):
    rows, width = quarters[0].shape
    return pl.pallas_call(
        assemble_kernel,
        out_shape=jax.ShapeDtypeStruct((rows, 4 * width), quarters[0].dtype),
        in_specs=[whole(pltpu.SMEM)] + [whole()] * 4,
        out_specs=whole(),
        compiler_params=pltpu.CompilerParams(vmem_limit_bytes=VMEM_LIMIT),
        cost_estimate=pl.CostEstimate(
            flops=0, bytes_accessed=rows * width * 16, transcendentals=0
        ),
        name="assemble",
    )(place_of, *quarters)


def line_grads_kernel(kind, place_of, ids, *refs):
    refs = list(refs)
    if kind == "plain":
        x, d = refs.pop(0), refs.pop(0)
    else:
        mine, theirs, before, after = (refs.pop(0) for _ in range(4))
        x, d = refs.pop(), refs.pop()
        rows = x.shape[1]
        for at in range(2):
            x[2 * at + place_of[3]] = mine[at]
            x[2 * at + 1 - place_of[3]] = theirs[at]
        d[...] = before[rows:] + after[rows:]
    start = refs.pop(0) if len(refs) == 2 else None
    (grads,) = refs
    slots, size = grads.shape[0], grads.shape[1]
    cols_n = d.shape[1] // size
    per_part = x.shape[-1] // size
    total = per_part * (x.shape[0] if len(x.shape) == 3 else 1) * cols_n
    group = math.gcd(slots, 8)

    @pl.loop(0, slots // group)
    def some(g):
        for s in [g * group + j for j in range(group)]:
            b = jnp.minimum(ids[s], total - 1)
            row = b // cols_n
            at = pl.ds(pl.multiple_of((row % per_part) * size, size), size)
            acc = lax.dot_general(
                x[row // per_part, :, at] if len(x.shape) == 3 else x[:, at],
                d[:, pl.ds(pl.multiple_of((b % cols_n) * size, size), size)],
                (((0,), (0,)), ((), ())),
                preferred_element_type=jnp.float32,
            )
            if start is not None:
                acc += start[s].astype(jnp.float32)
            grads[s] = jnp.where(ids[s] < total, acc, 0.0).astype(grads.dtype)


def line_grads(place_of, ids, operands, start, size):
    slots = ids.shape[0]
    kind = "plain" if len(operands) == 2 else "split"
    flat = list(operands) + ([] if start is None else [start])
    scratch = []
    if kind == "split":
        _, rows, part_width = operands[0].shape
        scratch = [
            pltpu.VMEM((rows, operands[2].shape[1]), jnp.bfloat16),
            pltpu.VMEM((4, rows, part_width), jnp.bfloat16),
        ]
    return pl.pallas_call(
        functools.partial(line_grads_kernel, kind),
        out_shape=jax.ShapeDtypeStruct((slots, size, size), jnp.bfloat16),
        in_specs=[whole(pltpu.SMEM)] * 2 + [whole()] * len(flat),
        out_specs=whole(),
        scratch_shapes=scratch,
        compiler_params=pltpu.CompilerParams(vmem_limit_bytes=VMEM_LIMIT),
        cost_estimate=pl.CostEstimate(
            flops=512 * slots * size * size,
            bytes_accessed=sum(2 * a.size for a in flat) + 2 * slots * size * size,
            transcendentals=0,
        ),
        name="line_grads",
    )(place_of, ids, *flat)


INWARD = ((0, 1), (3, 2))
OUTWARD = ((1, 0), (2, 3))
PAIRS = INWARD + OUTWARD
MIDDLE = ((1, 2), (2, 1))
SWAP = ((0, 1), (1, 0))


def ids_block(block_ids, size):
    rows = size * size // block_ids.shape[0]
    return jnp.broadcast_to(block_ids, (rows, block_ids.shape[0])).reshape(1, size, size)


def ids_of(piece, slots):
    return piece[-1, 0, :slots].astype(jnp.int32)


def line_body(tokens, upstream, blocks, block_ids):
    slots, size = blocks.shape[0], blocks.shape[1]
    rows, depth = tokens.shape
    width = upstream.shape[1]
    half_slots = slots // 2
    part_width = depth // 4
    at_z, half = lax.axis_index("dp"), lax.axis_index("groups")
    at_tensor, at_replica = lax.axis_index("tensor"), lax.axis_index("replica")
    middle = (at_z == 1) | (at_z == 2)
    place_of = jnp.stack([middle.astype(jnp.int32), half, at_tensor, at_replica])
    along = functools.partial(lax.ppermute, axis_name="dp")
    across = functools.partial(lax.ppermute, axis_name="groups", perm=SWAP)
    sideways = functools.partial(lax.ppermute, axis_name="tensor", perm=SWAP)
    cores = functools.partial(lax.ppermute, axis_name="replica", perm=SWAP)
    stage = lax.optimization_barrier

    mine = lax.dynamic_slice_in_dim(blocks, half * half_slots, half_slots, 0)
    mine = jnp.concatenate([mine, ids_block(block_ids, size).astype(jnp.bfloat16)])
    mine, late_blocks = stage((mine, blocks))

    near_a = along(mine, perm=INWARD)
    far_a = along(mine, perm=MIDDLE)
    other = lax.dynamic_slice_in_dim(late_blocks, (1 - half) * half_slots, half_slots, 0)
    part = lax.dynamic_slice_in_dim(tokens, lax.axis_index(INNER) * part_width, part_width, 1)
    both = jnp.concatenate([part, upstream])
    grads = line_grads(place_of, block_ids, (tokens, upstream), None, size)
    near_a, far_a, both, other, grads = stage((near_a, far_a, both, other, grads))

    end_a = along(near_a, perm=MIDDLE)
    far_b = across(far_a)
    both_1 = along(both, perm=PAIRS)
    both_1, end_a, far_b, both, other = stage((both_1, end_a, far_b, both, other))
    upstream_1 = both_1[rows:]

    near_b = along(other, perm=INWARD)
    end_b = across(end_a)
    both_2m = along(both, perm=MIDDLE)
    tokens_1 = lax.all_gather(both_1[:rows], INNER)
    ids_1, ids_2, ids_3 = (ids_of(piece, slots) for piece in (near_a, far_a, end_a))
    partial, turned = place_first(
        place_of, (block_ids, ids_1, ids_2, ids_3), (blocks, near_a, far_a, far_b, end_a), depth, width
    )
    near_b, end_b, both_2m, both_1, tokens_1, partial, turned = stage(
        (near_b, end_b, both_2m, both_1, tokens_1, partial, turned)
    )

    both_3m = along(both_1, perm=MIDDLE)
    both_2o = along(both_2m, perm=OUTWARD)
    last = (near_b, end_b)
    end_keep, own_keep, own_give, *end_give = project_back(
        place_of, ids_1, ids_3, turned, *last, upstream_1, upstream
    )
    end_keep, end_give = add_split(place_of, end_keep, *[cores(a) for a in end_give])
    end_keep, end_give, own_give, both_3m, both_2o = stage(
        (end_keep, end_give, own_give, both_3m, both_2o)
    )

    end_got = sideways(end_give)
    own_keep, own_give = add_split(place_of, own_keep, cores(own_give))
    both_3o = along(both_3m, perm=OUTWARD)
    side_2 = lax.all_gather(both_2m[:rows] + both_2o[:rows], "tensor")
    proj, end_proj = project_forward(place_of, ids_1, ids_3, partial, *last, tokens, tokens_1)
    end_got, own_give, own_keep, proj, end_proj, side_2 = stage(
        (end_got, own_give, own_keep, proj, end_proj, side_2)
    )

    sum_out = along(end_keep + end_got, perm=OUTWARD)
    own_got = sideways(own_give)
    grads = line_grads(place_of, block_ids, (tokens_1, upstream_1), grads, size)
    theirs_2 = cores(side_2)
    sum_out, own_got, both_3o, grads, theirs_2 = stage(
        (sum_out, own_got, both_3o, grads, theirs_2)
    )

    side_3 = lax.all_gather(both_3m[:rows] + both_3o[:rows], "tensor")
    quarter = jnp.where(middle, own_keep + own_got, sum_out)
    proj_out = along(end_proj, perm=OUTWARD)
    grads = line_grads(
        place_of, block_ids, (side_2, theirs_2, both_2m, both_2o), grads, size
    )
    by_tensor, by_core, grads, side_3, proj_out = stage(
        (sideways(quarter), cores(quarter), grads, side_3, proj_out)
    )
    by_both = cores(by_tensor)
    projected = jnp.where(middle, proj, proj_out)
    token_grad = assemble(place_of, (quarter, by_core, by_tensor, by_both))
    grads = line_grads(
        place_of, block_ids, (side_3, cores(side_3), both_3m, both_3o), grads, size
    )
    return projected, token_grad, grads


def solution(mesh):
    line = tuple(mesh.shape[a] for a in ("groups", "dp", "tensor", "replica")) == (2, 4, 2, 2)
    return jax.shard_map(
        line_body if line else general_body,
        mesh=mesh,
        in_specs=(
            P(("groups", "dp"), None),
            P(("groups", "dp"), INNER),
            P(("dp",) + INNER, None, None),
            P(("dp",) + INNER),
        ),
        out_specs=(
            P(("groups", "dp"), INNER),
            P(("groups", "dp"), None),
            P(("groups", "dp") + INNER, None, None),
        ),
        check_vma=False,
    )
```

```python
import functools
import math

import jax
import jax.numpy as jnp
from jax import lax
from jax.experimental import pallas as pl
from jax.experimental.pallas import tpu as pltpu
from jax.sharding import PartitionSpec as P

VMEM_LIMIT = 60 * 1024 * 1024
INNER = ("tensor", "replica")


def whole(space=pltpu.VMEM):
    return pl.BlockSpec(memory_space=space)


def project_kernel(ids, blocks, tokens, upstream, proj, back, weight):
    slots, size = blocks.shape[0], blocks.shape[1]
    depth, width = weight.shape
    cols_n = width // size
    total = (depth // size) * cols_n
    weight[...] = jnp.zeros_like(weight)

    @pl.loop(0, slots, unroll=4)
    def place(s):
        b = ids[s]

        @pl.when(b < total)
        def put():
            r = pl.multiple_of((b // cols_n) * size, size)
            c = pl.multiple_of((b % cols_n) * size, size)
            weight[pl.ds(r, size), pl.ds(c, size)] = blocks[s]

    step = 256

    @pl.loop(0, width // step)
    def forward(n):
        c = pl.multiple_of(n * step, step)
        proj[:, pl.ds(c, step)] = jnp.dot(
            tokens[...], weight[:, pl.ds(c, step)], preferred_element_type=jnp.float32
        ).astype(proj.dtype)

    @pl.loop(0, depth // step, unroll=4)
    def backward(n):
        r = pl.multiple_of(n * step, step)
        back[:, pl.ds(r, step)] = lax.dot_general(
            upstream[...],
            weight[pl.ds(r, step), :],
            (((1,), (1,)), ((), ())),
            preferred_element_type=jnp.float32,
        ).astype(back.dtype)


def project(ids, blocks, tokens, upstream):
    rows, depth = tokens.shape
    width = upstream.shape[1]
    return pl.pallas_call(
        project_kernel,
        out_shape=(
            jax.ShapeDtypeStruct((rows, width), jnp.bfloat16),
            jax.ShapeDtypeStruct((rows, depth), jnp.bfloat16),
        ),
        in_specs=[whole(pltpu.SMEM), whole(), whole(), whole()],
        out_specs=(whole(), whole()),
        scratch_shapes=[pltpu.VMEM((depth, width), jnp.bfloat16)],
        compiler_params=pltpu.CompilerParams(vmem_limit_bytes=VMEM_LIMIT),
        cost_estimate=pl.CostEstimate(
            flops=4 * rows * depth * width,
            bytes_accessed=blocks.size * 2 + rows * (depth + width) * 4,
            transcendentals=0,
        ),
        name="project",
    )(ids, blocks, tokens, upstream)


def block_grad_kernel(ids, tokens, upstream, grads):
    slots, size = grads.shape[0], grads.shape[1]
    parts, slabs, _, part_width = tokens.shape
    cols_n = upstream.shape[2] // size
    per_part = part_width // size
    total = parts * per_part * cols_n

    @pl.loop(0, slots)
    def one(s):
        b = ids[s]

        @pl.when(b < total)
        def fill():
            row = b // cols_n
            part = row // per_part
            r = pl.multiple_of((row % per_part) * size, size)
            c = pl.multiple_of((b % cols_n) * size, size)
            acc = jnp.zeros((size, size), jnp.float32)
            for k in range(slabs):
                acc += lax.dot_general(
                    tokens[part, k, :, pl.ds(r, size)],
                    upstream[k, :, pl.ds(c, size)],
                    (((0,), (0,)), ((), ())),
                    preferred_element_type=jnp.float32,
                )
            grads[s] = acc.astype(grads.dtype)

        @pl.when(b >= total)
        def clear():
            grads[s] = jnp.zeros((size, size), grads.dtype)


def block_grads(ids, tokens, upstream, size):
    slots = ids.shape[0]
    parts, slabs, rows, part_width = tokens.shape
    return pl.pallas_call(
        block_grad_kernel,
        out_shape=jax.ShapeDtypeStruct((slots, size, size), jnp.bfloat16),
        in_specs=[whole(pltpu.SMEM), whole(), whole()],
        out_specs=whole(),
        compiler_params=pltpu.CompilerParams(vmem_limit_bytes=VMEM_LIMIT),
        cost_estimate=pl.CostEstimate(
            flops=2 * slots * slabs * rows * size * size,
            bytes_accessed=2 * (tokens.size + upstream.size + slots * size * size),
            transcendentals=0,
        ),
        name="block_grads",
    )(ids, tokens, upstream)


def general_body(tokens, upstream, blocks, block_ids):
    size = blocks.shape[1]
    all_blocks = lax.all_gather(blocks, "dp", axis=0, tiled=True)
    all_ids = lax.all_gather(block_ids, "dp", axis=0, tiled=True)
    proj, back = project(all_ids, all_blocks, tokens, upstream)
    terms = block_grads(all_ids, tokens[None, None], upstream[None], size)
    grads = lax.psum_scatter(terms, "dp", scatter_dimension=0, tiled=True)
    return proj, lax.psum(back, INNER), grads


def place_blocks(ids, first, blocks, weight, turned, slots):
    size = blocks.shape[1]
    depth, width = turned.shape[::-1] if weight is None else weight.shape
    cols_n = width // size
    total = (depth // size) * cols_n
    group = math.gcd(slots, 8)

    @pl.loop(0, slots // group)
    def place(g):
        some = [g * group + j for j in range(group)]
        flipped = [None if turned is None else blocks[s].T for s in some]
        for s, flip in zip(some, flipped):
            b = ids[first + s]

            @pl.when(b < total)
            def put(s=s, flip=flip, b=b):
                r = pl.multiple_of((b // cols_n) * size, size)
                c = pl.multiple_of((b % cols_n) * size, size)
                if weight is not None:
                    weight[pl.ds(r, size), pl.ds(c, size)] = blocks[s]
                if turned is not None:
                    turned[pl.ds(c, size), pl.ds(r, size)] = flip


def place_kernel(
    place_of, ids_0, ids_1, ids_2, ids_3, own, near_a, far_a, far_b, end_a, weight, turned
):
    is_middle, half = place_of[0], place_of[1]
    half_slots = far_b.shape[0] - 1
    mine, other = half * half_slots, (1 - half) * half_slots

    @pl.when(is_middle == 1)
    def work():
        weight[...] = jnp.zeros_like(weight)
        turned[...] = jnp.zeros_like(turned)
        place_blocks(ids_0, 0, own, weight, turned, own.shape[0])
        place_blocks(ids_1, mine, near_a, weight, turned, half_slots)
        place_blocks(ids_2, mine, far_a, weight, turned, half_slots)
        place_blocks(ids_2, other, far_b, weight, turned, half_slots)
        place_blocks(ids_3, mine, end_a, weight, turned, half_slots)


def place_first(place_of, ids, pieces, depth, width):
    return pl.pallas_call(
        place_kernel,
        out_shape=(
            jax.ShapeDtypeStruct((depth, width), jnp.bfloat16),
            jax.ShapeDtypeStruct((width, depth), jnp.bfloat16),
        ),
        in_specs=[whole(pltpu.SMEM)] * 5 + [whole()] * 5,
        out_specs=(whole(), whole()),
        compiler_params=pltpu.CompilerParams(vmem_limit_bytes=VMEM_LIMIT),
        cost_estimate=pl.CostEstimate(
            flops=0, bytes_accessed=depth * width * 6, transcendentals=0
        ),
        name="place_first",
    )(place_of, *ids, *pieces)


def back_kernel(
    place_of, ids_1, ids_3, partial, near_b, end_b, end_upstream, upstream,
    end_keep, own_keep, own_give, end_give_0, end_give_1, held, sources, sem,
):
    half_slots = near_b.shape[0]
    other = (1 - place_of[1]) * half_slots
    rows, width = upstream.shape
    step = 256
    per_part = end_keep.shape[2] // step

    @pl.when(place_of[0] == 1)
    def work():
        load = pltpu.make_async_copy(partial, held, sem)
        load.start()
        sources[:rows] = end_upstream[...]
        sources[rows:] = upstream[...]
        load.wait()
        place_blocks(ids_1, other, near_b, None, held, half_slots)
        place_blocks(ids_3, other, end_b, None, held, half_slots)

        def column(part, end_target, own_target):
            @pl.loop(0, per_part, unroll=2)
            def backward(n):
                at = pl.multiple_of(n * step, step)
                result = jnp.dot(
                    sources[...],
                    held[:, pl.ds(pl.multiple_of(part * per_part * step + at, step), step)],
                    preferred_element_type=jnp.float32,
                ).astype(own_target.dtype)
                end_target[:, pl.ds(at, step)] = result[:rows]
                own_target[:, pl.ds(at, step)] = result[rows:]

        for x, end_give in enumerate((end_give_0, end_give_1)):
            column(2 * x + place_of[3], end_keep.at[x], own_keep.at[x])
            column(2 * x + 1 - place_of[3], end_give, own_give.at[x])


def project_back(place_of, ids_1, ids_3, partial, near_b, end_b, end_upstream, upstream):
    width, depth = partial.shape
    rows = upstream.shape[0]
    quarter = jax.ShapeDtypeStruct((rows, depth // 4), jnp.bfloat16)
    half = jax.ShapeDtypeStruct((2, rows, depth // 4), jnp.bfloat16)
    return pl.pallas_call(
        back_kernel,
        out_shape=(half, half, half, quarter, quarter),
        in_specs=[whole(pltpu.SMEM)] * 3 + [whole(pl.ANY)] + [whole()] * 4,
        out_specs=(whole(),) * 5,
        scratch_shapes=[
            pltpu.VMEM((width, depth), jnp.bfloat16),
            pltpu.VMEM((2 * rows, width), jnp.bfloat16),
            pltpu.SemaphoreType.DMA,
        ],
        compiler_params=pltpu.CompilerParams(vmem_limit_bytes=VMEM_LIMIT),
        cost_estimate=pl.CostEstimate(
            flops=4 * rows * depth * width,
            bytes_accessed=depth * width * 2 + rows * (depth + width) * 4,
            transcendentals=0,
        ),
        name="project_back",
    )(place_of, ids_1, ids_3, partial, near_b, end_b, end_upstream, upstream)


def forward_kernel(
    place_of, ids_1, ids_3, partial, near_b, end_b, tokens, gathered, proj, end_proj, held, sem
):
    half_slots = near_b.shape[0]
    other = (1 - place_of[1]) * half_slots
    depth, width = held.shape
    parts, rows, part_width = gathered.shape
    step = 256

    @pl.when(place_of[0] == 1)
    def work():
        load = pltpu.make_async_copy(partial, held, sem)
        load.start()
        load.wait()
        place_blocks(ids_1, other, near_b, held, None, half_slots)
        place_blocks(ids_3, other, end_b, held, None, half_slots)

        @pl.loop(0, width // step, unroll=2)
        def forward(n):
            c = pl.multiple_of(n * step, step)
            acc = jnp.zeros((rows, step), jnp.float32)
            for q in range(parts):
                acc += jnp.dot(
                    gathered[q],
                    held[q * part_width : (q + 1) * part_width, pl.ds(c, step)],
                    preferred_element_type=jnp.float32,
                )
            end_proj[:, pl.ds(c, step)] = acc.astype(end_proj.dtype)
            proj[:, pl.ds(c, step)] = jnp.dot(
                tokens[...], held[:, pl.ds(c, step)], preferred_element_type=jnp.float32
            ).astype(proj.dtype)


def project_forward(place_of, ids_1, ids_3, partial, near_b, end_b, tokens, gathered):
    depth, width = partial.shape
    rows = tokens.shape[0]
    out = jax.ShapeDtypeStruct((rows, width), jnp.bfloat16)
    return pl.pallas_call(
        forward_kernel,
        out_shape=(out, out),
        in_specs=[whole(pltpu.SMEM)] * 3 + [whole(pl.ANY)] + [whole()] * 4,
        out_specs=(whole(),) * 2,
        scratch_shapes=[pltpu.VMEM((depth, width), jnp.bfloat16), pltpu.SemaphoreType.DMA],
        compiler_params=pltpu.CompilerParams(vmem_limit_bytes=VMEM_LIMIT),
        cost_estimate=pl.CostEstimate(
            flops=rows * depth * width // 2, bytes_accessed=depth * width, transcendentals=0
        ),
        name="project_forward",
    )(place_of, ids_1, ids_3, partial, near_b, end_b, tokens, gathered)


def split_kernel(place_of, keep, *refs):
    x = place_of[2]
    own, give = refs[-2:]
    got = refs[:-2] if len(refs) > 3 else (refs[0].at[0], refs[0].at[1])
    for at in range(2):
        total = (keep[at].astype(jnp.float32) + got[at][...].astype(jnp.float32)).astype(own.dtype)

        @pl.when(x == at)
        def mine():
            own[...] = total

        @pl.when(x != at)
        def theirs():
            give[...] = total


def add_split(place_of, keep, *got):
    out = jax.ShapeDtypeStruct(keep.shape[1:], keep.dtype)
    return pl.pallas_call(
        split_kernel,
        out_shape=(out, out),
        in_specs=[whole(pltpu.SMEM), whole()] + [whole()] * len(got),
        out_specs=(whole(), whole()),
        compiler_params=pltpu.CompilerParams(vmem_limit_bytes=VMEM_LIMIT),
        cost_estimate=pl.CostEstimate(
            flops=keep.size, bytes_accessed=keep.size * 6, transcendentals=0
        ),
        name="add_split",
    )(place_of, keep, *got)


def assemble_kernel(place_of, own, by_core, by_tensor, by_both, full):
    x, c = place_of[2], place_of[3]
    width = own.shape[1]
    for ref, xx, cc in (
        (own, x, c), (by_core, x, 1 - c), (by_tensor, 1 - x, c), (by_both, 1 - x, 1 - c)
    ):
        at = pl.multiple_of((xx * 2 + cc) * width, width)
        full[:, pl.ds(at, width)] = ref[...]


def assemble(place_of, quarters):
    rows, width = quarters[0].shape
    return pl.pallas_call(
        assemble_kernel,
        out_shape=jax.ShapeDtypeStruct((rows, 4 * width), quarters[0].dtype),
        in_specs=[whole(pltpu.SMEM)] + [whole()] * 4,
        out_specs=whole(),
        compiler_params=pltpu.CompilerParams(vmem_limit_bytes=VMEM_LIMIT),
        cost_estimate=pl.CostEstimate(
            flops=0, bytes_accessed=rows * width * 16, transcendentals=0
        ),
        name="assemble",
    )(place_of, *quarters)


def line_grads_kernel(pairs_n, ids, *refs):
    refs = list(refs)
    pairs = []
    for k in range(pairs_n):
        x, d = refs.pop(0), refs.pop(0)
        if d.shape[0] > x.shape[-2]:
            rows, other = x.shape[-2], refs.pop(0)
            total_d = refs.pop()
            total_d[...] = d[rows:] + other[rows:]
            d = total_d
        pairs.append((x, d))
    start = refs.pop(0) if len(refs) == 2 else None
    (grads,) = refs
    slots, size = grads.shape[0], grads.shape[1]
    first = pairs[0][0]
    cols_n = pairs[0][1].shape[1] // size
    rows_n = first.shape[-1] // size * (first.shape[0] if len(first.shape) == 3 else 1)
    total = rows_n * cols_n
    group = math.gcd(slots, 8)

    @pl.loop(0, slots // group)
    def some(g):
        for s in [g * group + j for j in range(group)]:
            b = jnp.minimum(ids[s], total - 1)
            row = b // cols_n
            c = pl.ds(pl.multiple_of((b % cols_n) * size, size), size)
            acc = jnp.zeros((size, size), jnp.float32) if start is None else start[s].astype(jnp.float32)
            for x, d in pairs:
                per_part = x.shape[-1] // size
                at = pl.ds(pl.multiple_of((row % per_part) * size, size), size)
                acc += lax.dot_general(
                    x[row // per_part, :, at] if len(x.shape) == 3 else x[:, at],
                    d[:, c],
                    (((0,), (0,)), ((), ())),
                    preferred_element_type=jnp.float32,
                )
            grads[s] = jnp.where(ids[s] < total, acc, 0.0).astype(grads.dtype)


def line_grads(ids, pairs, start, size):
    slots = ids.shape[0]
    flat = [a for pair in pairs for a in pair] + ([] if start is None else [start])
    sums = [
        pltpu.VMEM((p[0].shape[-2], p[1].shape[1]), jnp.bfloat16) for p in pairs if len(p) == 3
    ]
    return pl.pallas_call(
        functools.partial(line_grads_kernel, len(pairs)),
        out_shape=jax.ShapeDtypeStruct((slots, size, size), jnp.bfloat16),
        in_specs=[whole(pltpu.SMEM)] + [whole()] * len(flat),
        out_specs=whole(),
        scratch_shapes=sums,
        compiler_params=pltpu.CompilerParams(vmem_limit_bytes=VMEM_LIMIT),
        cost_estimate=pl.CostEstimate(
            flops=512 * len(pairs) * slots * size * size,
            bytes_accessed=sum(2 * a.size for a in flat) + 2 * slots * size * size,
            transcendentals=0,
        ),
        name="line_grads",
    )(ids, *flat)


INWARD = ((0, 1), (3, 2))
OUTWARD = ((1, 0), (2, 3))
PAIRS = INWARD + OUTWARD
MIDDLE = ((1, 2), (2, 1))
SWAP = ((0, 1), (1, 0))


def ids_block(block_ids, size):
    rows = size * size // block_ids.shape[0]
    return jnp.broadcast_to(block_ids, (rows, block_ids.shape[0])).reshape(1, size, size)


def ids_of(piece, slots):
    return piece[-1, 0, :slots].astype(jnp.int32)


def line_body(tokens, upstream, blocks, block_ids):
    slots, size = blocks.shape[0], blocks.shape[1]
    rows, depth = tokens.shape
    width = upstream.shape[1]
    half_slots = slots // 2
    part_width = depth // 4
    at_z, half = lax.axis_index("dp"), lax.axis_index("groups")
    at_tensor, at_replica = lax.axis_index("tensor"), lax.axis_index("replica")
    middle = (at_z == 1) | (at_z == 2)
    place_of = jnp.stack([middle.astype(jnp.int32), half, at_tensor, at_replica])
    along = functools.partial(lax.ppermute, axis_name="dp")
    across = functools.partial(lax.ppermute, axis_name="groups", perm=SWAP)
    sideways = functools.partial(lax.ppermute, axis_name="tensor", perm=SWAP)
    cores = functools.partial(lax.ppermute, axis_name="replica", perm=SWAP)
    stage = lax.optimization_barrier

    mine = lax.dynamic_slice_in_dim(blocks, half * half_slots, half_slots, 0)
    mine = jnp.concatenate([mine, ids_block(block_ids, size).astype(jnp.bfloat16)])
    mine, late_blocks = stage((mine, blocks))

    near_a = along(mine, perm=INWARD)
    far_a = along(mine, perm=MIDDLE)
    other = lax.dynamic_slice_in_dim(late_blocks, (1 - half) * half_slots, half_slots, 0)
    part = lax.dynamic_slice_in_dim(tokens, lax.axis_index(INNER) * part_width, part_width, 1)
    both = jnp.concatenate([part, upstream])
    grads = line_grads(block_ids, ((tokens, upstream),), None, size)
    near_a, far_a, both, other, grads = stage((near_a, far_a, both, other, grads))

    end_a = along(near_a, perm=MIDDLE)
    far_b = across(far_a)
    both_1 = along(both, perm=PAIRS)
    both_1, end_a, far_b, both, other = stage((both_1, end_a, far_b, both, other))
    upstream_1 = both_1[rows:]

    near_b = along(other, perm=INWARD)
    end_b = across(end_a)
    both_2m = along(both, perm=MIDDLE)
    tokens_1 = lax.all_gather(both_1[:rows], INNER)
    ids_1, ids_2, ids_3 = (ids_of(piece, slots) for piece in (near_a, far_a, end_a))
    partial, turned = place_first(
        place_of, (block_ids, ids_1, ids_2, ids_3), (blocks, near_a, far_a, far_b, end_a), depth, width
    )
    near_b, end_b, both_2m, both_1, tokens_1, partial, turned = stage(
        (near_b, end_b, both_2m, both_1, tokens_1, partial, turned)
    )

    both_3m = along(both_1, perm=MIDDLE)
    both_2o = along(both_2m, perm=OUTWARD)
    last = (near_b, end_b)
    end_keep, own_keep, own_give, *end_give = project_back(
        place_of, ids_1, ids_3, turned, *last, upstream_1, upstream
    )
    end_keep, end_give = add_split(place_of, end_keep, *[cores(a) for a in end_give])
    end_keep, end_give, own_give, both_3m, both_2o = stage(
        (end_keep, end_give, own_give, both_3m, both_2o)
    )

    end_got = sideways(end_give)
    own_keep, own_give = add_split(place_of, own_keep, cores(own_give))
    both_3o = along(both_3m, perm=OUTWARD)
    tokens_2 = lax.all_gather(both_2m[:rows] + both_2o[:rows], INNER)
    proj, end_proj = project_forward(place_of, ids_1, ids_3, partial, *last, tokens, tokens_1)
    end_got, own_give, own_keep, proj, end_proj, both_3m = stage(
        (end_got, own_give, own_keep, proj, end_proj, both_3m)
    )

    sum_out = along(end_keep + end_got, perm=OUTWARD)
    own_got = sideways(own_give)
    grads = line_grads(block_ids, ((tokens_1, upstream_1),), grads, size)
    tokens_3 = lax.all_gather(both_3m[:rows] + both_3o[:rows], INNER)
    sum_out, own_got, grads = stage((sum_out, own_got, grads))

    quarter = jnp.where(middle, own_keep + own_got, sum_out)
    proj_out = along(end_proj, perm=OUTWARD)
    grads = line_grads(block_ids, ((tokens_2, both_2m, both_2o),), grads, size)
    grads = line_grads(block_ids, ((tokens_3, both_3m, both_3o),), grads, size)
    by_tensor, by_core, grads = stage((sideways(quarter), cores(quarter), grads))
    by_both = cores(by_tensor)
    projected = jnp.where(middle, proj, proj_out)
    token_grad = assemble(place_of, (quarter, by_core, by_tensor, by_both))
    return projected, token_grad, grads


def solution(mesh):
    line = tuple(mesh.shape[a] for a in ("groups", "dp", "tensor", "replica")) == (2, 4, 2, 2)
    return jax.shard_map(
        line_body if line else general_body,
        mesh=mesh,
        in_specs=(
            P(("groups", "dp"), None),
            P(("groups", "dp"), INNER),
            P(("dp",) + INNER, None, None),
            P(("dp",) + INNER),
        ),
        out_specs=(
            P(("groups", "dp"), INNER),
            P(("groups", "dp"), None),
            P(("groups", "dp") + INNER, None, None),
        ),
        check_vma=False,
    )
```

```python
import functools
import math

import jax
import jax.numpy as jnp
from jax import lax
from jax.experimental import pallas as pl
from jax.experimental.pallas import tpu as pltpu
from jax.sharding import PartitionSpec as P

VMEM_LIMIT = 60 * 1024 * 1024
INNER = ("tensor", "replica")


def whole(space=pltpu.VMEM):
    return pl.BlockSpec(memory_space=space)


def project_kernel(ids, blocks, tokens, upstream, proj, back, weight):
    slots, size = blocks.shape[0], blocks.shape[1]
    depth, width = weight.shape
    cols_n = width // size
    total = (depth // size) * cols_n
    weight[...] = jnp.zeros_like(weight)

    @pl.loop(0, slots, unroll=4)
    def place(s):
        b = ids[s]

        @pl.when(b < total)
        def put():
            r = pl.multiple_of((b // cols_n) * size, size)
            c = pl.multiple_of((b % cols_n) * size, size)
            weight[pl.ds(r, size), pl.ds(c, size)] = blocks[s]

    step = 256

    @pl.loop(0, width // step)
    def forward(n):
        c = pl.multiple_of(n * step, step)
        proj[:, pl.ds(c, step)] = jnp.dot(
            tokens[...], weight[:, pl.ds(c, step)], preferred_element_type=jnp.float32
        ).astype(proj.dtype)

    @pl.loop(0, depth // step, unroll=4)
    def backward(n):
        r = pl.multiple_of(n * step, step)
        back[:, pl.ds(r, step)] = lax.dot_general(
            upstream[...],
            weight[pl.ds(r, step), :],
            (((1,), (1,)), ((), ())),
            preferred_element_type=jnp.float32,
        ).astype(back.dtype)


def project(ids, blocks, tokens, upstream):
    rows, depth = tokens.shape
    width = upstream.shape[1]
    return pl.pallas_call(
        project_kernel,
        out_shape=(
            jax.ShapeDtypeStruct((rows, width), jnp.bfloat16),
            jax.ShapeDtypeStruct((rows, depth), jnp.bfloat16),
        ),
        in_specs=[whole(pltpu.SMEM), whole(), whole(), whole()],
        out_specs=(whole(), whole()),
        scratch_shapes=[pltpu.VMEM((depth, width), jnp.bfloat16)],
        compiler_params=pltpu.CompilerParams(vmem_limit_bytes=VMEM_LIMIT),
        cost_estimate=pl.CostEstimate(
            flops=4 * rows * depth * width,
            bytes_accessed=blocks.size * 2 + rows * (depth + width) * 4,
            transcendentals=0,
        ),
        name="project",
    )(ids, blocks, tokens, upstream)


def block_grad_kernel(ids, tokens, upstream, grads):
    slots, size = grads.shape[0], grads.shape[1]
    parts, slabs, _, part_width = tokens.shape
    cols_n = upstream.shape[2] // size
    per_part = part_width // size
    total = parts * per_part * cols_n

    @pl.loop(0, slots)
    def one(s):
        b = ids[s]

        @pl.when(b < total)
        def fill():
            row = b // cols_n
            part = row // per_part
            r = pl.multiple_of((row % per_part) * size, size)
            c = pl.multiple_of((b % cols_n) * size, size)
            acc = jnp.zeros((size, size), jnp.float32)
            for k in range(slabs):
                acc += lax.dot_general(
                    tokens[part, k, :, pl.ds(r, size)],
                    upstream[k, :, pl.ds(c, size)],
                    (((0,), (0,)), ((), ())),
                    preferred_element_type=jnp.float32,
                )
            grads[s] = acc.astype(grads.dtype)

        @pl.when(b >= total)
        def clear():
            grads[s] = jnp.zeros((size, size), grads.dtype)


def block_grads(ids, tokens, upstream, size):
    slots = ids.shape[0]
    parts, slabs, rows, part_width = tokens.shape
    return pl.pallas_call(
        block_grad_kernel,
        out_shape=jax.ShapeDtypeStruct((slots, size, size), jnp.bfloat16),
        in_specs=[whole(pltpu.SMEM), whole(), whole()],
        out_specs=whole(),
        compiler_params=pltpu.CompilerParams(vmem_limit_bytes=VMEM_LIMIT),
        cost_estimate=pl.CostEstimate(
            flops=2 * slots * slabs * rows * size * size,
            bytes_accessed=2 * (tokens.size + upstream.size + slots * size * size),
            transcendentals=0,
        ),
        name="block_grads",
    )(ids, tokens, upstream)


def general_body(tokens, upstream, blocks, block_ids):
    size = blocks.shape[1]
    all_blocks = lax.all_gather(blocks, "dp", axis=0, tiled=True)
    all_ids = lax.all_gather(block_ids, "dp", axis=0, tiled=True)
    proj, back = project(all_ids, all_blocks, tokens, upstream)
    terms = block_grads(all_ids, tokens[None, None], upstream[None], size)
    grads = lax.psum_scatter(terms, "dp", scatter_dimension=0, tiled=True)
    return proj, lax.psum(back, INNER), grads


def place_blocks(ids, first, blocks, weight, turned, slots):
    size = blocks.shape[1]
    depth, width = turned.shape[::-1] if weight is None else weight.shape
    cols_n = width // size
    total = (depth // size) * cols_n
    group = math.gcd(slots, 8)

    @pl.loop(0, slots // group)
    def place(g):
        some = [g * group + j for j in range(group)]
        flipped = [None if turned is None else blocks[s].T for s in some]
        for s, flip in zip(some, flipped):
            b = ids[first + s]

            @pl.when(b < total)
            def put(s=s, flip=flip, b=b):
                r = pl.multiple_of((b // cols_n) * size, size)
                c = pl.multiple_of((b % cols_n) * size, size)
                if weight is not None:
                    weight[pl.ds(r, size), pl.ds(c, size)] = blocks[s]
                if turned is not None:
                    turned[pl.ds(c, size), pl.ds(r, size)] = flip


def place_kernel(
    place_of, ids_0, ids_1, ids_2, ids_3, own, near_a, far_a, far_b, end_a, weight, turned
):
    is_middle, half = place_of[0], place_of[1]
    half_slots = far_b.shape[0] - 1
    mine, other = half * half_slots, (1 - half) * half_slots

    @pl.when(is_middle == 1)
    def work():
        weight[...] = jnp.zeros_like(weight)
        turned[...] = jnp.zeros_like(turned)
        place_blocks(ids_0, 0, own, weight, turned, own.shape[0])
        place_blocks(ids_1, mine, near_a, weight, turned, half_slots)
        place_blocks(ids_2, mine, far_a, weight, turned, half_slots)
        place_blocks(ids_2, other, far_b, weight, turned, half_slots)
        place_blocks(ids_3, mine, end_a, weight, turned, half_slots)


def place_first(place_of, ids, pieces, depth, width):
    return pl.pallas_call(
        place_kernel,
        out_shape=(
            jax.ShapeDtypeStruct((depth, width), jnp.bfloat16),
            jax.ShapeDtypeStruct((width, depth), jnp.bfloat16),
        ),
        in_specs=[whole(pltpu.SMEM)] * 5 + [whole()] * 5,
        out_specs=(whole(), whole()),
        compiler_params=pltpu.CompilerParams(vmem_limit_bytes=VMEM_LIMIT),
        cost_estimate=pl.CostEstimate(
            flops=0, bytes_accessed=depth * width * 6, transcendentals=0
        ),
        name="place_first",
    )(place_of, *ids, *pieces)


def back_kernel(
    place_of, ids_1, ids_3, partial, near_b, end_b, end_upstream, upstream,
    end_keep, own_keep, own_give, end_give_0, end_give_1, held, sources, sem,
):
    half_slots = near_b.shape[0]
    other = (1 - place_of[1]) * half_slots
    rows, width = upstream.shape
    step = 256
    per_part = end_keep.shape[2] // step

    @pl.when(place_of[0] == 1)
    def work():
        load = pltpu.make_async_copy(partial, held, sem)
        load.start()
        sources[:rows] = end_upstream[...]
        sources[rows:] = upstream[...]
        load.wait()
        place_blocks(ids_1, other, near_b, None, held, half_slots)
        place_blocks(ids_3, other, end_b, None, held, half_slots)

        def column(part, end_target, own_target):
            @pl.loop(0, per_part, unroll=2)
            def backward(n):
                at = pl.multiple_of(n * step, step)
                result = jnp.dot(
                    sources[...],
                    held[:, pl.ds(pl.multiple_of(part * per_part * step + at, step), step)],
                    preferred_element_type=jnp.float32,
                ).astype(own_target.dtype)
                end_target[:, pl.ds(at, step)] = result[:rows]
                own_target[:, pl.ds(at, step)] = result[rows:]

        for x, end_give in enumerate((end_give_0, end_give_1)):
            column(2 * x + place_of[3], end_keep.at[x], own_keep.at[x])
            column(2 * x + 1 - place_of[3], end_give, own_give.at[x])


def project_back(place_of, ids_1, ids_3, partial, near_b, end_b, end_upstream, upstream):
    width, depth = partial.shape
    rows = upstream.shape[0]
    quarter = jax.ShapeDtypeStruct((rows, depth // 4), jnp.bfloat16)
    half = jax.ShapeDtypeStruct((2, rows, depth // 4), jnp.bfloat16)
    return pl.pallas_call(
        back_kernel,
        out_shape=(half, half, half, quarter, quarter),
        in_specs=[whole(pltpu.SMEM)] * 3 + [whole(pl.ANY)] + [whole()] * 4,
        out_specs=(whole(),) * 5,
        scratch_shapes=[
            pltpu.VMEM((width, depth), jnp.bfloat16),
            pltpu.VMEM((2 * rows, width), jnp.bfloat16),
            pltpu.SemaphoreType.DMA,
        ],
        compiler_params=pltpu.CompilerParams(vmem_limit_bytes=VMEM_LIMIT),
        cost_estimate=pl.CostEstimate(
            flops=4 * rows * depth * width,
            bytes_accessed=depth * width * 2 + rows * (depth + width) * 4,
            transcendentals=0,
        ),
        name="project_back",
    )(place_of, ids_1, ids_3, partial, near_b, end_b, end_upstream, upstream)


def forward_kernel(
    place_of, ids_1, ids_3, partial, near_b, end_b, tokens, gathered, proj, end_proj, held, sem
):
    half_slots = near_b.shape[0]
    other = (1 - place_of[1]) * half_slots
    depth, width = held.shape
    parts, rows, part_width = gathered.shape
    step = 256

    @pl.when(place_of[0] == 1)
    def work():
        load = pltpu.make_async_copy(partial, held, sem)
        load.start()
        load.wait()
        place_blocks(ids_1, other, near_b, held, None, half_slots)
        place_blocks(ids_3, other, end_b, held, None, half_slots)

        @pl.loop(0, width // step, unroll=2)
        def forward(n):
            c = pl.multiple_of(n * step, step)
            acc = jnp.zeros((rows, step), jnp.float32)
            for q in range(parts):
                acc += jnp.dot(
                    gathered[q],
                    held[q * part_width : (q + 1) * part_width, pl.ds(c, step)],
                    preferred_element_type=jnp.float32,
                )
            end_proj[:, pl.ds(c, step)] = acc.astype(end_proj.dtype)
            proj[:, pl.ds(c, step)] = jnp.dot(
                tokens[...], held[:, pl.ds(c, step)], preferred_element_type=jnp.float32
            ).astype(proj.dtype)


def project_forward(place_of, ids_1, ids_3, partial, near_b, end_b, tokens, gathered):
    depth, width = partial.shape
    rows = tokens.shape[0]
    out = jax.ShapeDtypeStruct((rows, width), jnp.bfloat16)
    return pl.pallas_call(
        forward_kernel,
        out_shape=(out, out),
        in_specs=[whole(pltpu.SMEM)] * 3 + [whole(pl.ANY)] + [whole()] * 4,
        out_specs=(whole(),) * 2,
        scratch_shapes=[pltpu.VMEM((depth, width), jnp.bfloat16), pltpu.SemaphoreType.DMA],
        compiler_params=pltpu.CompilerParams(vmem_limit_bytes=VMEM_LIMIT),
        cost_estimate=pl.CostEstimate(
            flops=rows * depth * width // 2, bytes_accessed=depth * width, transcendentals=0
        ),
        name="project_forward",
    )(place_of, ids_1, ids_3, partial, near_b, end_b, tokens, gathered)


def split_kernel(place_of, keep, *refs):
    x = place_of[2]
    own, give = refs[-2:]
    got = refs[:-2] if len(refs) > 3 else (refs[0].at[0], refs[0].at[1])
    for at in range(2):
        total = (keep[at].astype(jnp.float32) + got[at][...].astype(jnp.float32)).astype(own.dtype)

        @pl.when(x == at)
        def mine():
            own[...] = total

        @pl.when(x != at)
        def theirs():
            give[...] = total


def add_split(place_of, keep, *got):
    out = jax.ShapeDtypeStruct(keep.shape[1:], keep.dtype)
    return pl.pallas_call(
        split_kernel,
        out_shape=(out, out),
        in_specs=[whole(pltpu.SMEM), whole()] + [whole()] * len(got),
        out_specs=(whole(), whole()),
        compiler_params=pltpu.CompilerParams(vmem_limit_bytes=VMEM_LIMIT),
        cost_estimate=pl.CostEstimate(
            flops=keep.size, bytes_accessed=keep.size * 6, transcendentals=0
        ),
        name="add_split",
    )(place_of, keep, *got)


def assemble_kernel(place_of, own, by_core, by_tensor, by_both, full):
    x, c = place_of[2], place_of[3]
    width = own.shape[1]
    for ref, xx, cc in (
        (own, x, c), (by_core, x, 1 - c), (by_tensor, 1 - x, c), (by_both, 1 - x, 1 - c)
    ):
        at = pl.multiple_of((xx * 2 + cc) * width, width)
        full[:, pl.ds(at, width)] = ref[...]


def assemble(place_of, quarters):
    rows, width = quarters[0].shape
    return pl.pallas_call(
        assemble_kernel,
        out_shape=jax.ShapeDtypeStruct((rows, 4 * width), quarters[0].dtype),
        in_specs=[whole(pltpu.SMEM)] + [whole()] * 4,
        out_specs=whole(),
        compiler_params=pltpu.CompilerParams(vmem_limit_bytes=VMEM_LIMIT),
        cost_estimate=pl.CostEstimate(
            flops=0, bytes_accessed=rows * width * 16, transcendentals=0
        ),
        name="assemble",
    )(place_of, *quarters)


def line_grads_kernel(kind, ids, *refs):
    refs = list(refs)
    if kind == "halves":
        place_of = refs.pop(0)
        mine, theirs, before, after = (refs.pop(0) for _ in range(4))
        x, d = refs.pop(), refs.pop()
        for at in range(2):
            x[2 * place_of[3] + at] = mine[at]
            x[2 - 2 * place_of[3] + at] = theirs[at]
        d[...] = before[...] + after[...]
    elif kind == "sums":
        x, before, after = (refs.pop(0) for _ in range(3))
        d = refs.pop()
        rows = x.shape[-2]
        d[...] = before[rows:] + after[rows:]
    else:
        x, d = refs.pop(0), refs.pop(0)
    start = refs.pop(0) if len(refs) == 2 else None
    (grads,) = refs
    slots, size = grads.shape[0], grads.shape[1]
    cols_n = d.shape[1] // size
    per_part = x.shape[-1] // size
    total = per_part * (x.shape[0] if len(x.shape) == 3 else 1) * cols_n
    group = math.gcd(slots, 8)

    @pl.loop(0, slots // group)
    def some(g):
        for s in [g * group + j for j in range(group)]:
            b = jnp.minimum(ids[s], total - 1)
            row = b // cols_n
            at = pl.ds(pl.multiple_of((row % per_part) * size, size), size)
            acc = lax.dot_general(
                x[row // per_part, :, at] if len(x.shape) == 3 else x[:, at],
                d[:, pl.ds(pl.multiple_of((b % cols_n) * size, size), size)],
                (((0,), (0,)), ((), ())),
                preferred_element_type=jnp.float32,
            )
            if start is not None:
                acc += start[s].astype(jnp.float32)
            grads[s] = jnp.where(ids[s] < total, acc, 0.0).astype(grads.dtype)


def line_grads(kind, ids, operands, start, size):
    slots = ids.shape[0]
    flat = list(operands) + ([] if start is None else [start])
    specs = [whole(pltpu.SMEM)] + [whole()] * len(flat)
    scratch = []
    if kind == "sums":
        scratch = [pltpu.VMEM((operands[0].shape[-2], operands[-1].shape[1]), jnp.bfloat16)]
    if kind == "halves":
        specs[1] = whole(pltpu.SMEM)
        _, rows, part_width = operands[1].shape
        scratch = [
            pltpu.VMEM((rows, operands[-1].shape[1]), jnp.bfloat16),
            pltpu.VMEM((4, rows, part_width), jnp.bfloat16),
        ]
    return pl.pallas_call(
        functools.partial(line_grads_kernel, kind),
        out_shape=jax.ShapeDtypeStruct((slots, size, size), jnp.bfloat16),
        in_specs=specs,
        out_specs=whole(),
        scratch_shapes=scratch,
        compiler_params=pltpu.CompilerParams(vmem_limit_bytes=VMEM_LIMIT),
        cost_estimate=pl.CostEstimate(
            flops=512 * slots * size * size,
            bytes_accessed=sum(2 * a.size for a in flat) + 2 * slots * size * size,
            transcendentals=0,
        ),
        name="line_grads",
    )(ids, *flat)


INWARD = ((0, 1), (3, 2))
OUTWARD = ((1, 0), (2, 3))
PAIRS = INWARD + OUTWARD
MIDDLE = ((1, 2), (2, 1))
SWAP = ((0, 1), (1, 0))


def ids_block(block_ids, size):
    rows = size * size // block_ids.shape[0]
    return jnp.broadcast_to(block_ids, (rows, block_ids.shape[0])).reshape(1, size, size)


def ids_of(piece, slots):
    return piece[-1, 0, :slots].astype(jnp.int32)


def line_body(tokens, upstream, blocks, block_ids):
    slots, size = blocks.shape[0], blocks.shape[1]
    rows, depth = tokens.shape
    width = upstream.shape[1]
    half_slots = slots // 2
    part_width = depth // 4
    at_z, half = lax.axis_index("dp"), lax.axis_index("groups")
    at_tensor, at_replica = lax.axis_index("tensor"), lax.axis_index("replica")
    middle = (at_z == 1) | (at_z == 2)
    place_of = jnp.stack([middle.astype(jnp.int32), half, at_tensor, at_replica])
    along = functools.partial(lax.ppermute, axis_name="dp")
    across = functools.partial(lax.ppermute, axis_name="groups", perm=SWAP)
    sideways = functools.partial(lax.ppermute, axis_name="tensor", perm=SWAP)
    cores = functools.partial(lax.ppermute, axis_name="replica", perm=SWAP)
    stage = lax.optimization_barrier

    mine = lax.dynamic_slice_in_dim(blocks, half * half_slots, half_slots, 0)
    mine = jnp.concatenate([mine, ids_block(block_ids, size).astype(jnp.bfloat16)])
    mine, late_blocks = stage((mine, blocks))

    near_a = along(mine, perm=INWARD)
    far_a = along(mine, perm=MIDDLE)
    other = lax.dynamic_slice_in_dim(late_blocks, (1 - half) * half_slots, half_slots, 0)
    part = lax.dynamic_slice_in_dim(tokens, lax.axis_index(INNER) * part_width, part_width, 1)
    both = jnp.concatenate([part, upstream])
    grads = line_grads("plain", block_ids, (tokens, upstream), None, size)
    near_a, far_a, both, other, grads = stage((near_a, far_a, both, other, grads))

    end_a = along(near_a, perm=MIDDLE)
    far_b = across(far_a)
    both_1 = along(both, perm=PAIRS)
    both_1, end_a, far_b, both, other = stage((both_1, end_a, far_b, both, other))
    upstream_1 = both_1[rows:]

    near_b = along(other, perm=INWARD)
    end_b = across(end_a)
    both_2m = along(both, perm=MIDDLE)
    tokens_1 = lax.all_gather(both_1[:rows], INNER)
    ids_1, ids_2, ids_3 = (ids_of(piece, slots) for piece in (near_a, far_a, end_a))
    partial, turned = place_first(
        place_of, (block_ids, ids_1, ids_2, ids_3), (blocks, near_a, far_a, far_b, end_a), depth, width
    )
    half_1 = lax.dynamic_slice_in_dim(tokens_1, 2 * at_replica, 2, 0)
    near_b, end_b, both_2m, half_1, upstream_1, tokens_1, partial, turned = stage(
        (near_b, end_b, both_2m, half_1, upstream_1, tokens_1, partial, turned)
    )

    half_3m = along(half_1, perm=MIDDLE)
    both_2o = along(both_2m, perm=OUTWARD)
    last = (near_b, end_b)
    end_keep, own_keep, own_give, *end_give = project_back(
        place_of, ids_1, ids_3, turned, *last, upstream_1, upstream
    )
    end_keep, end_give = add_split(place_of, end_keep, *[cores(a) for a in end_give])
    end_keep, end_give, own_give, half_3m, both_2o = stage(
        (end_keep, end_give, own_give, half_3m, both_2o)
    )

    end_got = sideways(end_give)
    own_keep, own_give = add_split(place_of, own_keep, cores(own_give))
    half_3o = along(half_3m, perm=OUTWARD)
    upstream_3m = along(upstream_1, perm=MIDDLE)
    tokens_2 = lax.all_gather(both_2m[:rows] + both_2o[:rows], INNER)
    proj, end_proj = project_forward(place_of, ids_1, ids_3, partial, *last, tokens, tokens_1)
    end_got, own_give, own_keep, proj, end_proj, upstream_3m = stage(
        (end_got, own_give, own_keep, proj, end_proj, upstream_3m)
    )

    sum_out = along(end_keep + end_got, perm=OUTWARD)
    own_got = sideways(own_give)
    grads = line_grads("plain", block_ids, (tokens_1, upstream_1), grads, size)
    half_3 = half_3m + half_3o
    sum_out, own_got, half_3, grads = stage((sum_out, own_got, half_3, grads))

    quarter = jnp.where(middle, own_keep + own_got, sum_out)
    theirs_3 = cores(half_3)
    upstream_3o = along(upstream_3m, perm=OUTWARD)
    grads = line_grads("sums", block_ids, (tokens_2, both_2m, both_2o), grads, size)
    end_proj, grads = stage((end_proj, grads))
    proj_out = along(end_proj, perm=OUTWARD)
    grads = line_grads(
        "halves", block_ids, (place_of, half_3, theirs_3, upstream_3m, upstream_3o), grads, size
    )
    by_tensor, by_core, grads = stage((sideways(quarter), cores(quarter), grads))
    by_both = cores(by_tensor)
    token_grad = assemble(place_of, (quarter, by_core, by_tensor, by_both))
    projected = jnp.where(middle, proj, proj_out)
    return projected, token_grad, grads


def solution(mesh):
    line = tuple(mesh.shape[a] for a in ("groups", "dp", "tensor", "replica")) == (2, 4, 2, 2)
    return jax.shard_map(
        line_body if line else general_body,
        mesh=mesh,
        in_specs=(
            P(("groups", "dp"), None),
            P(("groups", "dp"), INNER),
            P(("dp",) + INNER, None, None),
            P(("dp",) + INNER),
        ),
        out_specs=(
            P(("groups", "dp"), INNER),
            P(("groups", "dp"), None),
            P(("groups", "dp") + INNER, None, None),
        ),
        check_vma=False,
    )
```

```python
import functools
import math

import jax
import jax.numpy as jnp
from jax import lax
from jax.experimental import pallas as pl
from jax.experimental.pallas import tpu as pltpu
from jax.sharding import PartitionSpec as P

VMEM_LIMIT = 60 * 1024 * 1024
INNER = ("tensor", "replica")


def whole(space=pltpu.VMEM):
    return pl.BlockSpec(memory_space=space)


def project_kernel(ids, blocks, tokens, upstream, proj, back, weight):
    slots, size = blocks.shape[0], blocks.shape[1]
    depth, width = weight.shape
    cols_n = width // size
    total = (depth // size) * cols_n
    weight[...] = jnp.zeros_like(weight)

    @pl.loop(0, slots, unroll=4)
    def place(s):
        b = ids[s]

        @pl.when(b < total)
        def put():
            r = pl.multiple_of((b // cols_n) * size, size)
            c = pl.multiple_of((b % cols_n) * size, size)
            weight[pl.ds(r, size), pl.ds(c, size)] = blocks[s]

    step = 256

    @pl.loop(0, width // step)
    def forward(n):
        c = pl.multiple_of(n * step, step)
        proj[:, pl.ds(c, step)] = jnp.dot(
            tokens[...], weight[:, pl.ds(c, step)], preferred_element_type=jnp.float32
        ).astype(proj.dtype)

    @pl.loop(0, depth // step, unroll=4)
    def backward(n):
        r = pl.multiple_of(n * step, step)
        back[:, pl.ds(r, step)] = lax.dot_general(
            upstream[...],
            weight[pl.ds(r, step), :],
            (((1,), (1,)), ((), ())),
            preferred_element_type=jnp.float32,
        ).astype(back.dtype)


def project(ids, blocks, tokens, upstream):
    rows, depth = tokens.shape
    width = upstream.shape[1]
    return pl.pallas_call(
        project_kernel,
        out_shape=(
            jax.ShapeDtypeStruct((rows, width), jnp.bfloat16),
            jax.ShapeDtypeStruct((rows, depth), jnp.bfloat16),
        ),
        in_specs=[whole(pltpu.SMEM), whole(), whole(), whole()],
        out_specs=(whole(), whole()),
        scratch_shapes=[pltpu.VMEM((depth, width), jnp.bfloat16)],
        compiler_params=pltpu.CompilerParams(vmem_limit_bytes=VMEM_LIMIT),
        cost_estimate=pl.CostEstimate(
            flops=4 * rows * depth * width,
            bytes_accessed=blocks.size * 2 + rows * (depth + width) * 4,
            transcendentals=0,
        ),
        name="project",
    )(ids, blocks, tokens, upstream)


def block_grad_kernel(ids, tokens, upstream, grads):
    slots, size = grads.shape[0], grads.shape[1]
    parts, slabs, _, part_width = tokens.shape
    cols_n = upstream.shape[2] // size
    per_part = part_width // size
    total = parts * per_part * cols_n

    @pl.loop(0, slots)
    def one(s):
        b = ids[s]

        @pl.when(b < total)
        def fill():
            row = b // cols_n
            part = row // per_part
            r = pl.multiple_of((row % per_part) * size, size)
            c = pl.multiple_of((b % cols_n) * size, size)
            acc = jnp.zeros((size, size), jnp.float32)
            for k in range(slabs):
                acc += lax.dot_general(
                    tokens[part, k, :, pl.ds(r, size)],
                    upstream[k, :, pl.ds(c, size)],
                    (((0,), (0,)), ((), ())),
                    preferred_element_type=jnp.float32,
                )
            grads[s] = acc.astype(grads.dtype)

        @pl.when(b >= total)
        def clear():
            grads[s] = jnp.zeros((size, size), grads.dtype)


def block_grads(ids, tokens, upstream, size):
    slots = ids.shape[0]
    parts, slabs, rows, part_width = tokens.shape
    return pl.pallas_call(
        block_grad_kernel,
        out_shape=jax.ShapeDtypeStruct((slots, size, size), jnp.bfloat16),
        in_specs=[whole(pltpu.SMEM), whole(), whole()],
        out_specs=whole(),
        compiler_params=pltpu.CompilerParams(vmem_limit_bytes=VMEM_LIMIT),
        cost_estimate=pl.CostEstimate(
            flops=2 * slots * slabs * rows * size * size,
            bytes_accessed=2 * (tokens.size + upstream.size + slots * size * size),
            transcendentals=0,
        ),
        name="block_grads",
    )(ids, tokens, upstream)


def general_body(tokens, upstream, blocks, block_ids):
    size = blocks.shape[1]
    all_blocks = lax.all_gather(blocks, "dp", axis=0, tiled=True)
    all_ids = lax.all_gather(block_ids, "dp", axis=0, tiled=True)
    proj, back = project(all_ids, all_blocks, tokens, upstream)
    terms = block_grads(all_ids, tokens[None, None], upstream[None], size)
    grads = lax.psum_scatter(terms, "dp", scatter_dimension=0, tiled=True)
    return proj, lax.psum(back, INNER), grads


def place_blocks(ids, first, blocks, weight, turned, slots):
    size = blocks.shape[1]
    depth, width = turned.shape[::-1] if weight is None else weight.shape
    cols_n = width // size
    total = (depth // size) * cols_n
    group = math.gcd(slots, 8)

    @pl.loop(0, slots // group)
    def place(g):
        some = [g * group + j for j in range(group)]
        flipped = [None if turned is None else blocks[s].T for s in some]
        for s, flip in zip(some, flipped):
            b = ids[first + s]

            @pl.when(b < total)
            def put(s=s, flip=flip, b=b):
                r = pl.multiple_of((b // cols_n) * size, size)
                c = pl.multiple_of((b % cols_n) * size, size)
                if weight is not None:
                    weight[pl.ds(r, size), pl.ds(c, size)] = blocks[s]
                if turned is not None:
                    turned[pl.ds(c, size), pl.ds(r, size)] = flip


def place_kernel(
    place_of, ids_0, ids_1, ids_2, ids_3, own, near_a, far_a, far_b, end_a, weight, turned
):
    is_middle, half = place_of[0], place_of[1]
    half_slots = far_b.shape[0] - 1
    mine, other = half * half_slots, (1 - half) * half_slots

    @pl.when(is_middle == 1)
    def work():
        weight[...] = jnp.zeros_like(weight)
        turned[...] = jnp.zeros_like(turned)
        place_blocks(ids_0, 0, own, weight, turned, own.shape[0])
        place_blocks(ids_1, mine, near_a, weight, turned, half_slots)
        place_blocks(ids_2, mine, far_a, weight, turned, half_slots)
        place_blocks(ids_2, other, far_b, weight, turned, half_slots)
        place_blocks(ids_3, mine, end_a, weight, turned, half_slots)


def place_first(place_of, ids, pieces, depth, width):
    return pl.pallas_call(
        place_kernel,
        out_shape=(
            jax.ShapeDtypeStruct((depth, width), jnp.bfloat16),
            jax.ShapeDtypeStruct((width, depth), jnp.bfloat16),
        ),
        in_specs=[whole(pltpu.SMEM)] * 5 + [whole()] * 5,
        out_specs=(whole(), whole()),
        compiler_params=pltpu.CompilerParams(vmem_limit_bytes=VMEM_LIMIT),
        cost_estimate=pl.CostEstimate(
            flops=0, bytes_accessed=depth * width * 6, transcendentals=0
        ),
        name="place_first",
    )(place_of, *ids, *pieces)


def back_kernel(
    place_of, ids_1, ids_3, partial, near_b, end_b, end_upstream, upstream,
    end_keep, own_keep, own_give, end_give_0, end_give_1, held, sources, sem,
):
    half_slots = near_b.shape[0]
    other = (1 - place_of[1]) * half_slots
    rows, width = upstream.shape
    step = 256
    per_part = end_keep.shape[2] // step

    @pl.when(place_of[0] == 1)
    def work():
        load = pltpu.make_async_copy(partial, held, sem)
        load.start()
        sources[:rows] = end_upstream[...]
        sources[rows:] = upstream[...]
        load.wait()
        place_blocks(ids_1, other, near_b, None, held, half_slots)
        place_blocks(ids_3, other, end_b, None, held, half_slots)

        def column(part, end_target, own_target):
            @pl.loop(0, per_part, unroll=2)
            def backward(n):
                at = pl.multiple_of(n * step, step)
                result = jnp.dot(
                    sources[...],
                    held[:, pl.ds(pl.multiple_of(part * per_part * step + at, step), step)],
                    preferred_element_type=jnp.float32,
                ).astype(own_target.dtype)
                end_target[:, pl.ds(at, step)] = result[:rows]
                own_target[:, pl.ds(at, step)] = result[rows:]

        for x, end_give in enumerate((end_give_0, end_give_1)):
            column(2 * x + place_of[3], end_keep.at[x], own_keep.at[x])
            column(2 * x + 1 - place_of[3], end_give, own_give.at[x])


def project_back(place_of, ids_1, ids_3, partial, near_b, end_b, end_upstream, upstream):
    width, depth = partial.shape
    rows = upstream.shape[0]
    quarter = jax.ShapeDtypeStruct((rows, depth // 4), jnp.bfloat16)
    half = jax.ShapeDtypeStruct((2, rows, depth // 4), jnp.bfloat16)
    return pl.pallas_call(
        back_kernel,
        out_shape=(half, half, half, quarter, quarter),
        in_specs=[whole(pltpu.SMEM)] * 3 + [whole(pl.ANY)] + [whole()] * 4,
        out_specs=(whole(),) * 5,
        scratch_shapes=[
            pltpu.VMEM((width, depth), jnp.bfloat16),
            pltpu.VMEM((2 * rows, width), jnp.bfloat16),
            pltpu.SemaphoreType.DMA,
        ],
        compiler_params=pltpu.CompilerParams(vmem_limit_bytes=VMEM_LIMIT),
        cost_estimate=pl.CostEstimate(
            flops=4 * rows * depth * width,
            bytes_accessed=depth * width * 2 + rows * (depth + width) * 4,
            transcendentals=0,
        ),
        name="project_back",
    )(place_of, ids_1, ids_3, partial, near_b, end_b, end_upstream, upstream)


def forward_kernel(
    place_of, ids_1, ids_3, partial, near_b, end_b, tokens, gathered, proj, end_proj, held, sem
):
    half_slots = near_b.shape[0]
    other = (1 - place_of[1]) * half_slots
    depth, width = held.shape
    parts, rows, part_width = gathered.shape
    step = 256

    @pl.when(place_of[0] == 1)
    def work():
        load = pltpu.make_async_copy(partial, held, sem)
        load.start()
        load.wait()
        place_blocks(ids_1, other, near_b, held, None, half_slots)
        place_blocks(ids_3, other, end_b, held, None, half_slots)

        @pl.loop(0, width // step, unroll=2)
        def forward(n):
            c = pl.multiple_of(n * step, step)
            acc = jnp.zeros((rows, step), jnp.float32)
            for q in range(parts):
                acc += jnp.dot(
                    gathered[q],
                    held[q * part_width : (q + 1) * part_width, pl.ds(c, step)],
                    preferred_element_type=jnp.float32,
                )
            end_proj[:, pl.ds(c, step)] = acc.astype(end_proj.dtype)
            proj[:, pl.ds(c, step)] = jnp.dot(
                tokens[...], held[:, pl.ds(c, step)], preferred_element_type=jnp.float32
            ).astype(proj.dtype)


def project_forward(place_of, ids_1, ids_3, partial, near_b, end_b, tokens, gathered):
    depth, width = partial.shape
    rows = tokens.shape[0]
    out = jax.ShapeDtypeStruct((rows, width), jnp.bfloat16)
    return pl.pallas_call(
        forward_kernel,
        out_shape=(out, out),
        in_specs=[whole(pltpu.SMEM)] * 3 + [whole(pl.ANY)] + [whole()] * 4,
        out_specs=(whole(),) * 2,
        scratch_shapes=[pltpu.VMEM((depth, width), jnp.bfloat16), pltpu.SemaphoreType.DMA],
        compiler_params=pltpu.CompilerParams(vmem_limit_bytes=VMEM_LIMIT),
        cost_estimate=pl.CostEstimate(
            flops=rows * depth * width // 2, bytes_accessed=depth * width, transcendentals=0
        ),
        name="project_forward",
    )(place_of, ids_1, ids_3, partial, near_b, end_b, tokens, gathered)


def split_kernel(place_of, keep, *refs):
    x = place_of[2]
    own, give = refs[-2:]
    got = refs[:-2] if len(refs) > 3 else (refs[0].at[0], refs[0].at[1])
    for at in range(2):
        total = (keep[at].astype(jnp.float32) + got[at][...].astype(jnp.float32)).astype(own.dtype)

        @pl.when(x == at)
        def mine():
            own[...] = total

        @pl.when(x != at)
        def theirs():
            give[...] = total


def add_split(place_of, keep, *got):
    out = jax.ShapeDtypeStruct(keep.shape[1:], keep.dtype)
    return pl.pallas_call(
        split_kernel,
        out_shape=(out, out),
        in_specs=[whole(pltpu.SMEM), whole()] + [whole()] * len(got),
        out_specs=(whole(), whole()),
        compiler_params=pltpu.CompilerParams(vmem_limit_bytes=VMEM_LIMIT),
        cost_estimate=pl.CostEstimate(
            flops=keep.size, bytes_accessed=keep.size * 6, transcendentals=0
        ),
        name="add_split",
    )(place_of, keep, *got)


def assemble_kernel(place_of, own, by_core, by_tensor, by_both, full):
    x, c = place_of[2], place_of[3]
    width = own.shape[1]
    for ref, xx, cc in (
        (own, x, c), (by_core, x, 1 - c), (by_tensor, 1 - x, c), (by_both, 1 - x, 1 - c)
    ):
        at = pl.multiple_of((xx * 2 + cc) * width, width)
        full[:, pl.ds(at, width)] = ref[...]


def assemble(place_of, quarters):
    rows, width = quarters[0].shape
    return pl.pallas_call(
        assemble_kernel,
        out_shape=jax.ShapeDtypeStruct((rows, 4 * width), quarters[0].dtype),
        in_specs=[whole(pltpu.SMEM)] + [whole()] * 4,
        out_specs=whole(),
        compiler_params=pltpu.CompilerParams(vmem_limit_bytes=VMEM_LIMIT),
        cost_estimate=pl.CostEstimate(
            flops=0, bytes_accessed=rows * width * 16, transcendentals=0
        ),
        name="assemble",
    )(place_of, *quarters)


def line_grads_kernel(kind, ids, *refs):
    refs = list(refs)
    if kind == "halves":
        place_of = refs.pop(0)
        mine, theirs, before, after = (refs.pop(0) for _ in range(4))
        x, d = refs.pop(), refs.pop()
        for at in range(2):
            x[2 * place_of[3] + at] = mine[at]
            x[2 - 2 * place_of[3] + at] = theirs[at]
        d[...] = before[...] + after[...]
    elif kind == "sums":
        x, before, after = (refs.pop(0) for _ in range(3))
        d = refs.pop()
        rows = x.shape[-2]
        d[...] = before[rows:] + after[rows:]
    else:
        x, d = refs.pop(0), refs.pop(0)
    start = refs.pop(0) if len(refs) == 2 else None
    (grads,) = refs
    slots, size = grads.shape[0], grads.shape[1]
    cols_n = d.shape[1] // size
    per_part = x.shape[-1] // size
    total = per_part * (x.shape[0] if len(x.shape) == 3 else 1) * cols_n
    group = math.gcd(slots, 8)

    @pl.loop(0, slots // group)
    def some(g):
        for s in [g * group + j for j in range(group)]:
            b = jnp.minimum(ids[s], total - 1)
            row = b // cols_n
            at = pl.ds(pl.multiple_of((row % per_part) * size, size), size)
            acc = lax.dot_general(
                x[row // per_part, :, at] if len(x.shape) == 3 else x[:, at],
                d[:, pl.ds(pl.multiple_of((b % cols_n) * size, size), size)],
                (((0,), (0,)), ((), ())),
                preferred_element_type=jnp.float32,
            )
            if start is not None:
                acc += start[s].astype(jnp.float32)
            grads[s] = jnp.where(ids[s] < total, acc, 0.0).astype(grads.dtype)


def line_grads(kind, ids, operands, start, size):
    slots = ids.shape[0]
    flat = list(operands) + ([] if start is None else [start])
    specs = [whole(pltpu.SMEM)] + [whole()] * len(flat)
    scratch = []
    if kind == "sums":
        scratch = [pltpu.VMEM((operands[0].shape[-2], operands[-1].shape[1]), jnp.bfloat16)]
    if kind == "halves":
        specs[1] = whole(pltpu.SMEM)
        _, rows, part_width = operands[1].shape
        scratch = [
            pltpu.VMEM((rows, operands[-1].shape[1]), jnp.bfloat16),
            pltpu.VMEM((4, rows, part_width), jnp.bfloat16),
        ]
    return pl.pallas_call(
        functools.partial(line_grads_kernel, kind),
        out_shape=jax.ShapeDtypeStruct((slots, size, size), jnp.bfloat16),
        in_specs=specs,
        out_specs=whole(),
        scratch_shapes=scratch,
        compiler_params=pltpu.CompilerParams(vmem_limit_bytes=VMEM_LIMIT),
        cost_estimate=pl.CostEstimate(
            flops=512 * slots * size * size,
            bytes_accessed=sum(2 * a.size for a in flat) + 2 * slots * size * size,
            transcendentals=0,
        ),
        name="line_grads",
    )(ids, *flat)


INWARD = ((0, 1), (3, 2))
OUTWARD = ((1, 0), (2, 3))
PAIRS = INWARD + OUTWARD
MIDDLE = ((1, 2), (2, 1))
SWAP = ((0, 1), (1, 0))


def ids_block(block_ids, size):
    rows = size * size // block_ids.shape[0]
    return jnp.broadcast_to(block_ids, (rows, block_ids.shape[0])).reshape(1, size, size)


def ids_of(piece, slots):
    return piece[-1, 0, :slots].astype(jnp.int32)


def line_body(tokens, upstream, blocks, block_ids):
    slots, size = blocks.shape[0], blocks.shape[1]
    rows, depth = tokens.shape
    width = upstream.shape[1]
    half_slots = slots // 2
    part_width = depth // 4
    at_z, half = lax.axis_index("dp"), lax.axis_index("groups")
    at_tensor, at_replica = lax.axis_index("tensor"), lax.axis_index("replica")
    middle = (at_z == 1) | (at_z == 2)
    place_of = jnp.stack([middle.astype(jnp.int32), half, at_tensor, at_replica])
    along = functools.partial(lax.ppermute, axis_name="dp")
    across = functools.partial(lax.ppermute, axis_name="groups", perm=SWAP)
    sideways = functools.partial(lax.ppermute, axis_name="tensor", perm=SWAP)
    cores = functools.partial(lax.ppermute, axis_name="replica", perm=SWAP)
    stage = lax.optimization_barrier

    mine = lax.dynamic_slice_in_dim(blocks, half * half_slots, half_slots, 0)
    mine = jnp.concatenate([mine, ids_block(block_ids, size).astype(jnp.bfloat16)])
    mine, late_blocks = stage((mine, blocks))

    near_a = along(mine, perm=INWARD)
    far_a = along(mine, perm=MIDDLE)
    other = lax.dynamic_slice_in_dim(late_blocks, (1 - half) * half_slots, half_slots, 0)
    part = lax.dynamic_slice_in_dim(tokens, lax.axis_index(INNER) * part_width, part_width, 1)
    both = jnp.concatenate([part, upstream])
    grads = line_grads("plain", block_ids, (tokens, upstream), None, size)
    near_a, far_a, both, other, grads = stage((near_a, far_a, both, other, grads))

    end_a = along(near_a, perm=MIDDLE)
    far_b = across(far_a)
    both_1 = along(both, perm=PAIRS)
    both_1, end_a, far_b, both, other = stage((both_1, end_a, far_b, both, other))
    upstream_1 = both_1[rows:]

    near_b = along(other, perm=INWARD)
    end_b = across(end_a)
    both_2m = along(both, perm=MIDDLE)
    tokens_1 = lax.all_gather(both_1[:rows], INNER)
    ids_1, ids_2, ids_3 = (ids_of(piece, slots) for piece in (near_a, far_a, end_a))
    partial, turned = place_first(
        place_of, (block_ids, ids_1, ids_2, ids_3), (blocks, near_a, far_a, far_b, end_a), depth, width
    )
    half_1 = lax.dynamic_slice_in_dim(tokens_1, 2 * at_replica, 2, 0)
    near_b, end_b, both_2m, half_1, upstream_1, tokens_1, partial, turned = stage(
        (near_b, end_b, both_2m, half_1, upstream_1, tokens_1, partial, turned)
    )

    half_3m = along(half_1, perm=MIDDLE)
    both_2o = along(both_2m, perm=OUTWARD)
    last = (near_b, end_b)
    end_keep, own_keep, own_give, *end_give = project_back(
        place_of, ids_1, ids_3, turned, *last, upstream_1, upstream
    )
    end_keep, end_give = add_split(place_of, end_keep, *[cores(a) for a in end_give])
    end_keep, end_give, own_give, half_3m, both_2o = stage(
        (end_keep, end_give, own_give, half_3m, both_2o)
    )

    end_got = sideways(end_give)
    own_keep, own_give = add_split(place_of, own_keep, cores(own_give))
    half_3o = along(half_3m, perm=OUTWARD)
    upstream_3m = along(upstream_1, perm=MIDDLE)
    tokens_2 = lax.all_gather(both_2m[:rows] + both_2o[:rows], INNER)
    proj, end_proj = project_forward(place_of, ids_1, ids_3, partial, *last, tokens, tokens_1)
    end_got, own_give, own_keep, proj, end_proj, upstream_3m = stage(
        (end_got, own_give, own_keep, proj, end_proj, upstream_3m)
    )

    sum_out = along(end_keep + end_got, perm=OUTWARD)
    own_got = sideways(own_give)
    upstream_3o = along(upstream_3m, perm=OUTWARD)
    grads = line_grads("plain", block_ids, (tokens_1, upstream_1), grads, size)
    half_3 = half_3m + half_3o
    theirs_3 = cores(half_3)
    grads = line_grads("sums", block_ids, (tokens_2, both_2m, both_2o), grads, size)
    sum_out, own_got, half_3, theirs_3, upstream_3o, grads = stage(
        (sum_out, own_got, half_3, theirs_3, upstream_3o, grads)
    )

    quarter = jnp.where(middle, own_keep + own_got, sum_out)
    proj_out = along(end_proj, perm=OUTWARD)
    grads = line_grads(
        "halves", block_ids, (place_of, half_3, theirs_3, upstream_3m, upstream_3o), grads, size
    )
    by_tensor, by_core, proj_out, grads = stage(
        (sideways(quarter), cores(quarter), proj_out, grads)
    )
    by_both = cores(by_tensor)
    projected = jnp.where(middle, proj, proj_out)
    token_grad = assemble(place_of, (quarter, by_core, by_tensor, by_both))
    return projected, token_grad, grads


def solution(mesh):
    line = tuple(mesh.shape[a] for a in ("groups", "dp", "tensor", "replica")) == (2, 4, 2, 2)
    return jax.shard_map(
        line_body if line else general_body,
        mesh=mesh,
        in_specs=(
            P(("groups", "dp"), None),
            P(("groups", "dp"), INNER),
            P(("dp",) + INNER, None, None),
            P(("dp",) + INNER),
        ),
        out_specs=(
            P(("groups", "dp"), INNER),
            P(("groups", "dp"), None),
            P(("groups", "dp") + INNER, None, None),
        ),
        check_vma=False,
    )
```

```python
import functools
import math

import jax
import jax.numpy as jnp
from jax import lax
from jax.experimental import pallas as pl
from jax.experimental.pallas import tpu as pltpu
from jax.sharding import PartitionSpec as P

VMEM_LIMIT = 60 * 1024 * 1024
INNER = ("tensor", "replica")


def whole(space=pltpu.VMEM):
    return pl.BlockSpec(memory_space=space)


def project_kernel(ids, blocks, tokens, upstream, proj, back, weight):
    slots, size = blocks.shape[0], blocks.shape[1]
    depth, width = weight.shape
    cols_n = width // size
    total = (depth // size) * cols_n
    weight[...] = jnp.zeros_like(weight)

    @pl.loop(0, slots, unroll=4)
    def place(s):
        b = ids[s]

        @pl.when(b < total)
        def put():
            r = pl.multiple_of((b // cols_n) * size, size)
            c = pl.multiple_of((b % cols_n) * size, size)
            weight[pl.ds(r, size), pl.ds(c, size)] = blocks[s]

    step = 256

    @pl.loop(0, width // step)
    def forward(n):
        c = pl.multiple_of(n * step, step)
        proj[:, pl.ds(c, step)] = jnp.dot(
            tokens[...], weight[:, pl.ds(c, step)], preferred_element_type=jnp.float32
        ).astype(proj.dtype)

    @pl.loop(0, depth // step, unroll=4)
    def backward(n):
        r = pl.multiple_of(n * step, step)
        back[:, pl.ds(r, step)] = lax.dot_general(
            upstream[...],
            weight[pl.ds(r, step), :],
            (((1,), (1,)), ((), ())),
            preferred_element_type=jnp.float32,
        ).astype(back.dtype)


def project(ids, blocks, tokens, upstream):
    rows, depth = tokens.shape
    width = upstream.shape[1]
    return pl.pallas_call(
        project_kernel,
        out_shape=(
            jax.ShapeDtypeStruct((rows, width), jnp.bfloat16),
            jax.ShapeDtypeStruct((rows, depth), jnp.bfloat16),
        ),
        in_specs=[whole(pltpu.SMEM), whole(), whole(), whole()],
        out_specs=(whole(), whole()),
        scratch_shapes=[pltpu.VMEM((depth, width), jnp.bfloat16)],
        compiler_params=pltpu.CompilerParams(vmem_limit_bytes=VMEM_LIMIT),
        cost_estimate=pl.CostEstimate(
            flops=4 * rows * depth * width,
            bytes_accessed=blocks.size * 2 + rows * (depth + width) * 4,
            transcendentals=0,
        ),
        name="project",
    )(ids, blocks, tokens, upstream)


def block_grad_kernel(ids, tokens, upstream, grads):
    slots, size = grads.shape[0], grads.shape[1]
    parts, slabs, _, part_width = tokens.shape
    cols_n = upstream.shape[2] // size
    per_part = part_width // size
    total = parts * per_part * cols_n

    @pl.loop(0, slots)
    def one(s):
        b = ids[s]

        @pl.when(b < total)
        def fill():
            row = b // cols_n
            part = row // per_part
            r = pl.multiple_of((row % per_part) * size, size)
            c = pl.multiple_of((b % cols_n) * size, size)
            acc = jnp.zeros((size, size), jnp.float32)
            for k in range(slabs):
                acc += lax.dot_general(
                    tokens[part, k, :, pl.ds(r, size)],
                    upstream[k, :, pl.ds(c, size)],
                    (((0,), (0,)), ((), ())),
                    preferred_element_type=jnp.float32,
                )
            grads[s] = acc.astype(grads.dtype)

        @pl.when(b >= total)
        def clear():
            grads[s] = jnp.zeros((size, size), grads.dtype)


def block_grads(ids, tokens, upstream, size):
    slots = ids.shape[0]
    parts, slabs, rows, part_width = tokens.shape
    return pl.pallas_call(
        block_grad_kernel,
        out_shape=jax.ShapeDtypeStruct((slots, size, size), jnp.bfloat16),
        in_specs=[whole(pltpu.SMEM), whole(), whole()],
        out_specs=whole(),
        compiler_params=pltpu.CompilerParams(vmem_limit_bytes=VMEM_LIMIT),
        cost_estimate=pl.CostEstimate(
            flops=2 * slots * slabs * rows * size * size,
            bytes_accessed=2 * (tokens.size + upstream.size + slots * size * size),
            transcendentals=0,
        ),
        name="block_grads",
    )(ids, tokens, upstream)


def general_body(tokens, upstream, blocks, block_ids):
    size = blocks.shape[1]
    all_blocks = lax.all_gather(blocks, "dp", axis=0, tiled=True)
    all_ids = lax.all_gather(block_ids, "dp", axis=0, tiled=True)
    proj, back = project(all_ids, all_blocks, tokens, upstream)
    terms = block_grads(all_ids, tokens[None, None], upstream[None], size)
    grads = lax.psum_scatter(terms, "dp", scatter_dimension=0, tiled=True)
    return proj, lax.psum(back, INNER), grads


def place_blocks(ids, first, blocks, weight, turned, slots):
    size = blocks.shape[1]
    depth, width = turned.shape[::-1] if weight is None else weight.shape
    cols_n = width // size
    total = (depth // size) * cols_n
    group = math.gcd(slots, 8)

    @pl.loop(0, slots // group)
    def place(g):
        some = [g * group + j for j in range(group)]
        flipped = [None if turned is None else blocks[s].T for s in some]
        for s, flip in zip(some, flipped):
            b = ids[first + s]

            @pl.when(b < total)
            def put(s=s, flip=flip, b=b):
                r = pl.multiple_of((b // cols_n) * size, size)
                c = pl.multiple_of((b % cols_n) * size, size)
                if weight is not None:
                    weight[pl.ds(r, size), pl.ds(c, size)] = blocks[s]
                if turned is not None:
                    turned[pl.ds(c, size), pl.ds(r, size)] = flip


def place_kernel(
    place_of, ids_0, ids_1, ids_2, ids_3, own, near_a, far_a, far_b, end_a, weight, turned
):
    is_middle, half = place_of[0], place_of[1]
    half_slots = far_b.shape[0] - 1
    mine, other = half * half_slots, (1 - half) * half_slots

    @pl.when(is_middle == 1)
    def work():
        weight[...] = jnp.zeros_like(weight)
        turned[...] = jnp.zeros_like(turned)
        place_blocks(ids_0, 0, own, weight, turned, own.shape[0])
        place_blocks(ids_1, mine, near_a, weight, turned, half_slots)
        place_blocks(ids_2, mine, far_a, weight, turned, half_slots)
        place_blocks(ids_2, other, far_b, weight, turned, half_slots)
        place_blocks(ids_3, mine, end_a, weight, turned, half_slots)


def place_first(place_of, ids, pieces, depth, width):
    return pl.pallas_call(
        place_kernel,
        out_shape=(
            jax.ShapeDtypeStruct((depth, width), jnp.bfloat16),
            jax.ShapeDtypeStruct((width, depth), jnp.bfloat16),
        ),
        in_specs=[whole(pltpu.SMEM)] * 5 + [whole()] * 5,
        out_specs=(whole(), whole()),
        compiler_params=pltpu.CompilerParams(vmem_limit_bytes=VMEM_LIMIT),
        cost_estimate=pl.CostEstimate(
            flops=0, bytes_accessed=depth * width * 6, transcendentals=0
        ),
        name="place_first",
    )(place_of, *ids, *pieces)


def back_kernel(
    place_of, ids_1, ids_3, partial, near_b, end_b, end_upstream, upstream,
    end_keep, own_keep, own_give, end_give_0, end_give_1, held, sources, sem,
):
    half_slots = near_b.shape[0]
    other = (1 - place_of[1]) * half_slots
    rows, width = upstream.shape
    step = 256
    per_part = end_keep.shape[2] // step

    @pl.when(place_of[0] == 1)
    def work():
        load = pltpu.make_async_copy(partial, held, sem)
        load.start()
        sources[:rows] = end_upstream[...]
        sources[rows:] = upstream[...]
        load.wait()
        place_blocks(ids_1, other, near_b, None, held, half_slots)
        place_blocks(ids_3, other, end_b, None, held, half_slots)

        def column(part, end_target, own_target):
            @pl.loop(0, per_part, unroll=2)
            def backward(n):
                at = pl.multiple_of(n * step, step)
                result = jnp.dot(
                    sources[...],
                    held[:, pl.ds(pl.multiple_of(part * per_part * step + at, step), step)],
                    preferred_element_type=jnp.float32,
                ).astype(own_target.dtype)
                end_target[:, pl.ds(at, step)] = result[:rows]
                own_target[:, pl.ds(at, step)] = result[rows:]

        for x, end_give in enumerate((end_give_0, end_give_1)):
            column(2 * x + place_of[3], end_keep.at[x], own_keep.at[x])
            column(2 * x + 1 - place_of[3], end_give, own_give.at[x])


def project_back(place_of, ids_1, ids_3, partial, near_b, end_b, end_upstream, upstream):
    width, depth = partial.shape
    rows = upstream.shape[0]
    quarter = jax.ShapeDtypeStruct((rows, depth // 4), jnp.bfloat16)
    half = jax.ShapeDtypeStruct((2, rows, depth // 4), jnp.bfloat16)
    return pl.pallas_call(
        back_kernel,
        out_shape=(half, half, half, quarter, quarter),
        in_specs=[whole(pltpu.SMEM)] * 3 + [whole(pl.ANY)] + [whole()] * 4,
        out_specs=(whole(),) * 5,
        scratch_shapes=[
            pltpu.VMEM((width, depth), jnp.bfloat16),
            pltpu.VMEM((2 * rows, width), jnp.bfloat16),
            pltpu.SemaphoreType.DMA,
        ],
        compiler_params=pltpu.CompilerParams(vmem_limit_bytes=VMEM_LIMIT),
        cost_estimate=pl.CostEstimate(
            flops=4 * rows * depth * width,
            bytes_accessed=depth * width * 2 + rows * (depth + width) * 4,
            transcendentals=0,
        ),
        name="project_back",
    )(place_of, ids_1, ids_3, partial, near_b, end_b, end_upstream, upstream)


def forward_kernel(
    place_of, ids_1, ids_3, partial, near_b, end_b, tokens, gathered, proj, end_proj, held, sem
):
    half_slots = near_b.shape[0]
    other = (1 - place_of[1]) * half_slots
    depth, width = held.shape
    parts, rows, part_width = gathered.shape
    step = 256

    @pl.when(place_of[0] == 1)
    def work():
        load = pltpu.make_async_copy(partial, held, sem)
        load.start()
        load.wait()
        place_blocks(ids_1, other, near_b, held, None, half_slots)
        place_blocks(ids_3, other, end_b, held, None, half_slots)

        @pl.loop(0, width // step, unroll=2)
        def forward(n):
            c = pl.multiple_of(n * step, step)
            acc = jnp.zeros((rows, step), jnp.float32)
            for q in range(parts):
                acc += jnp.dot(
                    gathered[q],
                    held[q * part_width : (q + 1) * part_width, pl.ds(c, step)],
                    preferred_element_type=jnp.float32,
                )
            end_proj[:, pl.ds(c, step)] = acc.astype(end_proj.dtype)
            proj[:, pl.ds(c, step)] = jnp.dot(
                tokens[...], held[:, pl.ds(c, step)], preferred_element_type=jnp.float32
            ).astype(proj.dtype)


def project_forward(place_of, ids_1, ids_3, partial, near_b, end_b, tokens, gathered):
    depth, width = partial.shape
    rows = tokens.shape[0]
    out = jax.ShapeDtypeStruct((rows, width), jnp.bfloat16)
    return pl.pallas_call(
        forward_kernel,
        out_shape=(out, out),
        in_specs=[whole(pltpu.SMEM)] * 3 + [whole(pl.ANY)] + [whole()] * 4,
        out_specs=(whole(),) * 2,
        scratch_shapes=[pltpu.VMEM((depth, width), jnp.bfloat16), pltpu.SemaphoreType.DMA],
        compiler_params=pltpu.CompilerParams(vmem_limit_bytes=VMEM_LIMIT),
        cost_estimate=pl.CostEstimate(
            flops=rows * depth * width // 2, bytes_accessed=depth * width, transcendentals=0
        ),
        name="project_forward",
    )(place_of, ids_1, ids_3, partial, near_b, end_b, tokens, gathered)


def split_kernel(place_of, keep, *refs):
    x = place_of[2]
    own, give = refs[-2:]
    got = refs[:-2] if len(refs) > 3 else (refs[0].at[0], refs[0].at[1])
    for at in range(2):
        total = (keep[at].astype(jnp.float32) + got[at][...].astype(jnp.float32)).astype(own.dtype)

        @pl.when(x == at)
        def mine():
            own[...] = total

        @pl.when(x != at)
        def theirs():
            give[...] = total


def add_split(place_of, keep, *got):
    out = jax.ShapeDtypeStruct(keep.shape[1:], keep.dtype)
    return pl.pallas_call(
        split_kernel,
        out_shape=(out, out),
        in_specs=[whole(pltpu.SMEM), whole()] + [whole()] * len(got),
        out_specs=(whole(), whole()),
        compiler_params=pltpu.CompilerParams(vmem_limit_bytes=VMEM_LIMIT),
        cost_estimate=pl.CostEstimate(
            flops=keep.size, bytes_accessed=keep.size * 6, transcendentals=0
        ),
        name="add_split",
    )(place_of, keep, *got)


def assemble_kernel(place_of, own, by_core, by_tensor, by_both, full):
    x, c = place_of[2], place_of[3]
    width = own.shape[1]
    for ref, xx, cc in (
        (own, x, c), (by_core, x, 1 - c), (by_tensor, 1 - x, c), (by_both, 1 - x, 1 - c)
    ):
        at = pl.multiple_of((xx * 2 + cc) * width, width)
        full[:, pl.ds(at, width)] = ref[...]


def assemble(place_of, quarters):
    rows, width = quarters[0].shape
    return pl.pallas_call(
        assemble_kernel,
        out_shape=jax.ShapeDtypeStruct((rows, 4 * width), quarters[0].dtype),
        in_specs=[whole(pltpu.SMEM)] + [whole()] * 4,
        out_specs=whole(),
        compiler_params=pltpu.CompilerParams(vmem_limit_bytes=VMEM_LIMIT),
        cost_estimate=pl.CostEstimate(
            flops=0, bytes_accessed=rows * width * 16, transcendentals=0
        ),
        name="assemble",
    )(place_of, *quarters)


def line_grads_kernel(kind, ids, *refs):
    refs = list(refs)
    if kind == "halves":
        place_of = refs.pop(0)
        mine, theirs, before, after = (refs.pop(0) for _ in range(4))
        x, d = refs.pop(), refs.pop()
        for at in range(2):
            x[2 * place_of[3] + at] = mine[at]
            x[2 - 2 * place_of[3] + at] = theirs[at]
        d[...] = before[...] + after[...]
    elif kind == "sums":
        x, before, after = (refs.pop(0) for _ in range(3))
        d = refs.pop()
        rows = x.shape[-2]
        d[...] = before[rows:] + after[rows:]
    else:
        x, d = refs.pop(0), refs.pop(0)
    start = refs.pop(0) if len(refs) == 2 else None
    (grads,) = refs
    slots, size = grads.shape[0], grads.shape[1]
    cols_n = d.shape[1] // size
    per_part = x.shape[-1] // size
    total = per_part * (x.shape[0] if len(x.shape) == 3 else 1) * cols_n
    group = math.gcd(slots, 8)

    @pl.loop(0, slots // group)
    def some(g):
        for s in [g * group + j for j in range(group)]:
            b = jnp.minimum(ids[s], total - 1)
            row = b // cols_n
            at = pl.ds(pl.multiple_of((row % per_part) * size, size), size)
            acc = lax.dot_general(
                x[row // per_part, :, at] if len(x.shape) == 3 else x[:, at],
                d[:, pl.ds(pl.multiple_of((b % cols_n) * size, size), size)],
                (((0,), (0,)), ((), ())),
                preferred_element_type=jnp.float32,
            )
            if start is not None:
                acc += start[s].astype(jnp.float32)
            grads[s] = jnp.where(ids[s] < total, acc, 0.0).astype(grads.dtype)


def line_grads(kind, ids, operands, start, size):
    slots = ids.shape[0]
    flat = list(operands) + ([] if start is None else [start])
    specs = [whole(pltpu.SMEM)] + [whole()] * len(flat)
    scratch = []
    if kind == "sums":
        scratch = [pltpu.VMEM((operands[0].shape[-2], operands[-1].shape[1]), jnp.bfloat16)]
    if kind == "halves":
        specs[1] = whole(pltpu.SMEM)
        _, rows, part_width = operands[1].shape
        scratch = [
            pltpu.VMEM((rows, operands[-1].shape[1]), jnp.bfloat16),
            pltpu.VMEM((4, rows, part_width), jnp.bfloat16),
        ]
    return pl.pallas_call(
        functools.partial(line_grads_kernel, kind),
        out_shape=jax.ShapeDtypeStruct((slots, size, size), jnp.bfloat16),
        in_specs=specs,
        out_specs=whole(),
        scratch_shapes=scratch,
        compiler_params=pltpu.CompilerParams(vmem_limit_bytes=VMEM_LIMIT),
        cost_estimate=pl.CostEstimate(
            flops=512 * slots * size * size,
            bytes_accessed=sum(2 * a.size for a in flat) + 2 * slots * size * size,
            transcendentals=0,
        ),
        name="line_grads",
    )(ids, *flat)


INWARD = ((0, 1), (3, 2))
OUTWARD = ((1, 0), (2, 3))
PAIRS = INWARD + OUTWARD
MIDDLE = ((1, 2), (2, 1))
SWAP = ((0, 1), (1, 0))


def ids_block(block_ids, size):
    rows = size * size // block_ids.shape[0]
    return jnp.broadcast_to(block_ids, (rows, block_ids.shape[0])).reshape(1, size, size)


def ids_of(piece, slots):
    return piece[-1, 0, :slots].astype(jnp.int32)


def line_body(tokens, upstream, blocks, block_ids):
    slots, size = blocks.shape[0], blocks.shape[1]
    rows, depth = tokens.shape
    width = upstream.shape[1]
    half_slots = slots // 2
    part_width = depth // 4
    at_z, half = lax.axis_index("dp"), lax.axis_index("groups")
    at_tensor, at_replica = lax.axis_index("tensor"), lax.axis_index("replica")
    middle = (at_z == 1) | (at_z == 2)
    place_of = jnp.stack([middle.astype(jnp.int32), half, at_tensor, at_replica])
    along = functools.partial(lax.ppermute, axis_name="dp")
    across = functools.partial(lax.ppermute, axis_name="groups", perm=SWAP)
    sideways = functools.partial(lax.ppermute, axis_name="tensor", perm=SWAP)
    cores = functools.partial(lax.ppermute, axis_name="replica", perm=SWAP)
    stage = lax.optimization_barrier

    mine = lax.dynamic_slice_in_dim(blocks, half * half_slots, half_slots, 0)
    mine = jnp.concatenate([mine, ids_block(block_ids, size).astype(jnp.bfloat16)])
    mine, late_blocks = stage((mine, blocks))

    near_a = along(mine, perm=INWARD)
    far_a = along(mine, perm=MIDDLE)
    other = lax.dynamic_slice_in_dim(late_blocks, (1 - half) * half_slots, half_slots, 0)
    part = lax.dynamic_slice_in_dim(tokens, lax.axis_index(INNER) * part_width, part_width, 1)
    both = jnp.concatenate([part, upstream])
    grads = line_grads("plain", block_ids, (tokens, upstream), None, size)
    near_a, far_a, both, other, grads = stage((near_a, far_a, both, other, grads))

    end_a = along(near_a, perm=MIDDLE)
    far_b = across(far_a)
    both_1 = along(both, perm=PAIRS)
    both_1, end_a, far_b, both, other = stage((both_1, end_a, far_b, both, other))
    upstream_1 = both_1[rows:]

    near_b = along(other, perm=INWARD)
    end_b = across(end_a)
    both_2m = along(both, perm=MIDDLE)
    tokens_1 = lax.all_gather(both_1[:rows], INNER)
    ids_1, ids_2, ids_3 = (ids_of(piece, slots) for piece in (near_a, far_a, end_a))
    partial, turned = place_first(
        place_of, (block_ids, ids_1, ids_2, ids_3), (blocks, near_a, far_a, far_b, end_a), depth, width
    )
    half_1 = lax.dynamic_slice_in_dim(tokens_1, 2 * at_replica, 2, 0)
    near_b, end_b, both_2m, half_1, upstream_1, tokens_1, partial, turned = stage(
        (near_b, end_b, both_2m, half_1, upstream_1, tokens_1, partial, turned)
    )

    half_3m = along(half_1, perm=MIDDLE)
    both_2o = along(both_2m, perm=OUTWARD)
    last = (near_b, end_b)
    end_keep, own_keep, own_give, *end_give = project_back(
        place_of, ids_1, ids_3, turned, *last, upstream_1, upstream
    )
    end_keep, end_give = add_split(place_of, end_keep, *[cores(a) for a in end_give])
    end_keep, end_give, own_give, half_3m, both_2o = stage(
        (end_keep, end_give, own_give, half_3m, both_2o)
    )

    end_got = sideways(end_give)
    own_keep, own_give = add_split(place_of, own_keep, cores(own_give))
    half_3o = along(half_3m, perm=OUTWARD)
    upstream_3m = along(upstream_1, perm=MIDDLE)
    tokens_2 = lax.all_gather(both_2m[:rows] + both_2o[:rows], INNER)
    proj, end_proj = project_forward(place_of, ids_1, ids_3, partial, *last, tokens, tokens_1)
    end_got, own_give, own_keep, proj, end_proj, upstream_3m, upstream_1 = stage(
        (end_got, own_give, own_keep, proj, end_proj, upstream_3m, upstream_1)
    )

    sum_out = along(end_keep + end_got, perm=OUTWARD)
    own_got = sideways(own_give)
    upstream_3o = along(upstream_3m, perm=OUTWARD)
    grads = line_grads("plain", block_ids, (tokens_1, upstream_1), grads, size)
    half_3m, grads = stage((half_3m, grads))
    half_3 = half_3m + half_3o
    theirs_3 = cores(half_3)
    grads = line_grads("sums", block_ids, (tokens_2, both_2m, both_2o), grads, size)
    sum_out, own_got, half_3, theirs_3, upstream_3o, grads = stage(
        (sum_out, own_got, half_3, theirs_3, upstream_3o, grads)
    )

    quarter = jnp.where(middle, own_keep + own_got, sum_out)
    proj_out = along(end_proj, perm=OUTWARD)
    grads = line_grads(
        "halves", block_ids, (place_of, half_3, theirs_3, upstream_3m, upstream_3o), grads, size
    )
    by_tensor, by_core, proj_out, grads = stage(
        (sideways(quarter), cores(quarter), proj_out, grads)
    )
    by_both = cores(by_tensor)
    projected = jnp.where(middle, proj, proj_out)
    token_grad = assemble(place_of, (quarter, by_core, by_tensor, by_both))
    return projected, token_grad, grads


def solution(mesh):
    line = tuple(mesh.shape[a] for a in ("groups", "dp", "tensor", "replica")) == (2, 4, 2, 2)
    return jax.shard_map(
        line_body if line else general_body,
        mesh=mesh,
        in_specs=(
            P(("groups", "dp"), None),
            P(("groups", "dp"), INNER),
            P(("dp",) + INNER, None, None),
            P(("dp",) + INNER),
        ),
        out_specs=(
            P(("groups", "dp"), INNER),
            P(("groups", "dp"), None),
            P(("groups", "dp") + INNER, None, None),
        ),
        check_vma=False,
    )
```

```python
import functools
import math

import jax
import jax.numpy as jnp
from jax import lax
from jax.experimental import pallas as pl
from jax.experimental.pallas import tpu as pltpu
from jax.sharding import PartitionSpec as P

VMEM_LIMIT = 60 * 1024 * 1024
INNER = ("tensor", "replica")


def whole(space=pltpu.VMEM):
    return pl.BlockSpec(memory_space=space)


def project_kernel(ids, blocks, tokens, upstream, proj, back, weight):
    slots, size = blocks.shape[0], blocks.shape[1]
    depth, width = weight.shape
    cols_n = width // size
    total = (depth // size) * cols_n
    weight[...] = jnp.zeros_like(weight)

    @pl.loop(0, slots, unroll=4)
    def place(s):
        b = ids[s]

        @pl.when(b < total)
        def put():
            r = pl.multiple_of((b // cols_n) * size, size)
            c = pl.multiple_of((b % cols_n) * size, size)
            weight[pl.ds(r, size), pl.ds(c, size)] = blocks[s]

    step = 256

    @pl.loop(0, width // step)
    def forward(n):
        c = pl.multiple_of(n * step, step)
        proj[:, pl.ds(c, step)] = jnp.dot(
            tokens[...], weight[:, pl.ds(c, step)], preferred_element_type=jnp.float32
        ).astype(proj.dtype)

    @pl.loop(0, depth // step, unroll=4)
    def backward(n):
        r = pl.multiple_of(n * step, step)
        back[:, pl.ds(r, step)] = lax.dot_general(
            upstream[...],
            weight[pl.ds(r, step), :],
            (((1,), (1,)), ((), ())),
            preferred_element_type=jnp.float32,
        ).astype(back.dtype)


def project(ids, blocks, tokens, upstream):
    rows, depth = tokens.shape
    width = upstream.shape[1]
    return pl.pallas_call(
        project_kernel,
        out_shape=(
            jax.ShapeDtypeStruct((rows, width), jnp.bfloat16),
            jax.ShapeDtypeStruct((rows, depth), jnp.bfloat16),
        ),
        in_specs=[whole(pltpu.SMEM), whole(), whole(), whole()],
        out_specs=(whole(), whole()),
        scratch_shapes=[pltpu.VMEM((depth, width), jnp.bfloat16)],
        compiler_params=pltpu.CompilerParams(vmem_limit_bytes=VMEM_LIMIT),
        cost_estimate=pl.CostEstimate(
            flops=4 * rows * depth * width,
            bytes_accessed=blocks.size * 2 + rows * (depth + width) * 4,
            transcendentals=0,
        ),
        name="project",
    )(ids, blocks, tokens, upstream)


def block_grad_kernel(ids, tokens, upstream, grads):
    slots, size = grads.shape[0], grads.shape[1]
    parts, slabs, _, part_width = tokens.shape
    cols_n = upstream.shape[2] // size
    per_part = part_width // size
    total = parts * per_part * cols_n

    @pl.loop(0, slots)
    def one(s):
        b = ids[s]

        @pl.when(b < total)
        def fill():
            row = b // cols_n
            part = row // per_part
            r = pl.multiple_of((row % per_part) * size, size)
            c = pl.multiple_of((b % cols_n) * size, size)
            acc = jnp.zeros((size, size), jnp.float32)
            for k in range(slabs):
                acc += lax.dot_general(
                    tokens[part, k, :, pl.ds(r, size)],
                    upstream[k, :, pl.ds(c, size)],
                    (((0,), (0,)), ((), ())),
                    preferred_element_type=jnp.float32,
                )
            grads[s] = acc.astype(grads.dtype)

        @pl.when(b >= total)
        def clear():
            grads[s] = jnp.zeros((size, size), grads.dtype)


def block_grads(ids, tokens, upstream, size):
    slots = ids.shape[0]
    parts, slabs, rows, part_width = tokens.shape
    return pl.pallas_call(
        block_grad_kernel,
        out_shape=jax.ShapeDtypeStruct((slots, size, size), jnp.bfloat16),
        in_specs=[whole(pltpu.SMEM), whole(), whole()],
        out_specs=whole(),
        compiler_params=pltpu.CompilerParams(vmem_limit_bytes=VMEM_LIMIT),
        cost_estimate=pl.CostEstimate(
            flops=2 * slots * slabs * rows * size * size,
            bytes_accessed=2 * (tokens.size + upstream.size + slots * size * size),
            transcendentals=0,
        ),
        name="block_grads",
    )(ids, tokens, upstream)


def general_body(tokens, upstream, blocks, block_ids):
    size = blocks.shape[1]
    all_blocks = lax.all_gather(blocks, "dp", axis=0, tiled=True)
    all_ids = lax.all_gather(block_ids, "dp", axis=0, tiled=True)
    proj, back = project(all_ids, all_blocks, tokens, upstream)
    terms = block_grads(all_ids, tokens[None, None], upstream[None], size)
    grads = lax.psum_scatter(terms, "dp", scatter_dimension=0, tiled=True)
    return proj, lax.psum(back, INNER), grads


def place_blocks(ids, first, blocks, weight, turned, slots):
    size = blocks.shape[1]
    depth, width = turned.shape[::-1] if weight is None else weight.shape
    cols_n = width // size
    total = (depth // size) * cols_n
    group = math.gcd(slots, 8)

    @pl.loop(0, slots // group)
    def place(g):
        some = [g * group + j for j in range(group)]
        flipped = [None if turned is None else blocks[s].T for s in some]
        for s, flip in zip(some, flipped):
            b = ids[first + s]

            @pl.when(b < total)
            def put(s=s, flip=flip, b=b):
                r = pl.multiple_of((b // cols_n) * size, size)
                c = pl.multiple_of((b % cols_n) * size, size)
                if weight is not None:
                    weight[pl.ds(r, size), pl.ds(c, size)] = blocks[s]
                if turned is not None:
                    turned[pl.ds(c, size), pl.ds(r, size)] = flip


def place_kernel(
    place_of, ids_0, ids_1, ids_2, ids_3, own, near_a, far_a, far_b, end_a, weight, turned
):
    is_middle, half = place_of[0], place_of[1]
    half_slots = far_b.shape[0] - 1
    mine, other = half * half_slots, (1 - half) * half_slots

    @pl.when(is_middle == 1)
    def work():
        weight[...] = jnp.zeros_like(weight)
        turned[...] = jnp.zeros_like(turned)
        place_blocks(ids_0, 0, own, weight, turned, own.shape[0])
        place_blocks(ids_1, mine, near_a, weight, turned, half_slots)
        place_blocks(ids_2, mine, far_a, weight, turned, half_slots)
        place_blocks(ids_2, other, far_b, weight, turned, half_slots)
        place_blocks(ids_3, mine, end_a, weight, turned, half_slots)


def place_first(place_of, ids, pieces, depth, width):
    return pl.pallas_call(
        place_kernel,
        out_shape=(
            jax.ShapeDtypeStruct((depth, width), jnp.bfloat16),
            jax.ShapeDtypeStruct((width, depth), jnp.bfloat16),
        ),
        in_specs=[whole(pltpu.SMEM)] * 5 + [whole()] * 5,
        out_specs=(whole(), whole()),
        compiler_params=pltpu.CompilerParams(vmem_limit_bytes=VMEM_LIMIT),
        cost_estimate=pl.CostEstimate(
            flops=0, bytes_accessed=depth * width * 6, transcendentals=0
        ),
        name="place_first",
    )(place_of, *ids, *pieces)


def back_kernel(
    place_of, ids_1, ids_3, partial, near_b, end_b, end_upstream, upstream,
    end_keep, own_keep, own_give, end_give_0, end_give_1, held, sources, sem,
):
    half_slots = near_b.shape[0]
    other = (1 - place_of[1]) * half_slots
    rows, width = upstream.shape
    step = 256
    per_part = end_keep.shape[2] // step

    @pl.when(place_of[0] == 1)
    def work():
        load = pltpu.make_async_copy(partial, held, sem)
        load.start()
        sources[:rows] = end_upstream[...]
        sources[rows:] = upstream[...]
        load.wait()
        place_blocks(ids_1, other, near_b, None, held, half_slots)
        place_blocks(ids_3, other, end_b, None, held, half_slots)

        def column(part, end_target, own_target):
            @pl.loop(0, per_part, unroll=2)
            def backward(n):
                at = pl.multiple_of(n * step, step)
                result = jnp.dot(
                    sources[...],
                    held[:, pl.ds(pl.multiple_of(part * per_part * step + at, step), step)],
                    preferred_element_type=jnp.float32,
                ).astype(own_target.dtype)
                end_target[:, pl.ds(at, step)] = result[:rows]
                own_target[:, pl.ds(at, step)] = result[rows:]

        for x, end_give in enumerate((end_give_0, end_give_1)):
            column(2 * x + place_of[3], end_keep.at[x], own_keep.at[x])
            column(2 * x + 1 - place_of[3], end_give, own_give.at[x])


def project_back(place_of, ids_1, ids_3, partial, near_b, end_b, end_upstream, upstream):
    width, depth = partial.shape
    rows = upstream.shape[0]
    quarter = jax.ShapeDtypeStruct((rows, depth // 4), jnp.bfloat16)
    half = jax.ShapeDtypeStruct((2, rows, depth // 4), jnp.bfloat16)
    return pl.pallas_call(
        back_kernel,
        out_shape=(half, half, half, quarter, quarter),
        in_specs=[whole(pltpu.SMEM)] * 3 + [whole(pl.ANY)] + [whole()] * 4,
        out_specs=(whole(),) * 5,
        scratch_shapes=[
            pltpu.VMEM((width, depth), jnp.bfloat16),
            pltpu.VMEM((2 * rows, width), jnp.bfloat16),
            pltpu.SemaphoreType.DMA,
        ],
        compiler_params=pltpu.CompilerParams(vmem_limit_bytes=VMEM_LIMIT),
        cost_estimate=pl.CostEstimate(
            flops=4 * rows * depth * width,
            bytes_accessed=depth * width * 2 + rows * (depth + width) * 4,
            transcendentals=0,
        ),
        name="project_back",
    )(place_of, ids_1, ids_3, partial, near_b, end_b, end_upstream, upstream)


def forward_kernel(
    place_of, ids_1, ids_3, partial, near_b, end_b, tokens, gathered, proj, end_proj, held, sem
):
    half_slots = near_b.shape[0]
    other = (1 - place_of[1]) * half_slots
    depth, width = held.shape
    parts, rows, part_width = gathered.shape
    step = 256

    @pl.when(place_of[0] == 1)
    def work():
        load = pltpu.make_async_copy(partial, held, sem)
        load.start()
        load.wait()
        place_blocks(ids_1, other, near_b, held, None, half_slots)
        place_blocks(ids_3, other, end_b, held, None, half_slots)

        @pl.loop(0, width // step, unroll=2)
        def forward(n):
            c = pl.multiple_of(n * step, step)
            acc = jnp.zeros((rows, step), jnp.float32)
            for q in range(parts):
                acc += jnp.dot(
                    gathered[q],
                    held[q * part_width : (q + 1) * part_width, pl.ds(c, step)],
                    preferred_element_type=jnp.float32,
                )
            end_proj[:, pl.ds(c, step)] = acc.astype(end_proj.dtype)
            proj[:, pl.ds(c, step)] = jnp.dot(
                tokens[...], held[:, pl.ds(c, step)], preferred_element_type=jnp.float32
            ).astype(proj.dtype)


def project_forward(place_of, ids_1, ids_3, partial, near_b, end_b, tokens, gathered):
    depth, width = partial.shape
    rows = tokens.shape[0]
    out = jax.ShapeDtypeStruct((rows, width), jnp.bfloat16)
    return pl.pallas_call(
        forward_kernel,
        out_shape=(out, out),
        in_specs=[whole(pltpu.SMEM)] * 3 + [whole(pl.ANY)] + [whole()] * 4,
        out_specs=(whole(),) * 2,
        scratch_shapes=[pltpu.VMEM((depth, width), jnp.bfloat16), pltpu.SemaphoreType.DMA],
        compiler_params=pltpu.CompilerParams(vmem_limit_bytes=VMEM_LIMIT),
        cost_estimate=pl.CostEstimate(
            flops=rows * depth * width // 2, bytes_accessed=depth * width, transcendentals=0
        ),
        name="project_forward",
    )(place_of, ids_1, ids_3, partial, near_b, end_b, tokens, gathered)


def split_kernel(place_of, keep, *refs):
    x = place_of[2]
    own, give = refs[-2:]
    got = refs[:-2] if len(refs) > 3 else (refs[0].at[0], refs[0].at[1])
    for at in range(2):
        total = (keep[at].astype(jnp.float32) + got[at][...].astype(jnp.float32)).astype(own.dtype)

        @pl.when(x == at)
        def mine():
            own[...] = total

        @pl.when(x != at)
        def theirs():
            give[...] = total


def add_split(place_of, keep, *got):
    out = jax.ShapeDtypeStruct(keep.shape[1:], keep.dtype)
    return pl.pallas_call(
        split_kernel,
        out_shape=(out, out),
        in_specs=[whole(pltpu.SMEM), whole()] + [whole()] * len(got),
        out_specs=(whole(), whole()),
        compiler_params=pltpu.CompilerParams(vmem_limit_bytes=VMEM_LIMIT),
        cost_estimate=pl.CostEstimate(
            flops=keep.size, bytes_accessed=keep.size * 6, transcendentals=0
        ),
        name="add_split",
    )(place_of, keep, *got)


def assemble_kernel(place_of, own, by_core, by_tensor, by_both, full):
    x, c = place_of[2], place_of[3]
    width = own.shape[1]
    for ref, xx, cc in (
        (own, x, c), (by_core, x, 1 - c), (by_tensor, 1 - x, c), (by_both, 1 - x, 1 - c)
    ):
        at = pl.multiple_of((xx * 2 + cc) * width, width)
        full[:, pl.ds(at, width)] = ref[...]


def assemble(place_of, quarters):
    rows, width = quarters[0].shape
    return pl.pallas_call(
        assemble_kernel,
        out_shape=jax.ShapeDtypeStruct((rows, 4 * width), quarters[0].dtype),
        in_specs=[whole(pltpu.SMEM)] + [whole()] * 4,
        out_specs=whole(),
        compiler_params=pltpu.CompilerParams(vmem_limit_bytes=VMEM_LIMIT),
        cost_estimate=pl.CostEstimate(
            flops=0, bytes_accessed=rows * width * 16, transcendentals=0
        ),
        name="assemble",
    )(place_of, *quarters)


def line_grads_kernel(pairs_n, ids, *refs):
    refs = list(refs)
    pairs = []
    for k in range(pairs_n):
        x, d = refs.pop(0), refs.pop(0)
        if d.shape[0] > x.shape[-2]:
            rows, other = x.shape[-2], refs.pop(0)
            total_d = refs.pop()
            total_d[...] = d[rows:] + other[rows:]
            d = total_d
        pairs.append((x, d))
    start = refs.pop(0) if len(refs) == 2 else None
    (grads,) = refs
    slots, size = grads.shape[0], grads.shape[1]
    first = pairs[0][0]
    cols_n = pairs[0][1].shape[1] // size
    rows_n = first.shape[-1] // size * (first.shape[0] if len(first.shape) == 3 else 1)
    total = rows_n * cols_n
    group = math.gcd(slots, 16)

    @pl.loop(0, slots // group)
    def some(g):
        for s in [g * group + j for j in range(group)]:
            b = jnp.minimum(ids[s], total - 1)
            row = b // cols_n
            c = pl.ds(pl.multiple_of((b % cols_n) * size, size), size)
            acc = jnp.zeros((size, size), jnp.float32) if start is None else start[s].astype(jnp.float32)
            for x, d in pairs:
                per_part = x.shape[-1] // size
                at = pl.ds(pl.multiple_of((row % per_part) * size, size), size)
                acc += lax.dot_general(
                    x[row // per_part, :, at] if len(x.shape) == 3 else x[:, at],
                    d[:, c],
                    (((0,), (0,)), ((), ())),
                    preferred_element_type=jnp.float32,
                )
            grads[s] = jnp.where(ids[s] < total, acc, 0.0).astype(grads.dtype)


def line_grads(ids, pairs, start, size):
    slots = ids.shape[0]
    flat = [a for pair in pairs for a in pair] + ([] if start is None else [start])
    sums = [
        pltpu.VMEM((p[0].shape[-2], p[1].shape[1]), jnp.bfloat16) for p in pairs if len(p) == 3
    ]
    return pl.pallas_call(
        functools.partial(line_grads_kernel, len(pairs)),
        out_shape=jax.ShapeDtypeStruct((slots, size, size), jnp.bfloat16),
        in_specs=[whole(pltpu.SMEM)] + [whole()] * len(flat),
        out_specs=whole(),
        scratch_shapes=sums,
        compiler_params=pltpu.CompilerParams(vmem_limit_bytes=VMEM_LIMIT),
        cost_estimate=pl.CostEstimate(
            flops=512 * len(pairs) * slots * size * size,
            bytes_accessed=sum(2 * a.size for a in flat) + 2 * slots * size * size,
            transcendentals=0,
        ),
        name="line_grads",
    )(ids, *flat)


INWARD = ((0, 1), (3, 2))
OUTWARD = ((1, 0), (2, 3))
PAIRS = INWARD + OUTWARD
MIDDLE = ((1, 2), (2, 1))
SWAP = ((0, 1), (1, 0))


def ids_block(block_ids, size):
    rows = size * size // block_ids.shape[0]
    return jnp.broadcast_to(block_ids, (rows, block_ids.shape[0])).reshape(1, size, size)


def ids_of(piece, slots):
    return piece[-1, 0, :slots].astype(jnp.int32)


def line_body(tokens, upstream, blocks, block_ids):
    slots, size = blocks.shape[0], blocks.shape[1]
    rows, depth = tokens.shape
    width = upstream.shape[1]
    half_slots = slots // 2
    part_width = depth // 4
    at_z, half = lax.axis_index("dp"), lax.axis_index("groups")
    at_tensor, at_replica = lax.axis_index("tensor"), lax.axis_index("replica")
    middle = (at_z == 1) | (at_z == 2)
    place_of = jnp.stack([middle.astype(jnp.int32), half, at_tensor, at_replica])
    along = functools.partial(lax.ppermute, axis_name="dp")
    across = functools.partial(lax.ppermute, axis_name="groups", perm=SWAP)
    sideways = functools.partial(lax.ppermute, axis_name="tensor", perm=SWAP)
    cores = functools.partial(lax.ppermute, axis_name="replica", perm=SWAP)
    stage = lax.optimization_barrier

    mine = lax.dynamic_slice_in_dim(blocks, half * half_slots, half_slots, 0)
    mine = jnp.concatenate([mine, ids_block(block_ids, size).astype(jnp.bfloat16)])
    mine, late_blocks = stage((mine, blocks))

    near_a = along(mine, perm=INWARD)
    far_a = along(mine, perm=MIDDLE)
    other = lax.dynamic_slice_in_dim(late_blocks, (1 - half) * half_slots, half_slots, 0)
    part = lax.dynamic_slice_in_dim(tokens, lax.axis_index(INNER) * part_width, part_width, 1)
    both = jnp.concatenate([part, upstream])
    grads = line_grads(block_ids, ((tokens, upstream),), None, size)
    near_a, far_a, both, other, grads = stage((near_a, far_a, both, other, grads))

    end_a = along(near_a, perm=MIDDLE)
    far_b = across(far_a)
    both_1 = along(both, perm=PAIRS)
    both_1, end_a, far_b, both, other = stage((both_1, end_a, far_b, both, other))
    upstream_1 = both_1[rows:]

    near_b = along(other, perm=INWARD)
    end_b = across(end_a)
    both_2m = along(both, perm=MIDDLE)
    tokens_1 = lax.all_gather(both_1[:rows], INNER)
    ids_1, ids_2, ids_3 = (ids_of(piece, slots) for piece in (near_a, far_a, end_a))
    partial, turned = place_first(
        place_of, (block_ids, ids_1, ids_2, ids_3), (blocks, near_a, far_a, far_b, end_a), depth, width
    )
    near_b, end_b, both_2m, both_1, tokens_1, partial, turned = stage(
        (near_b, end_b, both_2m, both_1, tokens_1, partial, turned)
    )

    both_3m = along(both_1, perm=MIDDLE)
    both_2o = along(both_2m, perm=OUTWARD)
    last = (near_b, end_b)
    end_keep, own_keep, own_give, *end_give = project_back(
        place_of, ids_1, ids_3, turned, *last, upstream_1, upstream
    )
    end_keep, end_give = add_split(place_of, end_keep, *[cores(a) for a in end_give])
    end_keep, end_give, own_give, both_3m, both_2o = stage(
        (end_keep, end_give, own_give, both_3m, both_2o)
    )

    end_got = sideways(end_give)
    own_keep, own_give = add_split(place_of, own_keep, cores(own_give))
    both_3o = along(both_3m, perm=OUTWARD)
    tokens_2 = lax.all_gather(both_2m[:rows] + both_2o[:rows], INNER)
    proj, end_proj = project_forward(place_of, ids_1, ids_3, partial, *last, tokens, tokens_1)
    end_got, own_give, own_keep, proj, end_proj = stage(
        (end_got, own_give, own_keep, proj, end_proj)
    )

    sum_out = along(end_keep + end_got, perm=OUTWARD)
    own_got = sideways(own_give)
    grads = line_grads(block_ids, ((tokens_1, upstream_1),), grads, size)
    sum_out, own_got, both_3o, grads = stage((sum_out, own_got, both_3o, grads))

    tokens_3 = lax.all_gather(both_3m[:rows] + both_3o[:rows], INNER)
    quarter = jnp.where(middle, own_keep + own_got, sum_out)
    proj_out = along(end_proj, perm=OUTWARD)
    grads = line_grads(block_ids, ((tokens_2, both_2m, both_2o),), grads, size)
    projected = jnp.where(middle, proj, proj_out)
    by_tensor, by_core, grads, projected = stage(
        (sideways(quarter), cores(quarter), grads, projected)
    )
    by_both = cores(by_tensor)
    token_grad = assemble(place_of, (quarter, by_core, by_tensor, by_both))
    grads = line_grads(block_ids, ((tokens_3, both_3m, both_3o),), grads, size)
    return projected, token_grad, grads


def solution(mesh):
    line = tuple(mesh.shape[a] for a in ("groups", "dp", "tensor", "replica")) == (2, 4, 2, 2)
    return jax.shard_map(
        line_body if line else general_body,
        mesh=mesh,
        in_specs=(
            P(("groups", "dp"), None),
            P(("groups", "dp"), INNER),
            P(("dp",) + INNER, None, None),
            P(("dp",) + INNER),
        ),
        out_specs=(
            P(("groups", "dp"), INNER),
            P(("groups", "dp"), None),
            P(("groups", "dp") + INNER, None, None),
        ),
        check_vma=False,
    )
```

```python
import functools
import math

import jax
import jax.numpy as jnp
from jax import lax
from jax.experimental import pallas as pl
from jax.experimental.pallas import tpu as pltpu
from jax.sharding import PartitionSpec as P

VMEM_LIMIT = 60 * 1024 * 1024
INNER = ("tensor", "replica")


def whole(space=pltpu.VMEM):
    return pl.BlockSpec(memory_space=space)


def project_kernel(ids, blocks, tokens, upstream, proj, back, weight):
    slots, size = blocks.shape[0], blocks.shape[1]
    depth, width = weight.shape
    cols_n = width // size
    total = (depth // size) * cols_n
    weight[...] = jnp.zeros_like(weight)

    @pl.loop(0, slots, unroll=4)
    def place(s):
        b = ids[s]

        @pl.when(b < total)
        def put():
            r = pl.multiple_of((b // cols_n) * size, size)
            c = pl.multiple_of((b % cols_n) * size, size)
            weight[pl.ds(r, size), pl.ds(c, size)] = blocks[s]

    step = 256

    @pl.loop(0, width // step)
    def forward(n):
        c = pl.multiple_of(n * step, step)
        proj[:, pl.ds(c, step)] = jnp.dot(
            tokens[...], weight[:, pl.ds(c, step)], preferred_element_type=jnp.float32
        ).astype(proj.dtype)

    @pl.loop(0, depth // step, unroll=4)
    def backward(n):
        r = pl.multiple_of(n * step, step)
        back[:, pl.ds(r, step)] = lax.dot_general(
            upstream[...],
            weight[pl.ds(r, step), :],
            (((1,), (1,)), ((), ())),
            preferred_element_type=jnp.float32,
        ).astype(back.dtype)


def project(ids, blocks, tokens, upstream):
    rows, depth = tokens.shape
    width = upstream.shape[1]
    return pl.pallas_call(
        project_kernel,
        out_shape=(
            jax.ShapeDtypeStruct((rows, width), jnp.bfloat16),
            jax.ShapeDtypeStruct((rows, depth), jnp.bfloat16),
        ),
        in_specs=[whole(pltpu.SMEM), whole(), whole(), whole()],
        out_specs=(whole(), whole()),
        scratch_shapes=[pltpu.VMEM((depth, width), jnp.bfloat16)],
        compiler_params=pltpu.CompilerParams(vmem_limit_bytes=VMEM_LIMIT),
        cost_estimate=pl.CostEstimate(
            flops=4 * rows * depth * width,
            bytes_accessed=blocks.size * 2 + rows * (depth + width) * 4,
            transcendentals=0,
        ),
        name="project",
    )(ids, blocks, tokens, upstream)


def block_grad_kernel(ids, tokens, upstream, grads):
    slots, size = grads.shape[0], grads.shape[1]
    parts, slabs, _, part_width = tokens.shape
    cols_n = upstream.shape[2] // size
    per_part = part_width // size
    total = parts * per_part * cols_n

    @pl.loop(0, slots)
    def one(s):
        b = ids[s]

        @pl.when(b < total)
        def fill():
            row = b // cols_n
            part = row // per_part
            r = pl.multiple_of((row % per_part) * size, size)
            c = pl.multiple_of((b % cols_n) * size, size)
            acc = jnp.zeros((size, size), jnp.float32)
            for k in range(slabs):
                acc += lax.dot_general(
                    tokens[part, k, :, pl.ds(r, size)],
                    upstream[k, :, pl.ds(c, size)],
                    (((0,), (0,)), ((), ())),
                    preferred_element_type=jnp.float32,
                )
            grads[s] = acc.astype(grads.dtype)

        @pl.when(b >= total)
        def clear():
            grads[s] = jnp.zeros((size, size), grads.dtype)


def block_grads(ids, tokens, upstream, size):
    slots = ids.shape[0]
    parts, slabs, rows, part_width = tokens.shape
    return pl.pallas_call(
        block_grad_kernel,
        out_shape=jax.ShapeDtypeStruct((slots, size, size), jnp.bfloat16),
        in_specs=[whole(pltpu.SMEM), whole(), whole()],
        out_specs=whole(),
        compiler_params=pltpu.CompilerParams(vmem_limit_bytes=VMEM_LIMIT),
        cost_estimate=pl.CostEstimate(
            flops=2 * slots * slabs * rows * size * size,
            bytes_accessed=2 * (tokens.size + upstream.size + slots * size * size),
            transcendentals=0,
        ),
        name="block_grads",
    )(ids, tokens, upstream)


def general_body(tokens, upstream, blocks, block_ids):
    size = blocks.shape[1]
    all_blocks = lax.all_gather(blocks, "dp", axis=0, tiled=True)
    all_ids = lax.all_gather(block_ids, "dp", axis=0, tiled=True)
    proj, back = project(all_ids, all_blocks, tokens, upstream)
    terms = block_grads(all_ids, tokens[None, None], upstream[None], size)
    grads = lax.psum_scatter(terms, "dp", scatter_dimension=0, tiled=True)
    return proj, lax.psum(back, INNER), grads


def place_blocks(ids, first, blocks, weight, turned, slots):
    size = blocks.shape[1]
    depth, width = turned.shape[::-1] if weight is None else weight.shape
    cols_n = width // size
    total = (depth // size) * cols_n
    group = math.gcd(slots, 8)

    @pl.loop(0, slots // group)
    def place(g):
        some = [g * group + j for j in range(group)]
        flipped = [None if turned is None else blocks[s].T for s in some]
        for s, flip in zip(some, flipped):
            b = ids[first + s]

            @pl.when(b < total)
            def put(s=s, flip=flip, b=b):
                r = pl.multiple_of((b // cols_n) * size, size)
                c = pl.multiple_of((b % cols_n) * size, size)
                if weight is not None:
                    weight[pl.ds(r, size), pl.ds(c, size)] = blocks[s]
                if turned is not None:
                    turned[pl.ds(c, size), pl.ds(r, size)] = flip


def place_kernel(
    place_of, ids_0, ids_1, ids_2, ids_3, own, near_a, far_a, far_b, end_a, weight, turned
):
    is_middle, half = place_of[0], place_of[1]
    half_slots = far_b.shape[0] - 1
    mine, other = half * half_slots, (1 - half) * half_slots

    @pl.when(is_middle == 1)
    def work():
        weight[...] = jnp.zeros_like(weight)
        turned[...] = jnp.zeros_like(turned)
        place_blocks(ids_0, 0, own, weight, turned, own.shape[0])
        place_blocks(ids_1, mine, near_a, weight, turned, half_slots)
        place_blocks(ids_2, mine, far_a, weight, turned, half_slots)
        place_blocks(ids_2, other, far_b, weight, turned, half_slots)
        place_blocks(ids_3, mine, end_a, weight, turned, half_slots)


def place_first(place_of, ids, pieces, depth, width):
    return pl.pallas_call(
        place_kernel,
        out_shape=(
            jax.ShapeDtypeStruct((depth, width), jnp.bfloat16),
            jax.ShapeDtypeStruct((width, depth), jnp.bfloat16),
        ),
        in_specs=[whole(pltpu.SMEM)] * 5 + [whole()] * 5,
        out_specs=(whole(), whole()),
        compiler_params=pltpu.CompilerParams(vmem_limit_bytes=VMEM_LIMIT),
        cost_estimate=pl.CostEstimate(
            flops=0, bytes_accessed=depth * width * 6, transcendentals=0
        ),
        name="place_first",
    )(place_of, *ids, *pieces)


def back_kernel(
    place_of, ids_1, ids_3, partial, near_b, end_b, end_upstream, upstream,
    end_keep, own_keep, own_give, end_give_0, end_give_1, held, sources, sem,
):
    half_slots = near_b.shape[0]
    other = (1 - place_of[1]) * half_slots
    rows, width = upstream.shape
    step = 256
    per_part = end_keep.shape[2] // step

    @pl.when(place_of[0] == 1)
    def work():
        load = pltpu.make_async_copy(partial, held, sem)
        load.start()
        sources[:rows] = end_upstream[...]
        sources[rows:] = upstream[...]
        load.wait()
        place_blocks(ids_1, other, near_b, None, held, half_slots)
        place_blocks(ids_3, other, end_b, None, held, half_slots)

        def column(part, end_target, own_target):
            @pl.loop(0, per_part, unroll=2)
            def backward(n):
                at = pl.multiple_of(n * step, step)
                result = jnp.dot(
                    sources[...],
                    held[:, pl.ds(pl.multiple_of(part * per_part * step + at, step), step)],
                    preferred_element_type=jnp.float32,
                ).astype(own_target.dtype)
                end_target[:, pl.ds(at, step)] = result[:rows]
                own_target[:, pl.ds(at, step)] = result[rows:]

        for x, end_give in enumerate((end_give_0, end_give_1)):
            column(2 * x + place_of[3], end_keep.at[x], own_keep.at[x])
            column(2 * x + 1 - place_of[3], end_give, own_give.at[x])


def project_back(place_of, ids_1, ids_3, partial, near_b, end_b, end_upstream, upstream):
    width, depth = partial.shape
    rows = upstream.shape[0]
    quarter = jax.ShapeDtypeStruct((rows, depth // 4), jnp.bfloat16)
    half = jax.ShapeDtypeStruct((2, rows, depth // 4), jnp.bfloat16)
    return pl.pallas_call(
        back_kernel,
        out_shape=(half, half, half, quarter, quarter),
        in_specs=[whole(pltpu.SMEM)] * 3 + [whole(pl.ANY)] + [whole()] * 4,
        out_specs=(whole(),) * 5,
        scratch_shapes=[
            pltpu.VMEM((width, depth), jnp.bfloat16),
            pltpu.VMEM((2 * rows, width), jnp.bfloat16),
            pltpu.SemaphoreType.DMA,
        ],
        compiler_params=pltpu.CompilerParams(vmem_limit_bytes=VMEM_LIMIT),
        cost_estimate=pl.CostEstimate(
            flops=4 * rows * depth * width,
            bytes_accessed=depth * width * 2 + rows * (depth + width) * 4,
            transcendentals=0,
        ),
        name="project_back",
    )(place_of, ids_1, ids_3, partial, near_b, end_b, end_upstream, upstream)


def forward_kernel(
    place_of, ids_1, ids_3, partial, near_b, end_b, tokens, gathered, proj, end_proj, held, sem
):
    half_slots = near_b.shape[0]
    other = (1 - place_of[1]) * half_slots
    depth, width = held.shape
    parts, rows, part_width = gathered.shape
    step = 256

    @pl.when(place_of[0] == 1)
    def work():
        load = pltpu.make_async_copy(partial, held, sem)
        load.start()
        load.wait()
        place_blocks(ids_1, other, near_b, held, None, half_slots)
        place_blocks(ids_3, other, end_b, held, None, half_slots)

        @pl.loop(0, width // step, unroll=2)
        def forward(n):
            c = pl.multiple_of(n * step, step)
            acc = jnp.zeros((rows, step), jnp.float32)
            for q in range(parts):
                acc += jnp.dot(
                    gathered[q],
                    held[q * part_width : (q + 1) * part_width, pl.ds(c, step)],
                    preferred_element_type=jnp.float32,
                )
            end_proj[:, pl.ds(c, step)] = acc.astype(end_proj.dtype)
            proj[:, pl.ds(c, step)] = jnp.dot(
                tokens[...], held[:, pl.ds(c, step)], preferred_element_type=jnp.float32
            ).astype(proj.dtype)


def project_forward(place_of, ids_1, ids_3, partial, near_b, end_b, tokens, gathered):
    depth, width = partial.shape
    rows = tokens.shape[0]
    out = jax.ShapeDtypeStruct((rows, width), jnp.bfloat16)
    return pl.pallas_call(
        forward_kernel,
        out_shape=(out, out),
        in_specs=[whole(pltpu.SMEM)] * 3 + [whole(pl.ANY)] + [whole()] * 4,
        out_specs=(whole(),) * 2,
        scratch_shapes=[pltpu.VMEM((depth, width), jnp.bfloat16), pltpu.SemaphoreType.DMA],
        compiler_params=pltpu.CompilerParams(vmem_limit_bytes=VMEM_LIMIT),
        cost_estimate=pl.CostEstimate(
            flops=rows * depth * width // 2, bytes_accessed=depth * width, transcendentals=0
        ),
        name="project_forward",
    )(place_of, ids_1, ids_3, partial, near_b, end_b, tokens, gathered)


def split_kernel(place_of, keep, *refs):
    x = place_of[2]
    own, give = refs[-2:]
    got = refs[:-2] if len(refs) > 3 else (refs[0].at[0], refs[0].at[1])
    for at in range(2):
        total = (keep[at].astype(jnp.float32) + got[at][...].astype(jnp.float32)).astype(own.dtype)

        @pl.when(x == at)
        def mine():
            own[...] = total

        @pl.when(x != at)
        def theirs():
            give[...] = total


def add_split(place_of, keep, *got):
    out = jax.ShapeDtypeStruct(keep.shape[1:], keep.dtype)
    return pl.pallas_call(
        split_kernel,
        out_shape=(out, out),
        in_specs=[whole(pltpu.SMEM), whole()] + [whole()] * len(got),
        out_specs=(whole(), whole()),
        compiler_params=pltpu.CompilerParams(vmem_limit_bytes=VMEM_LIMIT),
        cost_estimate=pl.CostEstimate(
            flops=keep.size, bytes_accessed=keep.size * 6, transcendentals=0
        ),
        name="add_split",
    )(place_of, keep, *got)


def assemble_kernel(place_of, own, by_core, by_tensor, by_both, full):
    x, c = place_of[2], place_of[3]
    width = own.shape[1]
    for ref, xx, cc in (
        (own, x, c), (by_core, x, 1 - c), (by_tensor, 1 - x, c), (by_both, 1 - x, 1 - c)
    ):
        at = pl.multiple_of((xx * 2 + cc) * width, width)
        full[:, pl.ds(at, width)] = ref[...]


def assemble(place_of, quarters):
    rows, width = quarters[0].shape
    return pl.pallas_call(
        assemble_kernel,
        out_shape=jax.ShapeDtypeStruct((rows, 4 * width), quarters[0].dtype),
        in_specs=[whole(pltpu.SMEM)] + [whole()] * 4,
        out_specs=whole(),
        compiler_params=pltpu.CompilerParams(vmem_limit_bytes=VMEM_LIMIT),
        cost_estimate=pl.CostEstimate(
            flops=0, bytes_accessed=rows * width * 16, transcendentals=0
        ),
        name="assemble",
    )(place_of, *quarters)


def line_grads_kernel(pairs_n, ids, *refs):
    refs = list(refs)
    pairs = []
    for k in range(pairs_n):
        x, d = refs.pop(0), refs.pop(0)
        if d.shape[0] > x.shape[-2]:
            rows, other = x.shape[-2], refs.pop(0)
            total_d = refs.pop()
            total_d[...] = d[rows:] + other[rows:]
            d = total_d
        pairs.append((x, d))
    start = refs.pop(0) if len(refs) == 2 else None
    (grads,) = refs
    slots, size = grads.shape[0], grads.shape[1]
    first = pairs[0][0]
    cols_n = pairs[0][1].shape[1] // size
    rows_n = first.shape[-1] // size * (first.shape[0] if len(first.shape) == 3 else 1)
    total = rows_n * cols_n
    group = math.gcd(slots, 32)

    @pl.loop(0, slots // group)
    def some(g):
        for s in [g * group + j for j in range(group)]:
            b = jnp.minimum(ids[s], total - 1)
            row = b // cols_n
            c = pl.ds(pl.multiple_of((b % cols_n) * size, size), size)
            acc = jnp.zeros((size, size), jnp.float32) if start is None else start[s].astype(jnp.float32)
            for x, d in pairs:
                per_part = x.shape[-1] // size
                at = pl.ds(pl.multiple_of((row % per_part) * size, size), size)
                acc += lax.dot_general(
                    x[row // per_part, :, at] if len(x.shape) == 3 else x[:, at],
                    d[:, c],
                    (((0,), (0,)), ((), ())),
                    preferred_element_type=jnp.float32,
                )
            grads[s] = jnp.where(ids[s] < total, acc, 0.0).astype(grads.dtype)


def line_grads(ids, pairs, start, size):
    slots = ids.shape[0]
    flat = [a for pair in pairs for a in pair] + ([] if start is None else [start])
    sums = [
        pltpu.VMEM((p[0].shape[-2], p[1].shape[1]), jnp.bfloat16) for p in pairs if len(p) == 3
    ]
    return pl.pallas_call(
        functools.partial(line_grads_kernel, len(pairs)),
        out_shape=jax.ShapeDtypeStruct((slots, size, size), jnp.bfloat16),
        in_specs=[whole(pltpu.SMEM)] + [whole()] * len(flat),
        out_specs=whole(),
        scratch_shapes=sums,
        compiler_params=pltpu.CompilerParams(vmem_limit_bytes=VMEM_LIMIT),
        cost_estimate=pl.CostEstimate(
            flops=512 * len(pairs) * slots * size * size,
            bytes_accessed=sum(2 * a.size for a in flat) + 2 * slots * size * size,
            transcendentals=0,
        ),
        name="line_grads",
    )(ids, *flat)


INWARD = ((0, 1), (3, 2))
OUTWARD = ((1, 0), (2, 3))
PAIRS = INWARD + OUTWARD
MIDDLE = ((1, 2), (2, 1))
SWAP = ((0, 1), (1, 0))


def ids_block(block_ids, size):
    rows = size * size // block_ids.shape[0]
    return jnp.broadcast_to(block_ids, (rows, block_ids.shape[0])).reshape(1, size, size)


def ids_of(piece, slots):
    return piece[-1, 0, :slots].astype(jnp.int32)


def line_body(tokens, upstream, blocks, block_ids):
    slots, size = blocks.shape[0], blocks.shape[1]
    rows, depth = tokens.shape
    width = upstream.shape[1]
    half_slots = slots // 2
    part_width = depth // 4
    at_z, half = lax.axis_index("dp"), lax.axis_index("groups")
    at_tensor, at_replica = lax.axis_index("tensor"), lax.axis_index("replica")
    middle = (at_z == 1) | (at_z == 2)
    place_of = jnp.stack([middle.astype(jnp.int32), half, at_tensor, at_replica])
    along = functools.partial(lax.ppermute, axis_name="dp")
    across = functools.partial(lax.ppermute, axis_name="groups", perm=SWAP)
    sideways = functools.partial(lax.ppermute, axis_name="tensor", perm=SWAP)
    cores = functools.partial(lax.ppermute, axis_name="replica", perm=SWAP)
    stage = lax.optimization_barrier

    mine = lax.dynamic_slice_in_dim(blocks, half * half_slots, half_slots, 0)
    mine = jnp.concatenate([mine, ids_block(block_ids, size).astype(jnp.bfloat16)])
    mine, late_blocks = stage((mine, blocks))

    near_a = along(mine, perm=INWARD)
    far_a = along(mine, perm=MIDDLE)
    other = lax.dynamic_slice_in_dim(late_blocks, (1 - half) * half_slots, half_slots, 0)
    part = lax.dynamic_slice_in_dim(tokens, lax.axis_index(INNER) * part_width, part_width, 1)
    both = jnp.concatenate([part, upstream])
    grads = line_grads(block_ids, ((tokens, upstream),), None, size)
    near_a, far_a, both, other, grads = stage((near_a, far_a, both, other, grads))

    end_a = along(near_a, perm=MIDDLE)
    far_b = across(far_a)
    both_1 = along(both, perm=PAIRS)
    both_1, end_a, far_b, both, other = stage((both_1, end_a, far_b, both, other))
    upstream_1 = both_1[rows:]

    near_b = along(other, perm=INWARD)
    end_b = across(end_a)
    both_2m = along(both, perm=MIDDLE)
    tokens_1 = lax.all_gather(both_1[:rows], INNER)
    ids_1, ids_2, ids_3 = (ids_of(piece, slots) for piece in (near_a, far_a, end_a))
    partial, turned = place_first(
        place_of, (block_ids, ids_1, ids_2, ids_3), (blocks, near_a, far_a, far_b, end_a), depth, width
    )
    near_b, end_b, both_2m, both_1, tokens_1, partial, turned = stage(
        (near_b, end_b, both_2m, both_1, tokens_1, partial, turned)
    )

    both_3m = along(both_1, perm=MIDDLE)
    both_2o = along(both_2m, perm=OUTWARD)
    last = (near_b, end_b)
    end_keep, own_keep, own_give, *end_give = project_back(
        place_of, ids_1, ids_3, turned, *last, upstream_1, upstream
    )
    end_keep, end_give = add_split(place_of, end_keep, *[cores(a) for a in end_give])
    end_keep, end_give, own_give, both_3m, both_2o = stage(
        (end_keep, end_give, own_give, both_3m, both_2o)
    )

    end_got = sideways(end_give)
    own_keep, own_give = add_split(place_of, own_keep, cores(own_give))
    both_3o = along(both_3m, perm=OUTWARD)
    tokens_2 = lax.all_gather(both_2m[:rows] + both_2o[:rows], INNER)
    proj, end_proj = project_forward(place_of, ids_1, ids_3, partial, *last, tokens, tokens_1)
    end_got, own_give, own_keep, proj, end_proj = stage(
        (end_got, own_give, own_keep, proj, end_proj)
    )

    sum_out = along(end_keep + end_got, perm=OUTWARD)
    own_got = sideways(own_give)
    grads = line_grads(block_ids, ((tokens_1, upstream_1),), grads, size)
    sum_out, own_got, both_3o, grads = stage((sum_out, own_got, both_3o, grads))

    tokens_3 = lax.all_gather(both_3m[:rows] + both_3o[:rows], INNER)
    quarter = jnp.where(middle, own_keep + own_got, sum_out)
    proj_out = along(end_proj, perm=OUTWARD)
    grads = line_grads(block_ids, ((tokens_2, both_2m, both_2o),), grads, size)
    by_tensor, by_core, grads = stage((sideways(quarter), cores(quarter), grads))
    by_both = cores(by_tensor)
    projected = jnp.where(middle, proj, proj_out)
    token_grad = assemble(place_of, (quarter, by_core, by_tensor, by_both))
    grads = line_grads(block_ids, ((tokens_3, both_3m, both_3o),), grads, size)
    return projected, token_grad, grads


def solution(mesh):
    line = tuple(mesh.shape[a] for a in ("groups", "dp", "tensor", "replica")) == (2, 4, 2, 2)
    return jax.shard_map(
        line_body if line else general_body,
        mesh=mesh,
        in_specs=(
            P(("groups", "dp"), None),
            P(("groups", "dp"), INNER),
            P(("dp",) + INNER, None, None),
            P(("dp",) + INNER),
        ),
        out_specs=(
            P(("groups", "dp"), INNER),
            P(("groups", "dp"), None),
            P(("groups", "dp") + INNER, None, None),
        ),
        check_vma=False,
    )
```

```python
import functools
import math

import jax
import jax.numpy as jnp
from jax import lax
from jax.experimental import pallas as pl
from jax.experimental.pallas import tpu as pltpu
from jax.sharding import PartitionSpec as P

VMEM_LIMIT = 60 * 1024 * 1024
INNER = ("tensor", "replica")


def whole(space=pltpu.VMEM):
    return pl.BlockSpec(memory_space=space)


def project_kernel(ids, blocks, tokens, upstream, proj, back, weight):
    slots, size = blocks.shape[0], blocks.shape[1]
    depth, width = weight.shape
    cols_n = width // size
    total = (depth // size) * cols_n
    weight[...] = jnp.zeros_like(weight)

    @pl.loop(0, slots, unroll=4)
    def place(s):
        b = ids[s]

        @pl.when(b < total)
        def put():
            r = pl.multiple_of((b // cols_n) * size, size)
            c = pl.multiple_of((b % cols_n) * size, size)
            weight[pl.ds(r, size), pl.ds(c, size)] = blocks[s]

    step = 256

    @pl.loop(0, width // step)
    def forward(n):
        c = pl.multiple_of(n * step, step)
        proj[:, pl.ds(c, step)] = jnp.dot(
            tokens[...], weight[:, pl.ds(c, step)], preferred_element_type=jnp.float32
        ).astype(proj.dtype)

    @pl.loop(0, depth // step, unroll=4)
    def backward(n):
        r = pl.multiple_of(n * step, step)
        back[:, pl.ds(r, step)] = lax.dot_general(
            upstream[...],
            weight[pl.ds(r, step), :],
            (((1,), (1,)), ((), ())),
            preferred_element_type=jnp.float32,
        ).astype(back.dtype)


def project(ids, blocks, tokens, upstream):
    rows, depth = tokens.shape
    width = upstream.shape[1]
    return pl.pallas_call(
        project_kernel,
        out_shape=(
            jax.ShapeDtypeStruct((rows, width), jnp.bfloat16),
            jax.ShapeDtypeStruct((rows, depth), jnp.bfloat16),
        ),
        in_specs=[whole(pltpu.SMEM), whole(), whole(), whole()],
        out_specs=(whole(), whole()),
        scratch_shapes=[pltpu.VMEM((depth, width), jnp.bfloat16)],
        compiler_params=pltpu.CompilerParams(vmem_limit_bytes=VMEM_LIMIT),
        cost_estimate=pl.CostEstimate(
            flops=4 * rows * depth * width,
            bytes_accessed=blocks.size * 2 + rows * (depth + width) * 4,
            transcendentals=0,
        ),
        name="project",
    )(ids, blocks, tokens, upstream)


def block_grad_kernel(ids, tokens, upstream, grads):
    slots, size = grads.shape[0], grads.shape[1]
    parts, slabs, _, part_width = tokens.shape
    cols_n = upstream.shape[2] // size
    per_part = part_width // size
    total = parts * per_part * cols_n

    @pl.loop(0, slots)
    def one(s):
        b = ids[s]

        @pl.when(b < total)
        def fill():
            row = b // cols_n
            part = row // per_part
            r = pl.multiple_of((row % per_part) * size, size)
            c = pl.multiple_of((b % cols_n) * size, size)
            acc = jnp.zeros((size, size), jnp.float32)
            for k in range(slabs):
                acc += lax.dot_general(
                    tokens[part, k, :, pl.ds(r, size)],
                    upstream[k, :, pl.ds(c, size)],
                    (((0,), (0,)), ((), ())),
                    preferred_element_type=jnp.float32,
                )
            grads[s] = acc.astype(grads.dtype)

        @pl.when(b >= total)
        def clear():
            grads[s] = jnp.zeros((size, size), grads.dtype)


def block_grads(ids, tokens, upstream, size):
    slots = ids.shape[0]
    parts, slabs, rows, part_width = tokens.shape
    return pl.pallas_call(
        block_grad_kernel,
        out_shape=jax.ShapeDtypeStruct((slots, size, size), jnp.bfloat16),
        in_specs=[whole(pltpu.SMEM), whole(), whole()],
        out_specs=whole(),
        compiler_params=pltpu.CompilerParams(vmem_limit_bytes=VMEM_LIMIT),
        cost_estimate=pl.CostEstimate(
            flops=2 * slots * slabs * rows * size * size,
            bytes_accessed=2 * (tokens.size + upstream.size + slots * size * size),
            transcendentals=0,
        ),
        name="block_grads",
    )(ids, tokens, upstream)


def general_body(tokens, upstream, blocks, block_ids):
    size = blocks.shape[1]
    all_blocks = lax.all_gather(blocks, "dp", axis=0, tiled=True)
    all_ids = lax.all_gather(block_ids, "dp", axis=0, tiled=True)
    proj, back = project(all_ids, all_blocks, tokens, upstream)
    terms = block_grads(all_ids, tokens[None, None], upstream[None], size)
    grads = lax.psum_scatter(terms, "dp", scatter_dimension=0, tiled=True)
    return proj, lax.psum(back, INNER), grads


def place_blocks(ids, first, blocks, weight, turned, slots):
    size = blocks.shape[1]
    depth, width = turned.shape[::-1] if weight is None else weight.shape
    cols_n = width // size
    total = (depth // size) * cols_n
    group = math.gcd(slots, 8)

    @pl.loop(0, slots // group)
    def place(g):
        some = [g * group + j for j in range(group)]
        flipped = [None if turned is None else blocks[s].T for s in some]
        for s, flip in zip(some, flipped):
            b = ids[first + s]

            @pl.when(b < total)
            def put(s=s, flip=flip, b=b):
                r = pl.multiple_of((b // cols_n) * size, size)
                c = pl.multiple_of((b % cols_n) * size, size)
                if weight is not None:
                    weight[pl.ds(r, size), pl.ds(c, size)] = blocks[s]
                if turned is not None:
                    turned[pl.ds(c, size), pl.ds(r, size)] = flip


def place_kernel(
    place_of, ids_0, ids_1, ids_2, ids_3, own, near_a, far_a, far_b, end_a, weight, turned
):
    is_middle, half = place_of[0], place_of[1]
    half_slots = far_b.shape[0] - 1
    mine, other = half * half_slots, (1 - half) * half_slots

    @pl.when(is_middle == 1)
    def work():
        weight[...] = jnp.zeros_like(weight)
        turned[...] = jnp.zeros_like(turned)
        place_blocks(ids_0, 0, own, weight, turned, own.shape[0])
        place_blocks(ids_1, mine, near_a, weight, turned, half_slots)
        place_blocks(ids_2, mine, far_a, weight, turned, half_slots)
        place_blocks(ids_2, other, far_b, weight, turned, half_slots)
        place_blocks(ids_3, mine, end_a, weight, turned, half_slots)


def place_first(place_of, ids, pieces, depth, width):
    return pl.pallas_call(
        place_kernel,
        out_shape=(
            jax.ShapeDtypeStruct((depth, width), jnp.bfloat16),
            jax.ShapeDtypeStruct((width, depth), jnp.bfloat16),
        ),
        in_specs=[whole(pltpu.SMEM)] * 5 + [whole()] * 5,
        out_specs=(whole(), whole()),
        compiler_params=pltpu.CompilerParams(vmem_limit_bytes=VMEM_LIMIT),
        cost_estimate=pl.CostEstimate(
            flops=0, bytes_accessed=depth * width * 6, transcendentals=0
        ),
        name="place_first",
    )(place_of, *ids, *pieces)


def back_kernel(
    place_of, ids_1, ids_3, partial, near_b, end_b, end_upstream, upstream,
    end_keep, own_keep, own_give, end_give_0, end_give_1, held, sources, sem,
):
    half_slots = near_b.shape[0]
    other = (1 - place_of[1]) * half_slots
    rows, width = upstream.shape
    step = 256
    per_part = end_keep.shape[2] // step

    @pl.when(place_of[0] == 1)
    def work():
        load = pltpu.make_async_copy(partial, held, sem)
        load.start()
        sources[:rows] = end_upstream[...]
        sources[rows:] = upstream[...]
        load.wait()
        place_blocks(ids_1, other, near_b, None, held, half_slots)
        place_blocks(ids_3, other, end_b, None, held, half_slots)

        def column(part, end_target, own_target):
            @pl.loop(0, per_part, unroll=2)
            def backward(n):
                at = pl.multiple_of(n * step, step)
                result = jnp.dot(
                    sources[...],
                    held[:, pl.ds(pl.multiple_of(part * per_part * step + at, step), step)],
                    preferred_element_type=jnp.float32,
                ).astype(own_target.dtype)
                end_target[:, pl.ds(at, step)] = result[:rows]
                own_target[:, pl.ds(at, step)] = result[rows:]

        for x, end_give in enumerate((end_give_0, end_give_1)):
            column(2 * x + place_of[3], end_keep.at[x], own_keep.at[x])
            column(2 * x + 1 - place_of[3], end_give, own_give.at[x])


def project_back(place_of, ids_1, ids_3, partial, near_b, end_b, end_upstream, upstream):
    width, depth = partial.shape
    rows = upstream.shape[0]
    quarter = jax.ShapeDtypeStruct((rows, depth // 4), jnp.bfloat16)
    half = jax.ShapeDtypeStruct((2, rows, depth // 4), jnp.bfloat16)
    return pl.pallas_call(
        back_kernel,
        out_shape=(half, half, half, quarter, quarter),
        in_specs=[whole(pltpu.SMEM)] * 3 + [whole(pl.ANY)] + [whole()] * 4,
        out_specs=(whole(),) * 5,
        scratch_shapes=[
            pltpu.VMEM((width, depth), jnp.bfloat16),
            pltpu.VMEM((2 * rows, width), jnp.bfloat16),
            pltpu.SemaphoreType.DMA,
        ],
        compiler_params=pltpu.CompilerParams(vmem_limit_bytes=VMEM_LIMIT),
        cost_estimate=pl.CostEstimate(
            flops=4 * rows * depth * width,
            bytes_accessed=depth * width * 2 + rows * (depth + width) * 4,
            transcendentals=0,
        ),
        name="project_back",
    )(place_of, ids_1, ids_3, partial, near_b, end_b, end_upstream, upstream)


def forward_kernel(
    place_of, ids_1, ids_3, partial, near_b, end_b, tokens, gathered, proj, end_proj, held, sem
):
    half_slots = near_b.shape[0]
    other = (1 - place_of[1]) * half_slots
    depth, width = held.shape
    parts, rows, part_width = gathered.shape
    step = 256

    @pl.when(place_of[0] == 1)
    def work():
        load = pltpu.make_async_copy(partial, held, sem)
        load.start()
        load.wait()
        place_blocks(ids_1, other, near_b, held, None, half_slots)
        place_blocks(ids_3, other, end_b, held, None, half_slots)

        @pl.loop(0, width // step, unroll=2)
        def forward(n):
            c = pl.multiple_of(n * step, step)
            acc = jnp.zeros((rows, step), jnp.float32)
            for q in range(parts):
                acc += jnp.dot(
                    gathered[q],
                    held[q * part_width : (q + 1) * part_width, pl.ds(c, step)],
                    preferred_element_type=jnp.float32,
                )
            end_proj[:, pl.ds(c, step)] = acc.astype(end_proj.dtype)
            proj[:, pl.ds(c, step)] = jnp.dot(
                tokens[...], held[:, pl.ds(c, step)], preferred_element_type=jnp.float32
            ).astype(proj.dtype)


def project_forward(place_of, ids_1, ids_3, partial, near_b, end_b, tokens, gathered):
    depth, width = partial.shape
    rows = tokens.shape[0]
    out = jax.ShapeDtypeStruct((rows, width), jnp.bfloat16)
    return pl.pallas_call(
        forward_kernel,
        out_shape=(out, out),
        in_specs=[whole(pltpu.SMEM)] * 3 + [whole(pl.ANY)] + [whole()] * 4,
        out_specs=(whole(),) * 2,
        scratch_shapes=[pltpu.VMEM((depth, width), jnp.bfloat16), pltpu.SemaphoreType.DMA],
        compiler_params=pltpu.CompilerParams(vmem_limit_bytes=VMEM_LIMIT),
        cost_estimate=pl.CostEstimate(
            flops=rows * depth * width // 2, bytes_accessed=depth * width, transcendentals=0
        ),
        name="project_forward",
    )(place_of, ids_1, ids_3, partial, near_b, end_b, tokens, gathered)


def split_kernel(place_of, keep, *refs):
    x = place_of[2]
    own, give = refs[-2:]
    got = refs[:-2] if len(refs) > 3 else (refs[0].at[0], refs[0].at[1])
    for at in range(2):
        total = (keep[at].astype(jnp.float32) + got[at][...].astype(jnp.float32)).astype(own.dtype)

        @pl.when(x == at)
        def mine():
            own[...] = total

        @pl.when(x != at)
        def theirs():
            give[...] = total


def add_split(place_of, keep, *got):
    out = jax.ShapeDtypeStruct(keep.shape[1:], keep.dtype)
    return pl.pallas_call(
        split_kernel,
        out_shape=(out, out),
        in_specs=[whole(pltpu.SMEM), whole()] + [whole()] * len(got),
        out_specs=(whole(), whole()),
        compiler_params=pltpu.CompilerParams(vmem_limit_bytes=VMEM_LIMIT),
        cost_estimate=pl.CostEstimate(
            flops=keep.size, bytes_accessed=keep.size * 6, transcendentals=0
        ),
        name="add_split",
    )(place_of, keep, *got)


def assemble_kernel(place_of, own, by_core, by_tensor, by_both, full):
    x, c = place_of[2], place_of[3]
    width = own.shape[1]
    for ref, xx, cc in (
        (own, x, c), (by_core, x, 1 - c), (by_tensor, 1 - x, c), (by_both, 1 - x, 1 - c)
    ):
        at = pl.multiple_of((xx * 2 + cc) * width, width)
        full[:, pl.ds(at, width)] = ref[...]


def assemble(place_of, quarters):
    rows, width = quarters[0].shape
    return pl.pallas_call(
        assemble_kernel,
        out_shape=jax.ShapeDtypeStruct((rows, 4 * width), quarters[0].dtype),
        in_specs=[whole(pltpu.SMEM)] + [whole()] * 4,
        out_specs=whole(),
        compiler_params=pltpu.CompilerParams(vmem_limit_bytes=VMEM_LIMIT),
        cost_estimate=pl.CostEstimate(
            flops=0, bytes_accessed=rows * width * 16, transcendentals=0
        ),
        name="assemble",
    )(place_of, *quarters)


def line_grads_kernel(pairs_n, ids, *refs):
    refs = list(refs)
    pairs = []
    for k in range(pairs_n):
        x, d = refs.pop(0), refs.pop(0)
        if d.shape[0] > x.shape[-2]:
            rows, other = x.shape[-2], refs.pop(0)
            total_d = refs.pop()
            total_d[...] = d[rows:] + other[rows:]
            d = total_d
        pairs.append((x, d))
    start = refs.pop(0) if len(refs) == 2 else None
    (grads,) = refs
    slots, size = grads.shape[0], grads.shape[1]
    first = pairs[0][0]
    cols_n = pairs[0][1].shape[1] // size
    rows_n = first.shape[-1] // size * (first.shape[0] if len(first.shape) == 3 else 1)
    total = rows_n * cols_n
    group = math.gcd(slots, 32)

    @pl.loop(0, slots // group)
    def some(g):
        for s in [g * group + j for j in range(group)]:
            b = jnp.minimum(ids[s], total - 1)
            row = b // cols_n
            c = pl.ds(pl.multiple_of((b % cols_n) * size, size), size)
            acc = jnp.zeros((size, size), jnp.float32) if start is None else start[s].astype(jnp.float32)
            for x, d in pairs:
                per_part = x.shape[-1] // size
                at = pl.ds(pl.multiple_of((row % per_part) * size, size), size)
                acc += lax.dot_general(
                    x[row // per_part, :, at] if len(x.shape) == 3 else x[:, at],
                    d[:, c],
                    (((0,), (0,)), ((), ())),
                    preferred_element_type=jnp.float32,
                )
            grads[s] = jnp.where(ids[s] < total, acc, 0.0).astype(grads.dtype)


def line_grads(ids, pairs, start, size):
    slots = ids.shape[0]
    flat = [a for pair in pairs for a in pair] + ([] if start is None else [start])
    sums = [
        pltpu.VMEM((p[0].shape[-2], p[1].shape[1]), jnp.bfloat16) for p in pairs if len(p) == 3
    ]
    return pl.pallas_call(
        functools.partial(line_grads_kernel, len(pairs)),
        out_shape=jax.ShapeDtypeStruct((slots, size, size), jnp.bfloat16),
        in_specs=[whole(pltpu.SMEM)] + [whole()] * len(flat),
        out_specs=whole(),
        scratch_shapes=sums,
        compiler_params=pltpu.CompilerParams(vmem_limit_bytes=VMEM_LIMIT),
        cost_estimate=pl.CostEstimate(
            flops=512 * len(pairs) * slots * size * size,
            bytes_accessed=sum(2 * a.size for a in flat) + 2 * slots * size * size,
            transcendentals=0,
        ),
        name="line_grads",
    )(ids, *flat)


INWARD = ((0, 1), (3, 2))
OUTWARD = ((1, 0), (2, 3))
PAIRS = INWARD + OUTWARD
MIDDLE = ((1, 2), (2, 1))
SWAP = ((0, 1), (1, 0))


def ids_block(block_ids, size):
    rows = size * size // block_ids.shape[0]
    return jnp.broadcast_to(block_ids, (rows, block_ids.shape[0])).reshape(1, size, size)


def ids_of(piece, slots):
    return piece[-1, 0, :slots].astype(jnp.int32)


def line_body(tokens, upstream, blocks, block_ids):
    slots, size = blocks.shape[0], blocks.shape[1]
    rows, depth = tokens.shape
    width = upstream.shape[1]
    half_slots = slots // 2
    part_width = depth // 4
    at_z, half = lax.axis_index("dp"), lax.axis_index("groups")
    at_tensor, at_replica = lax.axis_index("tensor"), lax.axis_index("replica")
    middle = (at_z == 1) | (at_z == 2)
    place_of = jnp.stack([middle.astype(jnp.int32), half, at_tensor, at_replica])
    along = functools.partial(lax.ppermute, axis_name="dp")
    across = functools.partial(lax.ppermute, axis_name="groups", perm=SWAP)
    sideways = functools.partial(lax.ppermute, axis_name="tensor", perm=SWAP)
    cores = functools.partial(lax.ppermute, axis_name="replica", perm=SWAP)
    stage = lax.optimization_barrier

    mine = lax.dynamic_slice_in_dim(blocks, half * half_slots, half_slots, 0)
    mine = jnp.concatenate([mine, ids_block(block_ids, size).astype(jnp.bfloat16)])
    mine, late_blocks = stage((mine, blocks))

    near_a = along(mine, perm=INWARD)
    far_a = along(mine, perm=MIDDLE)
    other = lax.dynamic_slice_in_dim(late_blocks, (1 - half) * half_slots, half_slots, 0)
    part = lax.dynamic_slice_in_dim(tokens, lax.axis_index(INNER) * part_width, part_width, 1)
    both = jnp.concatenate([part, upstream])
    grads = line_grads(block_ids, ((tokens, upstream),), None, size)
    near_a, far_a, both, other, grads = stage((near_a, far_a, both, other, grads))

    end_a = along(near_a, perm=MIDDLE)
    far_b = across(far_a)
    both_1 = along(both, perm=PAIRS)
    both_1, end_a, far_b, both, other = stage((both_1, end_a, far_b, both, other))
    upstream_1 = both_1[rows:]

    near_b = along(other, perm=INWARD)
    end_b = across(end_a)
    both_2m = along(both, perm=MIDDLE)
    tokens_1 = lax.all_gather(both_1[:rows], INNER)
    ids_1, ids_2, ids_3 = (ids_of(piece, slots) for piece in (near_a, far_a, end_a))
    partial, turned = place_first(
        place_of, (block_ids, ids_1, ids_2, ids_3), (blocks, near_a, far_a, far_b, end_a), depth, width
    )
    near_b, end_b, both_2m, both_1, tokens_1, partial, turned = stage(
        (near_b, end_b, both_2m, both_1, tokens_1, partial, turned)
    )

    both_3m = along(both_1, perm=MIDDLE)
    both_2o = along(both_2m, perm=OUTWARD)
    last = (near_b, end_b)
    end_keep, own_keep, own_give, *end_give = project_back(
        place_of, ids_1, ids_3, turned, *last, upstream_1, upstream
    )
    end_keep, end_give = add_split(place_of, end_keep, *[cores(a) for a in end_give])
    end_keep, end_give, own_give, both_3m, both_2o = stage(
        (end_keep, end_give, own_give, both_3m, both_2o)
    )

    end_got = sideways(end_give)
    own_keep, own_give = add_split(place_of, own_keep, cores(own_give))
    both_3o = along(both_3m, perm=OUTWARD)
    tokens_2 = lax.all_gather(both_2m[:rows] + both_2o[:rows], INNER)
    proj, end_proj = project_forward(place_of, ids_1, ids_3, partial, *last, tokens, tokens_1)
    end_got, own_give, own_keep, proj, end_proj, both_3m = stage(
        (end_got, own_give, own_keep, proj, end_proj, both_3m)
    )

    sum_out = along(end_keep + end_got, perm=OUTWARD)
    own_got = sideways(own_give)
    grads = line_grads(block_ids, ((tokens_1, upstream_1),), grads, size)
    tokens_3 = lax.all_gather(both_3m[:rows] + both_3o[:rows], INNER)
    grads = line_grads(block_ids, ((tokens_2, both_2m, both_2o),), grads, size)
    sum_out, own_got, grads = stage((sum_out, own_got, grads))

    quarter = jnp.where(middle, own_keep + own_got, sum_out)
    proj_out = along(end_proj, perm=OUTWARD)
    grads = line_grads(block_ids, ((tokens_3, both_3m, both_3o),), grads, size)
    by_tensor, by_core, grads = stage((sideways(quarter), cores(quarter), grads))
    by_both = cores(by_tensor)
    projected = jnp.where(middle, proj, proj_out)
    token_grad = assemble(place_of, (quarter, by_core, by_tensor, by_both))
    return projected, token_grad, grads


def solution(mesh):
    line = tuple(mesh.shape[a] for a in ("groups", "dp", "tensor", "replica")) == (2, 4, 2, 2)
    return jax.shard_map(
        line_body if line else general_body,
        mesh=mesh,
        in_specs=(
            P(("groups", "dp"), None),
            P(("groups", "dp"), INNER),
            P(("dp",) + INNER, None, None),
            P(("dp",) + INNER),
        ),
        out_specs=(
            P(("groups", "dp"), INNER),
            P(("groups", "dp"), None),
            P(("groups", "dp") + INNER, None, None),
        ),
        check_vma=False,
    )
```

```python
import functools
import math

import jax
import jax.numpy as jnp
from jax import lax
from jax.experimental import pallas as pl
from jax.experimental.pallas import tpu as pltpu
from jax.sharding import PartitionSpec as P

VMEM_LIMIT = 60 * 1024 * 1024
INNER = ("tensor", "replica")


def whole(space=pltpu.VMEM):
    return pl.BlockSpec(memory_space=space)


def project_kernel(ids, blocks, tokens, upstream, proj, back, weight):
    slots, size = blocks.shape[0], blocks.shape[1]
    depth, width = weight.shape
    cols_n = width // size
    total = (depth // size) * cols_n
    weight[...] = jnp.zeros_like(weight)

    @pl.loop(0, slots, unroll=4)
    def place(s):
        b = ids[s]

        @pl.when(b < total)
        def put():
            r = pl.multiple_of((b // cols_n) * size, size)
            c = pl.multiple_of((b % cols_n) * size, size)
            weight[pl.ds(r, size), pl.ds(c, size)] = blocks[s]

    step = 256

    @pl.loop(0, width // step)
    def forward(n):
        c = pl.multiple_of(n * step, step)
        proj[:, pl.ds(c, step)] = jnp.dot(
            tokens[...], weight[:, pl.ds(c, step)], preferred_element_type=jnp.float32
        ).astype(proj.dtype)

    @pl.loop(0, depth // step, unroll=4)
    def backward(n):
        r = pl.multiple_of(n * step, step)
        back[:, pl.ds(r, step)] = lax.dot_general(
            upstream[...],
            weight[pl.ds(r, step), :],
            (((1,), (1,)), ((), ())),
            preferred_element_type=jnp.float32,
        ).astype(back.dtype)


def project(ids, blocks, tokens, upstream):
    rows, depth = tokens.shape
    width = upstream.shape[1]
    return pl.pallas_call(
        project_kernel,
        out_shape=(
            jax.ShapeDtypeStruct((rows, width), jnp.bfloat16),
            jax.ShapeDtypeStruct((rows, depth), jnp.bfloat16),
        ),
        in_specs=[whole(pltpu.SMEM), whole(), whole(), whole()],
        out_specs=(whole(), whole()),
        scratch_shapes=[pltpu.VMEM((depth, width), jnp.bfloat16)],
        compiler_params=pltpu.CompilerParams(vmem_limit_bytes=VMEM_LIMIT),
        cost_estimate=pl.CostEstimate(
            flops=4 * rows * depth * width,
            bytes_accessed=blocks.size * 2 + rows * (depth + width) * 4,
            transcendentals=0,
        ),
        name="project",
    )(ids, blocks, tokens, upstream)


def block_grad_kernel(ids, tokens, upstream, grads):
    slots, size = grads.shape[0], grads.shape[1]
    parts, slabs, _, part_width = tokens.shape
    cols_n = upstream.shape[2] // size
    per_part = part_width // size
    total = parts * per_part * cols_n

    @pl.loop(0, slots)
    def one(s):
        b = ids[s]

        @pl.when(b < total)
        def fill():
            row = b // cols_n
            part = row // per_part
            r = pl.multiple_of((row % per_part) * size, size)
            c = pl.multiple_of((b % cols_n) * size, size)
            acc = jnp.zeros((size, size), jnp.float32)
            for k in range(slabs):
                acc += lax.dot_general(
                    tokens[part, k, :, pl.ds(r, size)],
                    upstream[k, :, pl.ds(c, size)],
                    (((0,), (0,)), ((), ())),
                    preferred_element_type=jnp.float32,
                )
            grads[s] = acc.astype(grads.dtype)

        @pl.when(b >= total)
        def clear():
            grads[s] = jnp.zeros((size, size), grads.dtype)


def block_grads(ids, tokens, upstream, size):
    slots = ids.shape[0]
    parts, slabs, rows, part_width = tokens.shape
    return pl.pallas_call(
        block_grad_kernel,
        out_shape=jax.ShapeDtypeStruct((slots, size, size), jnp.bfloat16),
        in_specs=[whole(pltpu.SMEM), whole(), whole()],
        out_specs=whole(),
        compiler_params=pltpu.CompilerParams(vmem_limit_bytes=VMEM_LIMIT),
        cost_estimate=pl.CostEstimate(
            flops=2 * slots * slabs * rows * size * size,
            bytes_accessed=2 * (tokens.size + upstream.size + slots * size * size),
            transcendentals=0,
        ),
        name="block_grads",
    )(ids, tokens, upstream)


def general_body(tokens, upstream, blocks, block_ids):
    size = blocks.shape[1]
    all_blocks = lax.all_gather(blocks, "dp", axis=0, tiled=True)
    all_ids = lax.all_gather(block_ids, "dp", axis=0, tiled=True)
    proj, back = project(all_ids, all_blocks, tokens, upstream)
    terms = block_grads(all_ids, tokens[None, None], upstream[None], size)
    grads = lax.psum_scatter(terms, "dp", scatter_dimension=0, tiled=True)
    return proj, lax.psum(back, INNER), grads


def place_blocks(ids, first, blocks, weight, turned, slots):
    size = blocks.shape[1]
    depth, width = turned.shape[::-1] if weight is None else weight.shape
    cols_n = width // size
    total = (depth // size) * cols_n
    group = math.gcd(slots, 8)

    @pl.loop(0, slots // group)
    def place(g):
        some = [g * group + j for j in range(group)]
        flipped = [None if turned is None else blocks[s].T for s in some]
        for s, flip in zip(some, flipped):
            b = ids[first + s]

            @pl.when(b < total)
            def put(s=s, flip=flip, b=b):
                r = pl.multiple_of((b // cols_n) * size, size)
                c = pl.multiple_of((b % cols_n) * size, size)
                if weight is not None:
                    weight[pl.ds(r, size), pl.ds(c, size)] = blocks[s]
                if turned is not None:
                    turned[pl.ds(c, size), pl.ds(r, size)] = flip


def place_kernel(
    place_of, ids_0, ids_1, ids_2, ids_3, own, near_a, far_a, far_b, end_a, weight, turned
):
    is_middle, half = place_of[0], place_of[1]
    half_slots = far_b.shape[0] - 1
    mine, other = half * half_slots, (1 - half) * half_slots

    @pl.when(is_middle == 1)
    def work():
        weight[...] = jnp.zeros_like(weight)
        turned[...] = jnp.zeros_like(turned)
        place_blocks(ids_0, 0, own, weight, turned, own.shape[0])
        place_blocks(ids_1, mine, near_a, weight, turned, half_slots)
        place_blocks(ids_2, mine, far_a, weight, turned, half_slots)
        place_blocks(ids_2, other, far_b, weight, turned, half_slots)
        place_blocks(ids_3, mine, end_a, weight, turned, half_slots)


def place_first(place_of, ids, pieces, depth, width):
    return pl.pallas_call(
        place_kernel,
        out_shape=(
            jax.ShapeDtypeStruct((depth, width), jnp.bfloat16),
            jax.ShapeDtypeStruct((width, depth), jnp.bfloat16),
        ),
        in_specs=[whole(pltpu.SMEM)] * 5 + [whole()] * 5,
        out_specs=(whole(), whole()),
        compiler_params=pltpu.CompilerParams(vmem_limit_bytes=VMEM_LIMIT),
        cost_estimate=pl.CostEstimate(
            flops=0, bytes_accessed=depth * width * 6, transcendentals=0
        ),
        name="place_first",
    )(place_of, *ids, *pieces)


def back_kernel(
    place_of, ids_1, ids_3, partial, near_b, end_b, end_upstream, upstream,
    end_keep, own_keep, own_give, end_give_0, end_give_1, held, sources, sem,
):
    half_slots = near_b.shape[0]
    other = (1 - place_of[1]) * half_slots
    rows, width = upstream.shape
    step = 256
    per_part = end_keep.shape[2] // step

    @pl.when(place_of[0] == 1)
    def work():
        load = pltpu.make_async_copy(partial, held, sem)
        load.start()
        sources[:rows] = end_upstream[...]
        sources[rows:] = upstream[...]
        load.wait()
        place_blocks(ids_1, other, near_b, None, held, half_slots)
        place_blocks(ids_3, other, end_b, None, held, half_slots)

        def column(part, end_target, own_target):
            @pl.loop(0, per_part, unroll=2)
            def backward(n):
                at = pl.multiple_of(n * step, step)
                result = jnp.dot(
                    sources[...],
                    held[:, pl.ds(pl.multiple_of(part * per_part * step + at, step), step)],
                    preferred_element_type=jnp.float32,
                ).astype(own_target.dtype)
                end_target[:, pl.ds(at, step)] = result[:rows]
                own_target[:, pl.ds(at, step)] = result[rows:]

        for x, end_give in enumerate((end_give_0, end_give_1)):
            column(2 * x + place_of[3], end_keep.at[x], own_keep.at[x])
            column(2 * x + 1 - place_of[3], end_give, own_give.at[x])


def project_back(place_of, ids_1, ids_3, partial, near_b, end_b, end_upstream, upstream):
    width, depth = partial.shape
    rows = upstream.shape[0]
    quarter = jax.ShapeDtypeStruct((rows, depth // 4), jnp.bfloat16)
    half = jax.ShapeDtypeStruct((2, rows, depth // 4), jnp.bfloat16)
    return pl.pallas_call(
        back_kernel,
        out_shape=(half, half, half, quarter, quarter),
        in_specs=[whole(pltpu.SMEM)] * 3 + [whole(pl.ANY)] + [whole()] * 4,
        out_specs=(whole(),) * 5,
        scratch_shapes=[
            pltpu.VMEM((width, depth), jnp.bfloat16),
            pltpu.VMEM((2 * rows, width), jnp.bfloat16),
            pltpu.SemaphoreType.DMA,
        ],
        compiler_params=pltpu.CompilerParams(vmem_limit_bytes=VMEM_LIMIT),
        cost_estimate=pl.CostEstimate(
            flops=4 * rows * depth * width,
            bytes_accessed=depth * width * 2 + rows * (depth + width) * 4,
            transcendentals=0,
        ),
        name="project_back",
    )(place_of, ids_1, ids_3, partial, near_b, end_b, end_upstream, upstream)


def forward_kernel(
    place_of, ids_1, ids_3, partial, near_b, end_b, tokens, gathered, proj, end_proj, held, sem
):
    half_slots = near_b.shape[0]
    other = (1 - place_of[1]) * half_slots
    depth, width = held.shape
    parts, rows, part_width = gathered.shape
    step = 256

    @pl.when(place_of[0] == 1)
    def work():
        load = pltpu.make_async_copy(partial, held, sem)
        load.start()
        load.wait()
        place_blocks(ids_1, other, near_b, held, None, half_slots)
        place_blocks(ids_3, other, end_b, held, None, half_slots)

        @pl.loop(0, width // step, unroll=2)
        def forward(n):
            c = pl.multiple_of(n * step, step)
            acc = jnp.zeros((rows, step), jnp.float32)
            for q in range(parts):
                acc += jnp.dot(
                    gathered[q],
                    held[q * part_width : (q + 1) * part_width, pl.ds(c, step)],
                    preferred_element_type=jnp.float32,
                )
            end_proj[:, pl.ds(c, step)] = acc.astype(end_proj.dtype)
            proj[:, pl.ds(c, step)] = jnp.dot(
                tokens[...], held[:, pl.ds(c, step)], preferred_element_type=jnp.float32
            ).astype(proj.dtype)


def project_forward(place_of, ids_1, ids_3, partial, near_b, end_b, tokens, gathered):
    depth, width = partial.shape
    rows = tokens.shape[0]
    out = jax.ShapeDtypeStruct((rows, width), jnp.bfloat16)
    return pl.pallas_call(
        forward_kernel,
        out_shape=(out, out),
        in_specs=[whole(pltpu.SMEM)] * 3 + [whole(pl.ANY)] + [whole()] * 4,
        out_specs=(whole(),) * 2,
        scratch_shapes=[pltpu.VMEM((depth, width), jnp.bfloat16), pltpu.SemaphoreType.DMA],
        compiler_params=pltpu.CompilerParams(vmem_limit_bytes=VMEM_LIMIT),
        cost_estimate=pl.CostEstimate(
            flops=rows * depth * width // 2, bytes_accessed=depth * width, transcendentals=0
        ),
        name="project_forward",
    )(place_of, ids_1, ids_3, partial, near_b, end_b, tokens, gathered)


def split_kernel(place_of, keep, *refs):
    x = place_of[2]
    own, give = refs[-2:]
    got = refs[:-2] if len(refs) > 3 else (refs[0].at[0], refs[0].at[1])
    for at in range(2):
        total = (keep[at].astype(jnp.float32) + got[at][...].astype(jnp.float32)).astype(own.dtype)

        @pl.when(x == at)
        def mine():
            own[...] = total

        @pl.when(x != at)
        def theirs():
            give[...] = total


def add_split(place_of, keep, *got):
    out = jax.ShapeDtypeStruct(keep.shape[1:], keep.dtype)
    return pl.pallas_call(
        split_kernel,
        out_shape=(out, out),
        in_specs=[whole(pltpu.SMEM), whole()] + [whole()] * len(got),
        out_specs=(whole(), whole()),
        compiler_params=pltpu.CompilerParams(vmem_limit_bytes=VMEM_LIMIT),
        cost_estimate=pl.CostEstimate(
            flops=keep.size, bytes_accessed=keep.size * 6, transcendentals=0
        ),
        name="add_split",
    )(place_of, keep, *got)


def assemble_kernel(place_of, own, by_core, by_tensor, by_both, full):
    x, c = place_of[2], place_of[3]
    width = own.shape[1]
    for ref, xx, cc in (
        (own, x, c), (by_core, x, 1 - c), (by_tensor, 1 - x, c), (by_both, 1 - x, 1 - c)
    ):
        at = pl.multiple_of((xx * 2 + cc) * width, width)
        full[:, pl.ds(at, width)] = ref[...]


def assemble(place_of, quarters):
    rows, width = quarters[0].shape
    return pl.pallas_call(
        assemble_kernel,
        out_shape=jax.ShapeDtypeStruct((rows, 4 * width), quarters[0].dtype),
        in_specs=[whole(pltpu.SMEM)] + [whole()] * 4,
        out_specs=whole(),
        compiler_params=pltpu.CompilerParams(vmem_limit_bytes=VMEM_LIMIT),
        cost_estimate=pl.CostEstimate(
            flops=0, bytes_accessed=rows * width * 16, transcendentals=0
        ),
        name="assemble",
    )(place_of, *quarters)


def line_grads_kernel(pairs_n, ids, *refs):
    refs = list(refs)
    pairs = []
    for k in range(pairs_n):
        x, d = refs.pop(0), refs.pop(0)
        if d.shape[0] > x.shape[-2]:
            rows, other = x.shape[-2], refs.pop(0)
            total_d = refs.pop()
            total_d[...] = d[rows:] + other[rows:]
            d = total_d
        pairs.append((x, d))
    start = refs.pop(0) if len(refs) == 2 else None
    (grads,) = refs
    slots, size = grads.shape[0], grads.shape[1]
    first = pairs[0][0]
    cols_n = pairs[0][1].shape[1] // size
    rows_n = first.shape[-1] // size * (first.shape[0] if len(first.shape) == 3 else 1)
    total = rows_n * cols_n
    group = math.gcd(slots, 32)

    @pl.loop(0, slots // group)
    def some(g):
        for s in [g * group + j for j in range(group)]:
            b = jnp.minimum(ids[s], total - 1)
            row = b // cols_n
            c = pl.ds(pl.multiple_of((b % cols_n) * size, size), size)
            acc = jnp.zeros((size, size), jnp.float32) if start is None else start[s].astype(jnp.float32)
            for x, d in pairs:
                per_part = x.shape[-1] // size
                at = pl.ds(pl.multiple_of((row % per_part) * size, size), size)
                acc += lax.dot_general(
                    x[row // per_part, :, at] if len(x.shape) == 3 else x[:, at],
                    d[:, c],
                    (((0,), (0,)), ((), ())),
                    preferred_element_type=jnp.float32,
                )
            grads[s] = jnp.where(ids[s] < total, acc, 0.0).astype(grads.dtype)


def line_grads(ids, pairs, start, size):
    slots = ids.shape[0]
    flat = [a for pair in pairs for a in pair] + ([] if start is None else [start])
    sums = [
        pltpu.VMEM((p[0].shape[-2], p[1].shape[1]), jnp.bfloat16) for p in pairs if len(p) == 3
    ]
    return pl.pallas_call(
        functools.partial(line_grads_kernel, len(pairs)),
        out_shape=jax.ShapeDtypeStruct((slots, size, size), jnp.bfloat16),
        in_specs=[whole(pltpu.SMEM)] + [whole()] * len(flat),
        out_specs=whole(),
        scratch_shapes=sums,
        compiler_params=pltpu.CompilerParams(vmem_limit_bytes=VMEM_LIMIT),
        cost_estimate=pl.CostEstimate(
            flops=512 * len(pairs) * slots * size * size,
            bytes_accessed=sum(2 * a.size for a in flat) + 2 * slots * size * size,
            transcendentals=0,
        ),
        name="line_grads",
    )(ids, *flat)


INWARD = ((0, 1), (3, 2))
OUTWARD = ((1, 0), (2, 3))
PAIRS = INWARD + OUTWARD
MIDDLE = ((1, 2), (2, 1))
SWAP = ((0, 1), (1, 0))


def ids_block(block_ids, size):
    rows = size * size // block_ids.shape[0]
    return jnp.broadcast_to(block_ids, (rows, block_ids.shape[0])).reshape(1, size, size)


def ids_of(piece, slots):
    return piece[-1, 0, :slots].astype(jnp.int32)


def line_body(tokens, upstream, blocks, block_ids):
    slots, size = blocks.shape[0], blocks.shape[1]
    rows, depth = tokens.shape
    width = upstream.shape[1]
    half_slots = slots // 2
    part_width = depth // 4
    at_z, half = lax.axis_index("dp"), lax.axis_index("groups")
    at_tensor, at_replica = lax.axis_index("tensor"), lax.axis_index("replica")
    middle = (at_z == 1) | (at_z == 2)
    place_of = jnp.stack([middle.astype(jnp.int32), half, at_tensor, at_replica])
    along = functools.partial(lax.ppermute, axis_name="dp")
    across = functools.partial(
        lax.ppermute, axis_name=("groups", "dp"), perm=((1, 5), (5, 1), (2, 6), (6, 2))
    )
    middle_swap = ((2, 3), (3, 2), (4, 5), (5, 4))
    middle_sideways = functools.partial(
        lax.ppermute, axis_name=("dp", "tensor"), perm=middle_swap
    )
    middle_cores = functools.partial(lax.ppermute, axis_name=("dp", "replica"), perm=middle_swap)
    sideways = functools.partial(lax.ppermute, axis_name="tensor", perm=SWAP)
    cores = functools.partial(lax.ppermute, axis_name="replica", perm=SWAP)
    stage = lax.optimization_barrier

    mine = lax.dynamic_slice_in_dim(blocks, half * half_slots, half_slots, 0)
    mine = jnp.concatenate([mine, ids_block(block_ids, size).astype(jnp.bfloat16)])
    mine, late_blocks = stage((mine, blocks))

    near_a = along(mine, perm=INWARD)
    far_a = along(mine, perm=MIDDLE)
    other = lax.dynamic_slice_in_dim(late_blocks, (1 - half) * half_slots, half_slots, 0)
    part = lax.dynamic_slice_in_dim(tokens, lax.axis_index(INNER) * part_width, part_width, 1)
    both = jnp.concatenate([part, upstream])
    grads = line_grads(block_ids, ((tokens, upstream),), None, size)
    near_a, far_a, both, other, grads = stage((near_a, far_a, both, other, grads))

    end_a = along(near_a, perm=MIDDLE)
    far_b = across(far_a)
    both_1 = along(both, perm=PAIRS)
    both_1, end_a, far_b, both, other = stage((both_1, end_a, far_b, both, other))
    upstream_1 = both_1[rows:]

    near_b = along(other, perm=INWARD)
    end_b = across(end_a)
    both_2m = along(both, perm=MIDDLE)
    tokens_1 = lax.all_gather(both_1[:rows], INNER)
    ids_1, ids_2, ids_3 = (ids_of(piece, slots) for piece in (near_a, far_a, end_a))
    partial, turned = place_first(
        place_of, (block_ids, ids_1, ids_2, ids_3), (blocks, near_a, far_a, far_b, end_a), depth, width
    )
    near_b, end_b, both_2m, both_1, tokens_1, partial, turned = stage(
        (near_b, end_b, both_2m, both_1, tokens_1, partial, turned)
    )

    both_3m = along(both_1, perm=MIDDLE)
    both_2o = along(both_2m, perm=OUTWARD)
    last = (near_b, end_b)
    end_keep, own_keep, own_give, *end_give = project_back(
        place_of, ids_1, ids_3, turned, *last, upstream_1, upstream
    )
    end_keep, end_give = add_split(place_of, end_keep, *[middle_cores(a) for a in end_give])
    end_keep, end_give, own_give, both_3m, both_2o = stage(
        (end_keep, end_give, own_give, both_3m, both_2o)
    )

    end_got = middle_sideways(end_give)
    own_keep, own_give = add_split(place_of, own_keep, middle_cores(own_give))
    both_3o = along(both_3m, perm=OUTWARD)
    tokens_2 = lax.all_gather(both_2m[:rows] + both_2o[:rows], INNER)
    proj, end_proj = project_forward(place_of, ids_1, ids_3, partial, *last, tokens, tokens_1)
    end_got, own_give, own_keep, proj, end_proj, both_3m = stage(
        (end_got, own_give, own_keep, proj, end_proj, both_3m)
    )

    sum_out = along(end_keep + end_got, perm=OUTWARD)
    own_got = middle_sideways(own_give)
    grads = line_grads(block_ids, ((tokens_1, upstream_1),), grads, size)
    tokens_3 = lax.all_gather(both_3m[:rows] + both_3o[:rows], INNER)
    grads = line_grads(block_ids, ((tokens_2, both_2m, both_2o),), grads, size)
    sum_out, own_got, grads = stage((sum_out, own_got, grads))

    quarter = jnp.where(middle, own_keep + own_got, sum_out)
    proj_out = along(end_proj, perm=OUTWARD)
    grads = line_grads(block_ids, ((tokens_3, both_3m, both_3o),), grads, size)
    by_tensor, by_core, grads = stage((sideways(quarter), cores(quarter), grads))
    by_both = cores(by_tensor)
    projected = jnp.where(middle, proj, proj_out)
    token_grad = assemble(place_of, (quarter, by_core, by_tensor, by_both))
    return projected, token_grad, grads


def solution(mesh):
    line = tuple(mesh.shape[a] for a in ("groups", "dp", "tensor", "replica")) == (2, 4, 2, 2)
    return jax.shard_map(
        line_body if line else general_body,
        mesh=mesh,
        in_specs=(
            P(("groups", "dp"), None),
            P(("groups", "dp"), INNER),
            P(("dp",) + INNER, None, None),
            P(("dp",) + INNER),
        ),
        out_specs=(
            P(("groups", "dp"), INNER),
            P(("groups", "dp"), None),
            P(("groups", "dp") + INNER, None, None),
        ),
        check_vma=False,
    )
```

```python
import functools
import math

import jax
import jax.numpy as jnp
from jax import lax
from jax.experimental import pallas as pl
from jax.experimental.pallas import tpu as pltpu
from jax.sharding import PartitionSpec as P

VMEM_LIMIT = 60 * 1024 * 1024
INNER = ("tensor", "replica")


def whole(space=pltpu.VMEM):
    return pl.BlockSpec(memory_space=space)


def project_kernel(ids, blocks, tokens, upstream, proj, back, weight):
    slots, size = blocks.shape[0], blocks.shape[1]
    depth, width = weight.shape
    cols_n = width // size
    total = (depth // size) * cols_n
    weight[...] = jnp.zeros_like(weight)

    @pl.loop(0, slots, unroll=4)
    def place(s):
        b = ids[s]

        @pl.when(b < total)
        def put():
            r = pl.multiple_of((b // cols_n) * size, size)
            c = pl.multiple_of((b % cols_n) * size, size)
            weight[pl.ds(r, size), pl.ds(c, size)] = blocks[s]

    step = 256

    @pl.loop(0, width // step)
    def forward(n):
        c = pl.multiple_of(n * step, step)
        proj[:, pl.ds(c, step)] = jnp.dot(
            tokens[...], weight[:, pl.ds(c, step)], preferred_element_type=jnp.float32
        ).astype(proj.dtype)

    @pl.loop(0, depth // step, unroll=4)
    def backward(n):
        r = pl.multiple_of(n * step, step)
        back[:, pl.ds(r, step)] = lax.dot_general(
            upstream[...],
            weight[pl.ds(r, step), :],
            (((1,), (1,)), ((), ())),
            preferred_element_type=jnp.float32,
        ).astype(back.dtype)


def project(ids, blocks, tokens, upstream):
    rows, depth = tokens.shape
    width = upstream.shape[1]
    return pl.pallas_call(
        project_kernel,
        out_shape=(
            jax.ShapeDtypeStruct((rows, width), jnp.bfloat16),
            jax.ShapeDtypeStruct((rows, depth), jnp.bfloat16),
        ),
        in_specs=[whole(pltpu.SMEM), whole(), whole(), whole()],
        out_specs=(whole(), whole()),
        scratch_shapes=[pltpu.VMEM((depth, width), jnp.bfloat16)],
        compiler_params=pltpu.CompilerParams(vmem_limit_bytes=VMEM_LIMIT),
        cost_estimate=pl.CostEstimate(
            flops=4 * rows * depth * width,
            bytes_accessed=blocks.size * 2 + rows * (depth + width) * 4,
            transcendentals=0,
        ),
        name="project",
    )(ids, blocks, tokens, upstream)


def block_grad_kernel(ids, tokens, upstream, grads):
    slots, size = grads.shape[0], grads.shape[1]
    parts, slabs, _, part_width = tokens.shape
    cols_n = upstream.shape[2] // size
    per_part = part_width // size
    total = parts * per_part * cols_n

    @pl.loop(0, slots)
    def one(s):
        b = ids[s]

        @pl.when(b < total)
        def fill():
            row = b // cols_n
            part = row // per_part
            r = pl.multiple_of((row % per_part) * size, size)
            c = pl.multiple_of((b % cols_n) * size, size)
            acc = jnp.zeros((size, size), jnp.float32)
            for k in range(slabs):
                acc += lax.dot_general(
                    tokens[part, k, :, pl.ds(r, size)],
                    upstream[k, :, pl.ds(c, size)],
                    (((0,), (0,)), ((), ())),
                    preferred_element_type=jnp.float32,
                )
            grads[s] = acc.astype(grads.dtype)

        @pl.when(b >= total)
        def clear():
            grads[s] = jnp.zeros((size, size), grads.dtype)


def block_grads(ids, tokens, upstream, size):
    slots = ids.shape[0]
    parts, slabs, rows, part_width = tokens.shape
    return pl.pallas_call(
        block_grad_kernel,
        out_shape=jax.ShapeDtypeStruct((slots, size, size), jnp.bfloat16),
        in_specs=[whole(pltpu.SMEM), whole(), whole()],
        out_specs=whole(),
        compiler_params=pltpu.CompilerParams(vmem_limit_bytes=VMEM_LIMIT),
        cost_estimate=pl.CostEstimate(
            flops=2 * slots * slabs * rows * size * size,
            bytes_accessed=2 * (tokens.size + upstream.size + slots * size * size),
            transcendentals=0,
        ),
        name="block_grads",
    )(ids, tokens, upstream)


def general_body(tokens, upstream, blocks, block_ids):
    size = blocks.shape[1]
    all_blocks = lax.all_gather(blocks, "dp", axis=0, tiled=True)
    all_ids = lax.all_gather(block_ids, "dp", axis=0, tiled=True)
    proj, back = project(all_ids, all_blocks, tokens, upstream)
    terms = block_grads(all_ids, tokens[None, None], upstream[None], size)
    grads = lax.psum_scatter(terms, "dp", scatter_dimension=0, tiled=True)
    return proj, lax.psum(back, INNER), grads


def place_blocks(ids, first, blocks, weight, turned, slots):
    size = blocks.shape[1]
    depth, width = turned.shape[::-1] if weight is None else weight.shape
    cols_n = width // size
    total = (depth // size) * cols_n
    group = math.gcd(slots, 8)

    @pl.loop(0, slots // group)
    def place(g):
        some = [g * group + j for j in range(group)]
        flipped = [None if turned is None else blocks[s].T for s in some]
        for s, flip in zip(some, flipped):
            b = ids[first + s]

            @pl.when(b < total)
            def put(s=s, flip=flip, b=b):
                r = pl.multiple_of((b // cols_n) * size, size)
                c = pl.multiple_of((b % cols_n) * size, size)
                if weight is not None:
                    weight[pl.ds(r, size), pl.ds(c, size)] = blocks[s]
                if turned is not None:
                    turned[pl.ds(c, size), pl.ds(r, size)] = flip


def place_kernel(
    place_of, ids_0, ids_1, ids_2, ids_3, own, near_a, far_a, far_b, end_a, weight, turned
):
    is_middle, half = place_of[0], place_of[1]
    half_slots = far_b.shape[0] - 1
    mine, other = half * half_slots, (1 - half) * half_slots

    @pl.when(is_middle == 1)
    def work():
        weight[...] = jnp.zeros_like(weight)
        turned[...] = jnp.zeros_like(turned)
        place_blocks(ids_0, 0, own, weight, turned, own.shape[0])
        place_blocks(ids_1, mine, near_a, weight, turned, half_slots)
        place_blocks(ids_2, mine, far_a, weight, turned, half_slots)
        place_blocks(ids_2, other, far_b, weight, turned, half_slots)
        place_blocks(ids_3, mine, end_a, weight, turned, half_slots)


def place_first(place_of, ids, pieces, depth, width):
    return pl.pallas_call(
        place_kernel,
        out_shape=(
            jax.ShapeDtypeStruct((depth, width), jnp.bfloat16),
            jax.ShapeDtypeStruct((width, depth), jnp.bfloat16),
        ),
        in_specs=[whole(pltpu.SMEM)] * 5 + [whole()] * 5,
        out_specs=(whole(), whole()),
        compiler_params=pltpu.CompilerParams(vmem_limit_bytes=VMEM_LIMIT),
        cost_estimate=pl.CostEstimate(
            flops=0, bytes_accessed=depth * width * 6, transcendentals=0
        ),
        name="place_first",
    )(place_of, *ids, *pieces)


def back_kernel(
    place_of, ids_1, ids_3, partial, near_b, end_b, end_upstream, upstream,
    end_keep, own_keep, own_give, end_give_0, end_give_1, held, sources, sem,
):
    half_slots = near_b.shape[0]
    other = (1 - place_of[1]) * half_slots
    rows, width = upstream.shape
    step = 256
    per_part = end_keep.shape[2] // step

    @pl.when(place_of[0] == 1)
    def work():
        load = pltpu.make_async_copy(partial, held, sem)
        load.start()
        sources[:rows] = end_upstream[...]
        sources[rows:] = upstream[...]
        load.wait()
        place_blocks(ids_1, other, near_b, None, held, half_slots)
        place_blocks(ids_3, other, end_b, None, held, half_slots)

        def column(part, end_target, own_target):
            @pl.loop(0, per_part, unroll=2)
            def backward(n):
                at = pl.multiple_of(n * step, step)
                result = jnp.dot(
                    sources[...],
                    held[:, pl.ds(pl.multiple_of(part * per_part * step + at, step), step)],
                    preferred_element_type=jnp.float32,
                ).astype(own_target.dtype)
                end_target[:, pl.ds(at, step)] = result[:rows]
                own_target[:, pl.ds(at, step)] = result[rows:]

        for x, end_give in enumerate((end_give_0, end_give_1)):
            column(2 * x + place_of[3], end_keep.at[x], own_keep.at[x])
            column(2 * x + 1 - place_of[3], end_give, own_give.at[x])


def project_back(place_of, ids_1, ids_3, partial, near_b, end_b, end_upstream, upstream):
    width, depth = partial.shape
    rows = upstream.shape[0]
    quarter = jax.ShapeDtypeStruct((rows, depth // 4), jnp.bfloat16)
    half = jax.ShapeDtypeStruct((2, rows, depth // 4), jnp.bfloat16)
    return pl.pallas_call(
        back_kernel,
        out_shape=(half, half, half, quarter, quarter),
        in_specs=[whole(pltpu.SMEM)] * 3 + [whole(pl.ANY)] + [whole()] * 4,
        out_specs=(whole(),) * 5,
        scratch_shapes=[
            pltpu.VMEM((width, depth), jnp.bfloat16),
            pltpu.VMEM((2 * rows, width), jnp.bfloat16),
            pltpu.SemaphoreType.DMA,
        ],
        compiler_params=pltpu.CompilerParams(vmem_limit_bytes=VMEM_LIMIT),
        cost_estimate=pl.CostEstimate(
            flops=4 * rows * depth * width,
            bytes_accessed=depth * width * 2 + rows * (depth + width) * 4,
            transcendentals=0,
        ),
        name="project_back",
    )(place_of, ids_1, ids_3, partial, near_b, end_b, end_upstream, upstream)


def forward_kernel(
    place_of, ids_1, ids_3, partial, near_b, end_b, tokens, gathered, proj, end_proj, held, sem
):
    half_slots = near_b.shape[0]
    other = (1 - place_of[1]) * half_slots
    depth, width = held.shape
    parts, rows, part_width = gathered.shape
    step = 256

    @pl.when(place_of[0] == 1)
    def work():
        load = pltpu.make_async_copy(partial, held, sem)
        load.start()
        load.wait()
        place_blocks(ids_1, other, near_b, held, None, half_slots)
        place_blocks(ids_3, other, end_b, held, None, half_slots)

        @pl.loop(0, width // step, unroll=2)
        def forward(n):
            c = pl.multiple_of(n * step, step)
            acc = jnp.zeros((rows, step), jnp.float32)
            for q in range(parts):
                acc += jnp.dot(
                    gathered[q],
                    held[q * part_width : (q + 1) * part_width, pl.ds(c, step)],
                    preferred_element_type=jnp.float32,
                )
            end_proj[:, pl.ds(c, step)] = acc.astype(end_proj.dtype)
            proj[:, pl.ds(c, step)] = jnp.dot(
                tokens[...], held[:, pl.ds(c, step)], preferred_element_type=jnp.float32
            ).astype(proj.dtype)


def project_forward(place_of, ids_1, ids_3, partial, near_b, end_b, tokens, gathered):
    depth, width = partial.shape
    rows = tokens.shape[0]
    out = jax.ShapeDtypeStruct((rows, width), jnp.bfloat16)
    return pl.pallas_call(
        forward_kernel,
        out_shape=(out, out),
        in_specs=[whole(pltpu.SMEM)] * 3 + [whole(pl.ANY)] + [whole()] * 4,
        out_specs=(whole(),) * 2,
        scratch_shapes=[pltpu.VMEM((depth, width), jnp.bfloat16), pltpu.SemaphoreType.DMA],
        compiler_params=pltpu.CompilerParams(vmem_limit_bytes=VMEM_LIMIT),
        cost_estimate=pl.CostEstimate(
            flops=rows * depth * width // 2, bytes_accessed=depth * width, transcendentals=0
        ),
        name="project_forward",
    )(place_of, ids_1, ids_3, partial, near_b, end_b, tokens, gathered)


def split_kernel(place_of, keep, *refs):
    x = place_of[2]
    own, give = refs[-2:]
    got = refs[:-2] if len(refs) > 3 else (refs[0].at[0], refs[0].at[1])
    for at in range(2):
        total = (keep[at].astype(jnp.float32) + got[at][...].astype(jnp.float32)).astype(own.dtype)

        @pl.when(x == at)
        def mine():
            own[...] = total

        @pl.when(x != at)
        def theirs():
            give[...] = total


def add_split(place_of, keep, *got):
    out = jax.ShapeDtypeStruct(keep.shape[1:], keep.dtype)
    return pl.pallas_call(
        split_kernel,
        out_shape=(out, out),
        in_specs=[whole(pltpu.SMEM), whole()] + [whole()] * len(got),
        out_specs=(whole(), whole()),
        compiler_params=pltpu.CompilerParams(vmem_limit_bytes=VMEM_LIMIT),
        cost_estimate=pl.CostEstimate(
            flops=keep.size, bytes_accessed=keep.size * 6, transcendentals=0
        ),
        name="add_split",
    )(place_of, keep, *got)


def assemble_kernel(place_of, own, by_core, by_tensor, by_both, full):
    x, c = place_of[2], place_of[3]
    width = own.shape[1]
    for ref, xx, cc in (
        (own, x, c), (by_core, x, 1 - c), (by_tensor, 1 - x, c), (by_both, 1 - x, 1 - c)
    ):
        at = pl.multiple_of((xx * 2 + cc) * width, width)
        full[:, pl.ds(at, width)] = ref[...]


def assemble(place_of, quarters):
    rows, width = quarters[0].shape
    return pl.pallas_call(
        assemble_kernel,
        out_shape=jax.ShapeDtypeStruct((rows, 4 * width), quarters[0].dtype),
        in_specs=[whole(pltpu.SMEM)] + [whole()] * 4,
        out_specs=whole(),
        compiler_params=pltpu.CompilerParams(vmem_limit_bytes=VMEM_LIMIT),
        cost_estimate=pl.CostEstimate(
            flops=0, bytes_accessed=rows * width * 16, transcendentals=0
        ),
        name="assemble",
    )(place_of, *quarters)


def line_grads_kernel(pairs_n, summed, ids, *refs):
    refs = list(refs)
    pairs = []
    for k in range(pairs_n):
        x, d = refs.pop(0), refs.pop(0)
        if summed[k]:
            other = refs.pop(0)
            total_d = refs.pop()
            total_d[...] = d[...] + other[...]
            d = total_d
        pairs.append((x, d))
    start = refs.pop(0) if len(refs) == 2 else None
    (grads,) = refs
    slots, size = grads.shape[0], grads.shape[1]
    first = pairs[0][0]
    cols_n = pairs[0][1].shape[1] // size
    rows_n = first.shape[-1] // size * (first.shape[0] if len(first.shape) == 3 else 1)
    total = rows_n * cols_n
    group = math.gcd(slots, 32)

    @pl.loop(0, slots // group)
    def some(g):
        for s in [g * group + j for j in range(group)]:
            b = jnp.minimum(ids[s], total - 1)
            row = b // cols_n
            c = pl.ds(pl.multiple_of((b % cols_n) * size, size), size)
            acc = jnp.zeros((size, size), jnp.float32) if start is None else start[s].astype(jnp.float32)
            for x, d in pairs:
                per_part = x.shape[-1] // size
                at = pl.ds(pl.multiple_of((row % per_part) * size, size), size)
                acc += lax.dot_general(
                    x[row // per_part, :, at] if len(x.shape) == 3 else x[:, at],
                    d[:, c],
                    (((0,), (0,)), ((), ())),
                    preferred_element_type=jnp.float32,
                )
            grads[s] = jnp.where(ids[s] < total, acc, 0.0).astype(grads.dtype)


def line_grads(ids, pairs, start, size):
    slots = ids.shape[0]
    flat = [a for pair in pairs for a in pair] + ([] if start is None else [start])
    lower = [pl.BlockSpec((a.shape[0] // 2, a.shape[1]), lambda _: (1, 0)) for a in pairs[0][1:]]
    specs = [whole()] + (lower if len(pairs[0]) == 3 else [whole()])
    specs += [] if start is None else [whole()]
    sums = [
        pltpu.VMEM((p[0].shape[-2], p[1].shape[1]), jnp.bfloat16) for p in pairs if len(p) == 3
    ]
    return pl.pallas_call(
        functools.partial(line_grads_kernel, len(pairs), tuple(len(p) == 3 for p in pairs)),
        out_shape=jax.ShapeDtypeStruct((slots, size, size), jnp.bfloat16),
        grid=(1,),
        in_specs=[whole(pltpu.SMEM)] + specs,
        out_specs=whole(),
        scratch_shapes=sums,
        compiler_params=pltpu.CompilerParams(vmem_limit_bytes=VMEM_LIMIT),
        cost_estimate=pl.CostEstimate(
            flops=512 * len(pairs) * slots * size * size,
            bytes_accessed=sum(2 * a.size for a in flat) + 2 * slots * size * size,
            transcendentals=0,
        ),
        name="line_grads",
    )(ids, *flat)


INWARD = ((0, 1), (3, 2))
OUTWARD = ((1, 0), (2, 3))
PAIRS = INWARD + OUTWARD
MIDDLE = ((1, 2), (2, 1))
SWAP = ((0, 1), (1, 0))


def ids_block(block_ids, size):
    rows = size * size // block_ids.shape[0]
    return jnp.broadcast_to(block_ids, (rows, block_ids.shape[0])).reshape(1, size, size)


def ids_of(piece, slots):
    return piece[-1, 0, :slots].astype(jnp.int32)


def line_body(tokens, upstream, blocks, block_ids):
    slots, size = blocks.shape[0], blocks.shape[1]
    rows, depth = tokens.shape
    width = upstream.shape[1]
    half_slots = slots // 2
    part_width = depth // 4
    at_z, half = lax.axis_index("dp"), lax.axis_index("groups")
    at_tensor, at_replica = lax.axis_index("tensor"), lax.axis_index("replica")
    middle = (at_z == 1) | (at_z == 2)
    place_of = jnp.stack([middle.astype(jnp.int32), half, at_tensor, at_replica])
    along = functools.partial(lax.ppermute, axis_name="dp")
    across = functools.partial(lax.ppermute, axis_name="groups", perm=SWAP)
    sideways = functools.partial(lax.ppermute, axis_name="tensor", perm=SWAP)
    cores = functools.partial(lax.ppermute, axis_name="replica", perm=SWAP)
    stage = lax.optimization_barrier

    mine = lax.dynamic_slice_in_dim(blocks, half * half_slots, half_slots, 0)
    mine = jnp.concatenate([mine, ids_block(block_ids, size).astype(jnp.bfloat16)])
    mine, late_blocks = stage((mine, blocks))

    near_a = along(mine, perm=INWARD)
    far_a = along(mine, perm=MIDDLE)
    other = lax.dynamic_slice_in_dim(late_blocks, (1 - half) * half_slots, half_slots, 0)
    part = lax.dynamic_slice_in_dim(tokens, lax.axis_index(INNER) * part_width, part_width, 1)
    both = jnp.concatenate([part, upstream])
    grads = line_grads(block_ids, ((tokens, upstream),), None, size)
    near_a, far_a, both, other, grads = stage((near_a, far_a, both, other, grads))

    end_a = along(near_a, perm=MIDDLE)
    far_b = across(far_a)
    both_1 = along(both, perm=PAIRS)
    both_1, end_a, far_b, both, other = stage((both_1, end_a, far_b, both, other))
    upstream_1 = both_1[rows:]

    near_b = along(other, perm=INWARD)
    end_b = across(end_a)
    both_2m = along(both, perm=MIDDLE)
    tokens_1 = lax.all_gather(both_1[:rows], INNER)
    ids_1, ids_2, ids_3 = (ids_of(piece, slots) for piece in (near_a, far_a, end_a))
    partial, turned = place_first(
        place_of, (block_ids, ids_1, ids_2, ids_3), (blocks, near_a, far_a, far_b, end_a), depth, width
    )
    near_b, end_b, both_2m, both_1, tokens_1, partial, turned = stage(
        (near_b, end_b, both_2m, both_1, tokens_1, partial, turned)
    )

    both_3m = along(both_1, perm=MIDDLE)
    both_2o = along(both_2m, perm=OUTWARD)
    last = (near_b, end_b)
    end_keep, own_keep, own_give, *end_give = project_back(
        place_of, ids_1, ids_3, turned, *last, upstream_1, upstream
    )
    end_keep, end_give = add_split(place_of, end_keep, *[cores(a) for a in end_give])
    end_keep, end_give, own_give, both_3m, both_2o = stage(
        (end_keep, end_give, own_give, both_3m, both_2o)
    )

    end_got = sideways(end_give)
    own_keep, own_give = add_split(place_of, own_keep, cores(own_give))
    both_3o = along(both_3m, perm=OUTWARD)
    tokens_2 = lax.all_gather(both_2m[:rows] + both_2o[:rows], INNER)
    proj, end_proj = project_forward(place_of, ids_1, ids_3, partial, *last, tokens, tokens_1)
    end_got, own_give, own_keep, proj, end_proj, both_3m = stage(
        (end_got, own_give, own_keep, proj, end_proj, both_3m)
    )

    sum_out = along(end_keep + end_got, perm=OUTWARD)
    own_got = sideways(own_give)
    grads = line_grads(block_ids, ((tokens_1, upstream_1),), grads, size)
    tokens_3 = lax.all_gather(both_3m[:rows] + both_3o[:rows], INNER)
    grads = line_grads(block_ids, ((tokens_2, both_2m, both_2o),), grads, size)
    sum_out, own_got, grads = stage((sum_out, own_got, grads))

    quarter = jnp.where(middle, own_keep + own_got, sum_out)
    proj_out = along(end_proj, perm=OUTWARD)
    grads = line_grads(block_ids, ((tokens_3, both_3m, both_3o),), grads, size)
    by_tensor, by_core, grads = stage((sideways(quarter), cores(quarter), grads))
    by_both = cores(by_tensor)
    projected = jnp.where(middle, proj, proj_out)
    token_grad = assemble(place_of, (quarter, by_core, by_tensor, by_both))
    return projected, token_grad, grads


def solution(mesh):
    line = tuple(mesh.shape[a] for a in ("groups", "dp", "tensor", "replica")) == (2, 4, 2, 2)
    return jax.shard_map(
        line_body if line else general_body,
        mesh=mesh,
        in_specs=(
            P(("groups", "dp"), None),
            P(("groups", "dp"), INNER),
            P(("dp",) + INNER, None, None),
            P(("dp",) + INNER),
        ),
        out_specs=(
            P(("groups", "dp"), INNER),
            P(("groups", "dp"), None),
            P(("groups", "dp") + INNER, None, None),
        ),
        check_vma=False,
    )
```
